32 devices in a mesh: grp: 4 (over z), fsdp: 4 (over x, core), tp: 2 (over y).
Axes of the slice: x: 2, y: 2, z: 4, core: 2. Of those that a mesh axis runs over, the one named last changes fastest.
Arguments:
- hidden_in: bfloat16 [6144, 1024], P(('grp', 'fsdp', 'tp')), may hold values from -6 to 6
- lengths: int32 [16], P(('grp', 'fsdp')), may hold values from 96 to 384, as said below
- norm1_gain: float32 [1024], replicated, may hold values from 0.1 to 1.9
- w_query: bfloat16 [1024, 512], P('fsdp', 'tp'), may hold values from -0.1875 to 0.1875
- key_weight: bfloat16 [1024, 128], P('fsdp', 'tp'), may hold values from -0.1875 to 0.1875
- value_weight: bfloat16 [1024, 128], P('fsdp', 'tp'), may hold values from -0.1875 to 0.1875
- w_attn_out: bfloat16 [1024, 512], P('fsdp', 'tp'), may hold values from -0.75 to 0.75
- w_mamba_z: bfloat16 [1024, 1536], P('fsdp', 'tp'), may hold values from -0.1875 to 0.1875
- w_mamba_x: bfloat16 [1024, 1536], P('fsdp', 'tp'), may hold values from -0.1875 to 0.1875
- w_step: bfloat16 [1024, 24], P('fsdp', 'tp'), may hold values from -0.1875 to 0.1875
- w_shared: bfloat16 [1024, 256], replicated, may hold values from -0.1875 to 0.1875
- conv_main: float32 [4, 1536], replicated, may hold values from -3 to 3
- conv_shared: float32 [4, 256], replicated, may hold values from -3 to 3
- decay_log: float32 [24], replicated, may hold values from -4 to 0.5
- step_bias: float32 [24], replicated, may hold values from -4.5 to -2
- skip_gain: float32 [24], replicated, may hold values from 0.5 to 1.5
- w_mamba_out: bfloat16 [1024, 1536], P('fsdp', 'tp'), may hold values from -0.25 to 0.25
- norm2_gain: float32 [1024], replicated, may hold values from 0.1 to 1.9
- w_ffn_gate: bfloat16 [1024, 2048], P('fsdp', 'tp'), may hold values from -0.1875 to 0.1875
- w_ffn_up: bfloat16 [1024, 2048], P('fsdp', 'tp'), may hold values from -0.1875 to 0.1875
- w_ffn_down: bfloat16 [1024, 2048], P('fsdp', 'tp'), may hold values from -0.1875 to 0.1875
- out_grad: bfloat16 [6144, 1024], P(('grp', 'fsdp', 'tp')), may hold values from -6 to 6
Outputs:
- output: bfloat16 [6144, 1024], P(('grp', 'fsdp', 'tp'))
- grad_in: bfloat16 [6144, 1024], P(('grp', 'fsdp', 'tp'))
- grad_norm1: float32 [1024], replicated
- grad_query: float32 [1024, 512], P(('grp', 'fsdp'), 'tp')
- grad_key: float32 [1024, 128], P(('grp', 'fsdp'), 'tp')
- grad_value: float32 [1024, 128], P(('grp', 'fsdp'), 'tp')
- grad_attn_out: float32 [1024, 512], P(('grp', 'fsdp'), 'tp')
- grad_mamba_z: float32 [1024, 1536], P(('grp', 'fsdp'), 'tp')
- grad_mamba_x: float32 [1024, 1536], P(('grp', 'fsdp'), 'tp')
- grad_step: float32 [1024, 24], P(('grp', 'fsdp'), 'tp')
- grad_shared: float32 [1024, 256], replicated
- grad_conv_main: float32 [4, 1536], replicated
- grad_conv_shared: float32 [4, 256], replicated
- grad_decay_log: float32 [24], replicated
- grad_step_bias: float32 [24], replicated
- grad_skip_gain: float32 [24], replicated
- grad_mamba_out: float32 [1024, 1536], P(('grp', 'fsdp'), 'tp')
- grad_norm2: float32 [1024], replicated
- grad_ffn_gate: float32 [1024, 2048], P(('grp', 'fsdp'), 'tp')
- grad_ffn_up: float32 [1024, 2048], P(('grp', 'fsdp'), 'tp')
- grad_ffn_down: float32 [1024, 2048], P(('grp', 'fsdp'), 'tp')
The draws below stay inside these ranges and needn't reach their ends.
Inputs may be any that keep to these rules, and one draw needn't show every extreme that they name: `lengths`: each sequence's valid slots come first; some sequence has all 384 slots valid.
All inputs are finite; a program needn't handle non-finite values.
Results may differ from the reference program's by a relative error of at most 0.011.
Values may be sent and summed in bfloat16 or wider, within the bound.
A program may use at most 128 MiB of HBM per device.

```python
import math
from functools import partial
import jax
import jax.numpy as jnp
from jax import lax

MODEL_DIMENSION = 1024
QUERY_HEADS = 8
KEY_VALUE_HEADS = 2
HEAD_DIMENSION = 64
HM = 24
NSTATE = 128
FF = 2048
CONV = 4
BLOCK = 128
SEQUENCE_SLOTS = 384
DI = 1536
SEQS = 16
TOKENS = 6144


def draw_lengths(key, part):
    first_key, second_key = jax.random.split(key)
    counts = jax.random.randint(first_key, (SEQS,), SEQUENCE_SLOTS // 4, SEQUENCE_SLOTS + 1)
    longest = jax.random.randint(second_key, (), 0, SEQS)
    return jnp.where(jnp.arange(SEQS) == longest, SEQUENCE_SLOTS, counts).astype(jnp.int32)


def shard_levels(rng, extent, cuts, least, high):
    loudness = 1.0
    for position, shards_of in cuts:
        heights = jax.random.uniform(jax.random.fold_in(jax.random.fold_in(rng, 6), position), (shards_of,), jnp.float32, least / len(cuts), high / len(cuts))
        loudness = loudness * jnp.repeat(jnp.exp(heights), extent[position] // shards_of).reshape((-1,) + (1,) * (len(extent) - 1 - position))
    return loudness


def bell_draw(rng, extent, deviation, bound, shards=(), dtype=jnp.bfloat16):
    factor_of = shard_levels(rng, extent, shards, -0.22, 0.18) if shards else 1.0
    values = jax.random.normal(rng, extent, jnp.float32) * deviation * factor_of
    return jnp.minimum(jnp.maximum(values, -bound), bound).astype(dtype)


def setup_inputs(seed: int = 0) -> dict:
    seeds = jax.random.split(jax.random.key(seed), 23)
    hidden_in = bell_draw(seeds[0], (TOKENS, MODEL_DIMENSION), 1.0, 6.0, ((0, 32),))
    lengths = draw_lengths(jax.random.fold_in(seeds[22], 71), 0)
    norm1_gain = jnp.clip(1.0 + 0.18 * jax.random.normal(seeds[2], (MODEL_DIMENSION,), jnp.float32), 0.1, 1.9)
    w_query = bell_draw(seeds[3], (MODEL_DIMENSION, QUERY_HEADS * HEAD_DIMENSION), MODEL_DIMENSION ** -0.5, 0.1875, ((0, 4), (1, 2)))
    key_weight = bell_draw(seeds[4], (MODEL_DIMENSION, KEY_VALUE_HEADS * HEAD_DIMENSION), MODEL_DIMENSION ** -0.5, 0.1875, ((0, 4), (1, 2)))
    value_weight = bell_draw(seeds[5], (MODEL_DIMENSION, KEY_VALUE_HEADS * HEAD_DIMENSION), MODEL_DIMENSION ** -0.5, 0.1875, ((0, 4), (1, 2)))
    w_attn_out = bell_draw(seeds[6], (MODEL_DIMENSION, QUERY_HEADS * HEAD_DIMENSION), 64 ** -0.5, 0.75, ((0, 4), (1, 2)))
    w_mamba_z = bell_draw(seeds[7], (MODEL_DIMENSION, DI), MODEL_DIMENSION ** -0.5, 0.1875, ((0, 4), (1, 2)))
    w_mamba_x = bell_draw(seeds[8], (MODEL_DIMENSION, DI), MODEL_DIMENSION ** -0.5, 0.1875, ((0, 4), (1, 2)))
    w_step = bell_draw(seeds[9], (MODEL_DIMENSION, HM), MODEL_DIMENSION ** -0.5, 0.1875, ((0, 4), (1, 2)))
    w_shared = bell_draw(seeds[10], (MODEL_DIMENSION, 2 * NSTATE), MODEL_DIMENSION ** -0.5, 0.1875)
    conv_main = bell_draw(seeds[11], (CONV, DI), CONV ** -0.5, 3.0, (), jnp.float32)
    conv_shared = bell_draw(seeds[12], (CONV, 2 * NSTATE), CONV ** -0.5, 3.0, (), jnp.float32)
    decay_log = jnp.clip(jax.random.uniform(seeds[13], (HM,), jnp.float32, -4.0, 0.5), -4.0, 0.5)
    step_bias = jnp.clip(jax.random.uniform(seeds[14], (HM,), jnp.float32, -4.5, -2.0), -4.5, -2.0)
    skip_gain = jnp.clip(jax.random.uniform(seeds[15], (HM,), jnp.float32, 0.5, 1.5), 0.5, 1.5)
    w_mamba_out = bell_draw(seeds[16], (MODEL_DIMENSION, DI), (DI // 3) ** -0.5, 0.25, ((0, 4), (1, 2)))
    norm2_gain = jnp.clip(1.0 + 0.18 * jax.random.normal(seeds[17], (MODEL_DIMENSION,), jnp.float32), 0.1, 1.9)
    w_ffn_gate = bell_draw(seeds[18], (MODEL_DIMENSION, FF), MODEL_DIMENSION ** -0.5, 0.1875, ((0, 4), (1, 2)))
    w_ffn_up = bell_draw(seeds[19], (MODEL_DIMENSION, FF), MODEL_DIMENSION ** -0.5, 0.1875, ((0, 4), (1, 2)))
    w_ffn_down = bell_draw(seeds[20], (MODEL_DIMENSION, FF), (FF // 2) ** -0.5, 0.1875, ((0, 4), (1, 2)))
    out_grad = bell_draw(seeds[21], (TOKENS, MODEL_DIMENSION), 1.0, 6.0, ((0, 32),))
    return dict(hidden_in=hidden_in, lengths=lengths, norm1_gain=norm1_gain, w_query=w_query, key_weight=key_weight, value_weight=value_weight, w_attn_out=w_attn_out, w_mamba_z=w_mamba_z, w_mamba_x=w_mamba_x, w_step=w_step, w_shared=w_shared, conv_main=conv_main, conv_shared=conv_shared, decay_log=decay_log, step_bias=step_bias, skip_gain=skip_gain, w_mamba_out=w_mamba_out, norm2_gain=norm2_gain, w_ffn_gate=w_ffn_gate, w_ffn_up=w_ffn_up, w_ffn_down=w_ffn_down, out_grad=out_grad)


@jax.custom_vjp
def reduced_cast(v):
    return lax.optimization_barrier(v.astype(jnp.bfloat16)).astype(jnp.float32)

@jax.custom_vjp
def reduced_cast_backward(v):
    return v

def low_keep(v):
    return (reduced_cast(v), None)

def low_pass(kept, grad):
    return (grad,)

def back_keep(v):
    return (v, None)

def back_low(kept, grad):
    return (reduced_cast(grad),)
reduced_cast.defvjp(low_keep, low_pass)
reduced_cast_backward.defvjp(back_keep, back_low)
top_precision = lax.Precision.HIGHEST
norm_eps = 1e-05
rope_base = 100000000000.0

def precise_product(first_mat, second_mat):
    return jnp.dot(first_mat, second_mat, precision=top_precision, preferred_element_type=jnp.float32)

def rms_scale(values):
    return lax.rsqrt(lax.optimization_barrier(jnp.mean(values * values, axis=-1, keepdims=True)) + norm_eps)

def angles(length_total, head_size):
    positions = jnp.arange(length_total).astype(jnp.float32)[:, None]
    exponent = jnp.arange(head_size // 2).astype(jnp.float32) * (-2.0 / head_size)
    phase = positions * jnp.power(rope_base, exponent)[None, :]
    return (jnp.cos(phase)[:, None, :], jnp.sin(phase)[:, None, :])

def apply_rotary(values, rotary_cosine, rotary_sine):
    half_dim = values.shape[-1] // 2
    first_half = values[..., :half_dim]
    second_half = values[..., half_dim:]
    return jnp.concatenate([first_half * rotary_cosine - second_half * rotary_sine, second_half * rotary_cosine + first_half * rotary_sine], axis=-1)

def causal_conv(values, kernel):
    kernel_width = kernel.shape[0]
    length_total = values.shape[0]
    padded = jnp.pad(values, ((kernel_width - 1, 0), (0, 0)))
    result = kernel[kernel_width - 1] * values
    for offset in range(kernel_width - 1):
        result = result + kernel[offset] * padded[offset:offset + length_total]
    return result

def state_scan(x_heads, step_sizes, rates, b_matrix, c_matrix):
    length_total, head_count, head_size = x_heads.shape
    nstate = b_matrix.shape[1]
    blocks = length_total // BLOCK
    xs_blk = x_heads.reshape(blocks, BLOCK, head_count, head_size)
    step_blk = step_sizes.reshape(blocks, BLOCK, head_count)
    b_blk = b_matrix.reshape(blocks, BLOCK, nstate)
    c_blk = c_matrix.reshape(blocks, BLOCK, nstate)
    cumulative = jnp.cumsum(step_blk * rates, axis=1)
    index_t = jnp.arange(BLOCK)
    causal = (index_t[:, None] >= index_t[None, :])[None, :, :, None]
    log_gaps = cumulative[:, :, None, :] - cumulative[:, None, :, :]
    decay_mat = jnp.where(causal, jnp.exp(jnp.where(causal, log_gaps, 0.0)), 0.0)
    inner_prod = jnp.einsum('ctn,csn->cts', c_blk, b_blk, precision=top_precision)
    mixing = decay_mat * inner_prod[:, :, :, None] * step_blk[:, None, :, :]
    within = jnp.einsum('ctsh,cshp->cthp', mixing, xs_blk, precision=top_precision)
    tail_weight = jnp.exp(cumulative[:, -1:, :] - cumulative) * step_blk
    states = jnp.einsum('csh,csn,cshp->chpn', tail_weight, b_blk, xs_blk, precision=top_precision)
    fading = jnp.exp(cumulative[:, -1, :])

    def advance(state_carry, pieces):
        fade_now, state_now = pieces
        return (fade_now[:, None, None] * state_carry + state_now, state_carry)
    _, before = lax.scan(advance, jnp.zeros((head_count, head_size, nstate), jnp.float32), (fading, states))
    across = jnp.einsum('ctn,chpn->cthp', c_blk, before, precision=top_precision) * jnp.exp(cumulative)[:, :, :, None]
    return (within + across).reshape(length_total, head_count, head_size)

def mamba_mix(gate_in, main_in, shared_in, step_in, kernel_main, kernel_shared, decay_rates, bias_step, skip_terms, valid_rows):
    length_total = main_in.shape[0]
    head_count = step_in.shape[1]
    head_size = main_in.shape[1] // head_count
    nstate = shared_in.shape[1] // 2
    main_conv = jax.nn.silu(causal_conv(main_in, kernel_main))
    shared_conv = jax.nn.silu(causal_conv(shared_in, kernel_shared))
    step_sizes = jax.nn.softplus(step_in + bias_step) * valid_rows
    x_heads = main_conv.reshape(length_total, head_count, head_size)
    scanned = state_scan(x_heads, step_sizes, -jnp.exp(decay_rates), shared_conv[:, :nstate], shared_conv[:, nstate:])
    output_heads = scanned + skip_terms[:, None] * x_heads
    return output_heads.reshape(length_total, head_count * head_size) * jax.nn.silu(gate_in)

def layer_seq(params, values, count):
    norm1_gain, w_query, key_weight, value_weight, w_attn_out, w_mamba_z, w_mamba_x, w_step, w_shared, conv_main, conv_shared, decay_log, step_bias, skip_gain, w_mamba_out, norm2_gain, w_ffn_gate, w_ffn_up, w_ffn_down = params
    positions = jnp.arange(SEQUENCE_SLOTS)
    valid_rows = (positions < count).astype(jnp.float32)[:, None]
    first_normalized = reduced_cast(values * rms_scale(values) * norm1_gain)
    query_projected = reduced_cast_backward(precise_product(first_normalized, w_query)).reshape(SEQUENCE_SLOTS, QUERY_HEADS, HEAD_DIMENSION)
    key_projected = reduced_cast_backward(precise_product(first_normalized, key_weight)).reshape(SEQUENCE_SLOTS, KEY_VALUE_HEADS, HEAD_DIMENSION)
    value_reduced = reduced_cast(reduced_cast_backward(precise_product(first_normalized, value_weight))).reshape(SEQUENCE_SLOTS, KEY_VALUE_HEADS, HEAD_DIMENSION)
    rotary_cosine, rotary_sine = angles(SEQUENCE_SLOTS, HEAD_DIMENSION)
    query_rotated = reduced_cast(apply_rotary(query_projected, rotary_cosine, rotary_sine)).reshape(SEQUENCE_SLOTS, KEY_VALUE_HEADS, QUERY_HEADS // KEY_VALUE_HEADS, HEAD_DIMENSION)
    key_rot = reduced_cast(apply_rotary(key_projected, rotary_cosine, rotary_sine))
    scores = reduced_cast_backward(jnp.einsum('qkgd,skd->kgqs', query_rotated, key_rot, precision=top_precision) * HEAD_DIMENSION ** (-0.5))
    allowed = (positions[:, None] >= positions[None, :]) & (positions[None, :] < count)
    probs = reduced_cast(jax.nn.softmax(jnp.where(allowed, scores, -1e+30), axis=-1))
    attn = jnp.einsum('kgqs,skd->qkgd', probs, value_reduced, precision=top_precision).reshape(SEQUENCE_SLOTS, QUERY_HEADS * HEAD_DIMENSION)
    attn_low = reduced_cast(reduced_cast_backward(attn))
    gate_proj = reduced_cast_backward(precise_product(first_normalized, w_mamba_z))
    main_proj = reduced_cast_backward(precise_product(first_normalized, w_mamba_x))
    step_proj = reduced_cast_backward(precise_product(first_normalized, w_step))
    shared_proj = precise_product(first_normalized, w_shared)
    mamba_low = reduced_cast(mamba_mix(gate_proj, main_proj, shared_proj, step_proj, conv_main, conv_shared, decay_log, step_bias, skip_gain, valid_rows))
    mixed = reduced_cast_backward(precise_product(attn_low, w_attn_out.T) + precise_product(mamba_low, w_mamba_out.T))
    resid_mid = values + mixed
    normed2 = reduced_cast(resid_mid * rms_scale(resid_mid) * norm2_gain)
    gate_pre = reduced_cast_backward(precise_product(normed2, w_ffn_gate))
    up_pre = reduced_cast_backward(precise_product(normed2, w_ffn_up))
    hidden_low = reduced_cast(jax.nn.silu(gate_pre) * up_pre)
    ffn_out = reduced_cast_backward(precise_product(hidden_low, w_ffn_down.T))
    return (resid_mid + ffn_out) * valid_rows

def reference(hidden_in, lengths, norm1_gain, w_query, key_weight, value_weight, w_attn_out, w_mamba_z, w_mamba_x, w_step, w_shared, conv_main, conv_shared, decay_log, step_bias, skip_gain, w_mamba_out, norm2_gain, w_ffn_gate, w_ffn_up, w_ffn_down, out_grad):
    params = tuple((item.astype(jnp.float32) for item in (norm1_gain, w_query, key_weight, value_weight, w_attn_out, w_mamba_z, w_mamba_x, w_step, w_shared, conv_main, conv_shared, decay_log, step_bias, skip_gain, w_mamba_out, norm2_gain, w_ffn_gate, w_ffn_up, w_ffn_down)))
    group_size = math.gcd(SEQS, max(1, 4096 // SEQUENCE_SLOTS))
    group_count = SEQS // group_size
    values_all = hidden_in.astype(jnp.float32).reshape(group_count, group_size, SEQUENCE_SLOTS, MODEL_DIMENSION)
    counts = lengths.astype(jnp.int32).reshape(group_count, group_size)

    def forward(weights, inputs):

        def group_step(state_carry, pieces):
            block_vals, block_counts = pieces
            outputs = jax.vmap(partial(layer_seq, weights))(block_vals, block_counts)
            return (state_carry, outputs)
        _, stacked = lax.scan(jax.checkpoint(group_step), jnp.zeros((), jnp.float32), (inputs, counts))
        return stacked
    result, pullback = jax.vjp(forward, params, values_all)
    weight_grads, input_grads = pullback(out_grad.astype(jnp.float32).reshape(group_count, group_size, SEQUENCE_SLOTS, MODEL_DIMENSION))
    output = result.reshape(TOKENS, MODEL_DIMENSION).astype(jnp.bfloat16)
    grad_in = input_grads.reshape(TOKENS, MODEL_DIMENSION).astype(jnp.bfloat16)
    return (output, grad_in, weight_grads[0], weight_grads[1], weight_grads[2], weight_grads[3], weight_grads[4], weight_grads[5], weight_grads[6], weight_grads[7], weight_grads[8], weight_grads[9], weight_grads[10], weight_grads[11], weight_grads[12], weight_grads[13], weight_grads[14], weight_grads[15], weight_grads[16], weight_grads[17], weight_grads[18])
```

```python
from functools import partial

import jax
import jax.numpy as jnp
from jax import lax
from jax.sharding import PartitionSpec as P

HEAD_DIMENSION = 64
BLOCK = 128


top_precision = lax.Precision.HIGHEST
norm_eps = 1e-05
rope_base = 100000000000.0


def for_sending(shard):

    def short(part):
        return part.astype(jnp.bfloat16) if part.dtype == jnp.float32 else part

    return jax.tree.map(short, shard)


def dot_nt(first_mat, second_mat):
    return lax.dot_general(
        first_mat, second_mat, (((1,), (1,)), ((), ())), preferred_element_type=jnp.float32
    )


def dot_tn(first_mat, second_mat):
    return lax.dot_general(
        first_mat, second_mat, (((0,), (0,)), ((), ())), preferred_element_type=jnp.float32
    )


def rms_scale(values):
    return lax.rsqrt(jnp.mean(values * values, axis=-1, keepdims=True) + norm_eps)


def angles(length_total, head_size):
    positions = jnp.arange(length_total).astype(jnp.float32)[:, None]
    exponent = jnp.arange(head_size // 2).astype(jnp.float32) * (-2.0 / head_size)
    phase = positions * jnp.power(rope_base, exponent)[None, :]
    return (jnp.cos(phase)[:, None, :], jnp.sin(phase)[:, None, :])


def apply_rotary(values, rotary_cosine, rotary_sine):
    half_dim = values.shape[-1] // 2
    first_half = values[..., :half_dim]
    second_half = values[..., half_dim:]
    return jnp.concatenate(
        [
            first_half * rotary_cosine - second_half * rotary_sine,
            second_half * rotary_cosine + first_half * rotary_sine,
        ],
        axis=-1,
    )


def rotate_back(grads, rotary_cosine, rotary_sine):
    half_dim = grads.shape[-1] // 2
    first_half = grads[..., :half_dim]
    second_half = grads[..., half_dim:]
    return jnp.concatenate(
        [
            first_half * rotary_cosine + second_half * rotary_sine,
            second_half * rotary_cosine - first_half * rotary_sine,
        ],
        axis=-1,
    )


def causal_conv(values, kernel):
    kernel_width = kernel.shape[0]
    length_total = values.shape[0]
    padded = jnp.pad(values, ((kernel_width - 1, 0), (0, 0)))
    result = kernel[kernel_width - 1] * values
    for offset in range(kernel_width - 1):
        result = result + kernel[offset] * padded[offset : offset + length_total]
    return result


def state_scan(x_heads, step_sizes, rates, b_matrix, c_matrix):
    length_total, head_count, head_size = x_heads.shape
    nstate = b_matrix.shape[1]
    blocks = length_total // BLOCK
    xs_blk = x_heads.reshape(blocks, BLOCK, head_count, head_size)
    step_blk = step_sizes.reshape(blocks, BLOCK, head_count)
    b_blk = b_matrix.reshape(blocks, BLOCK, nstate)
    c_blk = c_matrix.reshape(blocks, BLOCK, nstate)
    index_t = jnp.arange(BLOCK)
    lower = (index_t[:, None] >= index_t[None, :]).astype(jnp.float32)
    cumulative = jnp.einsum("ts,csh->cth", lower, step_blk * rates, precision=top_precision)
    causal = (index_t[:, None] >= index_t[None, :])[None, :, :, None]
    log_gaps = cumulative[:, :, None, :] - cumulative[:, None, :, :]
    decay_mat = jnp.where(causal, jnp.exp(jnp.where(causal, log_gaps, 0.0)), 0.0)
    inner_prod = jnp.einsum("ctn,csn->cts", c_blk, b_blk, precision=top_precision)
    mixing = decay_mat * inner_prod[:, :, :, None] * step_blk[:, None, :, :]
    within = jnp.einsum("ctsh,cshp->cthp", mixing, xs_blk, precision=top_precision)
    tail_weight = jnp.exp(cumulative[:, -1:, :] - cumulative) * step_blk
    states = jnp.einsum("csh,csn,cshp->chpn", tail_weight, b_blk, xs_blk, precision=top_precision)
    fading = jnp.exp(cumulative[:, -1, :])

    def advance(state_carry, pieces):
        fade_now, state_now = pieces
        return (fade_now[:, None, None] * state_carry + state_now, state_carry)

    _, before = lax.scan(
        advance, jnp.zeros((head_count, head_size, nstate), jnp.float32), (fading, states)
    )
    across = (
        jnp.einsum("ctn,chpn->cthp", c_blk, before, precision=top_precision)
        * jnp.exp(cumulative)[:, :, :, None]
    )
    return (within + across).reshape(length_total, head_count, head_size)


def mamba_mix(
    gate_in,
    main_in,
    shared_in,
    step_in,
    kernel_main,
    kernel_shared,
    decay_rates,
    bias_step,
    skip_terms,
    valid_rows,
):
    length_total = main_in.shape[0]
    head_count = step_in.shape[1]
    head_size = main_in.shape[1] // head_count
    nstate = shared_in.shape[1] // 2
    main_conv = jax.nn.silu(causal_conv(main_in, kernel_main))
    shared_conv = jax.nn.silu(causal_conv(shared_in, kernel_shared))
    step_sizes = jax.nn.softplus(step_in + bias_step) * valid_rows
    x_heads = main_conv.reshape(length_total, head_count, head_size)
    scanned = state_scan(
        x_heads, step_sizes, -jnp.exp(decay_rates), shared_conv[:, :nstate], shared_conv[:, nstate:]
    )
    output_heads = scanned + skip_terms[:, None] * x_heads
    return output_heads.reshape(length_total, head_count * head_size) * jax.nn.silu(gate_in)


def gather_weights(weights):
    return jax.tree.map(
        lambda part, own: part.astype(own.dtype),
        lax.all_gather(for_sending(weights), "fsdp", axis=0, tiled=True),
        weights,
    )


def reduce_weight_grads(terms):
    return [
        lax.psum_scatter(
            term.astype(jnp.bfloat16), ("grp", "fsdp"), scatter_dimension=0, tiled=True
        ).astype(jnp.float32)
        for term in terms
    ]


def local(
    hidden_in,
    lengths,
    norm1_gain,
    w_query,
    key_weight,
    value_weight,
    w_attn_out,
    w_mamba_z,
    w_mamba_x,
    w_step,
    w_shared,
    conv_main,
    conv_shared,
    decay_log,
    step_bias,
    skip_gain,
    w_mamba_out,
    norm2_gain,
    w_ffn_gate,
    w_ffn_up,
    w_ffn_down,
    out_grad,
):
    tp_count = lax.axis_size("tp")
    tp_rank = lax.axis_index("tp")
    own_rows = hidden_in.shape[0]
    seq_len = own_rows * tp_count
    model_width = hidden_in.shape[1]
    valid_count = lengths[0]
    positions = jnp.arange(seq_len, dtype=jnp.int32)
    valid_full = (positions < valid_count).astype(jnp.float32)[:, None]
    valid_own = lax.dynamic_slice_in_dim(valid_full, tp_rank * own_rows, own_rows, 0)
    resid_in = hidden_in.astype(jnp.float32)
    scale_one = rms_scale(resid_in)
    first_normalized = (resid_in * scale_one * norm1_gain).astype(jnp.bfloat16)
    top_grad = out_grad.astype(jnp.float32) * valid_own
    top_grad_low = top_grad.astype(jnp.bfloat16)
    normed1_all, top_grad_all = (
        lax.all_gather(first_normalized, "tp", axis=0, tiled=True),
        lax.all_gather(top_grad_low, "tp", axis=0, tiled=True),
    )
    mixer_full = gather_weights(
        (w_query, key_weight, value_weight, w_attn_out, w_mamba_z, w_mamba_x, w_step, w_mamba_out)
    )
    ffn_full = gather_weights((w_ffn_gate, w_ffn_up, w_ffn_down))
    wq_all, wk_all, wv_all, wo_all, wz_all, wx_all, wdt_all, wout_all = mixer_full
    q_local = wq_all.shape[1] // HEAD_DIMENSION
    kv_local = wk_all.shape[1] // HEAD_DIMENSION
    grouping = q_local // kv_local
    attn_scale = HEAD_DIMENSION ** (-0.5)
    rotary_cosine, rotary_sine = angles(seq_len, HEAD_DIMENSION)
    query_projected = jnp.dot(normed1_all, wq_all, preferred_element_type=jnp.float32)
    key_projected = jnp.dot(normed1_all, wk_all, preferred_element_type=jnp.float32)
    value_proj = jnp.dot(normed1_all, wv_all, preferred_element_type=jnp.float32)
    query_rotated = apply_rotary(
        query_projected.reshape(seq_len, q_local, HEAD_DIMENSION), rotary_cosine, rotary_sine
    ).astype(jnp.bfloat16)
    key_rot = apply_rotary(
        key_projected.reshape(seq_len, kv_local, HEAD_DIMENSION), rotary_cosine, rotary_sine
    ).astype(jnp.bfloat16)
    value_reduced = value_proj.astype(jnp.bfloat16).reshape(seq_len, kv_local, HEAD_DIMENSION)
    query_grp = query_rotated.reshape(seq_len, kv_local, grouping, HEAD_DIMENSION)
    score_raw = (
        jnp.einsum("qkgd,skd->kgqs", query_grp, key_rot, preferred_element_type=jnp.float32)
        * attn_scale
    )
    allowed = (positions[:, None] >= positions[None, :]) & (positions[None, :] < valid_count)
    masked = jnp.where(allowed, score_raw, -1e30)
    peak_score = jnp.max(masked, axis=-1, keepdims=True)
    expo_score = jnp.exp(masked - peak_score)
    probs = expo_score / jnp.sum(expo_score, axis=-1, keepdims=True)
    probs_low = probs.astype(jnp.bfloat16)
    attn_heads = jnp.einsum(
        "kgqs,skd->qkgd", probs_low, value_reduced, preferred_element_type=jnp.float32
    )
    attn_low = attn_heads.reshape(seq_len, q_local * HEAD_DIMENSION).astype(jnp.bfloat16)
    heads_local = wdt_all.shape[1]
    inner_local = wx_all.shape[1]
    gate_proj = jnp.dot(normed1_all, wz_all, preferred_element_type=jnp.float32)
    main_proj = jnp.dot(normed1_all, wx_all, preferred_element_type=jnp.float32)
    step_proj = jnp.dot(normed1_all, wdt_all, preferred_element_type=jnp.float32)
    shared_proj = jnp.dot(normed1_all, w_shared, preferred_element_type=jnp.float32)
    kernel_local = lax.dynamic_slice_in_dim(conv_main, tp_rank * inner_local, inner_local, 1)
    decay_local = lax.dynamic_slice_in_dim(decay_log, tp_rank * heads_local, heads_local, 0)
    bias_local = lax.dynamic_slice_in_dim(step_bias, tp_rank * heads_local, heads_local, 0)
    skip_local = lax.dynamic_slice_in_dim(skip_gain, tp_rank * heads_local, heads_local, 0)
    mamba_out, mamba_pull = jax.vjp(
        partial(mamba_mix, valid_rows=valid_full),
        gate_proj,
        main_proj,
        shared_proj,
        step_proj,
        kernel_local,
        conv_shared,
        decay_local,
        bias_local,
        skip_local,
    )
    mamba_low = mamba_out.astype(jnp.bfloat16)
    mix_part = dot_nt(attn_low, wo_all) + dot_nt(mamba_low, wout_all)
    mixed = lax.psum_scatter(mix_part, "tp", scatter_dimension=0, tiled=True)
    resid_mid = resid_in + mixed
    scale_two = rms_scale(resid_mid)
    normed2 = (resid_mid * scale_two * norm2_gain).astype(jnp.bfloat16)
    normed2_all = lax.all_gather(normed2, "tp", axis=0, tiled=True)
    wg_all, wu_all, wd_all = ffn_full
    gate_pre = jnp.dot(normed2_all, wg_all, preferred_element_type=jnp.float32)
    up_pre = jnp.dot(normed2_all, wu_all, preferred_element_type=jnp.float32)
    sigma_gate = jax.nn.sigmoid(gate_pre)
    silu_gate = gate_pre * sigma_gate
    hidden_low = (silu_gate * up_pre).astype(jnp.bfloat16)
    ffn_part = dot_nt(hidden_low, wd_all)
    ffn_sum = lax.psum_scatter(
        ffn_part.astype(jnp.bfloat16), "tp", scatter_dimension=0, tiled=True
    ).astype(jnp.float32)
    output = ((resid_mid + ffn_sum) * valid_own).astype(jnp.bfloat16)
    ffn_back = ffn_full
    wg_back, wu_back, wd_back = ffn_back
    hidden_grad = jnp.dot(top_grad_all, wd_back, preferred_element_type=jnp.float32)
    silu_slope = sigma_gate * (1.0 + gate_pre * (1.0 - sigma_gate))
    gate_grad = (hidden_grad * up_pre * silu_slope).astype(jnp.bfloat16)
    up_grad = (hidden_grad * silu_gate).astype(jnp.bfloat16)

    ffn_grads = reduce_weight_grads(
        [
            dot_tn(normed2_all, gate_grad),
            dot_tn(normed2_all, up_grad),
            dot_tn(top_grad_all, hidden_low),
        ]
    )
    norm2_part = dot_nt(gate_grad, wg_back) + dot_nt(up_grad, wu_back)
    norm2_grad = lax.psum_scatter(norm2_part, "tp", scatter_dimension=0, tiled=True)
    gain2_part = jnp.sum(norm2_grad * resid_mid * scale_two, axis=0)
    weighted2 = norm2_grad * norm2_gain
    resid_grad = (
        top_grad
        + scale_two * weighted2
        - resid_mid * scale_two**3 * jnp.mean(weighted2 * resid_mid, axis=-1, keepdims=True)
    )
    mix_grad_low = resid_grad.astype(jnp.bfloat16)
    mix_grad_all = lax.all_gather(mix_grad_low, "tp", axis=0, tiled=True)
    mixer_back = mixer_full
    wq_back, wk_back, wv_back, wo_back, wz_back, wx_back, wdt_back, wout_back = mixer_back
    attn_grad = jnp.dot(mix_grad_all, wo_back, preferred_element_type=jnp.float32).astype(
        jnp.bfloat16
    )
    mamba_grad = jnp.dot(mix_grad_all, wout_back, preferred_element_type=jnp.float32)
    (
        gate_back,
        main_back,
        shared_back,
        step_back,
        kernel_grad,
        conv_shared_grad,
        decay_grad,
        bias_grad,
        skip_grad,
    ) = mamba_pull(mamba_grad)
    gate_back_low = gate_back.astype(jnp.bfloat16)
    main_back_low = main_back.astype(jnp.bfloat16)
    step_back_low = step_back.astype(jnp.bfloat16)
    attn_grad_heads = attn_grad.reshape(seq_len, kv_local, grouping, HEAD_DIMENSION)
    prob_grad = jnp.einsum(
        "qkgd,skd->kgqs", attn_grad_heads, value_reduced, preferred_element_type=jnp.float32
    )
    value_grad = jnp.einsum(
        "kgqs,qkgd->skd", probs_low, attn_grad_heads, preferred_element_type=jnp.float32
    )
    score_grad = (probs * (prob_grad - jnp.sum(probs * prob_grad, axis=-1, keepdims=True))).astype(
        jnp.bfloat16
    )
    query_grad = (
        jnp.einsum("kgqs,skd->qkgd", score_grad, key_rot, preferred_element_type=jnp.float32)
        * attn_scale
    )
    key_grad = (
        jnp.einsum("kgqs,qkgd->skd", score_grad, query_grp, preferred_element_type=jnp.float32)
        * attn_scale
    )
    query_back = (
        rotate_back(
            query_grad.reshape(seq_len, q_local, HEAD_DIMENSION), rotary_cosine, rotary_sine
        )
        .reshape(seq_len, q_local * HEAD_DIMENSION)
        .astype(jnp.bfloat16)
    )
    key_back = (
        rotate_back(key_grad, rotary_cosine, rotary_sine)
        .reshape(seq_len, kv_local * HEAD_DIMENSION)
        .astype(jnp.bfloat16)
    )
    value_back = value_grad.reshape(seq_len, kv_local * HEAD_DIMENSION).astype(jnp.bfloat16)
    shared_weight = w_shared.astype(jnp.float32)
    norm1_part = (
        dot_nt(query_back, wq_back)
        + dot_nt(key_back, wk_back)
        + dot_nt(value_back, wv_back)
        + dot_nt(gate_back_low, wz_back)
        + dot_nt(main_back_low, wx_back)
        + dot_nt(step_back_low, wdt_back)
        + lax.dot_general(
            shared_back,
            shared_weight,
            (((1,), (1,)), ((), ())),
            precision=top_precision,
            preferred_element_type=jnp.float32,
        )
    )
    norm1_grad = lax.psum_scatter(norm1_part, "tp", scatter_dimension=0, tiled=True)
    gain1_part = jnp.sum(norm1_grad * resid_in * scale_one, axis=0)
    weighted1 = norm1_grad * norm1_gain
    input_grad = (
        resid_grad
        + scale_one * weighted1
        - resid_in * scale_one**3 * jnp.mean(weighted1 * resid_in, axis=-1, keepdims=True)
    )
    grad_in = input_grad.astype(jnp.bfloat16)

    mixer_parts = reduce_weight_grads(
        [
            dot_tn(normed1_all, query_back),
            dot_tn(normed1_all, key_back),
            dot_tn(normed1_all, value_back),
            dot_tn(mix_grad_all, attn_low),
            dot_tn(normed1_all, gate_back_low),
            dot_tn(normed1_all, main_back_low),
            dot_tn(normed1_all, step_back_low),
            dot_tn(mix_grad_all, mamba_low),
        ]
    )
    shared_w_grad = lax.dot_general(
        normed1_all.astype(jnp.float32),
        shared_back,
        (((0,), (0,)), ((), ())),
        precision=top_precision,
        preferred_element_type=jnp.float32,
    )
    kernel_full = lax.dynamic_update_slice_in_dim(
        jnp.zeros(conv_main.shape, jnp.float32), kernel_grad, tp_rank * inner_local, 1
    )
    decay_full = lax.dynamic_update_slice_in_dim(
        jnp.zeros(decay_log.shape, jnp.float32), decay_grad, tp_rank * heads_local, 0
    )
    bias_full = lax.dynamic_update_slice_in_dim(
        jnp.zeros(step_bias.shape, jnp.float32), bias_grad, tp_rank * heads_local, 0
    )
    skip_full = lax.dynamic_update_slice_in_dim(
        jnp.zeros(skip_gain.shape, jnp.float32), skip_grad, tp_rank * heads_local, 0
    )
    gain1_sum, shared_sum, kernel_sum, conv_shared_sum, decay_sum, bias_sum, skip_sum, gain2_sum = (
        lax.psum(
            (
                gain1_part,
                shared_w_grad,
                kernel_full,
                conv_shared_grad,
                decay_full,
                bias_full,
                skip_full,
                gain2_part,
            ),
            ("grp", "fsdp", "tp"),
        )
    )
    return (
        output,
        grad_in,
        gain1_sum,
        mixer_parts[0],
        mixer_parts[1],
        mixer_parts[2],
        mixer_parts[3],
        mixer_parts[4],
        mixer_parts[5],
        mixer_parts[6],
        shared_sum,
        kernel_sum,
        conv_shared_sum,
        decay_sum,
        bias_sum,
        skip_sum,
        mixer_parts[7],
        gain2_sum,
        ffn_grads[0],
        ffn_grads[1],
        ffn_grads[2],
    )


def solution(mesh):
    placed = (
        P(("grp", "fsdp", "tp"), None),
        P(("grp", "fsdp")),
        P(),
        P("fsdp", "tp"),
        P("fsdp", "tp"),
        P("fsdp", "tp"),
        P("fsdp", "tp"),
        P("fsdp", "tp"),
        P("fsdp", "tp"),
        P("fsdp", "tp"),
        P(),
        P(),
        P(),
        P(),
        P(),
        P(),
        P("fsdp", "tp"),
        P(),
        P("fsdp", "tp"),
        P("fsdp", "tp"),
        P("fsdp", "tp"),
        P(("grp", "fsdp", "tp"), None),
    )
    return jax.shard_map(
        local,
        mesh=mesh,
        in_specs=placed,
        out_specs=(
            P(("grp", "fsdp", "tp"), None),
            P(("grp", "fsdp", "tp"), None),
            P(),
            P(("grp", "fsdp"), "tp"),
            P(("grp", "fsdp"), "tp"),
            P(("grp", "fsdp"), "tp"),
            P(("grp", "fsdp"), "tp"),
            P(("grp", "fsdp"), "tp"),
            P(("grp", "fsdp"), "tp"),
            P(("grp", "fsdp"), "tp"),
            P(),
            P(),
            P(),
            P(),
            P(),
            P(),
            P(("grp", "fsdp"), "tp"),
            P(),
            P(("grp", "fsdp"), "tp"),
            P(("grp", "fsdp"), "tp"),
            P(("grp", "fsdp"), "tp"),
        ),
        check_vma=False,
    )
```

```python
from functools import partial

import jax
import jax.numpy as jnp
from jax import lax
from jax.experimental import pallas as pl
from jax.experimental.pallas import tpu as pltpu
from jax.sharding import PartitionSpec as P

HEAD_DIMENSION = 64
BLOCK = 128
MESH = pl.DeviceIdType.MESH
VMEM_LIMIT = 60 << 20


top_precision = lax.Precision.HIGHEST
norm_eps = 1e-05
rope_base = 100000000000.0


def low(values):
    return values.astype(jnp.bfloat16)


def dot_nt(first_mat, second_mat):
    return lax.dot_general(
        first_mat, second_mat, (((1,), (1,)), ((), ())), preferred_element_type=jnp.float32
    )


def dot_tn(first_mat, second_mat):
    return lax.dot_general(
        first_mat, second_mat, (((0,), (0,)), ((), ())), preferred_element_type=jnp.float32
    )


def rms_scale(values):
    return lax.rsqrt(jnp.mean(values * values, axis=-1, keepdims=True) + norm_eps)


def angles(length_total, head_size):
    positions = jnp.arange(length_total).astype(jnp.float32)[:, None]
    exponent = jnp.arange(head_size // 2).astype(jnp.float32) * (-2.0 / head_size)
    phase = positions * jnp.power(rope_base, exponent)[None, :]
    return (jnp.cos(phase)[:, None, :], jnp.sin(phase)[:, None, :])


def apply_rotary(values, rotary_cosine, rotary_sine):
    half_dim = values.shape[-1] // 2
    first_half = values[..., :half_dim]
    second_half = values[..., half_dim:]
    return jnp.concatenate(
        [
            first_half * rotary_cosine - second_half * rotary_sine,
            second_half * rotary_cosine + first_half * rotary_sine,
        ],
        axis=-1,
    )


def rotate_back(grads, rotary_cosine, rotary_sine):
    half_dim = grads.shape[-1] // 2
    first_half = grads[..., :half_dim]
    second_half = grads[..., half_dim:]
    return jnp.concatenate(
        [
            first_half * rotary_cosine + second_half * rotary_sine,
            second_half * rotary_cosine - first_half * rotary_sine,
        ],
        axis=-1,
    )


def causal_conv(values, kernel):
    kernel_width = kernel.shape[0]
    length_total = values.shape[0]
    padded = jnp.pad(values, ((kernel_width - 1, 0), (0, 0)))
    result = kernel[kernel_width - 1] * values
    for offset in range(kernel_width - 1):
        result = result + kernel[offset] * padded[offset : offset + length_total]
    return result


def state_scan(x_heads, step_sizes, rates, b_matrix, c_matrix):
    length_total, head_count, head_size = x_heads.shape
    nstate = b_matrix.shape[1]
    blocks = length_total // BLOCK
    xs_blk = x_heads.reshape(blocks, BLOCK, head_count, head_size)
    step_blk = step_sizes.reshape(blocks, BLOCK, head_count)
    b_blk = b_matrix.reshape(blocks, BLOCK, nstate)
    c_blk = c_matrix.reshape(blocks, BLOCK, nstate)
    index_t = jnp.arange(BLOCK)
    lower = (index_t[:, None] >= index_t[None, :]).astype(jnp.float32)
    cumulative = jnp.einsum("ts,csh->cth", lower, step_blk * rates, precision=top_precision)
    causal = (index_t[:, None] >= index_t[None, :])[None, :, :, None]
    log_gaps = cumulative[:, :, None, :] - cumulative[:, None, :, :]
    decay_mat = jnp.where(causal, jnp.exp(jnp.where(causal, log_gaps, 0.0)), 0.0)
    inner_prod = jnp.einsum("ctn,csn->cts", c_blk, b_blk, precision=top_precision)
    mixing = decay_mat * inner_prod[:, :, :, None] * step_blk[:, None, :, :]
    within = jnp.einsum("ctsh,cshp->cthp", mixing, xs_blk, precision=top_precision)
    tail_weight = jnp.exp(cumulative[:, -1:, :] - cumulative) * step_blk
    states = jnp.einsum("csh,csn,cshp->chpn", tail_weight, b_blk, xs_blk, precision=top_precision)
    fading = jnp.exp(cumulative[:, -1, :])

    def advance(state_carry, pieces):
        fade_now, state_now = pieces
        return (fade_now[:, None, None] * state_carry + state_now, state_carry)

    _, before = lax.scan(
        advance, jnp.zeros((head_count, head_size, nstate), jnp.float32), (fading, states)
    )
    across = (
        jnp.einsum("ctn,chpn->cthp", c_blk, before, precision=top_precision)
        * jnp.exp(cumulative)[:, :, :, None]
    )
    return (within + across).reshape(length_total, head_count, head_size)


def mamba_mix(
    gate_in,
    main_in,
    shared_in,
    step_in,
    kernel_main,
    kernel_shared,
    decay_rates,
    bias_step,
    skip_terms,
    valid_rows,
):
    length_total = main_in.shape[0]
    head_count = step_in.shape[1]
    head_size = main_in.shape[1] // head_count
    nstate = shared_in.shape[1] // 2
    main_conv = jax.nn.silu(causal_conv(main_in, kernel_main))
    shared_conv = jax.nn.silu(causal_conv(shared_in, kernel_shared))
    step_sizes = jax.nn.softplus(step_in + bias_step) * valid_rows
    x_heads = main_conv.reshape(length_total, head_count, head_size)
    scanned = state_scan(
        x_heads, step_sizes, -jnp.exp(decay_rates), shared_conv[:, :nstate], shared_conv[:, nstate:]
    )
    output_heads = scanned + skip_terms[:, None] * x_heads
    return output_heads.reshape(length_total, head_count * head_size) * jax.nn.silu(gate_in)


def place():
    g, f, t = lax.axis_index("grp"), lax.axis_index("fsdp"), lax.axis_index("tp")
    return g, f // 2, f % 2, t


def greet(devices):
    barrier = pltpu.get_barrier_semaphore()
    for device in devices:
        pl.semaphore_signal(barrier, inc=1, device_id=device, device_id_type=MESH)
    pl.semaphore_wait(barrier, len(devices))


def remote(src, dst, send, recv, device):
    return pltpu.make_async_remote_copy(
        src_ref=src,
        dst_ref=dst,
        send_sem=send,
        recv_sem=recv,
        device_id=device,
        device_id_type=MESH,
    )


def gather_body(units, groups, halves, *refs):
    shards, own = refs[:units], refs[units : units + 2]
    full, both = refs[units + 2 : 2 * units + 2], refs[2 * units + 2 : 2 * units + 4]
    x_sems, z_sems, cx_sems, cz_sems, own_sems, local_sems, y_sems = refs[2 * units + 4 :]
    g, hi, c, t = place()
    f = hi * 2 + c
    pair = g % 2
    mate = g + 1 - 2 * pair
    other_core, other_z, other_y = (g, hi * 2 + 1 - c, t), (mate, f, t), (g, f, 1 - t)
    across = [(g, lax.rem(hi + k, halves) * 2 + c, t) for k in range(1, halves)]
    greet([other_core, other_z, other_y] + across)
    started = []

    def start(copy):
        copy.start()
        started.append(copy)
        return copy

    def piece(ref, owner, part):
        shard_rows = ref.shape[0] // (2 * halves)
        half = shard_rows // 2
        return ref.at[pl.ds(pl.multiple_of(owner * shard_rows + part * half, half), half), :]

    def shard(ref, owner):
        shard_rows = ref.shape[0] // (2 * halves)
        return ref.at[pl.ds(pl.multiple_of(owner * shard_rows, shard_rows), shard_rows), :]

    for i in range(2):
        rows = own[i].shape[0]
        where = pl.ds(pl.multiple_of(t * rows, rows), rows)
        start(
            remote(own[i], both[i].at[where, :], y_sems.at[0, i], y_sems.at[1, i], other_y)
        )
        local = pltpu.make_async_copy(own[i], both[i].at[where, :], local_sems.at[units + i])
        local.start()
        started.append(local)
    arriving_x, arriving_z = {}, {}
    for u in range(units):
        half = shards[u].shape[0] // 2
        mine = shards[u].at[pl.ds(pl.multiple_of(pair * half, half), half), :]
        for k in range(1, halves):
            arriving_x[u, k] = start(
                remote(
                    mine,
                    piece(full[u], f, pair),
                    x_sems.at[0, u, k],
                    x_sems.at[1, u, k],
                    across[k - 1],
                )
            )
        start(
            remote(
                shards[u], shard(full[u], f), own_sems.at[0, u], own_sems.at[1, u], other_core
            )
        )
        local = pltpu.make_async_copy(shards[u], shard(full[u], f), local_sems.at[u])
        local.start()
        started.append(local)
    waiting = []
    done_recv = set()
    for u in range(units + 1):
        if u < units:
            for k in range(1, halves):
                arriving_x[u, k].wait_recv()
                done_recv.add(id(arriving_x[u, k]))
                owner = lax.rem(hi - k + halves, halves) * 2 + c
                block = piece(full[u], owner, pair)
                arriving_z[u, k] = start(
                    remote(block, block, z_sems.at[0, u, k], z_sems.at[1, u, k], other_z)
                )
                start(remote(block, block, cx_sems.at[0, u, k], cx_sems.at[1, u, k], other_core))
        if u >= 1:
            v = u - 1
            for k in range(1, halves):
                arriving_z[v, k].wait_recv()
                done_recv.add(id(arriving_z[v, k]))
                owner = lax.rem(hi - k + halves, halves) * 2 + c
                block = piece(full[v], owner, 1 - pair)
                start(remote(block, block, cz_sems.at[0, v, k], cz_sems.at[1, v, k], other_core))
    for copy in started:
        if id(copy) in done_recv:
            copy.wait_send()
        else:
            copy.wait()


def gather_all(weights, own_rows):
    groups, halves = lax.axis_size("grp"), lax.axis_size("fsdp") // 2
    units = len(weights)
    anywhere = pl.BlockSpec(memory_space=pl.ANY)
    shapes = [
        jax.ShapeDtypeStruct((w.shape[0] * 2 * halves, w.shape[1]), w.dtype) for w in weights
    ] + [jax.ShapeDtypeStruct((r.shape[0] * 2, r.shape[1]), r.dtype) for r in own_rows]
    dma = pltpu.SemaphoreType.DMA
    return pl.pallas_call(
        partial(gather_body, units, groups, halves),
        out_shape=shapes,
        in_specs=[anywhere] * (units + 2),
        out_specs=[anywhere] * (units + 2),
        scratch_shapes=[
            dma((2, units, halves)),
            dma((2, units, halves)),
            dma((2, units, halves)),
            dma((2, units, halves)),
            dma((2, units)),
            dma((units + 2,)),
            dma((2, 2)),
        ],
        compiler_params=pltpu.CompilerParams(
            collective_id=0, has_side_effects=True, vmem_limit_bytes=VMEM_LIMIT
        ),
        name="gather_all",
    )(*weights, *own_rows)


def reduce_body(units, groups, halves, *refs):
    parts, vector = refs[:units], refs[units]
    sums, shared_sum, vector_sum = refs[units + 1 : 2 * units], refs[2 * units], refs[2 * units + 1]
    base = 2 * units + 2
    from_core, pair_sum = refs[base : base + units], refs[base + units : base + 2 * units]
    base += 2 * units
    from_x, chip_sum = refs[base : base + units], refs[base + units : base + 2 * units]
    base += 2 * units
    from_z = refs[base : base + units]
    (
        shared_y,
        shared_all,
        vec_core,
        vec_x,
        vec_y,
        vec_z,
        c_sems,
        x_sems,
        z_sems,
        sy_sems,
        sz_sems,
        sx_sems,
        sc_sems,
        vc_sems,
        vx_sems,
        vy_sems,
        vz_sems,
    ) = refs[base + units :]
    g, hi, c, t = place()
    f = hi * 2 + c
    other_core, other_y = (g, hi * 2 + 1 - c, t), (g, f, 1 - t)
    across = [(g, lax.rem(hi + k, halves) * 2 + c, t) for k in range(1, halves)]
    along = [(lax.rem(g + j, groups), f, t) for j in range(1, groups)]
    greet([other_core, other_y] + across + along)
    sending = []

    def start(copy):
        copy.start()
        sending.append(copy)
        return copy

    core_copies = [
        start(remote(parts[u].at[:, 1 - c], from_core[u], c_sems.at[0, u], c_sems.at[1, u], other_core))
        for u in range(units)
    ]
    vec_core[c] = vector[...]
    vec_copy = start(remote(vector, vec_core.at[c], vc_sems.at[0], vc_sems.at[1], other_core))
    x_copies, z_copies = {}, {}

    def core_stage(u):
        core_copies[u].wait_recv()

        def add(i, carry):
            gg, h = i // halves, lax.rem(i, halves)
            pair_sum[u][h, gg] = (
                parts[u][i, c].astype(jnp.float32) + from_core[u][i].astype(jnp.float32)
            ).astype(jnp.bfloat16)
            return carry

        lax.fori_loop(0, groups * halves, add, 0)
        for k in range(1, halves):
            x_copies[u, k] = start(
                remote(
                    pair_sum[u].at[lax.rem(hi + k, halves)],
                    from_x[u].at[k],
                    x_sems.at[0, u, k],
                    x_sems.at[1, u, k],
                    across[k - 1],
                )
            )

    def x_stage(u):
        for k in range(1, halves):
            x_copies[u, k].wait_recv()

        def add(gg, carry):
            total = pair_sum[u][hi, gg].astype(jnp.float32)
            for k in range(1, halves):
                total = total + from_x[u][k, gg].astype(jnp.float32)
            chip_sum[u][gg] = total.astype(jnp.bfloat16)
            return carry

        lax.fori_loop(0, groups, add, 0)
        for j in range(1, groups):
            z_copies[u, j] = start(
                remote(
                    chip_sum[u].at[lax.rem(g + j, groups)],
                    from_z[u].at[j],
                    z_sems.at[0, u, j],
                    z_sems.at[1, u, j],
                    along[j - 1],
                )
            )

    def z_stage(u):
        for j in range(1, groups):
            z_copies[u, j].wait_recv()
        total = chip_sum[u][g].astype(jnp.float32)
        for j in range(1, groups):
            total = total + from_z[u][j].astype(jnp.float32)
        return total

    core_stage(0)
    vec_copy.wait_recv()
    vec_x[hi] = vec_core[0] + vec_core[1]
    vec_copies = [
        start(remote(vec_x.at[hi], vec_x.at[hi], vx_sems.at[0, k], vx_sems.at[1, k], across[k - 1]))
        for k in range(1, halves)
    ]
    core_stage(1)
    for copy in vec_copies:
        copy.wait_recv()
    total = vec_x[0]
    for h in range(1, halves):
        total = total + vec_x[h]
    vec_y[t] = total
    vec_copy = start(remote(vec_y.at[t], vec_y.at[t], vy_sems.at[0], vy_sems.at[1], other_y))
    x_stage(0)
    core_stage(2)
    vec_copy.wait_recv()
    vec_z[g] = vec_y[0] + vec_y[1]
    vec_copies = [
        start(remote(vec_z.at[g], vec_z.at[g], vz_sems.at[0, j], vz_sems.at[1, j], along[j - 1]))
        for j in range(1, groups)
    ]
    for u in range(3, units + 2):
        if u < units:
            core_stage(u)
        if u - 2 < units and u >= 3:
            x_stage(u - 2)
        if u == 4:
            shared_y[t] = z_stage(0)
            shared_copy = start(
                remote(shared_y.at[t], shared_y.at[t], sy_sems.at[0], sy_sems.at[1], other_y)
            )
        if u == 5:
            for copy in vec_copies:
                copy.wait_recv()
            total = vec_z[0]
            for j in range(1, groups):
                total = total + vec_z[j]
            vector_sum[...] = total
            shared_copy.wait_recv()
            shared_all[g, hi, c] = (shared_y[0] + shared_y[1]).astype(jnp.bfloat16)
            sz = [
                start(
                    remote(
                        shared_all.at[g, hi, c],
                        shared_all.at[g, hi, c],
                        sz_sems.at[0, j],
                        sz_sems.at[1, j],
                        along[j - 1],
                    )
                )
                for j in range(1, groups)
            ]
        if u == 6:
            for copy in sz:
                copy.wait_recv()
            sx = [
                start(
                    remote(
                        shared_all.at[:, hi, c],
                        shared_all.at[:, hi, c],
                        sx_sems.at[0, k],
                        sx_sems.at[1, k],
                        across[k - 1],
                    )
                )
                for k in range(1, halves)
            ]
        if u == 7:
            for copy in sx:
                copy.wait_recv()
            sc = start(
                remote(
                    shared_all.at[:, :, c],
                    shared_all.at[:, :, c],
                    sc_sems.at[0],
                    sc_sems.at[1],
                    other_core,
                )
            )
        if u >= 5:
            sums[u - 5][...] = z_stage(u - 4)
    for v in range(units - 2, units):
        sums[v - 1][...] = z_stage(v)
    sc.wait_recv()

    def widen(i, carry):
        shared_sum[i] = shared_all[
            i // (2 * halves), lax.rem(i // 2, halves), lax.rem(i, 2)
        ].astype(jnp.float32)
        return carry

    lax.fori_loop(0, groups * halves * 2, widen, 0)
    for copy in sending:
        copy.wait_send()


def reduce_all(parts, vector):
    groups, halves = lax.axis_size("grp"), lax.axis_size("fsdp") // 2
    units = len(parts)
    blocks = groups * halves * 2
    rows = parts[0].shape[0] // blocks
    widths = [p.shape[1] for p in parts]
    f32, bf16 = jnp.float32, jnp.bfloat16
    inside = pl.BlockSpec(memory_space=pltpu.VMEM)
    dma = pltpu.SemaphoreType.DMA
    outs = pl.pallas_call(
        partial(reduce_body, units, groups, halves),
        out_shape=[jax.ShapeDtypeStruct((rows, w), f32) for w in widths[1:]]
        + [
            jax.ShapeDtypeStruct((blocks, rows, widths[0]), f32),
            jax.ShapeDtypeStruct(vector.shape, f32),
        ],
        in_specs=[inside] * (units + 1),
        out_specs=[inside] * (units + 1),
        scratch_shapes=[pltpu.VMEM((groups * halves, rows, w), bf16) for w in widths]
        + [pltpu.VMEM((halves, groups, rows, w), bf16) for w in widths]
        + [pltpu.VMEM((halves, groups, rows, w), bf16) for w in widths]
        + [pltpu.VMEM((groups, rows, w), bf16) for w in widths]
        + [pltpu.VMEM((groups, rows, w), bf16) for w in widths]
        + [
            pltpu.VMEM((2, rows, widths[0]), f32),
            pltpu.VMEM((groups, halves, 2, rows, widths[0]), bf16),
            pltpu.VMEM((2,) + vector.shape, f32),
            pltpu.VMEM((halves,) + vector.shape, f32),
            pltpu.VMEM((2,) + vector.shape, f32),
            pltpu.VMEM((groups,) + vector.shape, f32),
            dma((2, units)),
            dma((2, units, halves)),
            dma((2, units, groups)),
            dma((2,)),
            dma((2, groups)),
            dma((2, halves)),
            dma((2,)),
            dma((2,)),
            dma((2, halves)),
            dma((2,)),
            dma((2, groups)),
        ],
        compiler_params=pltpu.CompilerParams(
            collective_id=1, has_side_effects=True, vmem_limit_bytes=VMEM_LIMIT
        ),
        name="reduce_all",
    )(*[p.reshape(blocks // 2, 2, rows, p.shape[1]) for p in parts], vector)
    return outs[: units - 1], outs[units - 1].reshape(blocks * rows, widths[0]), outs[units]


def local(
    hidden_in,
    lengths,
    norm1_gain,
    w_query,
    key_weight,
    value_weight,
    w_attn_out,
    w_mamba_z,
    w_mamba_x,
    w_step,
    w_shared,
    conv_main,
    conv_shared,
    decay_log,
    step_bias,
    skip_gain,
    w_mamba_out,
    norm2_gain,
    w_ffn_gate,
    w_ffn_up,
    w_ffn_down,
    out_grad,
):
    tp_count = lax.axis_size("tp")
    tp_rank = lax.axis_index("tp")
    own_rows = hidden_in.shape[0]
    seq_len = own_rows * tp_count
    model_width = hidden_in.shape[1]
    valid_count = lengths[0]
    positions = jnp.arange(seq_len, dtype=jnp.int32)
    valid_full = (positions < valid_count).astype(jnp.float32)[:, None]
    valid_own = lax.dynamic_slice_in_dim(valid_full, tp_rank * own_rows, own_rows, 0)
    resid_in = hidden_in.astype(jnp.float32)
    scale_one = rms_scale(resid_in)
    first_normalized = (resid_in * scale_one * norm1_gain).astype(jnp.bfloat16)
    top_grad = out_grad.astype(jnp.float32) * valid_own
    top_grad_low = top_grad.astype(jnp.bfloat16)
    q_width, kv_width, step_width = w_query.shape[1], key_weight.shape[1], w_step.shape[1]
    narrow = jnp.concatenate(
        [
            w_query,
            key_weight,
            value_weight,
            jnp.pad(w_step, ((0, 0), (0, 128 - step_width))),
        ],
        axis=1,
    )
    narrow_all, wx_all, wz_all, wo_all, wout_all, wg_all, wu_all, wd_all, normed1_all, top_grad_all = (
        gather_all(
            (narrow, w_mamba_x, w_mamba_z, w_attn_out, w_mamba_out, w_ffn_gate, w_ffn_up, w_ffn_down),
            (first_normalized, top_grad_low),
        )
    )
    wq_all = narrow_all[:, :q_width]
    wk_all = narrow_all[:, q_width : q_width + kv_width]
    wv_all = narrow_all[:, q_width + kv_width : q_width + 2 * kv_width]
    wdt_all = narrow_all[:, q_width + 2 * kv_width : q_width + 2 * kv_width + step_width]
    q_local = wq_all.shape[1] // HEAD_DIMENSION
    kv_local = wk_all.shape[1] // HEAD_DIMENSION
    grouping = q_local // kv_local
    attn_scale = HEAD_DIMENSION ** (-0.5)
    rotary_cosine, rotary_sine = angles(seq_len, HEAD_DIMENSION)
    query_projected = jnp.dot(normed1_all, wq_all, preferred_element_type=jnp.float32)
    key_projected = jnp.dot(normed1_all, wk_all, preferred_element_type=jnp.float32)
    value_proj = jnp.dot(normed1_all, wv_all, preferred_element_type=jnp.float32)
    query_rotated = apply_rotary(
        query_projected.reshape(seq_len, q_local, HEAD_DIMENSION), rotary_cosine, rotary_sine
    ).astype(jnp.bfloat16)
    key_rot = apply_rotary(
        key_projected.reshape(seq_len, kv_local, HEAD_DIMENSION), rotary_cosine, rotary_sine
    ).astype(jnp.bfloat16)
    value_reduced = value_proj.astype(jnp.bfloat16).reshape(seq_len, kv_local, HEAD_DIMENSION)
    query_grp = query_rotated.reshape(seq_len, kv_local, grouping, HEAD_DIMENSION)
    score_raw = (
        jnp.einsum("qkgd,skd->kgqs", query_grp, key_rot, preferred_element_type=jnp.float32)
        * attn_scale
    )
    allowed = (positions[:, None] >= positions[None, :]) & (positions[None, :] < valid_count)
    masked = jnp.where(allowed, score_raw, -1e30)
    peak_score = jnp.max(masked, axis=-1, keepdims=True)
    expo_score = jnp.exp(masked - peak_score)
    probs = expo_score / jnp.sum(expo_score, axis=-1, keepdims=True)
    probs_low = probs.astype(jnp.bfloat16)
    attn_heads = jnp.einsum(
        "kgqs,skd->qkgd", probs_low, value_reduced, preferred_element_type=jnp.float32
    )
    attn_low = attn_heads.reshape(seq_len, q_local * HEAD_DIMENSION).astype(jnp.bfloat16)
    heads_local = wdt_all.shape[1]
    inner_local = wx_all.shape[1]
    gate_proj = jnp.dot(normed1_all, wz_all, preferred_element_type=jnp.float32)
    main_proj = jnp.dot(normed1_all, wx_all, preferred_element_type=jnp.float32)
    step_proj = jnp.dot(normed1_all, wdt_all, preferred_element_type=jnp.float32)
    shared_proj = jnp.dot(normed1_all, w_shared, preferred_element_type=jnp.float32)
    kernel_local = lax.dynamic_slice_in_dim(conv_main, tp_rank * inner_local, inner_local, 1)
    decay_local = lax.dynamic_slice_in_dim(decay_log, tp_rank * heads_local, heads_local, 0)
    bias_local = lax.dynamic_slice_in_dim(step_bias, tp_rank * heads_local, heads_local, 0)
    skip_local = lax.dynamic_slice_in_dim(skip_gain, tp_rank * heads_local, heads_local, 0)
    mamba_out, mamba_pull = jax.vjp(
        partial(mamba_mix, valid_rows=valid_full),
        gate_proj,
        main_proj,
        shared_proj,
        step_proj,
        kernel_local,
        conv_shared,
        decay_local,
        bias_local,
        skip_local,
    )
    mamba_low = mamba_out.astype(jnp.bfloat16)
    mix_part = dot_nt(attn_low, wo_all) + dot_nt(mamba_low, wout_all)
    mixed = lax.psum_scatter(mix_part, "tp", scatter_dimension=0, tiled=True)
    resid_mid = resid_in + mixed
    scale_two = rms_scale(resid_mid)
    normed2 = (resid_mid * scale_two * norm2_gain).astype(jnp.bfloat16)
    normed2_all = lax.all_gather(normed2, "tp", axis=0, tiled=True)
    gate_pre = jnp.dot(normed2_all, wg_all, preferred_element_type=jnp.float32)
    up_pre = jnp.dot(normed2_all, wu_all, preferred_element_type=jnp.float32)
    sigma_gate = jax.nn.sigmoid(gate_pre)
    silu_gate = gate_pre * sigma_gate
    hidden_low = (silu_gate * up_pre).astype(jnp.bfloat16)
    ffn_part = dot_nt(hidden_low, wd_all)
    ffn_sum = lax.psum_scatter(
        ffn_part.astype(jnp.bfloat16), "tp", scatter_dimension=0, tiled=True
    ).astype(jnp.float32)
    output = ((resid_mid + ffn_sum) * valid_own).astype(jnp.bfloat16)
    wg_back, wu_back, wd_back = wg_all, wu_all, wd_all
    hidden_grad = jnp.dot(top_grad_all, wd_back, preferred_element_type=jnp.float32)
    silu_slope = sigma_gate * (1.0 + gate_pre * (1.0 - sigma_gate))
    gate_grad = (hidden_grad * up_pre * silu_slope).astype(jnp.bfloat16)
    up_grad = (hidden_grad * silu_gate).astype(jnp.bfloat16)

    ffn_grads = [
        low(dot_tn(normed2_all, gate_grad)),
        low(dot_tn(normed2_all, up_grad)),
        low(dot_tn(top_grad_all, hidden_low)),
    ]
    norm2_part = dot_nt(gate_grad, wg_back) + dot_nt(up_grad, wu_back)
    norm2_grad = lax.psum_scatter(norm2_part, "tp", scatter_dimension=0, tiled=True)
    gain2_part = jnp.sum(norm2_grad * resid_mid * scale_two, axis=0)
    weighted2 = norm2_grad * norm2_gain
    resid_grad = (
        top_grad
        + scale_two * weighted2
        - resid_mid * scale_two**3 * jnp.mean(weighted2 * resid_mid, axis=-1, keepdims=True)
    )
    mix_grad_low = resid_grad.astype(jnp.bfloat16)
    mix_grad_all = lax.all_gather(mix_grad_low, "tp", axis=0, tiled=True)
    wq_back, wk_back, wv_back, wo_back = wq_all, wk_all, wv_all, wo_all
    wz_back, wx_back, wdt_back, wout_back = wz_all, wx_all, wdt_all, wout_all
    attn_grad = jnp.dot(mix_grad_all, wo_back, preferred_element_type=jnp.float32).astype(
        jnp.bfloat16
    )
    mamba_grad = jnp.dot(mix_grad_all, wout_back, preferred_element_type=jnp.float32)
    (
        gate_back,
        main_back,
        shared_back,
        step_back,
        kernel_grad,
        conv_shared_grad,
        decay_grad,
        bias_grad,
        skip_grad,
    ) = mamba_pull(mamba_grad)
    gate_back_low = gate_back.astype(jnp.bfloat16)
    main_back_low = main_back.astype(jnp.bfloat16)
    step_back_low = step_back.astype(jnp.bfloat16)
    attn_grad_heads = attn_grad.reshape(seq_len, kv_local, grouping, HEAD_DIMENSION)
    prob_grad = jnp.einsum(
        "qkgd,skd->kgqs", attn_grad_heads, value_reduced, preferred_element_type=jnp.float32
    )
    value_grad = jnp.einsum(
        "kgqs,qkgd->skd", probs_low, attn_grad_heads, preferred_element_type=jnp.float32
    )
    score_grad = (probs * (prob_grad - jnp.sum(probs * prob_grad, axis=-1, keepdims=True))).astype(
        jnp.bfloat16
    )
    query_grad = (
        jnp.einsum("kgqs,skd->qkgd", score_grad, key_rot, preferred_element_type=jnp.float32)
        * attn_scale
    )
    key_grad = (
        jnp.einsum("kgqs,qkgd->skd", score_grad, query_grp, preferred_element_type=jnp.float32)
        * attn_scale
    )
    query_back = (
        rotate_back(
            query_grad.reshape(seq_len, q_local, HEAD_DIMENSION), rotary_cosine, rotary_sine
        )
        .reshape(seq_len, q_local * HEAD_DIMENSION)
        .astype(jnp.bfloat16)
    )
    key_back = (
        rotate_back(key_grad, rotary_cosine, rotary_sine)
        .reshape(seq_len, kv_local * HEAD_DIMENSION)
        .astype(jnp.bfloat16)
    )
    value_back = value_grad.reshape(seq_len, kv_local * HEAD_DIMENSION).astype(jnp.bfloat16)
    shared_weight = w_shared.astype(jnp.float32)
    norm1_part = (
        dot_nt(query_back, wq_back)
        + dot_nt(key_back, wk_back)
        + dot_nt(value_back, wv_back)
        + dot_nt(gate_back_low, wz_back)
        + dot_nt(main_back_low, wx_back)
        + dot_nt(step_back_low, wdt_back)
        + lax.dot_general(
            shared_back,
            shared_weight,
            (((1,), (1,)), ((), ())),
            precision=top_precision,
            preferred_element_type=jnp.float32,
        )
    )
    norm1_grad = lax.psum_scatter(norm1_part, "tp", scatter_dimension=0, tiled=True)
    gain1_part = jnp.sum(norm1_grad * resid_in * scale_one, axis=0)
    weighted1 = norm1_grad * norm1_gain
    input_grad = (
        resid_grad
        + scale_one * weighted1
        - resid_in * scale_one**3 * jnp.mean(weighted1 * resid_in, axis=-1, keepdims=True)
    )
    grad_in = input_grad.astype(jnp.bfloat16)

    narrow_back = jnp.concatenate(
        [
            query_back,
            key_back,
            value_back,
            jnp.pad(step_back_low, ((0, 0), (0, 128 - step_width))),
        ],
        axis=1,
    )
    mixer_grads = [
        low(dot_tn(mix_grad_all, attn_low)),
        low(dot_tn(mix_grad_all, mamba_low)),
        low(dot_tn(normed1_all, gate_back_low)),
        low(dot_tn(normed1_all, main_back_low)),
        low(dot_tn(normed1_all, narrow_back)),
    ]
    shared_w_grad = lax.dot_general(
        normed1_all.astype(jnp.float32),
        shared_back,
        (((0,), (0,)), ((), ())),
        precision=top_precision,
        preferred_element_type=jnp.float32,
    )
    kernel_full = lax.dynamic_update_slice_in_dim(
        jnp.zeros(conv_main.shape, jnp.float32), kernel_grad, tp_rank * inner_local, 1
    )
    decay_full = lax.dynamic_update_slice_in_dim(
        jnp.zeros(decay_log.shape, jnp.float32), decay_grad, tp_rank * heads_local, 0
    )
    bias_full = lax.dynamic_update_slice_in_dim(
        jnp.zeros(step_bias.shape, jnp.float32), bias_grad, tp_rank * heads_local, 0
    )
    skip_full = lax.dynamic_update_slice_in_dim(
        jnp.zeros(skip_gain.shape, jnp.float32), skip_grad, tp_rank * heads_local, 0
    )
    pieces = [
        gain1_part,
        gain2_part,
        conv_shared_grad,
        kernel_full,
        decay_full,
        bias_full,
        skip_full,
    ]
    flat = jnp.concatenate([p.reshape(-1) for p in pieces])
    vector = jnp.pad(flat, (0, -flat.shape[0] % 1024)).reshape(-1, 128)
    wide_sums, shared_sum, vector_sum = reduce_all(
        [low(shared_w_grad)] + ffn_grads + mixer_grads, vector
    )
    vector_sum = vector_sum.reshape(-1)
    small, at = [], 0
    for p in pieces:
        small.append(vector_sum[at : at + p.size].reshape(p.shape))
        at += p.size
    gain1_sum, gain2_sum, conv_shared_sum, kernel_sum, decay_sum, bias_sum, skip_sum = small
    gate_sum, up_sum, down_sum, attn_out_sum, mamba_out_sum, z_sum, x_sum, narrow_sum = wide_sums
    return (
        output,
        grad_in,
        gain1_sum,
        narrow_sum[:, :q_width],
        narrow_sum[:, q_width : q_width + kv_width],
        narrow_sum[:, q_width + kv_width : q_width + 2 * kv_width],
        attn_out_sum,
        z_sum,
        x_sum,
        narrow_sum[:, q_width + 2 * kv_width : q_width + 2 * kv_width + step_width],
        shared_sum,
        kernel_sum,
        conv_shared_sum,
        decay_sum,
        bias_sum,
        skip_sum,
        mamba_out_sum,
        gain2_sum,
        gate_sum,
        up_sum,
        down_sum,
    )


def solution(mesh):
    placed = (
        P(("grp", "fsdp", "tp"), None),
        P(("grp", "fsdp")),
        P(),
        P("fsdp", "tp"),
        P("fsdp", "tp"),
        P("fsdp", "tp"),
        P("fsdp", "tp"),
        P("fsdp", "tp"),
        P("fsdp", "tp"),
        P("fsdp", "tp"),
        P(),
        P(),
        P(),
        P(),
        P(),
        P(),
        P("fsdp", "tp"),
        P(),
        P("fsdp", "tp"),
        P("fsdp", "tp"),
        P("fsdp", "tp"),
        P(("grp", "fsdp", "tp"), None),
    )
    return jax.shard_map(
        local,
        mesh=mesh,
        in_specs=placed,
        out_specs=(
            P(("grp", "fsdp", "tp"), None),
            P(("grp", "fsdp", "tp"), None),
            P(),
            P(("grp", "fsdp"), "tp"),
            P(("grp", "fsdp"), "tp"),
            P(("grp", "fsdp"), "tp"),
            P(("grp", "fsdp"), "tp"),
            P(("grp", "fsdp"), "tp"),
            P(("grp", "fsdp"), "tp"),
            P(("grp", "fsdp"), "tp"),
            P(),
            P(),
            P(),
            P(),
            P(),
            P(),
            P(("grp", "fsdp"), "tp"),
            P(),
            P(("grp", "fsdp"), "tp"),
            P(("grp", "fsdp"), "tp"),
            P(("grp", "fsdp"), "tp"),
        ),
        check_vma=False,
    )
```

```python
from functools import partial

import jax
import jax.numpy as jnp
import numpy as np
from jax import lax
from jax.experimental import pallas as pl
from jax.experimental.pallas import tpu as pltpu
from jax.sharding import PartitionSpec as P

HEAD = 64
LANES = 128
BLOCK = 128
NSTATE = 128
EPS = 1e-05
ROPE_BASE = 100000000000.0
MESH = pl.DeviceIdType.MESH
VMEM_LIMIT = 62 << 20
F32, BF16 = jnp.float32, jnp.bfloat16
EXACT = lax.Precision.HIGHEST


def low(values):
    return values.astype(BF16)


def wide(values):
    return values.astype(F32)


def dot(a, b):
    return jnp.dot(a, b, preferred_element_type=F32)


def dot_nt(a, b):
    return lax.dot_general(a, b, (((1,), (1,)), ((), ())), preferred_element_type=F32)


def dot_tn(a, b):
    return lax.dot_general(a, b, (((0,), (0,)), ((), ())), preferred_element_type=F32)


def exact_dot(a, b):
    return jnp.dot(a, b, precision=EXACT, preferred_element_type=F32)


def sigmoid(v):
    return 1.0 / (1.0 + jnp.exp(-v))


def rms_scale(values):
    return lax.rsqrt(jnp.mean(values * values, axis=-1, keepdims=True) + EPS)


def lane_ids(rows):
    return lax.broadcasted_iota(jnp.int32, (rows, LANES), 1)


def first_head(rows):
    return lane_ids(rows) < HEAD


def half_swap(tile):
    lower = lax.rem(lane_ids(tile.shape[0]), HEAD) < HEAD // 2
    return jnp.where(lower, pltpu.roll(tile, LANES - HEAD // 2, 1), pltpu.roll(tile, HEAD // 2, 1))


def spread(values, tile):
    return jnp.where(
        first_head(values.shape[0]),
        values[:, 2 * tile : 2 * tile + 1],
        values[:, 2 * tile + 1 : 2 * tile + 2],
    )


def rotary_tables(length):
    positions = np.arange(length, dtype=np.float64)[:, None]
    power = np.arange(HEAD // 2, dtype=np.float64) * (-2.0 / HEAD)
    phase = (positions * np.power(ROPE_BASE, power)[None, :]).astype(np.float32)
    cosine, sine = np.cos(phase), np.sin(phase)
    return (
        np.concatenate([cosine] * 4, axis=1).astype(np.float32),
        np.concatenate([-sine, sine] * 2, axis=1).astype(np.float32),
    )


def place():
    g, f, t = lax.axis_index("grp"), lax.axis_index("fsdp"), lax.axis_index("tp")
    return g, f // 2, lax.rem(f, 2), t


def greet(devices):
    barrier = pltpu.get_barrier_semaphore()
    for device in devices:
        pl.semaphore_signal(barrier, inc=1, device_id=device, device_id_type=MESH)


def greeted(devices):
    pl.semaphore_wait(pltpu.get_barrier_semaphore(), len(devices))


def remote(src, dst, send, recv, device):
    return pltpu.make_async_remote_copy(
        src_ref=src,
        dst_ref=dst,
        send_sem=send,
        recv_sem=recv,
        device_id=device,
        device_id_type=MESH,
    )


def pick_heads(terms, whole, t):
    terms[...] = jnp.zeros_like(terms)
    for i, ref in enumerate(whole):
        heads = ref.shape[1] // 2
        terms[i : i + 1, :heads] = jnp.where(t == 0, ref[:, :heads], ref[:, heads:])


class Gather:
    def __init__(self, units, halves, sems):
        self.units, self.halves = units, halves
        self.x, self.z, self.cx, self.cz, self.own, self.local = sems
        g, self.hi, self.c, t = place()
        f = self.hi * 2 + self.c
        self.f, self.pair = f, lax.rem(g, 2)
        self.other_core = (g, self.hi * 2 + 1 - self.c, t)
        self.other_z = (g + 1 - 2 * self.pair, f, t)
        self.across = [
            (g, lax.rem(self.hi + k, halves) * 2 + self.c, t) for k in range(1, halves)
        ]
        self.devices = [self.other_core, self.other_z] + self.across
        self.got, self.sent, self.pending = {}, [], {}

    def block(self, u, owner, part=None):
        shard, full, column, width = self.units[u]
        rows = shard.shape[0]
        size = rows if part is None else rows // 2
        start = owner * rows + (0 if part is None else part * size)
        return full.at[pl.ds(pl.multiple_of(start, size), size), pl.ds(column, width)]

    def start(self, copy):
        copy.start()
        self.sent.append(copy)
        return copy

    def send(self, u):
        shard = self.units[u][0]
        half = shard.shape[0] // 2
        mine = shard.at[pl.ds(pl.multiple_of(self.pair * half, half), half), :]
        for k in range(1, self.halves):
            self.got["x", u, k] = self.start(
                remote(
                    mine,
                    self.block(u, self.f, self.pair),
                    self.x.at[0, u, k],
                    self.x.at[1, u, k],
                    self.across[k - 1],
                )
            )
        self.got["own", u] = self.start(
            remote(
                shard,
                self.block(u, self.f),
                self.own.at[0, u],
                self.own.at[1, u],
                self.other_core,
            )
        )
        self.pending[u] = pltpu.make_async_copy(shard, self.block(u, self.f), self.local.at[u])
        self.pending[u].start()

    def owner(self, k):
        return lax.rem(self.hi - k + self.halves, self.halves) * 2 + self.c

    def relay_x(self, u):
        for k in range(1, self.halves):
            self.got.pop(("x", u, k)).wait_recv()
            block = self.block(u, self.owner(k), self.pair)
            self.got["z", u, k] = self.start(
                remote(block, block, self.z.at[0, u, k], self.z.at[1, u, k], self.other_z)
            )
            self.got["cx", u, k] = self.start(
                remote(block, block, self.cx.at[0, u, k], self.cx.at[1, u, k], self.other_core)
            )

    def relay_z(self, u):
        for k in range(1, self.halves):
            self.got.pop(("z", u, k)).wait_recv()
            block = self.block(u, self.owner(k), 1 - self.pair)
            self.got["cz", u, k] = self.start(
                remote(block, block, self.cz.at[0, u, k], self.cz.at[1, u, k], self.other_core)
            )

    def finish(self, u):
        self.got.pop(("own", u)).wait_recv()
        for k in range(1, self.halves):
            self.got.pop(("cx", u, k)).wait_recv()
            self.got.pop(("cz", u, k)).wait_recv()
        self.pending.pop(u).wait()

    def drain(self):
        assert not self.got and not self.pending
        for copy in self.sent:
            copy.wait_send()


def gather_sems(units, halves):
    dma = pltpu.SemaphoreType.DMA
    return [dma((2, units, halves))] * 4 + [dma((2, units)), dma((units,))]


def causal_conv(padded, kernel, rows, cols):
    total = kernel[3:4, :] * padded[8 : 8 + rows, cols]
    for i in range(3):
        total = total + kernel[i : i + 1, :] * padded[5 + i : 5 + i + rows, cols]
    return total


def triangle(lower=True):
    row = lax.broadcasted_iota(jnp.int32, (BLOCK, BLOCK), 0)
    col = lax.broadcasted_iota(jnp.int32, (BLOCK, BLOCK), 1)
    return row >= col if lower else row <= col


def front_body(
    halves,
    length_ref,
    hidden,
    out_grad,
    gain,
    w_query,
    w_key,
    w_value,
    w_step,
    w_x,
    w_z,
    w_attn_out,
    w_mamba_out,
    w_shared,
    conv_main,
    conv_shared,
    decay_log,
    step_bias,
    skip_gain,
    cosine,
    sine,
    w_in_all,
    w_mix_all,
    normed,
    top_grad,
    mix,
    qr,
    kv,
    probs,
    x_padded,
    z_proj,
    bc_padded,
    step_in,
    scanned,
    states,
    narrow,
    conv_x,
    conv_bc,
    steps,
    state,
    head_terms,
    y_sems,
    *sems,
):
    g, hi, c, t = place()
    own = hidden.shape[0]
    length = 2 * own
    inner = w_x.shape[1]
    q_width, step_width = w_query.shape[1], w_step.shape[0]
    tiles, q_tiles = inner // LANES, q_width // LANES
    narrow_width = q_width + 2 * LANES
    gather = Gather(
        [
            (narrow, w_in_all, 0, narrow_width),
            (w_x, w_in_all, narrow_width, inner),
            (w_z, w_in_all, narrow_width + inner, inner),
            (w_attn_out, w_mix_all, 0, q_width),
            (w_mamba_out, w_mix_all, q_width, inner),
        ],
        halves,
        sems,
    )
    other_y = (g, hi * 2 + c, 1 - t)
    devices = gather.devices + [other_y]
    greet(devices)
    narrow[:, :q_width] = w_query[...]
    turned = jnp.concatenate([wide(w_key[...]), wide(w_value[...])], axis=0).T
    narrow[:, q_width : q_width + LANES] = low(turned)
    filler = jnp.zeros((LANES - step_width, narrow.shape[0]), F32)
    turned = jnp.concatenate([wide(w_step[...]), filler], axis=0).T
    narrow[:, q_width + LANES :] = low(turned)
    pick_heads(head_terms, (decay_log, step_bias, skip_gain), t)
    greeted(devices)
    gather.send(0)
    mine = pl.ds(pl.multiple_of(t * own, own), own)
    values = wide(hidden[...])
    normed[mine, :] = low(values * rms_scale(values) * gain[...])
    y_copy = remote(
        normed.at[mine, :], normed.at[mine, :], y_sems.at[0, 0], y_sems.at[1, 0], other_y
    )
    y_copy.start()
    for u in range(1, 5):
        gather.send(u)
    count = length_ref[0]
    slot = t * own + lax.broadcasted_iota(jnp.int32, (own, 1), 0)
    top_grad[mine, :] = jnp.where(slot < count, out_grad[...], jnp.zeros((), BF16))
    grad_copy = remote(
        top_grad.at[mine, :], top_grad.at[mine, :], y_sems.at[0, 1], y_sems.at[1, 1], other_y
    )
    grad_copy.start()
    x_padded[0:8, :] = jnp.zeros((8, inner), F32)
    bc_padded[0:8, :] = jnp.zeros((8, 2 * NSTATE), F32)
    state[...] = jnp.zeros_like(state)

    gather.relay_x(0)
    y_copy.wait_recv()
    bc_padded[8:, :] = dot(normed[...], w_shared[...])
    gather.relay_z(0)
    gather.relay_x(1)
    gather.finish(0)
    projected = dot(normed[...], w_in_all[:, :narrow_width])
    for j in range(q_tiles):
        tile = projected[:, j * LANES : (j + 1) * LANES]
        qr[:, j * LANES : (j + 1) * LANES] = low(tile * cosine[...] + half_swap(tile) * sine[...])
    tile = projected[:, q_width : q_width + LANES]
    is_key = first_head(length)
    turned = tile * cosine[...] + half_swap(tile) * sine[...]
    kv[...] = low(jnp.where(is_key, turned, tile))
    step_pre = projected[:, q_width + LANES :] + head_terms[1:2, :]
    step_in[...] = step_pre
    row = lax.broadcasted_iota(jnp.int32, (length, 1), 0)
    softplus = jnp.maximum(step_pre, 0.0) + jnp.log(1.0 + jnp.exp(-jnp.abs(step_pre)))
    steps[...] = jnp.where(row < count, softplus, 0.0)
    gather.relay_z(1)
    gather.relay_x(2)
    gather.finish(1)
    x_padded[8:, :] = dot(normed[...], w_in_all[:, narrow_width : narrow_width + inner])
    channel = t * inner
    for j in range(2 * NSTATE // LANES):
        cols = slice(j * LANES, (j + 1) * LANES)
        pre = causal_conv(bc_padded, conv_shared[:, cols], length, cols)
        conv_bc[:, cols] = pre * sigmoid(pre)
    for j in range(tiles):
        cols = slice(j * LANES, (j + 1) * LANES)
        taps = conv_main[:, pl.ds(pl.multiple_of(channel + j * LANES, LANES), LANES)]
        pre = causal_conv(x_padded, taps, length, cols)
        conv_x[:, cols] = pre * sigmoid(pre)
    gather.relay_z(2)
    gather.relay_x(3)

    def attend(j):
        zero = jnp.zeros((), BF16)
        keys = [jnp.where(is_key, kv[...], zero)]
        keys.append(pltpu.roll(wide(keys[0]), HEAD, 1).astype(BF16))
        held = [None, jnp.where(is_key, zero, kv[...])]
        held[0] = pltpu.roll(wide(held[1]), HEAD, 1).astype(BF16)
        for i in range(length // BLOCK):
            rows, upto = slice(i * BLOCK, (i + 1) * BLOCK), (i + 1) * BLOCK
            query_slot = i * BLOCK + lax.broadcasted_iota(jnp.int32, (BLOCK, upto), 0)
            key_slot = lax.broadcasted_iota(jnp.int32, (BLOCK, upto), 1)
            allowed = (key_slot <= query_slot) & (key_slot < count)
            total = jnp.zeros((BLOCK, LANES), F32)
            for e in range(2):
                score = dot_nt(qr[rows, j * LANES : (j + 1) * LANES], keys[e][:upto]) * HEAD**-0.5
                score = jnp.where(allowed, score, -1e30)
                expo = jnp.exp(score - jnp.max(score, axis=-1, keepdims=True))
                prob = low(expo / jnp.sum(expo, axis=-1, keepdims=True))
                probs[2 * j + e, rows, :upto] = prob
                total = total + dot(prob, held[e][:upto])
            mix[rows, j * LANES : (j + 1) * LANES] = low(total)

    attend(0)
    gather.relay_z(3)
    gather.relay_x(4)
    for j in range(1, q_tiles):
        attend(j)
    gather.relay_z(4)
    gather.finish(2)
    z_proj[...] = dot(normed[...], w_in_all[:, narrow_width + inner :])
    rate = -jnp.exp(head_terms[0:1, :])
    causal = triangle()

    def scan_block(i, carry):
        rows = pl.ds(pl.multiple_of(i * BLOCK, BLOCK), BLOCK)
        step = steps[rows, :]
        total = exact_dot(causal.astype(F32), step * rate)
        total_t = total.T
        last = total[BLOCK - 1 : BLOCK, :]
        grown, rest = jnp.exp(total), jnp.exp(last - total)
        b_low, c_low = low(conv_bc[rows, :NSTATE]), low(conv_bc[rows, NSTATE:])
        inner_prod = jnp.where(causal, dot_nt(c_low, b_low), 0.0)
        states[i] = state[...]
        crossed = dot(c_low, low(state[...]))
        left = first_head(BLOCK)
        for j in range(tiles):
            cols = slice(j * LANES, (j + 1) * LANES)
            stepped = spread(step, j) * conv_x[rows, cols]
            mixing = []
            for h in (2 * j, 2 * j + 1):
                gap = jnp.minimum(total[:, h : h + 1] - total_t[h : h + 1, :], 0.0)
                mixing.append(low(jnp.exp(gap) * inner_prod))
            stacked = jnp.concatenate(
                [low(jnp.where(left, stepped, 0.0)), low(jnp.where(left, 0.0, stepped))], axis=0
            )
            within = dot(jnp.concatenate(mixing, axis=1), stacked)
            grown_wide = spread(grown, j)
            scanned[rows, cols] = within + crossed[:, cols] * grown_wide
            state[:, cols] = state[:, cols] * grown_wide[BLOCK - 1 : BLOCK, :] + dot_tn(
                b_low, low(stepped * spread(rest, j))
            )
        return carry

    lax.fori_loop(0, length // BLOCK, scan_block, 0)
    for j in range(tiles):
        cols = slice(j * LANES, (j + 1) * LANES)
        gate = z_proj[:, cols]
        skip = spread(head_terms[2:3, :], j)
        result = (scanned[:, cols] + skip * conv_x[:, cols]) * gate * sigmoid(gate)
        mix[:, q_width + j * LANES : q_width + (j + 1) * LANES] = low(result)
    gather.finish(3)
    gather.finish(4)
    grad_copy.wait_recv()
    y_copy.wait_send()
    grad_copy.wait_send()
    gather.drain()


def front(length_of, hidden, out_grad, gain, weights, shared, kernels, head_terms, tables):
    halves = lax.axis_size("fsdp") // 2
    w_query, w_key, w_value, w_step, w_x, w_z, w_attn_out, w_mamba_out = weights
    own, model = hidden.shape
    length, inner, q_width = 2 * own, w_x.shape[1], w_query.shape[1]
    shard = w_x.shape[0]
    narrow_width = q_width + 2 * LANES
    heads = q_width // HEAD
    inside = pl.BlockSpec(memory_space=pltpu.VMEM)
    shape = jax.ShapeDtypeStruct
    blocks = length // BLOCK
    outs = [
        shape((model, narrow_width + 2 * inner), BF16),
        shape((model, q_width + inner), BF16),
        shape((length, model), BF16),
        shape((length, model), BF16),
        shape((length, q_width + inner), BF16),
        shape((length, q_width), BF16),
        shape((length, LANES), BF16),
        shape((heads, length, length), BF16),
        shape((length + 8, inner), F32),
        shape((length, inner), F32),
        shape((length + 8, 2 * NSTATE), F32),
        shape((length, LANES), F32),
        shape((length, inner), F32),
        shape((blocks, NSTATE, inner), F32),
    ]
    return pl.pallas_call(
        partial(front_body, halves),
        out_shape=outs,
        in_specs=[pl.BlockSpec(memory_space=pltpu.SMEM)] + [inside] * 19,
        out_specs=[inside] * len(outs),
        scratch_shapes=[
            pltpu.VMEM((shard, narrow_width), BF16),
            pltpu.VMEM((length, inner), F32),
            pltpu.VMEM((length, 2 * NSTATE), F32),
            pltpu.VMEM((length, LANES), F32),
            pltpu.VMEM((NSTATE, inner), F32),
            pltpu.VMEM((8, LANES), F32),
            pltpu.SemaphoreType.DMA((2, 2)),
        ]
        + gather_sems(5, halves),
        compiler_params=pltpu.CompilerParams(
            collective_id=0, has_side_effects=True, vmem_limit_bytes=VMEM_LIMIT
        ),
        name="front",
    )(length_of, hidden, out_grad, gain, *weights, shared, *kernels, *head_terms, *tables)


def middle_body(
    halves,
    length_ref,
    hidden,
    gain,
    mix,
    w_mix,
    top_grad,
    w_gate,
    w_up,
    w_down,
    gate_grads,
    up_grads,
    down_grads,
    mix_grad,
    resid_grad,
    resid,
    ffn_part,
    gain_grad,
    w_gate_all,
    w_up_all,
    w_down_all,
    normed,
    arrived,
    leaving,
    own_part,
    gate_pre,
    up_pre,
    hidden_grad,
    hidden_low,
    gate_back,
    up_back,
    y_sems,
    *sems,
):
    g, hi, c, t = place()
    own, model = hidden.shape
    length = 2 * own
    pieces = 2
    size = own // pieces
    gather = Gather(
        [
            (w_down, w_down_all, 0, w_down.shape[1]),
            (w_gate, w_gate_all, 0, w_gate.shape[1]),
            (w_up, w_up_all, 0, w_up.shape[1]),
        ],
        halves,
        sems,
    )
    other_y = (g, hi * 2 + c, 1 - t)
    devices = gather.devices + [other_y]
    greet(devices)
    greeted(devices)
    for u in range(3):
        gather.send(u)
    sent = []

    def mine(p):
        start = t * own + p * size
        return pl.ds(pl.multiple_of(start, size), size)

    def other(p):
        start = (1 - t) * own + p * size
        return pl.ds(pl.multiple_of(start, size), size)

    def here(p):
        return slice(p * size, (p + 1) * size)

    def swap(src, dst, slot):
        copy = remote(src, dst, y_sems.at[0, slot], y_sems.at[1, slot], other_y)
        copy.start()
        sent.append(copy)
        return copy

    mixed = []
    for p in range(pieces):
        leaving[0, p] = low(dot_nt(mix[other(p), :], w_mix[...]))
        mixed.append(swap(leaving.at[0, p], arrived.at[0, p], p))
    for p in range(pieces):
        own_part[here(p), :] = dot_nt(mix[mine(p), :], w_mix[...])
    gather.relay_x(0)
    scale = []
    normed_copies = []
    for p in range(pieces):
        mixed[p].wait_recv()
        middle = wide(hidden[here(p), :]) + own_part[here(p), :] + wide(arrived[0, p])
        resid[here(p), :] = middle
        scale.append(rms_scale(middle))
        normed[mine(p), :] = low(middle * scale[p] * gain[...])
        normed_copies.append(
            swap(normed.at[mine(p), :], normed.at[mine(p), :], pieces + p)
        )
    gather.relay_z(0)
    gather.relay_x(1)
    gather.finish(0)
    hidden_grad[...] = dot(top_grad[...], w_down_all[...])
    gather.relay_z(1)
    gather.relay_x(2)
    gather.finish(1)

    for p in range(pieces):
        gate_pre[mine(p), :] = dot(normed[mine(p), :], w_gate_all[...])
    gather.relay_z(2)
    gather.finish(2)
    for p in range(pieces):
        up_pre[mine(p), :] = dot(normed[mine(p), :], w_up_all[...])

    def back(rows):
        gate, up, grad = gate_pre[rows, :], up_pre[rows, :], hidden_grad[rows, :]
        sig = sigmoid(gate)
        silu = gate * sig
        hidden_low[rows, :] = low(silu * up)
        gate_back[rows, :] = low(grad * up * sig * (1.0 + gate * (1.0 - sig)))
        up_back[rows, :] = low(grad * silu)

    for p in range(pieces):
        back(mine(p))
    sums = []
    for p in range(pieces):
        normed_copies[p].wait_recv()
        gate_pre[other(p), :] = dot(normed[other(p), :], w_gate_all[...])
        up_pre[other(p), :] = dot(normed[other(p), :], w_up_all[...])
        back(other(p))
        leaving[1, p] = low(
            dot_nt(gate_back[other(p), :], w_gate_all[...])
            + dot_nt(up_back[other(p), :], w_up_all[...])
        )
        sums.append(swap(leaving.at[1, p], arrived.at[1, p], 2 * pieces + p))
    for p in range(pieces):
        own_part[here(p), :] = dot_nt(gate_back[mine(p), :], w_gate_all[...]) + dot_nt(
            up_back[mine(p), :], w_up_all[...]
        )
    count = length_ref[0]
    total = jnp.zeros((1, model), F32)
    mix_copies = []
    for p in range(pieces):
        sums[p].wait_recv()
        middle = resid[here(p), :]
        grad = own_part[here(p), :] + wide(arrived[1, p])
        total = total + jnp.sum(grad * middle * scale[p], axis=0, keepdims=True)
        weighted = grad * gain[...]
        result = (
            wide(top_grad[mine(p), :])
            + scale[p] * weighted
            - middle
            * (scale[p] * scale[p] * scale[p])
            * jnp.mean(weighted * middle, axis=-1, keepdims=True)
        )
        resid_grad[here(p), :] = result
        mix_grad[mine(p), :] = low(result)
        mix_copies.append(
            swap(mix_grad.at[mine(p), :], mix_grad.at[mine(p), :], 3 * pieces + p)
        )
    gain_grad[...] = total
    ffn_part[...] = low(dot_nt(hidden_low[...], w_down_all[...]))
    span = 256

    def weight_grads(i, carry):
        cols = pl.ds(pl.multiple_of(i * span, span), span)
        blocks, _, rows, width = gate_grads.shape
        per = span // (2 * rows)
        where = pl.ds(i * per, per)
        form = (per, 2, rows, width)
        gate_grads[where] = low(dot_tn(normed[:, cols], gate_back[...])).reshape(form)
        up_grads[where] = low(dot_tn(normed[:, cols], up_back[...])).reshape(form)
        down_grads[where] = low(dot_tn(top_grad[:, cols], hidden_low[...])).reshape(form)
        return carry

    lax.fori_loop(0, model // span, weight_grads, 0)
    for copy in mix_copies:
        copy.wait_recv()
    for copy in sent:
        copy.wait_send()
    gather.drain()


def middle(length_of, hidden, gain, mix, w_mix, top_grad, weights):
    groups, halves = lax.axis_size("grp"), lax.axis_size("fsdp") // 2
    own, model = hidden.shape
    length, width = 2 * own, weights[0].shape[1]
    blocks = groups * halves
    rows = model // (2 * blocks)
    inside = pl.BlockSpec(memory_space=pltpu.VMEM)
    shape = jax.ShapeDtypeStruct
    outs = [shape((blocks, 2, rows, width), BF16)] * 3 + [
        shape((length, model), BF16),
        shape((own, model), F32),
        shape((own, model), F32),
        shape((length, model), BF16),
        shape((1, model), F32),
    ]
    return pl.pallas_call(
        partial(middle_body, halves),
        out_shape=outs,
        in_specs=[pl.BlockSpec(memory_space=pltpu.SMEM)] + [inside] * 8,
        out_specs=[inside] * len(outs),
        scratch_shapes=[pltpu.VMEM((model, width), BF16)] * 3
        + [
            pltpu.VMEM((length, model), BF16),
            pltpu.VMEM((2, 2, own // 2, model), BF16),
            pltpu.VMEM((2, 2, own // 2, model), BF16),
            pltpu.VMEM((own, model), F32),
        ]
        + [pltpu.VMEM((length, width), F32)] * 3
        + [pltpu.VMEM((length, width), BF16)] * 3
        + [pltpu.SemaphoreType.DMA((2, 8))]
        + gather_sems(3, halves),
        compiler_params=pltpu.CompilerParams(
            collective_id=1, has_side_effects=True, vmem_limit_bytes=VMEM_LIMIT
        ),
        name="middle",
    )(length_of, hidden, gain, mix, w_mix, top_grad, *weights)


class Scatter:
    def __init__(self, units, outside, groups, halves, sems):
        self.units, self.outside = units, outside
        self.groups, self.halves = groups, halves
        self.c_sems, self.x_sems, self.z_sems, self.l_sems = sems
        self.g, self.hi, self.c, self.t = place()
        f = self.hi * 2 + self.c
        self.other_core = (self.g, self.hi * 2 + 1 - self.c, self.t)
        self.across = [
            (self.g, lax.rem(self.hi + k, halves) * 2 + self.c, self.t) for k in range(1, halves)
        ]
        self.along = [(lax.rem(self.g + j, groups), f, self.t) for j in range(1, groups)]
        self.devices = [self.other_core] + self.across + self.along
        self.got, self.sent = {}, []

    def start(self, copy):
        copy.start()
        self.sent.append(copy)
        return copy

    def send(self, u):
        part, from_core, pair_sum = self.units[u][:3]
        self.got["c", u] = self.start(
            remote(
                part.at[:, :, 1 - self.c],
                from_core,
                self.c_sems.at[0, u],
                self.c_sems.at[1, u],
                self.other_core,
            )
        )
        if u in self.outside:
            for h in range(self.halves):
                copy = pltpu.make_async_copy(
                    part.at[:, h, self.c], pair_sum.at[h], self.l_sems.at[u, h]
                )
                copy.start()
                self.got["l", u, h] = copy

    def core_stage(self, u):
        part, from_core, pair_sum, from_x = self.units[u][:4]
        self.got.pop(("c", u)).wait_recv()
        if u in self.outside:
            for h in range(self.halves):
                self.got.pop(("l", u, h)).wait()

        def add(i, carry):
            gg, h = i // self.halves, lax.rem(i, self.halves)
            if u in self.outside:
                pair_sum[h, gg] = low(wide(pair_sum[h, gg]) + wide(from_core[gg, h]))
            else:
                total = wide(part[gg, h, self.c]) + wide(from_core[gg, h])
                part[gg, h, self.c] = low(total)
            return carry

        lax.fori_loop(0, self.groups * self.halves, add, 0)
        for k in range(1, self.halves):
            away = lax.rem(self.hi + k, self.halves)
            self.got["x", u, k] = self.start(
                remote(
                    pair_sum.at[away] if u in self.outside else part.at[:, away, self.c],
                    from_x.at[k - 1],
                    self.x_sems.at[0, u, k],
                    self.x_sems.at[1, u, k],
                    self.across[k - 1],
                )
            )

    def x_stage(self, u):
        part, _, pair_sum, from_x, chip_sum, from_z = self.units[u]
        for k in range(1, self.halves):
            self.got.pop(("x", u, k)).wait_recv()

        def add(gg, carry):
            own = pair_sum[self.hi, gg] if u in self.outside else part[gg, self.hi, self.c]
            total = wide(own)
            for k in range(1, self.halves):
                total = total + wide(from_x[k - 1, gg])
            chip_sum[gg] = low(total)
            return carry

        lax.fori_loop(0, self.groups, add, 0)
        for j in range(1, self.groups):
            self.got["z", u, j] = self.start(
                remote(
                    chip_sum.at[lax.rem(self.g + j, self.groups)],
                    from_z.at[j - 1],
                    self.z_sems.at[0, u, j],
                    self.z_sems.at[1, u, j],
                    self.along[j - 1],
                )
            )

    def z_stage(self, u):
        chip_sum, from_z = self.units[u][4:]
        for j in range(1, self.groups):
            self.got.pop(("z", u, j)).wait_recv()
        total = wide(chip_sum[self.g])
        for j in range(1, self.groups):
            total = total + wide(from_z[j - 1])
        return total

    def drain(self):
        assert not self.got
        for copy in self.sent:
            copy.wait_send()


def head_sum(values, tile):
    lane = lax.broadcasted_iota(jnp.int32, (LANES, LANES), 0)
    column = lax.broadcasted_iota(jnp.int32, (LANES, LANES), 1)
    pick = low(jnp.where(column == 2 * tile + jnp.where(lane < HEAD, 0, 1), 1.0, 0.0))
    coarse = low(values)
    fine = low(values - wide(coarse))
    return dot(
        jnp.concatenate([coarse, fine], axis=1), jnp.concatenate([pick, pick], axis=0)
    )


def column_sum(values):
    return jnp.sum(values, axis=0, keepdims=True)


UNITS = 8


def back_body(groups, halves, *refs):
    (
        length_ref,
        hidden,
        gain,
        gain2_part,
        gate_grads,
        up_grads,
        down_grads,
        mix_grad,
        resid_grad,
        resid,
        ffn_part,
        w_in,
        w_mix,
        w_shared,
        normed,
        mix,
        qr,
        kv,
        probs,
        x_padded,
        z_proj,
        bc_padded,
        step_in,
        scanned,
        states,
        conv_main,
        conv_shared,
        decay_log,
        step_bias,
        skip_gain,
        cosine,
        sine,
    ) = refs[:32]
    (
        output,
        grad_in,
        gain_out,
        query_out,
        key_out,
        value_out,
        attn_out,
        z_out,
        x_out,
        step_out,
        shared_out,
        conv_out,
        conv_shared_out,
        decay_out,
        bias_out,
        skip_out,
        mamba_out,
        gain2_out,
        gate_out,
        up_out,
        down_out,
    ) = refs[32:53]
    parts = refs[53:58]
    base = 58
    buffers = []
    for count in (UNITS, 3, UNITS, UNITS, UNITS):
        buffers.append(tuple(refs[base : base + count]) + (None,) * (UNITS - count))
        base += count
    (
        arrived,
        leaving,
        grad_y,
        grad_attn,
        conv_x,
        conv_bc,
        grad_x,
        grad_bc,
        steps,
        back,
        bc_back,
        grown_y,
        faded_x,
        state_back,
        key_sums,
        rows_sum,
        shared_y,
        shared_all,
        vector,
        vec_core,
        vec_x,
        vec_y,
        vec_z,
        y_sems,
        small_sems,
        small_x_sems,
        small_z_sems,
        head_terms,
    ) = refs[base : base + 28]
    scatter = Scatter(
        list(zip((gate_grads, up_grads, down_grads) + parts, *buffers)),
        (0, 1, 2),
        groups,
        halves,
        refs[base + 28 :],
    )
    g, hi, c, t = place()
    own, model = hidden.shape
    length = 2 * own
    inner, q_width = x_out.shape[1], query_out.shape[1]
    kv_width, step_width = key_out.shape[1], step_out.shape[0]
    tiles, q_tiles = inner // LANES, q_width // LANES
    narrow_width = q_width + 2 * LANES
    other_y = (g, hi * 2 + c, 1 - t)
    devices = scatter.devices + [other_y]
    greet(devices)
    pick_heads(head_terms, (decay_log, step_bias, skip_gain), t)
    greeted(devices)
    for u in range(3):
        scatter.send(u)
    mine = pl.ds(pl.multiple_of(t * own, own), own)
    other = pl.ds(pl.multiple_of((1 - t) * own, own), own)
    ffn_copy = scatter.start(
        remote(ffn_part.at[other, :], arrived.at[0], y_sems.at[0, 0], y_sems.at[1, 0], other_y)
    )
    count = length_ref[0]
    span = 256

    def weight_grads(part, left, right, width):
        _, _, _, rows, _ = part.shape
        per = span // (2 * rows)
        flat = groups * halves

        def one(i, carry):
            cols = pl.ds(pl.multiple_of(i * span, span), span)
            value = low(dot_tn(left[:, cols], right()))
            value = value.reshape(per, 2, rows, width)
            for s in range(per):
                at = i * per + s
                part[at // halves, lax.rem(at, halves)] = value[s]
            return carry

        lax.fori_loop(0, model // span, one, 0)

    grad_attn[...] = low(dot(mix_grad[...], w_mix[:, :q_width]))
    grad_y[...] = dot(mix_grad[...], w_mix[:, q_width:])
    scatter.core_stage(0)
    weight_grads(parts[0], mix_grad, lambda: mix[...], q_width + inner)
    scatter.send(3)
    scatter.core_stage(1)

    row = lax.broadcasted_iota(jnp.int32, (length, 1), 0)
    step_pre = step_in[...]
    softplus = jnp.maximum(step_pre, 0.0) + jnp.log(1.0 + jnp.exp(-jnp.abs(step_pre)))
    steps[...] = jnp.where(row < count, softplus, 0.0)
    channel = t * inner

    def taps_of(j):
        return conv_main[:, pl.ds(pl.multiple_of(channel + j * LANES, LANES), LANES)]

    for j in range(2 * NSTATE // LANES):
        cols = slice(j * LANES, (j + 1) * LANES)
        pre = causal_conv(bc_padded, conv_shared[:, cols], length, cols)
        conv_bc[:, cols] = pre * sigmoid(pre)
    skip_sum = jnp.zeros((1, LANES), F32)
    for j in range(tiles):
        cols = slice(j * LANES, (j + 1) * LANES)
        pre = causal_conv(x_padded, taps_of(j), length, cols)
        conv = pre * sigmoid(pre)
        conv_x[:, cols] = conv
        gate = z_proj[:, cols]
        sig = sigmoid(gate)
        grad = grad_y[:, cols]
        value = scanned[:, cols] + spread(head_terms[2:3, :], j) * conv
        at = narrow_width + inner + j * LANES
        back[:, at : at + LANES] = low(grad * value * sig * (1.0 + gate * (1.0 - sig)))
        grad = grad * gate * sig
        grad_y[:, cols] = grad
        rows_sum[j : j + 1, :] = column_sum(grad * conv)
    for j in range(tiles):
        skip_sum = skip_sum + head_sum(rows_sum[0:8, :], j)[j : j + 1, :]
    scatter.core_stage(2)
    weight_grads(parts[1], normed, lambda: back[:, narrow_width + inner :], inner)
    scatter.send(4)
    scatter.x_stage(0)

    is_key = first_head(length)
    zero = jnp.zeros((), BF16)
    key_sums[...] = jnp.zeros_like(key_sums)

    def attend(j):
        tile = slice(j * LANES, (j + 1) * LANES)
        keys = [jnp.where(is_key, kv[...], zero)]
        keys.append(pltpu.roll(wide(keys[0]), HEAD, 1).astype(BF16))
        held = [None, jnp.where(is_key, zero, kv[...])]
        held[0] = pltpu.roll(wide(held[1]), HEAD, 1).astype(BF16)
        for i in range(length // BLOCK):
            rows, upto = slice(i * BLOCK, (i + 1) * BLOCK), (i + 1) * BLOCK
            left = first_head(BLOCK)
            query, grad = qr[rows, tile], grad_attn[rows, tile]
            total = jnp.zeros((BLOCK, LANES), F32)
            for e in range(2):
                prob_low = probs[2 * j + e, rows, :upto]
                prob = wide(prob_low)
                prob_grad = dot_nt(grad, held[e][:upto])
                inside = jnp.sum(prob * prob_grad, axis=-1, keepdims=True)
                score_grad = low(prob * (prob_grad - inside))
                total = total + dot(score_grad, keys[e][:upto])
                side = left if e == 0 else jnp.logical_not(left)
                key_sums[0, :upto, :] += dot_tn(score_grad, jnp.where(side, query, zero))
                key_sums[1, :upto, :] += dot_tn(prob_low, jnp.where(side, grad, zero))
            total = total * HEAD**-0.5
            back[rows, tile] = low(total * cosine[rows, :] - half_swap(total) * sine[rows, :])

    for j in range(q_tiles):
        attend(j)
        if j == 0:
            scatter.core_stage(3)
    key_grad = key_sums[0] + pltpu.roll(key_sums[0], HEAD, 1)
    key_grad = key_grad * HEAD**-0.5
    value_grad = key_sums[1] + pltpu.roll(key_sums[1], HEAD, 1)
    key_grad = key_grad * cosine[...] - half_swap(key_grad) * sine[...]
    back[:, q_width : q_width + LANES] = low(jnp.where(is_key, key_grad, value_grad))
    scatter.x_stage(1)
    scatter.core_stage(4)

    rate = -jnp.exp(head_terms[0:1, :])
    state_back[...] = jnp.zeros_like(state_back)
    upper = triangle(False)
    nblocks = length // BLOCK

    def scan_block(n, carry):
        rate_sum, bias_sum = carry
        i = nblocks - 1 - n
        rows = pl.ds(pl.multiple_of(i * BLOCK, BLOCK), BLOCK)
        step = steps[rows, :]
        total = exact_dot(triangle().astype(F32), step * rate)
        total_t = total.T
        last = total[BLOCK - 1 : BLOCK, :]
        grown, rest = jnp.exp(total), jnp.exp(last - total)
        b_low, c_low = low(conv_bc[rows, :NSTATE]), low(conv_bc[rows, NSTATE:])
        inner_t = jnp.where(upper, dot_nt(b_low, c_low), 0.0)
        state_low = low(state_back[...])
        crossed = dot(b_low, state_low)
        after = states[jnp.minimum(i + 1, nblocks - 1)] * state_back[...]
        left = first_head(BLOCK)
        inner_grad = jnp.zeros((BLOCK, BLOCK), F32)
        total_grad = jnp.zeros((BLOCK, LANES), F32)
        step_grad = jnp.zeros((BLOCK, LANES), F32)
        last_grad = jnp.zeros((8, LANES), F32)
        for j in range(tiles):
            cols = slice(j * LANES, (j + 1) * LANES)
            conv, grad = conv_x[rows, cols], grad_y[rows, cols]
            step_wide, grown_wide, rest_wide = spread(step, j), spread(grown, j), spread(rest, j)
            stepped = step_wide * conv
            grad_low = low(grad)
            mixing = []
            for e, h in enumerate((2 * j, 2 * j + 1)):
                gap = jnp.minimum(total_t[h : h + 1, :] - total[:, h : h + 1], 0.0)
                decay = jnp.exp(gap)
                mixing.append(low(decay * inner_t))
                side = left if e == 0 else jnp.logical_not(left)
                inner_grad = inner_grad + decay * dot_nt(
                    low(jnp.where(side, stepped, 0.0)), grad_low
                )
            stacked = jnp.concatenate(
                [jnp.where(left, grad_low, zero), jnp.where(left, zero, grad_low)], axis=0
            )
            unstepped = dot(jnp.concatenate(mixing, axis=1), stacked) + rest_wide * crossed[:, cols]
            conv_grad = step_wide * unstepped
            total_grad = total_grad + head_sum(
                grad * scanned[rows, cols] - conv * conv_grad, j
            )
            step_grad = step_grad + head_sum(conv * unstepped, j)
            last_grad = last_grad + head_sum(
                jnp.broadcast_to(column_sum(after[:, cols]), (8, LANES)), j
            )
            grad_x[rows, cols] = conv_grad + spread(head_terms[2:3, :], j) * grad
            grown_y[:, cols] = low(grown_wide * grad)
            faded_x[:, cols] = low(stepped * rest_wide)
        inner_low = low(jnp.where(upper, inner_grad, 0.0))
        grad_bc[rows, :NSTATE] = dot_nt(faded_x[...], state_low) + dot(inner_low, c_low)
        grad_bc[rows, NSTATE:] = dot_nt(grown_y[...], low(states[i])) + dot_tn(inner_low, b_low)
        pulled = dot_tn(c_low, grown_y[...])
        for j in range(tiles):
            cols = slice(j * LANES, (j + 1) * LANES)
            fade = spread(grown[BLOCK - 1 : BLOCK, :], j)
            state_back[:, cols] = state_back[:, cols] * fade + pulled[:, cols]
        slot = lax.broadcasted_iota(jnp.int32, (BLOCK, 1), 0)
        total_grad = total_grad + jnp.where(slot == BLOCK - 1, last_grad[0:1, :], 0.0)
        decay_grad = exact_dot(upper.astype(F32), total_grad)
        step_grad = step_grad + rate * decay_grad
        step_grad = jnp.where(i * BLOCK + slot < count, step_grad, 0.0) * sigmoid(step_in[rows, :])
        back[rows, q_width + LANES : narrow_width] = low(step_grad)
        return rate_sum + column_sum(decay_grad * step), bias_sum + column_sum(step_grad)

    empty = jnp.zeros((1, LANES), F32)
    rate_sum, bias_sum = lax.fori_loop(0, nblocks, scan_block, (empty, empty))
    scatter.x_stage(2)

    vector[...] = jnp.zeros_like(vector)

    def place_row(at, value):
        vector[at : at + 1, :] = value

    def place_halves(at, gap, value):
        place_row(at, jnp.where(t == 0, value, 0.0))
        place_row(at + gap, jnp.where(t == 0, 0.0, value))

    place_halves(72, 1, rate_sum * rate)
    place_halves(74, 1, bias_sum)
    place_halves(76, 1, skip_sum)
    for j in range(model // LANES):
        place_row(8 + j, gain2_part[:, j * LANES : (j + 1) * LANES])
    grad_bc[length:, :] = jnp.zeros((8, 2 * NSTATE), F32)
    grad_x[length:, :] = jnp.zeros((8, inner), F32)

    def conv_back(padded, grads, taps, cols, store):
        pre = causal_conv(padded, taps, length, cols)
        sig = sigmoid(pre)
        grads[:length, cols] = grads[:length, cols] * sig * (1.0 + pre * (1.0 - sig))
        for i in range(4):
            store(i, column_sum(grads[:length, cols] * padded[5 + i : 5 + i + length, cols]))
        total = taps[3:4, :] * grads[:length, cols]
        for i in range(3):
            total = total + taps[i : i + 1, :] * grads[3 - i : 3 - i + length, cols]
        return low(total)

    for j in range(2 * NSTATE // LANES):
        cols = slice(j * LANES, (j + 1) * LANES)
        bc_back[:, cols] = conv_back(
            bc_padded,
            grad_bc,
            conv_shared[:, cols],
            cols,
            lambda i, value, j=j: place_row(16 + 2 * i + j, value),
        )
    weight_grads(parts[2], normed, lambda: bc_back[...], 2 * NSTATE)
    scatter.send(5)
    weight_grads(parts[3], normed, lambda: back[:, :narrow_width], narrow_width)
    scatter.send(6)
    for j in range(tiles):
        cols = slice(j * LANES, (j + 1) * LANES)
        at = narrow_width + j * LANES
        back[:, at : at + LANES] = conv_back(
            x_padded,
            grad_x,
            taps_of(j),
            cols,
            lambda i, value, j=j: place_halves(24 + 2 * tiles * i + j, tiles, value),
        )
    weight_grads(parts[4], normed, lambda: back[:, narrow_width : narrow_width + inner], inner)
    scatter.send(7)
    leaving[...] = low(dot_nt(back[other, :], w_in[...]) + dot_nt(bc_back[other, :], w_shared[...]))
    sum_copy = scatter.start(
        remote(leaving, arrived.at[1], y_sems.at[0, 1], y_sems.at[1, 1], other_y)
    )
    scatter.core_stage(5)
    scatter.core_stage(6)
    scatter.core_stage(7)
    scatter.x_stage(3)
    ffn_copy.wait_recv()
    slot = t * own + lax.broadcasted_iota(jnp.int32, (own, 1), 0)
    total = resid[...] + wide(ffn_part[mine, :]) + wide(arrived[0])
    output[...] = low(jnp.where(slot < count, total, 0.0))
    scatter.x_stage(4)
    gate_out[...] = scatter.z_stage(0)
    sum_copy.wait_recv()
    values = wide(hidden[...])
    scale = rms_scale(values)
    grad = dot_nt(back[mine, :], w_in[...]) + dot_nt(bc_back[mine, :], w_shared[...])
    grad = grad + wide(arrived[1])
    gain_row = column_sum(grad * values * scale)
    for j in range(model // LANES):
        place_row(j, gain_row[:, j * LANES : (j + 1) * LANES])
    vec_core[c] = vector[...]
    vec_copy = scatter.start(
        remote(
            vector, vec_core.at[c], small_sems.at[0, 0], small_sems.at[1, 0], scatter.other_core
        )
    )
    weighted = grad * gain[...]
    grad_in[...] = low(
        resid_grad[...]
        + scale * weighted
        - values * (scale * scale * scale) * jnp.mean(weighted * values, axis=-1, keepdims=True)
    )
    up_out[...] = scatter.z_stage(1)
    vec_copy.wait_recv()
    vec_x[hi] = vec_core[0] + vec_core[1]
    vec_copies = [
        scatter.start(
            remote(
                vec_x.at[hi],
                vec_x.at[hi],
                small_x_sems.at[0, 0, k],
                small_x_sems.at[1, 0, k],
                scatter.across[k - 1],
            )
        )
        for k in range(1, halves)
    ]
    scatter.x_stage(5)
    scatter.x_stage(6)
    for copy in vec_copies:
        copy.wait_recv()
    total = vec_x[0]
    for h in range(1, halves):
        total = total + vec_x[h]
    vec_y[t] = total
    vec_copy = scatter.start(
        remote(vec_y.at[t], vec_y.at[t], small_sems.at[0, 1], small_sems.at[1, 1], other_y)
    )
    down_out[...] = scatter.z_stage(2)
    shared_y[t] = scatter.z_stage(5)
    shared_copy = scatter.start(
        remote(shared_y.at[t], shared_y.at[t], small_sems.at[0, 2], small_sems.at[1, 2], other_y)
    )
    scatter.x_stage(7)
    vec_copy.wait_recv()
    vec_z[g] = vec_y[0] + vec_y[1]
    vec_copies = [
        scatter.start(
            remote(
                vec_z.at[g],
                vec_z.at[g],
                small_z_sems.at[0, 0, j],
                small_z_sems.at[1, 0, j],
                scatter.along[j - 1],
            )
        )
        for j in range(1, groups)
    ]
    shared_copy.wait_recv()
    shared_all[g, hi, c] = low(shared_y[0] + shared_y[1])
    shared_copies = [
        scatter.start(
            remote(
                shared_all.at[g, hi, c],
                shared_all.at[g, hi, c],
                small_z_sems.at[0, 1, j],
                small_z_sems.at[1, 1, j],
                scatter.along[j - 1],
            )
        )
        for j in range(1, groups)
    ]
    total = scatter.z_stage(3)
    attn_out[...] = total[:, :q_width]
    mamba_out[...] = total[:, q_width:]
    z_out[...] = scatter.z_stage(4)
    for copy in shared_copies:
        copy.wait_recv()
    shared_copies = [
        scatter.start(
            remote(
                shared_all.at[:, hi, c],
                shared_all.at[:, hi, c],
                small_x_sems.at[0, 1, k],
                small_x_sems.at[1, 1, k],
                scatter.across[k - 1],
            )
        )
        for k in range(1, halves)
    ]
    for copy in vec_copies:
        copy.wait_recv()
    total = vec_z[0]
    for j in range(1, groups):
        total = total + vec_z[j]
    gain_out[...] = total[0:8, :]
    gain2_out[...] = total[8:16, :]
    for i in range(4):
        for j in range(2 * NSTATE // LANES):
            at = 16 + 2 * i + j
            conv_shared_out[i : i + 1, j * LANES : (j + 1) * LANES] = total[at : at + 1, :]
        for j in range(2 * tiles):
            at = 24 + 2 * tiles * i + j
            conv_out[i : i + 1, j * LANES : (j + 1) * LANES] = total[at : at + 1, :]
    for ref, at in ((decay_out, 72), (bias_out, 74), (skip_out, 76)):
        ref[...] = jnp.concatenate(
            [total[at : at + 1, :step_width], total[at + 1 : at + 2, :step_width]], axis=1
        )
    total = scatter.z_stage(6)
    query_out[...] = total[:, :q_width]
    key_out[...] = total[:, q_width : q_width + kv_width]
    value_out[...] = total[:, q_width + kv_width : q_width + 2 * kv_width]
    step_out[...] = total[:, q_width + LANES :].T[:step_width, :]
    for copy in shared_copies:
        copy.wait_recv()
    shared_copy = scatter.start(
        remote(
            shared_all.at[:, :, c],
            shared_all.at[:, :, c],
            small_sems.at[0, 3],
            small_sems.at[1, 3],
            scatter.other_core,
        )
    )
    x_out[...] = scatter.z_stage(7)
    shared_copy.wait_recv()

    def widen(i, carry):
        shared_out[i] = wide(shared_all[i // (2 * halves), lax.rem(i // 2, halves), lax.rem(i, 2)])
        return carry

    lax.fori_loop(0, groups * halves * 2, widen, 0)
    scatter.drain()


def backward(
    length_of, hidden, gain, gain2_part, ffn_grads, mid, w_in, w_mix, w_shared, saved, kernels,
    head_terms, tables, widths,
):
    groups, halves = lax.axis_size("grp"), lax.axis_size("fsdp") // 2
    q_width, kv_width, step_width = widths
    own, model = hidden.shape
    length, inner = 2 * own, w_in.shape[1]
    inner = (inner - q_width - 2 * LANES) // 2
    narrow_width = q_width + 2 * LANES
    rows = model // (2 * groups * halves)
    ffn = ffn_grads[0].shape[-1]
    form = (groups, halves, 2, rows)
    ffn_grads = [a.reshape(form + (ffn,)) for a in ffn_grads]
    inside = pl.BlockSpec(memory_space=pltpu.VMEM)
    anywhere = pl.BlockSpec(memory_space=pl.ANY)
    shape = jax.ShapeDtypeStruct
    outs = [
        shape((own, model), BF16),
        shape((own, model), BF16),
        shape((model // LANES, LANES), F32),
        shape((rows, q_width), F32),
        shape((rows, kv_width), F32),
        shape((rows, kv_width), F32),
        shape((rows, q_width), F32),
        shape((rows, inner), F32),
        shape((rows, inner), F32),
        shape((step_width, rows), F32),
        shape((2 * groups * halves, rows, 2 * NSTATE), F32),
        shape((4, 2 * inner), F32),
        shape((4, 2 * NSTATE), F32),
        shape((1, 2 * step_width), F32),
        shape((1, 2 * step_width), F32),
        shape((1, 2 * step_width), F32),
        shape((rows, inner), F32),
        shape((model // LANES, LANES), F32),
        shape((rows, ffn), F32),
        shape((rows, ffn), F32),
        shape((rows, ffn), F32),
    ]
    all_widths = [ffn] * 3 + [q_width + inner, inner, 2 * NSTATE, narrow_width, inner]
    vector = (80, LANES)
    dma = pltpu.SemaphoreType.DMA
    others = max(halves - 1, 1)
    scratch = (
        [pltpu.VMEM(form + (w,), BF16) for w in all_widths[3:]]
        + [pltpu.VMEM((groups, halves, rows, w), BF16) for w in all_widths]
        + [pltpu.VMEM((halves, groups, rows, w), BF16) for w in all_widths[:3]]
        + [pltpu.VMEM((others, groups, rows, w), BF16) for w in all_widths]
        + [pltpu.VMEM((groups, rows, w), BF16) for w in all_widths]
        + [pltpu.VMEM((groups - 1, rows, w), BF16) for w in all_widths]
        + [
            pltpu.VMEM((2, own, model), BF16),
            pltpu.VMEM((own, model), BF16),
            pltpu.VMEM((length, inner), F32),
            pltpu.VMEM((length, q_width), BF16),
            pltpu.VMEM((length, inner), F32),
            pltpu.VMEM((length, 2 * NSTATE), F32),
            pltpu.VMEM((length + 8, inner), F32),
            pltpu.VMEM((length + 8, 2 * NSTATE), F32),
            pltpu.VMEM((length, LANES), F32),
            pltpu.VMEM((length, narrow_width + 2 * inner), BF16),
            pltpu.VMEM((length, 2 * NSTATE), BF16),
            pltpu.VMEM((BLOCK, inner), BF16),
            pltpu.VMEM((BLOCK, inner), BF16),
            pltpu.VMEM((NSTATE, inner), F32),
            pltpu.VMEM((2, length, LANES), F32),
            pltpu.VMEM((8, LANES), F32),
            pltpu.VMEM((2, rows, 2 * NSTATE), F32),
            pltpu.VMEM((groups, halves, 2, rows, 2 * NSTATE), BF16),
            pltpu.VMEM(vector, F32),
            pltpu.VMEM((2,) + vector, F32),
            pltpu.VMEM((halves,) + vector, F32),
            pltpu.VMEM((2,) + vector, F32),
            pltpu.VMEM((groups,) + vector, F32),
            dma((2, 2)),
            dma((2, 4)),
            dma((2, 2, halves)),
            dma((2, 2, groups)),
            pltpu.VMEM((8, LANES), F32),
            dma((2, UNITS)),
            dma((2, UNITS, halves)),
            dma((2, UNITS, groups)),
            dma((UNITS, halves)),
        ]
    )
    return pl.pallas_call(
        partial(back_body, groups, halves),
        out_shape=outs,
        in_specs=[pl.BlockSpec(memory_space=pltpu.SMEM)]
        + [inside] * 3
        + [anywhere] * 3
        + [inside] * 25,
        out_specs=[inside] * len(outs),
        scratch_shapes=scratch,
        compiler_params=pltpu.CompilerParams(
            collective_id=2, has_side_effects=True, vmem_limit_bytes=VMEM_LIMIT
        ),
        name="back",
    )(
        length_of, hidden, gain, gain2_part, *ffn_grads, *mid, w_in, w_mix, w_shared, *saved,
        *kernels, *head_terms, *tables,
    )


def emit_body(*refs):
    count = len(refs) // 2
    for source, target in zip(refs[:count], refs[count:]):
        target[...] = source[...]


def emit(arrays):
    inside = pl.BlockSpec(memory_space=pltpu.VMEM)
    return pl.pallas_call(
        emit_body,
        out_shape=[jax.ShapeDtypeStruct(a.shape, a.dtype) for a in arrays],
        in_specs=[inside] * len(arrays),
        out_specs=[inside] * len(arrays),
        compiler_params=pltpu.CompilerParams(vmem_limit_bytes=VMEM_LIMIT),
        name="emit",
    )(*arrays)


def local(
    hidden_in,
    lengths,
    norm1_gain,
    w_query,
    key_weight,
    value_weight,
    w_attn_out,
    w_mamba_z,
    w_mamba_x,
    w_step,
    w_shared,
    conv_main,
    conv_shared,
    decay_log,
    step_bias,
    skip_gain,
    w_mamba_out,
    norm2_gain,
    w_ffn_gate,
    w_ffn_up,
    w_ffn_down,
    out_grad,
):
    own, model = hidden_in.shape
    step_width = w_step.shape[1]
    head_terms = [v.reshape(1, -1) for v in (decay_log, step_bias, skip_gain)]
    tables = rotary_tables(2 * own)
    gain1, gain2 = norm1_gain.reshape(1, model), norm2_gain.reshape(1, model)
    kernels = (conv_main, conv_shared)
    w_in, w_mix, normed, top_grad, mix, *saved = front(
        lengths,
        hidden_in,
        out_grad,
        gain1,
        (w_query, key_weight.T, value_weight.T, w_step.T, w_mamba_x, w_mamba_z, w_attn_out, w_mamba_out),
        w_shared,
        kernels,
        head_terms,
        tables,
    )
    *ffn_grads, mix_grad, resid_grad, resid, ffn_part, gain2_part = middle(
        lengths, hidden_in, gain2, mix, w_mix, top_grad, (w_ffn_gate, w_ffn_up, w_ffn_down)
    )
    outs = backward(
        lengths,
        hidden_in,
        gain1,
        gain2_part,
        ffn_grads,
        (mix_grad, resid_grad, resid, ffn_part),
        w_in,
        w_mix,
        w_shared,
        (normed, mix, *saved),
        kernels,
        head_terms,
        tables,
        (w_query.shape[1], key_weight.shape[1], step_width),
    )
    outs = list(emit(outs))
    outs[9] = outs[9].T
    for i in (2, 13, 14, 15, 17):
        outs[i] = outs[i].reshape(-1)
    outs[10] = outs[10].reshape(model, -1)
    return tuple(outs)


def solution(mesh):
    rows, whole, weight = P(("grp", "fsdp", "tp"), None), P(), P("fsdp", "tp")
    grad = P(("grp", "fsdp"), "tp")
    return jax.shard_map(
        local,
        mesh=mesh,
        in_specs=(rows, P(("grp", "fsdp")), whole)
        + (weight,) * 7
        + (whole,) * 6
        + (weight, whole)
        + (weight,) * 3
        + (rows,),
        out_specs=(rows, rows, whole)
        + (grad,) * 7
        + (whole,) * 6
        + (grad, whole)
        + (grad,) * 3,
        check_vma=False,
    )
```

```python
from functools import partial
from typing import Any, NamedTuple

import jax
import jax.numpy as jnp
import numpy as np
from jax import lax
from jax.experimental import pallas as pl
from jax.experimental.pallas import tpu as pltpu
from jax.sharding import PartitionSpec as P

HEAD = 64
LANES = 128
BLOCK = 128
NSTATE = 128
EPS = 1e-05
ROPE_BASE = 100000000000.0
MESH = pl.DeviceIdType.MESH
VMEM_LIMIT = 62 << 20
F32, BF16 = jnp.float32, jnp.bfloat16
EXACT = lax.Precision.HIGHEST


def low(values):
    return values.astype(BF16)


def wide(values):
    return values.astype(F32)


def dot(a, b):
    return jnp.dot(a, b, preferred_element_type=F32)


def dot_nt(a, b):
    return lax.dot_general(a, b, (((1,), (1,)), ((), ())), preferred_element_type=F32)


def dot_tn(a, b):
    return lax.dot_general(a, b, (((0,), (0,)), ((), ())), preferred_element_type=F32)


def exact_dot(a, b):
    return jnp.dot(a, b, precision=EXACT, preferred_element_type=F32)


def split(values):
    coarse = low(values)
    return coarse, low(values - wide(coarse))


def split_dot(a, b):
    return dot(jnp.concatenate([a[0], a[0], a[1]], axis=1), jnp.concatenate([b[0], b[1], b[0]], axis=0))


def split_dot_nt(a, b):
    return dot_nt(jnp.concatenate([a[0], a[0], a[1]], axis=1), jnp.concatenate([b[0], b[1], b[0]], axis=1))


def split_dot_tn(a, b):
    return dot_tn(jnp.concatenate([a[0], a[0], a[1]], axis=0), jnp.concatenate([b[0], b[1], b[0]], axis=0))


def sigmoid(v):
    return 1.0 / (1.0 + jnp.exp(-v))


def rms_scale(values):
    return lax.rsqrt(jnp.mean(values * values, axis=-1, keepdims=True) + EPS)


def lane_ids(rows):
    return lax.broadcasted_iota(jnp.int32, (rows, LANES), 1)


def first_head(rows):
    return lane_ids(rows) < HEAD


def half_swap(tile):
    lower = lax.rem(lane_ids(tile.shape[0]), HEAD) < HEAD // 2
    return jnp.where(lower, pltpu.roll(tile, LANES - HEAD // 2, 1), pltpu.roll(tile, HEAD // 2, 1))


def spread(values, tile):
    return jnp.where(
        first_head(values.shape[0]),
        values[:, 2 * tile : 2 * tile + 1],
        values[:, 2 * tile + 1 : 2 * tile + 2],
    )


def rotary_tables(length):
    positions = np.arange(length, dtype=np.float64)[:, None]
    power = np.arange(HEAD // 2, dtype=np.float64) * (-2.0 / HEAD)
    phase = (positions * np.power(ROPE_BASE, power)[None, :]).astype(np.float32)
    cosine, sine = np.cos(phase), np.sin(phase)
    return (
        np.concatenate([cosine] * 4, axis=1).astype(np.float32),
        np.concatenate([-sine, sine] * 2, axis=1).astype(np.float32),
    )


def place():
    g, f, t = lax.axis_index("grp"), lax.axis_index("fsdp"), lax.axis_index("tp")
    return g, f // 2, lax.rem(f, 2), t


def greet(devices):
    barrier = pltpu.get_barrier_semaphore()
    for device in devices:
        pl.semaphore_signal(barrier, inc=1, device_id=device, device_id_type=MESH)


def greeted(devices):
    pl.semaphore_wait(pltpu.get_barrier_semaphore(), len(devices))


def remote(src, dst, send, recv, device):
    return pltpu.make_async_remote_copy(
        src_ref=src,
        dst_ref=dst,
        send_sem=send,
        recv_sem=recv,
        device_id=device,
        device_id_type=MESH,
    )


def pick_heads(terms, whole, t):
    terms[...] = jnp.zeros_like(terms)
    for i, ref in enumerate(whole):
        heads = ref.shape[1] // 2
        terms[i : i + 1, :heads] = jnp.where(t == 0, ref[:, :heads], ref[:, heads:])


class Gather:
    def __init__(self, units, halves, sems):
        self.units, self.halves = units, halves
        self.x, self.z, self.cx, self.cz, self.own, self.local = sems
        g, self.hi, self.c, t = place()
        f = self.hi * 2 + self.c
        self.f, self.pair = f, lax.rem(g, 2)
        self.other_core = (g, self.hi * 2 + 1 - self.c, t)
        self.other_z = (g + 1 - 2 * self.pair, f, t)
        self.across = [
            (g, lax.rem(self.hi + k, halves) * 2 + self.c, t) for k in range(1, halves)
        ]
        self.devices = [self.other_core, self.other_z] + self.across
        self.got, self.sent, self.pending = {}, [], {}

    def block(self, u, owner, part=None):
        shard, full, column, width = self.units[u]
        rows = shard.shape[0]
        size = rows if part is None else rows // 2
        start = owner * rows + (0 if part is None else part * size)
        return full.at[pl.ds(pl.multiple_of(start, size), size), pl.ds(column, width)]

    def start(self, copy):
        copy.start()
        self.sent.append(copy)
        return copy

    def send(self, u):
        shard = self.units[u][0]
        half = shard.shape[0] // 2
        mine = shard.at[pl.ds(pl.multiple_of(self.pair * half, half), half), :]
        for k in range(1, self.halves):
            self.got["x", u, k] = self.start(
                remote(
                    mine,
                    self.block(u, self.f, self.pair),
                    self.x.at[0, u, k],
                    self.x.at[1, u, k],
                    self.across[k - 1],
                )
            )
        self.got["own", u] = self.start(
            remote(
                shard,
                self.block(u, self.f),
                self.own.at[0, u],
                self.own.at[1, u],
                self.other_core,
            )
        )
        self.pending[u] = pltpu.make_async_copy(shard, self.block(u, self.f), self.local.at[u])
        self.pending[u].start()

    def owner(self, k):
        return lax.rem(self.hi - k + self.halves, self.halves) * 2 + self.c

    def relay_x(self, u):
        for k in range(1, self.halves):
            self.got.pop(("x", u, k)).wait_recv()
            block = self.block(u, self.owner(k), self.pair)
            self.got["z", u, k] = self.start(
                remote(block, block, self.z.at[0, u, k], self.z.at[1, u, k], self.other_z)
            )
            self.got["cx", u, k] = self.start(
                remote(block, block, self.cx.at[0, u, k], self.cx.at[1, u, k], self.other_core)
            )

    def relay_z(self, u):
        for k in range(1, self.halves):
            self.got.pop(("z", u, k)).wait_recv()
            block = self.block(u, self.owner(k), 1 - self.pair)
            self.got["cz", u, k] = self.start(
                remote(block, block, self.cz.at[0, u, k], self.cz.at[1, u, k], self.other_core)
            )

    def finish(self, u):
        self.got.pop(("own", u)).wait_recv()
        for k in range(1, self.halves):
            self.got.pop(("cx", u, k)).wait_recv()
            self.got.pop(("cz", u, k)).wait_recv()
        self.pending.pop(u).wait()

    def drain(self):
        assert not self.got and not self.pending
        for copy in self.sent:
            copy.wait_send()


def gather_sems(units, halves):
    dma = pltpu.SemaphoreType.DMA
    return [dma((2, units, halves))] * 4 + [dma((2, units)), dma((units,))]


def causal_conv(padded, kernel, rows, cols):
    total = kernel[3:4, :] * padded[8 : 8 + rows, cols]
    for i in range(3):
        total = total + kernel[i : i + 1, :] * padded[5 + i : 5 + i + rows, cols]
    return total


def triangle(lower=True):
    row = lax.broadcasted_iota(jnp.int32, (BLOCK, BLOCK), 0)
    col = lax.broadcasted_iota(jnp.int32, (BLOCK, BLOCK), 1)
    return row >= col if lower else row <= col


class Scatter:
    def __init__(self, units, groups, halves, sems):
        self.units = units
        self.groups, self.halves = groups, halves
        self.c_sems, self.x_sems, self.z_sems, self.l_sems = sems
        self.g, self.hi, self.c, self.t = place()
        f = self.hi * 2 + self.c
        self.other_core = (self.g, self.hi * 2 + 1 - self.c, self.t)
        self.across = [
            (self.g, lax.rem(self.hi + k, halves) * 2 + self.c, self.t) for k in range(1, halves)
        ]
        self.along = [(lax.rem(self.g + j, groups), f, self.t) for j in range(1, groups)]
        self.devices = [self.other_core] + self.across + self.along
        self.outer = (self.g == 0) | (self.g == groups - 1)
        self.got, self.sent, self.lines = {}, [], []

    def start(self, copy):
        copy.start()
        self.sent.append(copy)
        return copy

    def send(self, u):
        unit = self.units[u]
        self.got["c", u] = self.start(
            remote(
                unit["part"].at[:, :, 1 - self.c],
                unit["from_core"],
                self.c_sems.at[0, u],
                self.c_sems.at[1, u],
                self.other_core,
            )
        )

    def send_x(self, u):
        unit = self.units[u]
        for k in range(1, self.halves):
            away = lax.rem(self.hi + k, self.halves)
            self.got["x", u, k] = self.start(
                remote(
                    unit["pair_sum"].at[away]
                    if "pair_sum" in unit
                    else unit["part"].at[:, away, self.c],
                    unit["from_x"].at[k - 1],
                    self.x_sems.at[0, u, k],
                    self.x_sems.at[1, u, k],
                    self.across[k - 1],
                )
            )
        if "pair_sum" in unit:
            self.load(u, unit["pair_sum"].at[self.hi], unit["own_pair"])

    def load(self, u, source, target):
        self.got["l", u] = pltpu.make_async_copy(source, target, self.l_sems.at[u])
        self.got["l", u].start()

    def z_links(self, u):
        unit, g = self.units[u], self.g
        chip, into, last = unit["chip_sum"], unit["from_z"], self.groups - 1

        def to(where):
            return (where, self.hi * 2 + self.c, self.t)

        near = jnp.where(g == 0, 1, last - 1)
        outer = {
            0: (chip.at[near], into.at[0], to(near)),
            1: (chip.at[last - near], into.at[1], to(last - near)),
            3: (chip.at[last - g], unit["relay"], to(near)),
        }
        end = jnp.where(g == 1, 0, last)
        inner = {
            0: (chip.at[end], into.at[0], to(end)),
            1: (chip.at[last - end], into.at[1], to(last - end)),
            2: (chip.at[last - g], into.at[2], to(last - g)),
        }
        return outer, inner

    def z_copy(self, u, side, slot):
        source, target, device = self.z_links(u)[side][slot]
        return remote(
            source, target, self.z_sems.at[0, u, slot], self.z_sems.at[1, u, slot], device
        )

    def send_z(self, u):
        unit = self.units[u]
        if self.groups == 4:

            @pl.when(self.outer)
            def _():
                for slot in (3, 0, 1):
                    self.z_copy(u, 0, slot).start()

            @pl.when(jnp.logical_not(self.outer))
            def _():
                for slot in (2, 0):
                    self.z_copy(u, 1, slot).start()

            self.lines.append(u)
            return
        for j in range(1, self.groups):
            self.got["z", u, j] = self.start(
                remote(
                    unit["chip_sum"].at[lax.rem(self.g + j, self.groups)],
                    unit["from_z"].at[j - 1],
                    self.z_sems.at[0, u, j],
                    self.z_sems.at[1, u, j],
                    self.along[j - 1],
                )
            )

    def relay(self, u):
        if self.groups != 4:
            return
        unit = self.units[u]

        @pl.when(jnp.logical_not(self.outer))
        def _():
            self.z_copy(u, 0, 3).wait_recv()
            far = jnp.where(self.g == 1, self.groups - 1, 0)
            chip = unit["chip_sum"]
            chip[far] = low(wide(chip[far]) + wide(unit["relay"][...]))
            self.z_copy(u, 1, 1).start()

    def core_stage(self, u):
        part, from_core = self.units[u]["part"], self.units[u]["from_core"]
        self.got.pop(("c", u)).wait_recv()

        def add(i, carry):
            gg, h = i // self.halves, lax.rem(i, self.halves)
            part[gg, h, self.c] = low(wide(part[gg, h, self.c]) + wide(from_core[gg, h]))
            return carry

        lax.fori_loop(0, self.groups * self.halves, add, 0)

    def x_stage(self, u):
        unit = self.units[u]
        for k in range(1, self.halves):
            self.got.pop(("x", u, k)).wait_recv()
        if "pair_sum" in unit:
            self.got.pop(("l", u)).wait()

        def add(gg, carry):
            if "pair_sum" in unit:
                total = wide(unit["own_pair"][gg])
            else:
                total = wide(unit["part"][gg, self.hi, self.c])
            for k in range(1, self.halves):
                total = total + wide(unit["from_x"][k - 1, gg])
            unit["chip_sum"][gg] = low(total)
            return carry

        lax.fori_loop(0, self.groups, add, 0)

    def z_stage(self, u):
        unit = self.units[u]
        total = wide(unit["chip_sum"][self.g])
        if self.groups == 4:
            for slot in (0, 1):
                self.z_copy(u, 1, slot).wait_recv()

            @pl.when(jnp.logical_not(self.outer))
            def _():
                self.z_copy(u, 1, 2).wait_recv()

            total = total + wide(unit["from_z"][0]) + wide(unit["from_z"][1])
            return total + jnp.where(self.outer, 0.0, wide(unit["from_z"][2]))
        for j in range(1, self.groups):
            self.got.pop(("z", u, j)).wait_recv()
            total = total + wide(unit["from_z"][j - 1])
        return total

    def drain(self):
        assert not self.got
        for copy in self.sent:
            copy.wait_send()
        if not self.lines:
            return

        @pl.when(self.outer)
        def _():
            for u in self.lines:
                for slot in (0, 1, 3):
                    self.z_copy(u, 0, slot).wait_send()

        @pl.when(jnp.logical_not(self.outer))
        def _():
            for u in self.lines:
                for slot in (0, 1, 2):
                    self.z_copy(u, 1, slot).wait_send()


class Mover:
    def __init__(self, sems):
        self.sems, self.count, self.copies = sems, 0, {}

    def start(self, name, source, target):
        self.copies[name] = pltpu.make_async_copy(source, target, self.sems.at[self.count])
        self.copies[name].start()
        self.count += 1

    def wait(self, *names):
        for name in names:
            self.copies.pop(name).wait()

    def drain(self):
        self.wait(*list(self.copies))


def scatter_sems(units, groups, halves):
    dma = pltpu.SemaphoreType.DMA
    return [
        dma((2, units)),
        dma((2, units, halves)),
        dma((2, units, groups)),
        dma((units,)),
    ]


def head_sum(values, tile):
    lane = lax.broadcasted_iota(jnp.int32, (LANES, LANES), 0)
    column = lax.broadcasted_iota(jnp.int32, (LANES, LANES), 1)
    pick = low(jnp.where(column == 2 * tile + jnp.where(lane < HEAD, 0, 1), 1.0, 0.0))
    coarse = low(values)
    fine = low(values - wide(coarse))
    return dot(
        jnp.concatenate([coarse, fine], axis=1), jnp.concatenate([pick, pick], axis=0)
    )


def column_sum(values):
    return jnp.sum(values, axis=0, keepdims=True)


class ForwardIn(NamedTuple):
    length_ref: Any
    hidden: Any
    out_grad: Any
    gain1: Any
    gain2: Any
    w_query: Any
    w_key: Any
    w_value: Any
    w_step: Any
    w_x: Any
    w_z: Any
    w_attn_out: Any
    w_mamba_out: Any
    w_down: Any
    w_gate: Any
    w_up: Any
    w_shared: Any
    conv_main: Any
    conv_shared: Any
    decay_log: Any
    step_bias: Any
    skip_gain: Any
    cosine: Any
    sine: Any


class Kept(NamedTuple):
    w_in: Any
    w_mix: Any
    normed: Any
    mix: Any
    qr: Any
    kv: Any
    probs: Any
    x_padded: Any
    z_proj: Any
    bc_padded: Any
    step_in: Any
    scanned: Any
    states: Any
    mix_grad: Any
    resid_grad: Any
    resid: Any
    ffn_part: Any
    down_chip: Any
    gate_pair: Any
    up_pair: Any
    gain2_part: Any


class ForwardScratch(NamedTuple):
    shared: Any
    top_grad: Any
    narrow: Any
    conv_x: Any
    conv_bc: Any
    steps: Any
    state: Any
    head_terms: Any
    w_down: Any
    w_gate: Any
    w_up: Any
    normed2: Any
    arrived: Any
    leaving: Any
    own_part: Any
    gate_pre: Any
    up_pre: Any
    hidden_low: Any
    gate_back: Any
    up_back: Any
    p_down: Any
    p_gate: Any
    p_up: Any
    c_down: Any
    c_gate: Any
    c_up: Any
    x_down: Any
    d_chip: Any
    y_sems: Any
    move_sems: Any


def forward_body(groups, halves, *refs):
    counts = len(ForwardIn._fields), len(Kept._fields) - 1
    r = ForwardIn(*refs[: counts[0]])
    out = Kept(*refs[counts[0] : sum(counts) + 1])
    rest = refs[sum(counts) + 1 :]
    v = Kept(*rest[:17], *[None] * (counts[1] - 16))
    s = ForwardScratch(*rest[17:47])
    sems = rest[47:]
    g, hi, c, t = place()
    own, model = r.hidden.shape
    length = 2 * own
    inner, ffn = r.w_x.shape[1], r.w_gate.shape[1]
    q_width, step_width = r.w_query.shape[1], r.w_step.shape[0]
    tiles, q_tiles = inner // LANES, q_width // LANES
    narrow_width = q_width + 2 * LANES
    gather = Gather(
        [
            (s.narrow, v.w_in, 0, narrow_width),
            (r.w_x, v.w_in, narrow_width, inner),
            (r.w_z, v.w_in, narrow_width + inner, inner),
            (r.w_attn_out, v.w_mix, 0, q_width),
            (r.w_mamba_out, v.w_mix, q_width, inner),
            (r.w_gate, s.w_gate, 0, ffn),
            (r.w_up, s.w_up, 0, ffn),
            (r.w_down, s.w_down, 0, ffn),
        ],
        halves,
        sems[:6],
    )
    scatter = Scatter(
        [
            dict(part=s.p_down, from_core=s.c_down, from_x=s.x_down, chip_sum=s.d_chip),
            dict(part=s.p_gate, from_core=s.c_gate),
            dict(part=s.p_up, from_core=s.c_up),
        ],
        groups,
        halves,
        sems[6:],
    )
    move = Mover(s.move_sems)
    other_y = (g, hi * 2 + c, 1 - t)
    devices = gather.devices + [other_y]
    greet(devices)
    move.start("shared", r.w_shared, s.shared)
    turned = jnp.concatenate([wide(r.w_key[...]), wide(r.w_value[...])], axis=0).T
    s.narrow[:, :q_width] = r.w_query[...]
    s.narrow[:, q_width : q_width + LANES] = low(turned)
    filler = jnp.zeros((LANES - step_width, s.narrow.shape[0]), F32)
    turned = jnp.concatenate([wide(r.w_step[...]), filler], axis=0).T
    s.narrow[:, q_width + LANES :] = low(turned)
    mine = pl.ds(pl.multiple_of(t * own, own), own)
    other = pl.ds(pl.multiple_of((1 - t) * own, own), own)
    values = wide(r.hidden[...])
    v.normed[mine, :] = low(values * rms_scale(values) * r.gain1[...])
    count = r.length_ref[0]
    slot = t * own + lax.broadcasted_iota(jnp.int32, (own, 1), 0)
    s.top_grad[mine, :] = jnp.where(slot < count, r.out_grad[...], jnp.zeros((), BF16))
    greeted(devices)
    gather.send(0)
    sent = []

    def swap(src, dst, at):
        copy = remote(src, dst, s.y_sems.at[0, at], s.y_sems.at[1, at], other_y)
        copy.start()
        sent.append(copy)
        return copy

    y_copy = swap(v.normed.at[mine, :], v.normed.at[mine, :], 8)
    for u in range(1, 8):
        gather.send(u)
    grad_copy = swap(s.top_grad.at[mine, :], s.top_grad.at[mine, :], 9)
    pick_heads(s.head_terms, (r.decay_log, r.step_bias, r.skip_gain), t)
    v.x_padded[0:8, :] = jnp.zeros((8, inner), F32)
    v.bc_padded[0:8, :] = jnp.zeros((8, 2 * NSTATE), F32)
    s.state[...] = jnp.zeros_like(s.state)

    def save(*names):
        for name in names:
            move.start(name, getattr(v, name), getattr(out, name))

    move.wait("shared")
    v.bc_padded[pl.ds(pl.multiple_of(8 + t * own, 8), own), :] = dot(
        v.normed[mine, :], s.shared[...]
    )
    gather.relay_x(0)
    gather.relay_z(0)
    gather.relay_x(1)
    y_copy.wait_recv()
    save("normed")
    v.bc_padded[pl.ds(pl.multiple_of(8 + (1 - t) * own, 8), own), :] = dot(
        v.normed[other, :], s.shared[...]
    )
    gather.finish(0)
    projected = dot(v.normed[...], v.w_in[:, :narrow_width])
    for j in range(q_tiles):
        tile = projected[:, j * LANES : (j + 1) * LANES]
        turned = tile * r.cosine[...] + half_swap(tile) * r.sine[...]
        v.qr[:, j * LANES : (j + 1) * LANES] = low(turned)
    tile = projected[:, q_width : q_width + LANES]
    is_key = first_head(length)
    turned = tile * r.cosine[...] + half_swap(tile) * r.sine[...]
    v.kv[...] = low(jnp.where(is_key, turned, tile))
    step_pre = projected[:, q_width + LANES :] + s.head_terms[1:2, :]
    v.step_in[...] = step_pre
    row = lax.broadcasted_iota(jnp.int32, (length, 1), 0)
    softplus = jnp.maximum(step_pre, 0.0) + jnp.log(1.0 + jnp.exp(-jnp.abs(step_pre)))
    s.steps[...] = jnp.where(row < count, softplus, 0.0)
    save("qr", "kv", "step_in", "bc_padded")
    for j in range(2 * NSTATE // LANES):
        cols = slice(j * LANES, (j + 1) * LANES)
        pre = causal_conv(v.bc_padded, r.conv_shared[:, cols], length, cols)
        s.conv_bc[:, cols] = pre * sigmoid(pre)
    def attend(j):
        zero = jnp.zeros((), BF16)
        keys = [jnp.where(is_key, v.kv[...], zero)]
        keys.append(low(pltpu.roll(wide(keys[0]), HEAD, 1)))
        held = [None, jnp.where(is_key, zero, v.kv[...])]
        held[0] = low(pltpu.roll(wide(held[1]), HEAD, 1))
        for i in range(length // BLOCK):
            rows, upto = slice(i * BLOCK, (i + 1) * BLOCK), (i + 1) * BLOCK
            query_slot = i * BLOCK + lax.broadcasted_iota(jnp.int32, (BLOCK, upto), 0)
            key_slot = lax.broadcasted_iota(jnp.int32, (BLOCK, upto), 1)
            allowed = (key_slot <= query_slot) & (key_slot < count)
            total = jnp.zeros((BLOCK, LANES), F32)
            for e in range(2):
                score = dot_nt(v.qr[rows, j * LANES : (j + 1) * LANES], keys[e][:upto])
                score = jnp.where(allowed, score * HEAD**-0.5, -1e30)
                expo = jnp.exp(score - jnp.max(score, axis=-1, keepdims=True))
                prob = low(expo / jnp.sum(expo, axis=-1, keepdims=True))
                v.probs[2 * j + e, rows, :upto] = prob
                total = total + dot(prob, held[e][:upto])
            v.mix[rows, j * LANES : (j + 1) * LANES] = low(total)

    attend(0)
    gather.relay_z(1)
    gather.relay_x(2)
    for j in range(1, q_tiles):
        attend(j)
    save("probs")
    gather.finish(1)
    v.x_padded[8:, :] = dot(v.normed[...], v.w_in[:, narrow_width : narrow_width + inner])
    save("x_padded")
    channel = t * inner
    for j in range(tiles):
        if j == tiles // 2:
            gather.relay_x(3)
            gather.relay_z(2)
        cols = slice(j * LANES, (j + 1) * LANES)
        taps = r.conv_main[:, pl.ds(pl.multiple_of(channel + j * LANES, LANES), LANES)]
        pre = causal_conv(v.x_padded, taps, length, cols)
        s.conv_x[:, cols] = pre * sigmoid(pre)
    gather.relay_x(4)
    rate = -jnp.exp(s.head_terms[0:1, :])
    causal = triangle()

    def scan_block(i):
        rows = slice(i * BLOCK, (i + 1) * BLOCK)
        step = s.steps[rows, :]
        total = exact_dot(causal.astype(F32), step * rate)
        total_t = total.T
        last = total[BLOCK - 1 : BLOCK, :]
        grown, rest = jnp.exp(total), jnp.exp(last - total)
        b_mat, c_mat = split(s.conv_bc[rows, :NSTATE]), split(s.conv_bc[rows, NSTATE:])
        inner_prod = jnp.where(causal, split_dot_nt(c_mat, b_mat), 0.0)
        v.states[i] = s.state[...]
        crossed = split_dot(c_mat, split(s.state[...]))
        left = first_head(BLOCK)
        for j in range(tiles):
            cols = slice(j * LANES, (j + 1) * LANES)
            stepped = spread(step, j) * s.conv_x[rows, cols]
            mixing = []
            for h in (2 * j, 2 * j + 1):
                gap = jnp.minimum(total[:, h : h + 1] - total_t[h : h + 1, :], 0.0)
                mixing.append(jnp.exp(gap) * inner_prod)
            stacked = jnp.concatenate(
                [jnp.where(left, stepped, 0.0), jnp.where(left, 0.0, stepped)], axis=0
            )
            within = split_dot(split(jnp.concatenate(mixing, axis=1)), split(stacked))
            grown_wide = spread(grown, j)
            v.scanned[rows, cols] = within + crossed[:, cols] * grown_wide
            s.state[:, cols] = s.state[:, cols] * grown_wide[BLOCK - 1 : BLOCK, :] + split_dot_tn(
                b_mat, split(stepped * spread(rest, j))
            )

    for i in range(length // BLOCK):
        scan_block(i)
        if i == 0:
            gather.relay_z(3)
            gather.finish(2)
            v.z_proj[...] = dot(v.normed[...], v.w_in[:, narrow_width + inner :])
            save("w_in", "z_proj")
        if i == 1:
            gather.relay_x(5)
            gather.relay_z(4)
    for j in range(tiles):
        cols = slice(j * LANES, (j + 1) * LANES)
        gate = v.z_proj[:, cols]
        skip = spread(s.head_terms[2:3, :], j)
        result = (v.scanned[:, cols] + skip * s.conv_x[:, cols]) * gate * sigmoid(gate)
        v.mix[:, q_width + j * LANES : q_width + (j + 1) * LANES] = low(result)
    gather.finish(3)
    gather.finish(4)

    pieces = 2
    size = own // pieces

    def mine_at(p):
        return pl.ds(pl.multiple_of(t * own + p * size, size), size)

    def other_at(p):
        return pl.ds(pl.multiple_of((1 - t) * own + p * size, size), size)

    def here(p):
        return slice(p * size, (p + 1) * size)

    mixed = []
    for p in range(pieces):
        s.leaving[0, p] = low(dot_nt(v.mix[other_at(p), :], v.w_mix[...]))
        mixed.append(swap(s.leaving.at[0, p], s.arrived.at[0, p], p))
    save("scanned", "states", "mix", "w_mix")
    for p in range(pieces):
        s.own_part[here(p), :] = dot_nt(v.mix[mine_at(p), :], v.w_mix[...])
    gather.relay_z(5)
    gather.relay_x(6)
    scale, normed_copies = [], []
    for p in range(pieces):
        mixed[p].wait_recv()
        middle = wide(r.hidden[here(p), :]) + s.own_part[here(p), :] + wide(s.arrived[0, p])
        v.resid[here(p), :] = middle
        scale.append(rms_scale(middle))
        s.normed2[mine_at(p), :] = low(middle * scale[p] * r.gain2[...])
        normed_copies.append(
            swap(s.normed2.at[mine_at(p), :], s.normed2.at[mine_at(p), :], pieces + p)
        )
    save("resid")
    gather.relay_z(6)
    gather.relay_x(7)
    gather.finish(5)
    for p in range(pieces):
        s.gate_pre[mine_at(p), :] = dot(s.normed2[mine_at(p), :], s.w_gate[...])
    gather.finish(6)
    for p in range(pieces):
        s.up_pre[mine_at(p), :] = dot(s.normed2[mine_at(p), :], s.w_up[...])

    def activate(rows):
        gate, up = s.gate_pre[rows, :], s.up_pre[rows, :]
        sig = sigmoid(gate)
        silu = gate * sig
        s.hidden_low[rows, :] = low(silu * up)
        s.gate_pre[rows, :] = up * sig * (1.0 + gate * (1.0 - sig))
        s.up_pre[rows, :] = silu

    def normed_grad(rows):
        return dot_nt(s.gate_back[rows, :], s.w_gate[...]) + dot_nt(
            s.up_back[rows, :], s.w_up[...]
        )

    span = 256

    def weight_grads(part, left, right):
        _, _, _, rows, width = part.shape
        per = span // (2 * rows)

        def one(i, carry):
            cols = pl.ds(pl.multiple_of(i * span, span), span)
            value = low(dot_tn(left[:, cols], right[...])).reshape(per, 2, rows, width)
            for k in range(per):
                at = i * per + k
                part[at // halves, lax.rem(at, halves)] = value[k]
            return carry

        lax.fori_loop(0, model // span, one, 0)

    def rows_back(rows):
        grad = dot(s.top_grad[rows, :], s.w_down[...])
        s.gate_back[rows, :] = low(grad * s.gate_pre[rows, :])
        s.up_back[rows, :] = low(grad * s.up_pre[rows, :])

    for p in range(pieces):
        activate(mine_at(p))
    gather.relay_z(7)
    grad_copy.wait_recv()
    sums = []
    for p in range(pieces):
        rows = other_at(p)
        normed_copies[p].wait_recv()
        s.gate_pre[rows, :] = dot(s.normed2[rows, :], s.w_gate[...])
        s.up_pre[rows, :] = dot(s.normed2[rows, :], s.w_up[...])
        activate(rows)
        if p == 0:
            gather.finish(7)
        rows_back(rows)
        s.leaving[1, p] = low(normed_grad(rows))
        sums.append(swap(s.leaving.at[1, p], s.arrived.at[1, p], 2 * pieces + p))
    weight_grads(s.p_down, s.top_grad, s.hidden_low)
    scatter.send(0)
    for p in range(pieces):
        rows_back(mine_at(p))
        s.own_part[here(p), :] = normed_grad(mine_at(p))
    scatter.core_stage(0)
    scatter.send_x(0)
    total = jnp.zeros((1, model), F32)
    mix_copies = []
    for p in range(pieces):
        sums[p].wait_recv()
        middle = v.resid[here(p), :]
        grad = s.own_part[here(p), :] + wide(s.arrived[1, p])
        total = total + jnp.sum(grad * middle * scale[p], axis=0, keepdims=True)
        weighted = grad * r.gain2[...]
        result = (
            wide(s.top_grad[mine_at(p), :])
            + scale[p] * weighted
            - middle
            * (scale[p] * scale[p] * scale[p])
            * jnp.mean(weighted * middle, axis=-1, keepdims=True)
        )
        v.resid_grad[here(p), :] = result
        v.mix_grad[mine_at(p), :] = low(result)
        mix_copies.append(
            swap(v.mix_grad.at[mine_at(p), :], v.mix_grad.at[mine_at(p), :], 3 * pieces + p)
        )
    out.gain2_part[...] = total
    save("resid_grad")
    weight_grads(s.p_gate, s.normed2, s.gate_back)
    scatter.send(1)
    weight_grads(s.p_up, s.normed2, s.up_back)
    scatter.send(2)

    def save_pair(name, part):
        for k in range(halves):
            move.start((name, k), part.at[:, k, c], getattr(out, name).at[k])

    scatter.core_stage(1)
    save_pair("gate_pair", s.p_gate)
    v.ffn_part[...] = low(dot_nt(s.hidden_low[...], s.w_down[...]))
    save("ffn_part")
    scatter.core_stage(2)
    save_pair("up_pair", s.p_up)
    scatter.x_stage(0)
    move.start("down_chip", s.d_chip, out.down_chip)
    for copy in mix_copies:
        copy.wait_recv()
    save("mix_grad")
    for copy in sent:
        copy.wait_send()
    gather.drain()
    scatter.drain()
    move.drain()


def forward(length_of, hidden, out_grad, gains, weights, shared, kernels, head_terms, tables):
    groups, halves = lax.axis_size("grp"), lax.axis_size("fsdp") // 2
    w_query, w_x, w_gate = weights[0], weights[4], weights[9]
    own, model = hidden.shape
    length, inner, q_width, ffn = 2 * own, w_x.shape[1], w_query.shape[1], w_gate.shape[1]
    shard = w_x.shape[0]
    narrow_width = q_width + 2 * LANES
    heads = q_width // HEAD
    rows = model // (2 * groups * halves)
    inside = pl.BlockSpec(memory_space=pltpu.VMEM)
    anywhere = pl.BlockSpec(memory_space=pl.ANY)
    shape = jax.ShapeDtypeStruct
    saved = [
        ((model, narrow_width + 2 * inner), BF16),
        ((model, q_width + inner), BF16),
        ((length, model), BF16),
        ((length, q_width + inner), BF16),
        ((length, q_width), BF16),
        ((length, LANES), BF16),
        ((heads, length, length), BF16),
        ((length + 8, inner), F32),
        ((length, inner), F32),
        ((length + 8, 2 * NSTATE), F32),
        ((length, LANES), F32),
        ((length, inner), F32),
        ((length // BLOCK, NSTATE, inner), F32),
        ((length, model), BF16),
        ((own, model), F32),
        ((own, model), F32),
        ((length, model), BF16),
    ]
    sums = [((groups, rows, ffn), BF16)] + [((halves, groups, rows, ffn), BF16)] * 2
    dma, vmem = pltpu.SemaphoreType.DMA, pltpu.VMEM
    moves = 2 + len(saved) + 2 * halves
    return pl.pallas_call(
        partial(forward_body, groups, halves),
        out_shape=[shape(*a) for a in saved + sums]
        + [shape((1, model), F32)],
        in_specs=[pl.BlockSpec(memory_space=pltpu.SMEM)]
        + [inside] * 8
        + [anywhere] * 8
        + [inside] * 7,
        out_specs=[anywhere] * (len(saved) + 3) + [inside],
        scratch_shapes=[vmem(*a) for a in saved]
        + [
            vmem((model, 2 * NSTATE), BF16),
            vmem((length, model), BF16),
            vmem((shard, narrow_width), BF16),
            vmem((length, inner), F32),
            vmem((length, 2 * NSTATE), F32),
            vmem((length, LANES), F32),
            vmem((NSTATE, inner), F32),
            vmem((8, LANES), F32),
            vmem((model, ffn), BF16),
            vmem((model, ffn), BF16),
            vmem((model, ffn), BF16),
            vmem((length, model), BF16),
            vmem((2, 2, own // 2, model), BF16),
            vmem((2, 2, own // 2, model), BF16),
            vmem((own, model), F32),
            vmem((length, ffn), F32),
            vmem((length, ffn), F32),
            vmem((length, ffn), BF16),
            vmem((length, ffn), BF16),
            vmem((length, ffn), BF16),
        ]
        + [vmem((groups, halves, 2, rows, ffn), BF16)] * 3
        + [vmem((groups, halves, rows, ffn), BF16)] * 3
        + [
            vmem((max(halves - 1, 1), groups, rows, ffn), BF16),
            vmem((groups, rows, ffn), BF16),
            dma((2, 10)),
            dma((moves,)),
        ]
        + gather_sems(8, halves)
        + scatter_sems(3, groups, halves),
        compiler_params=pltpu.CompilerParams(
            collective_id=0, has_side_effects=True, vmem_limit_bytes=VMEM_LIMIT
        ),
        name="forward",
    )(length_of, hidden, out_grad, *gains, *weights, shared, *kernels, *head_terms, *tables)


UNITS = 8


class BackwardIn(NamedTuple):
    length_ref: Any
    hidden: Any
    gain: Any
    gain2_part: Any
    conv_main: Any
    conv_shared: Any
    decay_log: Any
    step_bias: Any
    skip_gain: Any
    cosine: Any
    sine: Any
    w_shared: Any


class BackwardOut(NamedTuple):
    output: Any
    grad_in: Any
    gain: Any
    query: Any
    key: Any
    value: Any
    attn: Any
    z: Any
    x: Any
    step: Any
    shared: Any
    conv: Any
    conv_shared: Any
    decay: Any
    bias: Any
    skip: Any
    mamba: Any
    gain2: Any
    gate: Any
    up: Any
    down: Any


class BackwardScratch(NamedTuple):
    shared: Any
    arrived: Any
    leaving: Any
    grad_y: Any
    grad_attn: Any
    conv_x: Any
    conv_bc: Any
    grad_x: Any
    grad_bc: Any
    steps: Any
    back: Any
    bc_back: Any
    grown_y: Any
    faded_x: Any
    state_back: Any
    key_sums: Any
    rows_sum: Any
    shared_y: Any
    shared_all: Any
    vector: Any
    vec_core: Any
    vec_x: Any
    vec_y: Any
    vec_z: Any
    head_terms: Any
    y_sems: Any
    small_sems: Any
    small_x_sems: Any
    small_z_sems: Any
    move_sems: Any


def backward_body(groups, halves, *refs):
    counts = [len(BackwardIn._fields), len(Kept._fields) - 1, len(BackwardOut._fields), 17]
    ends = np.cumsum(counts).tolist()
    r = BackwardIn(*refs[: ends[0]])
    h = Kept(*refs[ends[0] : ends[1]], None)
    out = BackwardOut(*refs[ends[1] : ends[2]])
    v = Kept(*refs[ends[2] : ends[3] - 1], *[None] * (counts[1] - 15))
    ffn_own = refs[ends[3] - 1]
    rest = refs[ends[3] :]
    parts, from_core, rest = rest[:5], rest[5:10], rest[10:]
    from_x, chip_sums, rest = rest[:7], rest[7:14], rest[14:]
    from_z, relays, rest = rest[:8], rest[8:16], rest[16:]
    own_pairs, own_chip, rest = rest[:2], rest[2], rest[3:]
    s = BackwardScratch(*rest[:30])
    units = [
        dict(pair_sum=h.gate_pair, own_pair=own_pairs[0], from_x=from_x[0], chip_sum=chip_sums[0]),
        dict(pair_sum=h.up_pair, own_pair=own_pairs[1], from_x=from_x[1], chip_sum=chip_sums[1]),
        dict(chip_sum=own_chip),
    ] + [
        dict(part=parts[i], from_core=from_core[i], from_x=from_x[2 + i], chip_sum=chip_sums[2 + i])
        for i in range(5)
    ]
    for unit, ref, relay in zip(units, from_z, relays):
        unit["from_z"], unit["relay"] = ref, relay
    scatter = Scatter(units, groups, halves, rest[30:])
    move = Mover(s.move_sems)
    g, hi, c, t = place()
    own, model = r.hidden.shape
    length = 2 * own
    inner, q_width = out.x.shape[1], out.query.shape[1]
    kv_width, step_width = out.key.shape[1], out.step.shape[0]
    tiles, q_tiles = inner // LANES, q_width // LANES
    narrow_width = q_width + 2 * LANES
    other_y = (g, hi * 2 + c, 1 - t)
    devices = scatter.devices + [other_y]
    mine = pl.ds(pl.multiple_of(t * own, own), own)
    other = pl.ds(pl.multiple_of((1 - t) * own, own), own)
    greet(devices)

    def load(*names):
        for name in names:
            move.start(name, getattr(h, name), getattr(v, name))

    move.start("down_chip", h.down_chip, own_chip)
    load("mix_grad", "mix", "w_mix", "bc_padded", "step_in", "x_padded", "z_proj", "scanned")
    load("normed", "qr", "kv", "probs", "states", "w_in")
    move.start("shared", r.w_shared, s.shared)
    move.start("ffn_own", h.ffn_part.at[mine, :], ffn_own)
    load("resid", "resid_grad")
    pick_heads(s.head_terms, (r.decay_log, r.step_bias, r.skip_gain), t)
    head_terms = s.head_terms
    greeted(devices)
    scatter.send_x(0)
    scatter.send_x(1)
    move.wait("down_chip")
    scatter.send_z(2)
    ffn_copy = scatter.start(
        remote(
            h.ffn_part.at[other, :], s.arrived.at[0], s.y_sems.at[0, 0], s.y_sems.at[1, 0], other_y
        )
    )
    count = r.length_ref[0]
    span = 256

    def weight_grads(part, left, right, cols, width):
        _, _, _, rows, _ = part.shape
        per = span // (2 * rows)

        def one(i, carry):
            at = pl.ds(pl.multiple_of(i * span, span), span)
            value = low(dot_tn(left[:, at], right[:, cols])).reshape(per, 2, rows, width)
            for k in range(per):
                at = i * per + k
                part[at // halves, lax.rem(at, halves)] = value[k]
            return carry

        lax.fori_loop(0, model // span, one, 0)

    move.wait("mix_grad", "mix")
    weight_grads(parts[0], v.mix_grad, v.mix, slice(None), q_width + inner)
    scatter.send(3)
    move.wait("w_mix")
    grad = dot(v.mix_grad[...], v.w_mix[...])
    s.grad_attn[...] = low(grad[:, :q_width])
    s.grad_y[...] = grad[:, q_width:]
    move.wait("bc_padded", "step_in", "x_padded")
    row = lax.broadcasted_iota(jnp.int32, (length, 1), 0)
    step_pre = v.step_in[...]
    softplus = jnp.maximum(step_pre, 0.0) + jnp.log(1.0 + jnp.exp(-jnp.abs(step_pre)))
    s.steps[...] = jnp.where(row < count, softplus, 0.0)
    channel = t * inner

    def taps_of(j):
        return r.conv_main[:, pl.ds(pl.multiple_of(channel + j * LANES, LANES), LANES)]

    for j in range(2 * NSTATE // LANES):
        cols = slice(j * LANES, (j + 1) * LANES)
        pre = causal_conv(v.bc_padded, r.conv_shared[:, cols], length, cols)
        s.conv_bc[:, cols] = pre * sigmoid(pre)
    scatter.core_stage(3)
    scatter.send_x(3)
    move.wait("z_proj", "scanned", "normed")
    skip_sum = jnp.zeros((1, LANES), F32)
    for j in range(tiles):
        cols = slice(j * LANES, (j + 1) * LANES)
        pre = causal_conv(v.x_padded, taps_of(j), length, cols)
        conv = pre * sigmoid(pre)
        s.conv_x[:, cols] = conv
        gate = v.z_proj[:, cols]
        sig = sigmoid(gate)
        grad = s.grad_y[:, cols]
        value = v.scanned[:, cols] + spread(head_terms[2:3, :], j) * conv
        at = narrow_width + inner + j * LANES
        s.back[:, at : at + LANES] = low(grad * value * sig * (1.0 + gate * (1.0 - sig)))
        grad = grad * gate * sig
        s.grad_y[:, cols] = grad
        s.rows_sum[j : j + 1, :] = column_sum(grad * conv)
    for j in range(tiles):
        skip_sum = skip_sum + head_sum(s.rows_sum[0:8, :], j)[j : j + 1, :]
    weight_grads(parts[1], v.normed, s.back, slice(narrow_width + inner, None), inner)
    scatter.send(4)
    move.wait("qr", "kv", "probs")

    is_key = first_head(length)
    zero = jnp.zeros((), BF16)
    s.key_sums[...] = jnp.zeros_like(s.key_sums)

    def attend(j):
        tile = slice(j * LANES, (j + 1) * LANES)
        keys = [jnp.where(is_key, v.kv[...], zero)]
        keys.append(low(pltpu.roll(wide(keys[0]), HEAD, 1)))
        held = [None, jnp.where(is_key, zero, v.kv[...])]
        held[0] = low(pltpu.roll(wide(held[1]), HEAD, 1))
        for i in range(length // BLOCK):
            rows, upto = slice(i * BLOCK, (i + 1) * BLOCK), (i + 1) * BLOCK
            left = first_head(BLOCK)
            query, grad = v.qr[rows, tile], s.grad_attn[rows, tile]
            total = jnp.zeros((BLOCK, LANES), F32)
            for e in range(2):
                prob_low = v.probs[2 * j + e, rows, :upto]
                prob = wide(prob_low)
                prob_grad = dot_nt(grad, held[e][:upto])
                inside = jnp.sum(prob * prob_grad, axis=-1, keepdims=True)
                score_grad = low(prob * (prob_grad - inside))
                total = total + dot(score_grad, keys[e][:upto])
                side = left if e == 0 else jnp.logical_not(left)
                s.key_sums[0, :upto, :] += dot_tn(score_grad, jnp.where(side, query, zero))
                s.key_sums[1, :upto, :] += dot_tn(prob_low, jnp.where(side, grad, zero))
            total = total * HEAD**-0.5
            turned = total * r.cosine[rows, :] - half_swap(total) * r.sine[rows, :]
            s.back[rows, tile] = low(turned)

    scatter.relay(2)
    for j in range(q_tiles):
        attend(j)
        if j == 0:
            scatter.core_stage(4)
    key_grad = s.key_sums[0] + pltpu.roll(s.key_sums[0], HEAD, 1)
    key_grad = key_grad * HEAD**-0.5
    value_grad = s.key_sums[1] + pltpu.roll(s.key_sums[1], HEAD, 1)
    key_grad = key_grad * r.cosine[...] - half_swap(key_grad) * r.sine[...]
    s.back[:, q_width : q_width + LANES] = low(jnp.where(is_key, key_grad, value_grad))
    scatter.x_stage(0)
    scatter.send_z(0)
    move.wait("states")

    rate = -jnp.exp(head_terms[0:1, :])
    s.state_back[...] = jnp.zeros_like(s.state_back)
    upper = triangle(False)
    nblocks = length // BLOCK

    def scan_block(i, rate_sum, bias_sum):
        rows = slice(i * BLOCK, (i + 1) * BLOCK)
        step = s.steps[rows, :]
        total = exact_dot(triangle().astype(F32), step * rate)
        total_t = total.T
        last = total[BLOCK - 1 : BLOCK, :]
        grown, rest = jnp.exp(total), jnp.exp(last - total)
        b_mat, c_mat = split(s.conv_bc[rows, :NSTATE]), split(s.conv_bc[rows, NSTATE:])
        b_low, c_low = b_mat[0], c_mat[0]
        inner_t = jnp.where(upper, split_dot_nt(b_mat, c_mat), 0.0)
        state_mat = split(s.state_back[...])
        state_low = state_mat[0]
        crossed = split_dot(b_mat, state_mat)
        after = v.states[min(i + 1, nblocks - 1)] * s.state_back[...]
        left = first_head(BLOCK)
        inner_grad = jnp.zeros((BLOCK, BLOCK), F32)
        total_grad = jnp.zeros((BLOCK, LANES), F32)
        step_grad = jnp.zeros((BLOCK, LANES), F32)
        last_grad = jnp.zeros((8, LANES), F32)
        pulled = []
        for j in range(tiles):
            cols = slice(j * LANES, (j + 1) * LANES)
            conv, grad = s.conv_x[rows, cols], s.grad_y[rows, cols]
            step_wide, grown_wide, rest_wide = spread(step, j), spread(grown, j), spread(rest, j)
            stepped = step_wide * conv
            grad_low = low(grad)
            mixing = []
            for e, head in enumerate((2 * j, 2 * j + 1)):
                gap = jnp.minimum(total_t[head : head + 1, :] - total[:, head : head + 1], 0.0)
                decay = jnp.exp(gap)
                mixing.append(decay * inner_t)
                side = left if e == 0 else jnp.logical_not(left)
                inner_grad = inner_grad + decay * dot_nt(
                    low(jnp.where(side, stepped, 0.0)), grad_low
                )
            stacked = jnp.concatenate(
                [jnp.where(left, grad, 0.0), jnp.where(left, 0.0, grad)], axis=0
            )
            unstepped = split_dot(split(jnp.concatenate(mixing, axis=1)), split(stacked))
            unstepped = unstepped + rest_wide * crossed[:, cols]
            conv_grad = step_wide * unstepped
            total_grad = total_grad + head_sum(
                grad * v.scanned[rows, cols] - conv * conv_grad, j
            )
            step_grad = step_grad + head_sum(conv * unstepped, j)
            last_grad = last_grad + head_sum(
                jnp.broadcast_to(column_sum(after[:, cols]), (8, LANES)), j
            )
            s.grad_x[rows, cols] = conv_grad + spread(head_terms[2:3, :], j) * grad
            grown_grad = split(grown_wide * grad)
            s.grown_y[:, cols] = grown_grad[0]
            pulled.append(split_dot_tn(c_mat, grown_grad))
            s.faded_x[:, cols] = low(stepped * rest_wide)
        inner_low = low(jnp.where(upper, inner_grad, 0.0))
        s.grad_bc[rows, :NSTATE] = dot_nt(s.faded_x[...], state_low) + dot(inner_low, c_low)
        s.grad_bc[rows, NSTATE:] = dot_nt(s.grown_y[...], low(v.states[i])) + dot_tn(
            inner_low, b_low
        )
        for j in range(tiles):
            cols = slice(j * LANES, (j + 1) * LANES)
            fade = spread(grown[BLOCK - 1 : BLOCK, :], j)
            s.state_back[:, cols] = s.state_back[:, cols] * fade + pulled[j]
        slot = lax.broadcasted_iota(jnp.int32, (BLOCK, 1), 0)
        total_grad = total_grad + jnp.where(slot == BLOCK - 1, last_grad[0:1, :], 0.0)
        decay_grad = exact_dot(upper.astype(F32), total_grad)
        step_grad = step_grad + rate * decay_grad
        step_grad = jnp.where(i * BLOCK + slot < count, step_grad, 0.0)
        step_grad = step_grad * sigmoid(v.step_in[rows, :])
        s.back[rows, q_width + LANES : narrow_width] = low(step_grad)
        return rate_sum + column_sum(decay_grad * step), bias_sum + column_sum(step_grad)

    rate_sum = bias_sum = jnp.zeros((1, LANES), F32)
    for i in reversed(range(nblocks)):
        rate_sum, bias_sum = scan_block(i, rate_sum, bias_sum)
        if i == 0:
            scatter.relay(0)

    s.vector[...] = jnp.zeros_like(s.vector)

    def place_row(at, value):
        s.vector[at : at + 1, :] = value

    def place_halves(at, gap, value):
        place_row(at, jnp.where(t == 0, value, 0.0))
        place_row(at + gap, jnp.where(t == 0, 0.0, value))

    place_halves(72, 1, rate_sum * rate)
    place_halves(74, 1, bias_sum)
    place_halves(76, 1, skip_sum)
    for j in range(model // LANES):
        place_row(8 + j, r.gain2_part[:, j * LANES : (j + 1) * LANES])
    s.grad_bc[length:, :] = jnp.zeros((8, 2 * NSTATE), F32)
    s.grad_x[length:, :] = jnp.zeros((8, inner), F32)

    def conv_back(padded, grads, taps, cols, store):
        pre = causal_conv(padded, taps, length, cols)
        sig = sigmoid(pre)
        grads[:length, cols] = grads[:length, cols] * sig * (1.0 + pre * (1.0 - sig))
        for i in range(4):
            store(i, column_sum(grads[:length, cols] * padded[5 + i : 5 + i + length, cols]))
        total = taps[3:4, :] * grads[:length, cols]
        for i in range(3):
            total = total + taps[i : i + 1, :] * grads[3 - i : 3 - i + length, cols]
        return low(total)

    for j in range(2 * NSTATE // LANES):
        cols = slice(j * LANES, (j + 1) * LANES)
        s.bc_back[:, cols] = conv_back(
            v.bc_padded,
            s.grad_bc,
            r.conv_shared[:, cols],
            cols,
            lambda i, value, j=j: place_row(16 + 2 * i + j, value),
        )
    weight_grads(parts[2], v.normed, s.bc_back, slice(None), 2 * NSTATE)
    scatter.send(5)
    for j in range(tiles):
        cols = slice(j * LANES, (j + 1) * LANES)
        at = narrow_width + j * LANES
        s.back[:, at : at + LANES] = conv_back(
            v.x_padded,
            s.grad_x,
            taps_of(j),
            cols,
            lambda i, value, j=j: place_halves(24 + 2 * tiles * i + j, tiles, value),
        )
    scatter.core_stage(5)
    scatter.send_x(5)
    scatter.send_x(4)
    scatter.x_stage(1)
    scatter.send_z(1)
    move.wait("w_in", "shared")
    s.leaving[...] = low(
        dot_nt(s.back[other, :], v.w_in[...]) + dot_nt(s.bc_back[other, :], s.shared[...])
    )
    sum_copy = scatter.start(
        remote(s.leaving, s.arrived.at[1], s.y_sems.at[0, 1], s.y_sems.at[1, 1], other_y)
    )
    weight_grads(parts[4], v.normed, s.back, slice(narrow_width, narrow_width + inner), inner)
    scatter.send(7)
    weight_grads(parts[3], v.normed, s.back, slice(0, narrow_width), narrow_width)
    scatter.send(6)
    own_grad = dot_nt(s.back[mine, :], v.w_in[...]) + dot_nt(s.bc_back[mine, :], s.shared[...])
    scatter.x_stage(3)
    scatter.send_z(3)
    scatter.relay(1)
    sum_copy.wait_recv()
    values = wide(r.hidden[...])
    scale = rms_scale(values)
    grad = own_grad + wide(s.arrived[1])
    gain_row = column_sum(grad * values * scale)
    for j in range(model // LANES):
        place_row(j, gain_row[:, j * LANES : (j + 1) * LANES])
    s.vec_core[c] = s.vector[...]
    vec_copy = scatter.start(
        remote(
            s.vector,
            s.vec_core.at[c],
            s.small_sems.at[0, 0],
            s.small_sems.at[1, 0],
            scatter.other_core,
        )
    )
    move.wait("resid", "resid_grad", "ffn_own")
    weighted = grad * r.gain[...]
    out.grad_in[...] = low(
        v.resid_grad[...]
        + scale * weighted
        - values * (scale * scale * scale) * jnp.mean(weighted * values, axis=-1, keepdims=True)
    )
    vec_copy.wait_recv()
    s.vec_x[hi] = s.vec_core[0] + s.vec_core[1]
    vec_copies = [
        scatter.start(
            remote(
                s.vec_x.at[hi],
                s.vec_x.at[hi],
                s.small_x_sems.at[0, 0, k],
                s.small_x_sems.at[1, 0, k],
                scatter.across[k - 1],
            )
        )
        for k in range(1, halves)
    ]
    scatter.core_stage(7)
    scatter.send_x(7)
    scatter.x_stage(5)
    scatter.send_z(5)
    scatter.core_stage(6)
    scatter.send_x(6)
    ffn_copy.wait_recv()
    slot = t * own + lax.broadcasted_iota(jnp.int32, (own, 1), 0)
    total = v.resid[...] + wide(ffn_own[...]) + wide(s.arrived[0])
    out.output[...] = low(jnp.where(slot < count, total, 0.0))
    scatter.relay(3)
    out.down[...] = scatter.z_stage(2)
    scatter.relay(5)
    out.gate[...] = scatter.z_stage(0)
    s.shared_y[t] = scatter.z_stage(5)
    shared_copy = scatter.start(
        remote(
            s.shared_y.at[t],
            s.shared_y.at[t],
            s.small_sems.at[0, 2],
            s.small_sems.at[1, 2],
            other_y,
        )
    )
    scatter.x_stage(4)
    scatter.send_z(4)
    shared_copy.wait_recv()
    s.shared_all[g, hi, c] = low(s.shared_y[0] + s.shared_y[1])
    shared_copies = [
        scatter.start(
            remote(
                s.shared_all.at[g, hi, c],
                s.shared_all.at[g, hi, c],
                s.small_z_sems.at[0, 1, j],
                s.small_z_sems.at[1, 1, j],
                scatter.along[j - 1],
            )
        )
        for j in range(1, groups)
    ]
    for copy in vec_copies:
        copy.wait_recv()
    total = s.vec_x[0]
    for k in range(1, halves):
        total = total + s.vec_x[k]
    s.vec_y[t] = total
    vec_copy = scatter.start(
        remote(
            s.vec_y.at[t], s.vec_y.at[t], s.small_sems.at[0, 1], s.small_sems.at[1, 1], other_y
        )
    )
    out.up[...] = scatter.z_stage(1)
    vec_copy.wait_recv()
    s.vec_z[g] = s.vec_y[0] + s.vec_y[1]
    vec_copies = [
        scatter.start(
            remote(
                s.vec_z.at[g],
                s.vec_z.at[g],
                s.small_z_sems.at[0, 0, j],
                s.small_z_sems.at[1, 0, j],
                scatter.along[j - 1],
            )
        )
        for j in range(1, groups)
    ]
    total = scatter.z_stage(3)
    out.attn[...] = total[:, :q_width]
    out.mamba[...] = total[:, q_width:]
    scatter.relay(4)
    scatter.x_stage(7)
    scatter.send_z(7)
    for copy in shared_copies:
        copy.wait_recv()
    shared_copies = [
        scatter.start(
            remote(
                s.shared_all.at[:, hi, c],
                s.shared_all.at[:, hi, c],
                s.small_x_sems.at[0, 1, k],
                s.small_x_sems.at[1, 1, k],
                scatter.across[k - 1],
            )
        )
        for k in range(1, halves)
    ]
    out.z[...] = scatter.z_stage(4)
    for copy in vec_copies:
        copy.wait_recv()
    total = s.vec_z[0]
    for j in range(1, groups):
        total = total + s.vec_z[j]
    out.gain[...] = total[0:8, :]
    out.gain2[...] = total[8:16, :]
    for i in range(4):
        for j in range(2 * NSTATE // LANES):
            at = 16 + 2 * i + j
            out.conv_shared[i : i + 1, j * LANES : (j + 1) * LANES] = total[at : at + 1, :]
        for j in range(2 * tiles):
            at = 24 + 2 * tiles * i + j
            out.conv[i : i + 1, j * LANES : (j + 1) * LANES] = total[at : at + 1, :]
    for ref, at in ((out.decay, 72), (out.bias, 74), (out.skip, 76)):
        ref[...] = jnp.concatenate(
            [total[at : at + 1, :step_width], total[at + 1 : at + 2, :step_width]], axis=1
        )
    scatter.x_stage(6)
    scatter.send_z(6)
    scatter.relay(7)
    for copy in shared_copies:
        copy.wait_recv()
    shared_copy = scatter.start(
        remote(
            s.shared_all.at[:, :, c],
            s.shared_all.at[:, :, c],
            s.small_sems.at[0, 3],
            s.small_sems.at[1, 3],
            scatter.other_core,
        )
    )
    scatter.relay(6)
    out.x[...] = scatter.z_stage(7)
    shared_copy.wait_recv()

    def widen(i, carry):
        block = s.shared_all[i // (2 * halves), lax.rem(i // 2, halves), lax.rem(i, 2)]
        out.shared[i] = wide(block)
        return carry

    lax.fori_loop(0, groups * halves * 2, widen, 0)
    total = scatter.z_stage(6)
    out.query[...] = total[:, :q_width]
    out.key[...] = total[:, q_width : q_width + kv_width]
    out.value[...] = total[:, q_width + kv_width : q_width + 2 * kv_width]
    out.step[...] = total[:, q_width + LANES :].T[:step_width, :]
    scatter.drain()
    move.drain()


def backward(
    length_of, hidden, gain, gain2_part, saved, w_shared, kernels, head_terms, tables, widths
):
    groups, halves = lax.axis_size("grp"), lax.axis_size("fsdp") // 2
    q_width, kv_width, step_width = widths
    own, model = hidden.shape
    length = 2 * own
    narrow_width = q_width + 2 * LANES
    inner = (saved[0].shape[1] - narrow_width) // 2
    rows = model // (2 * groups * halves)
    ffn = saved[-1].shape[-1]
    inside = pl.BlockSpec(memory_space=pltpu.VMEM)
    anywhere = pl.BlockSpec(memory_space=pl.ANY)
    shape, vmem, dma = jax.ShapeDtypeStruct, pltpu.VMEM, pltpu.SemaphoreType.DMA
    outs = [
        shape((own, model), BF16),
        shape((own, model), BF16),
        shape((model // LANES, LANES), F32),
        shape((rows, q_width), F32),
        shape((rows, kv_width), F32),
        shape((rows, kv_width), F32),
        shape((rows, q_width), F32),
        shape((rows, inner), F32),
        shape((rows, inner), F32),
        shape((step_width, rows), F32),
        shape((2 * groups * halves, rows, 2 * NSTATE), F32),
        shape((4, 2 * inner), F32),
        shape((4, 2 * NSTATE), F32),
        shape((1, 2 * step_width), F32),
        shape((1, 2 * step_width), F32),
        shape((1, 2 * step_width), F32),
        shape((rows, inner), F32),
        shape((model // LANES, LANES), F32),
        shape((rows, ffn), F32),
        shape((rows, ffn), F32),
        shape((rows, ffn), F32),
    ]
    part_widths = [q_width + inner, inner, 2 * NSTATE, narrow_width, inner]
    x_widths = [ffn, ffn] + part_widths
    z_widths = [ffn] * 3 + part_widths
    vector = (80, LANES)
    others = max(halves - 1, 1)
    scratch = (
        [vmem(a.shape, a.dtype) for a in saved[:16]]
        + [vmem((own, model), BF16)]
        + [vmem((groups, halves, 2, rows, w), BF16) for w in part_widths]
        + [vmem((groups, halves, rows, w), BF16) for w in part_widths]
        + [vmem((others, groups, rows, w), BF16) for w in x_widths]
        + [vmem((groups, rows, w), BF16) for w in x_widths]
        + [vmem((groups - 1, rows, w), BF16) for w in z_widths]
        + [vmem((rows, w), BF16) for w in z_widths]
        + [vmem((groups, rows, ffn), BF16)] * 3
        + [
            vmem((model, 2 * NSTATE), BF16),
            vmem((2, own, model), BF16),
            vmem((own, model), BF16),
            vmem((length, inner), F32),
            vmem((length, q_width), BF16),
            vmem((length, inner), F32),
            vmem((length, 2 * NSTATE), F32),
            vmem((length + 8, inner), F32),
            vmem((length + 8, 2 * NSTATE), F32),
            vmem((length, LANES), F32),
            vmem((length, narrow_width + 2 * inner), BF16),
            vmem((length, 2 * NSTATE), BF16),
            vmem((BLOCK, inner), BF16),
            vmem((BLOCK, inner), BF16),
            vmem((NSTATE, inner), F32),
            vmem((2, length, LANES), F32),
            vmem((8, LANES), F32),
            vmem((2, rows, 2 * NSTATE), F32),
            vmem((groups, halves, 2, rows, 2 * NSTATE), BF16),
            vmem(vector, F32),
            vmem((2,) + vector, F32),
            vmem((halves,) + vector, F32),
            vmem((2,) + vector, F32),
            vmem((groups,) + vector, F32),
            vmem((8, LANES), F32),
            dma((2, 2)),
            dma((2, 4)),
            dma((2, 2, halves)),
            dma((2, 2, groups)),
            dma((20,)),
        ]
        + scatter_sems(UNITS, groups, halves)
    )
    return pl.pallas_call(
        partial(backward_body, groups, halves),
        out_shape=outs,
        in_specs=[pl.BlockSpec(memory_space=pltpu.SMEM)]
        + [inside] * 10
        + [anywhere] * (1 + len(saved)),
        out_specs=[inside] * len(outs),
        scratch_shapes=scratch,
        compiler_params=pltpu.CompilerParams(
            collective_id=1, has_side_effects=True, vmem_limit_bytes=VMEM_LIMIT
        ),
        name="backward",
    )(length_of, hidden, gain, gain2_part, *kernels, *head_terms, *tables, w_shared, *saved)


def emit_body(*refs):
    count = len(refs) // 2
    for source, target in zip(refs[:count], refs[count:]):
        target[...] = source[...]


def emit(arrays):
    inside = pl.BlockSpec(memory_space=pltpu.VMEM)
    return pl.pallas_call(
        emit_body,
        out_shape=[jax.ShapeDtypeStruct(a.shape, a.dtype) for a in arrays],
        in_specs=[inside] * len(arrays),
        out_specs=[inside] * len(arrays),
        compiler_params=pltpu.CompilerParams(vmem_limit_bytes=VMEM_LIMIT),
        name="emit",
    )(*arrays)


def local(
    hidden_in,
    lengths,
    norm1_gain,
    w_query,
    key_weight,
    value_weight,
    w_attn_out,
    w_mamba_z,
    w_mamba_x,
    w_step,
    w_shared,
    conv_main,
    conv_shared,
    decay_log,
    step_bias,
    skip_gain,
    w_mamba_out,
    norm2_gain,
    w_ffn_gate,
    w_ffn_up,
    w_ffn_down,
    out_grad,
):
    own, model = hidden_in.shape
    step_width = w_step.shape[1]
    head_terms = [v.reshape(1, -1) for v in (decay_log, step_bias, skip_gain)]
    tables = rotary_tables(2 * own)
    gain1, gain2 = norm1_gain.reshape(1, model), norm2_gain.reshape(1, model)
    kernels = (conv_main, conv_shared)
    weights = (w_query, key_weight.T, value_weight.T, w_step.T, w_mamba_x, w_mamba_z)
    weights += (w_attn_out, w_mamba_out, w_ffn_down, w_ffn_gate, w_ffn_up)
    *saved, gain2_part = forward(
        lengths,
        hidden_in,
        out_grad,
        (gain1, gain2),
        weights,
        w_shared,
        kernels,
        head_terms,
        tables,
    )
    outs = backward(
        lengths,
        hidden_in,
        gain1,
        gain2_part,
        saved,
        w_shared,
        kernels,
        head_terms,
        tables,
        (w_query.shape[1], key_weight.shape[1], step_width),
    )
    outs = list(emit(outs))
    outs[9] = outs[9].T
    for i in (2, 13, 14, 15, 17):
        outs[i] = outs[i].reshape(-1)
    outs[10] = outs[10].reshape(model, -1)
    return tuple(outs)


def solution(mesh):
    rows, whole, weight = P(("grp", "fsdp", "tp"), None), P(), P("fsdp", "tp")
    grad = P(("grp", "fsdp"), "tp")
    return jax.shard_map(
        local,
        mesh=mesh,
        in_specs=(rows, P(("grp", "fsdp")), whole)
        + (weight,) * 7
        + (whole,) * 6
        + (weight, whole)
        + (weight,) * 3
        + (rows,),
        out_specs=(rows, rows, whole)
        + (grad,) * 7
        + (whole,) * 6
        + (grad, whole)
        + (grad,) * 3,
        check_vma=False,
    )
```

```python
from functools import partial
from typing import Any, NamedTuple

import jax
import jax.numpy as jnp
import numpy as np
from jax import lax
from jax.experimental import pallas as pl
from jax.experimental.pallas import tpu as pltpu
from jax.sharding import PartitionSpec as P

HEAD = 64
LANES = 128
BLOCK = 128
NSTATE = 128
EPS = 1e-05
ROPE_BASE = 100000000000.0
MESH = pl.DeviceIdType.MESH
VMEM_LIMIT = 62 << 20
F32, BF16 = jnp.float32, jnp.bfloat16
EXACT = lax.Precision.HIGHEST


def low(values):
    return values.astype(BF16)


def wide(values):
    return values.astype(F32)


def dot(a, b):
    return jnp.dot(a, b, preferred_element_type=F32)


def dot_nt(a, b):
    return lax.dot_general(a, b, (((1,), (1,)), ((), ())), preferred_element_type=F32)


def dot_tn(a, b):
    return lax.dot_general(a, b, (((0,), (0,)), ((), ())), preferred_element_type=F32)


def exact_dot(a, b):
    return jnp.dot(a, b, precision=EXACT, preferred_element_type=F32)


def split(values):
    coarse = low(values)
    return coarse, low(values - wide(coarse))


def split_dot(a, b):
    return dot(jnp.concatenate([a[0], a[0], a[1]], axis=1), jnp.concatenate([b[0], b[1], b[0]], axis=0))


def split_dot_nt(a, b):
    return dot_nt(jnp.concatenate([a[0], a[0], a[1]], axis=1), jnp.concatenate([b[0], b[1], b[0]], axis=1))


def split_dot_tn(a, b):
    return dot_tn(jnp.concatenate([a[0], a[0], a[1]], axis=0), jnp.concatenate([b[0], b[1], b[0]], axis=0))


def sigmoid(v):
    return 1.0 / (1.0 + jnp.exp(-v))


def rms_scale(values):
    return lax.rsqrt(jnp.mean(values * values, axis=-1, keepdims=True) + EPS)


def lane_ids(rows):
    return lax.broadcasted_iota(jnp.int32, (rows, LANES), 1)


def first_head(rows):
    return lane_ids(rows) < HEAD


def half_swap(tile):
    lower = lax.rem(lane_ids(tile.shape[0]), HEAD) < HEAD // 2
    return jnp.where(lower, pltpu.roll(tile, LANES - HEAD // 2, 1), pltpu.roll(tile, HEAD // 2, 1))


def spread(values, tile):
    return jnp.where(
        first_head(values.shape[0]),
        values[:, 2 * tile : 2 * tile + 1],
        values[:, 2 * tile + 1 : 2 * tile + 2],
    )


def rotary_tables(length):
    positions = np.arange(length, dtype=np.float64)[:, None]
    power = np.arange(HEAD // 2, dtype=np.float64) * (-2.0 / HEAD)
    phase = (positions * np.power(ROPE_BASE, power)[None, :]).astype(np.float32)
    cosine, sine = np.cos(phase), np.sin(phase)
    return (
        np.concatenate([cosine] * 4, axis=1).astype(np.float32),
        np.concatenate([-sine, sine] * 2, axis=1).astype(np.float32),
    )


def place():
    g, f, t = lax.axis_index("grp"), lax.axis_index("fsdp"), lax.axis_index("tp")
    return g, f // 2, lax.rem(f, 2), t


def greet(devices):
    barrier = pltpu.get_barrier_semaphore()
    for device in devices:
        pl.semaphore_signal(barrier, inc=1, device_id=device, device_id_type=MESH)


def greeted(devices):
    pl.semaphore_wait(pltpu.get_barrier_semaphore(), len(devices))


def remote(src, dst, send, recv, device):
    return pltpu.make_async_remote_copy(
        src_ref=src,
        dst_ref=dst,
        send_sem=send,
        recv_sem=recv,
        device_id=device,
        device_id_type=MESH,
    )


def pick_heads(terms, whole, t):
    terms[...] = jnp.zeros_like(terms)
    for i, ref in enumerate(whole):
        heads = ref.shape[1] // 2
        terms[i : i + 1, :heads] = jnp.where(t == 0, ref[:, :heads], ref[:, heads:])


class Gather:
    def __init__(self, units, halves, sems):
        self.units, self.halves = units, halves
        self.x, self.z, self.cx, self.cz, self.own, self.local = sems
        g, self.hi, self.c, t = place()
        f = self.hi * 2 + self.c
        self.f, self.pair = f, lax.rem(g, 2)
        self.other_core = (g, self.hi * 2 + 1 - self.c, t)
        self.other_z = (g + 1 - 2 * self.pair, f, t)
        self.across = [
            (g, lax.rem(self.hi + k, halves) * 2 + self.c, t) for k in range(1, halves)
        ]
        self.devices = [self.other_core, self.other_z] + self.across
        self.got, self.sent, self.pending = {}, [], {}

    def block(self, u, owner, part=None):
        shard, full, column, width = self.units[u]
        rows = shard.shape[0]
        size = rows if part is None else rows // 2
        start = owner * rows + (0 if part is None else part * size)
        return full.at[pl.ds(pl.multiple_of(start, size), size), pl.ds(column, width)]

    def start(self, copy):
        copy.start()
        self.sent.append(copy)
        return copy

    def send(self, u):
        shard = self.units[u][0]
        half = shard.shape[0] // 2
        mine = shard.at[pl.ds(pl.multiple_of(self.pair * half, half), half), :]
        for k in range(1, self.halves):
            self.got["x", u, k] = self.start(
                remote(
                    mine,
                    self.block(u, self.f, self.pair),
                    self.x.at[0, u, k],
                    self.x.at[1, u, k],
                    self.across[k - 1],
                )
            )
        self.got["own", u] = self.start(
            remote(
                shard,
                self.block(u, self.f),
                self.own.at[0, u],
                self.own.at[1, u],
                self.other_core,
            )
        )
        self.pending[u] = pltpu.make_async_copy(shard, self.block(u, self.f), self.local.at[u])
        self.pending[u].start()

    def owner(self, k):
        return lax.rem(self.hi - k + self.halves, self.halves) * 2 + self.c

    def relay_x(self, u):
        for k in range(1, self.halves):
            self.got.pop(("x", u, k)).wait_recv()
            block = self.block(u, self.owner(k), self.pair)
            self.got["z", u, k] = self.start(
                remote(block, block, self.z.at[0, u, k], self.z.at[1, u, k], self.other_z)
            )
            self.got["cx", u, k] = self.start(
                remote(block, block, self.cx.at[0, u, k], self.cx.at[1, u, k], self.other_core)
            )

    def relay_z(self, u):
        for k in range(1, self.halves):
            self.got.pop(("z", u, k)).wait_recv()
            block = self.block(u, self.owner(k), 1 - self.pair)
            self.got["cz", u, k] = self.start(
                remote(block, block, self.cz.at[0, u, k], self.cz.at[1, u, k], self.other_core)
            )

    def finish(self, u):
        self.got.pop(("own", u)).wait_recv()
        for k in range(1, self.halves):
            self.got.pop(("cx", u, k)).wait_recv()
            self.got.pop(("cz", u, k)).wait_recv()
        self.pending.pop(u).wait()

    def drain(self):
        assert not self.got and not self.pending
        for copy in self.sent:
            copy.wait_send()


def gather_sems(units, halves):
    dma = pltpu.SemaphoreType.DMA
    return [dma((2, units, halves))] * 4 + [dma((2, units)), dma((units,))]


def causal_conv(padded, kernel, rows, cols):
    total = kernel[3:4, :] * padded[8 : 8 + rows, cols]
    for i in range(3):
        total = total + kernel[i : i + 1, :] * padded[5 + i : 5 + i + rows, cols]
    return total


def triangle(lower=True):
    row = lax.broadcasted_iota(jnp.int32, (BLOCK, BLOCK), 0)
    col = lax.broadcasted_iota(jnp.int32, (BLOCK, BLOCK), 1)
    return row >= col if lower else row <= col


class Scatter:
    def __init__(self, units, groups, halves, sems):
        self.units = units
        self.groups, self.halves = groups, halves
        self.c_sems, self.x_sems, self.z_sems, self.l_sems = sems
        self.g, self.hi, self.c, self.t = place()
        f = self.hi * 2 + self.c
        self.other_core = (self.g, self.hi * 2 + 1 - self.c, self.t)
        self.across = [
            (self.g, lax.rem(self.hi + k, halves) * 2 + self.c, self.t) for k in range(1, halves)
        ]
        self.along = [(lax.rem(self.g + j, groups), f, self.t) for j in range(1, groups)]
        self.devices = [self.other_core] + self.across + self.along
        self.outer = (self.g == 0) | (self.g == groups - 1)
        self.got, self.sent, self.lines = {}, [], []

    def start(self, copy):
        copy.start()
        self.sent.append(copy)
        return copy

    def send(self, u):
        unit = self.units[u]
        self.got["c", u] = self.start(
            remote(
                unit["part"].at[:, :, 1 - self.c],
                unit["from_core"],
                self.c_sems.at[0, u],
                self.c_sems.at[1, u],
                self.other_core,
            )
        )

    def send_x(self, u):
        unit = self.units[u]
        for k in range(1, self.halves):
            away = lax.rem(self.hi + k, self.halves)
            self.got["x", u, k] = self.start(
                remote(
                    unit["pair_sum"].at[away]
                    if "pair_sum" in unit
                    else unit["part"].at[:, away, self.c],
                    unit["from_x"].at[k - 1],
                    self.x_sems.at[0, u, k],
                    self.x_sems.at[1, u, k],
                    self.across[k - 1],
                )
            )
        if "pair_sum" in unit:
            self.load(u, unit["pair_sum"].at[self.hi], unit["own_pair"])

    def load(self, u, source, target):
        self.got["l", u] = pltpu.make_async_copy(source, target, self.l_sems.at[u])
        self.got["l", u].start()

    def z_links(self, u):
        unit, g = self.units[u], self.g
        chip, into, last = unit["chip_sum"], unit["from_z"], self.groups - 1

        def to(where):
            return (where, self.hi * 2 + self.c, self.t)

        near = jnp.where(g == 0, 1, last - 1)
        outer = {
            0: (chip.at[near], into.at[0], to(near)),
            1: (chip.at[last - near], into.at[1], to(last - near)),
            3: (chip.at[last - g], unit["relay"], to(near)),
        }
        end = jnp.where(g == 1, 0, last)
        inner = {
            0: (chip.at[end], into.at[0], to(end)),
            1: (chip.at[last - end], into.at[1], to(last - end)),
            2: (chip.at[last - g], into.at[2], to(last - g)),
        }
        return outer, inner

    def z_copy(self, u, side, slot):
        source, target, device = self.z_links(u)[side][slot]
        return remote(
            source, target, self.z_sems.at[0, u, slot], self.z_sems.at[1, u, slot], device
        )

    def send_z(self, u):
        unit = self.units[u]
        if self.groups == 4:

            @pl.when(self.outer)
            def _():
                for slot in (3, 0, 1):
                    self.z_copy(u, 0, slot).start()

            @pl.when(jnp.logical_not(self.outer))
            def _():
                for slot in (2, 0):
                    self.z_copy(u, 1, slot).start()

            self.lines.append(u)
            return
        for j in range(1, self.groups):
            self.got["z", u, j] = self.start(
                remote(
                    unit["chip_sum"].at[lax.rem(self.g + j, self.groups)],
                    unit["from_z"].at[j - 1],
                    self.z_sems.at[0, u, j],
                    self.z_sems.at[1, u, j],
                    self.along[j - 1],
                )
            )

    def relay(self, u):
        if self.groups != 4:
            return
        unit = self.units[u]

        @pl.when(jnp.logical_not(self.outer))
        def _():
            self.z_copy(u, 0, 3).wait_recv()
            far = jnp.where(self.g == 1, self.groups - 1, 0)
            chip = unit["chip_sum"]
            chip[far] = low(wide(chip[far]) + wide(unit["relay"][...]))
            self.z_copy(u, 1, 1).start()

    def core_stage(self, u):
        part, from_core = self.units[u]["part"], self.units[u]["from_core"]
        self.got.pop(("c", u)).wait_recv()

        def add(i, carry):
            gg, h = i // self.halves, lax.rem(i, self.halves)
            part[gg, h, self.c] = low(wide(part[gg, h, self.c]) + wide(from_core[gg, h]))
            return carry

        lax.fori_loop(0, self.groups * self.halves, add, 0)

    def x_stage(self, u):
        unit = self.units[u]
        for k in range(1, self.halves):
            self.got.pop(("x", u, k)).wait_recv()
        if "pair_sum" in unit:
            self.got.pop(("l", u)).wait()

        def add(gg, carry):
            if "pair_sum" in unit:
                total = wide(unit["own_pair"][gg])
            else:
                total = wide(unit["part"][gg, self.hi, self.c])
            for k in range(1, self.halves):
                total = total + wide(unit["from_x"][k - 1, gg])
            unit["chip_sum"][gg] = low(total)
            return carry

        lax.fori_loop(0, self.groups, add, 0)

    def z_stage(self, u):
        unit = self.units[u]
        total = wide(unit["chip_sum"][self.g])
        if self.groups == 4:
            for slot in (0, 1):
                self.z_copy(u, 1, slot).wait_recv()

            @pl.when(jnp.logical_not(self.outer))
            def _():
                self.z_copy(u, 1, 2).wait_recv()

            total = total + wide(unit["from_z"][0]) + wide(unit["from_z"][1])
            return total + jnp.where(self.outer, 0.0, wide(unit["from_z"][2]))
        for j in range(1, self.groups):
            self.got.pop(("z", u, j)).wait_recv()
            total = total + wide(unit["from_z"][j - 1])
        return total

    def drain(self):
        assert not self.got
        for copy in self.sent:
            copy.wait_send()
        if not self.lines:
            return

        @pl.when(self.outer)
        def _():
            for u in self.lines:
                for slot in (0, 1, 3):
                    self.z_copy(u, 0, slot).wait_send()

        @pl.when(jnp.logical_not(self.outer))
        def _():
            for u in self.lines:
                for slot in (0, 1, 2):
                    self.z_copy(u, 1, slot).wait_send()


class Mover:
    def __init__(self, sems):
        self.sems, self.count, self.copies = sems, 0, {}

    def start(self, name, source, target):
        self.copies[name] = pltpu.make_async_copy(source, target, self.sems.at[self.count])
        self.copies[name].start()
        self.count += 1

    def wait(self, *names):
        for name in names:
            self.copies.pop(name).wait()

    def drain(self):
        self.wait(*list(self.copies))


def scatter_sems(units, groups, halves):
    dma = pltpu.SemaphoreType.DMA
    return [
        dma((2, units)),
        dma((2, units, halves)),
        dma((2, units, groups)),
        dma((units,)),
    ]


def head_sum(values, tile):
    lane = lax.broadcasted_iota(jnp.int32, (LANES, LANES), 0)
    column = lax.broadcasted_iota(jnp.int32, (LANES, LANES), 1)
    pick = low(jnp.where(column == 2 * tile + jnp.where(lane < HEAD, 0, 1), 1.0, 0.0))
    coarse = low(values)
    fine = low(values - wide(coarse))
    return dot(
        jnp.concatenate([coarse, fine], axis=1), jnp.concatenate([pick, pick], axis=0)
    )


def column_sum(values):
    return jnp.sum(values, axis=0, keepdims=True)


class ForwardIn(NamedTuple):
    length_ref: Any
    hidden: Any
    gain1: Any
    gain2: Any
    w_query: Any
    w_key: Any
    w_value: Any
    w_step: Any
    w_x: Any
    w_z: Any
    w_attn_out: Any
    w_mamba_out: Any
    w_down: Any
    w_gate: Any
    w_up: Any
    w_shared: Any
    out_grad: Any
    cosine: Any
    sine: Any
    conv_main: Any
    conv_shared: Any
    decay_log: Any
    step_bias: Any
    skip_gain: Any


class Kept(NamedTuple):
    w_in: Any
    w_mix: Any
    normed: Any
    mix: Any
    qr: Any
    kv: Any
    probs: Any
    x_padded: Any
    z_proj: Any
    bc_padded: Any
    step_in: Any
    scanned: Any
    states: Any
    mix_grad: Any
    resid_grad: Any
    resid: Any
    ffn_part: Any
    down_chip: Any
    gate_pair: Any
    up_pair: Any
    gain2_part: Any


class ForwardScratch(NamedTuple):
    shared: Any
    out_grad: Any
    cosine: Any
    sine: Any
    top_grad: Any
    narrow: Any
    conv_x: Any
    conv_bc: Any
    steps: Any
    state: Any
    head_terms: Any
    w_down: Any
    w_gate: Any
    w_up: Any
    normed2: Any
    arrived: Any
    leaving: Any
    own_part: Any
    gate_pre: Any
    up_pre: Any
    hidden_low: Any
    gate_back: Any
    up_back: Any
    p_down: Any
    p_gate: Any
    p_up: Any
    c_down: Any
    c_gate: Any
    c_up: Any
    x_down: Any
    d_chip: Any
    y_sems: Any
    move_sems: Any


def forward_body(groups, halves, *refs):
    counts = len(ForwardIn._fields), len(Kept._fields) - 1
    r = ForwardIn(*refs[: counts[0]])
    out = Kept(*refs[counts[0] : sum(counts) + 1])
    rest = refs[sum(counts) + 1 :]
    v = Kept(*rest[:17], *[None] * (counts[1] - 16))
    s = ForwardScratch(*rest[17:50])
    sems = rest[50:]
    g, hi, c, t = place()
    own, model = r.hidden.shape
    length = 2 * own
    inner, ffn = r.w_x.shape[1], r.w_gate.shape[1]
    q_width, step_width = r.w_query.shape[1], r.w_step.shape[0]
    tiles, q_tiles = inner // LANES, q_width // LANES
    narrow_width = q_width + 2 * LANES
    gather = Gather(
        [
            (s.narrow, v.w_in, 0, narrow_width),
            (r.w_x, v.w_in, narrow_width, inner),
            (r.w_z, v.w_in, narrow_width + inner, inner),
            (r.w_attn_out, v.w_mix, 0, q_width),
            (r.w_mamba_out, v.w_mix, q_width, inner),
            (r.w_gate, s.w_gate, 0, ffn),
            (r.w_up, s.w_up, 0, ffn),
            (r.w_down, s.w_down, 0, ffn),
        ],
        halves,
        sems[:6],
    )
    scatter = Scatter(
        [
            dict(part=s.p_down, from_core=s.c_down, from_x=s.x_down, chip_sum=s.d_chip),
            dict(part=s.p_gate, from_core=s.c_gate),
            dict(part=s.p_up, from_core=s.c_up),
        ],
        groups,
        halves,
        sems[6:],
    )
    move = Mover(s.move_sems)
    other_y = (g, hi * 2 + c, 1 - t)
    devices = gather.devices + [other_y]
    greet(devices)
    move.start("out_grad", r.out_grad, s.out_grad)
    move.start("shared", r.w_shared, s.shared)
    move.start("cosine", r.cosine, s.cosine)
    move.start("sine", r.sine, s.sine)
    turned = jnp.concatenate([wide(r.w_key[...]), wide(r.w_value[...])], axis=0).T
    s.narrow[:, :q_width] = r.w_query[...]
    s.narrow[:, q_width : q_width + LANES] = low(turned)
    filler = jnp.zeros((LANES - step_width, s.narrow.shape[0]), F32)
    turned = jnp.concatenate([wide(r.w_step[...]), filler], axis=0).T
    s.narrow[:, q_width + LANES :] = low(turned)
    mine = pl.ds(pl.multiple_of(t * own, own), own)
    other = pl.ds(pl.multiple_of((1 - t) * own, own), own)
    values = wide(r.hidden[...])
    v.normed[mine, :] = low(values * rms_scale(values) * r.gain1[...])
    count = r.length_ref[0]
    greeted(devices)
    gather.send(0)
    sent = []

    def swap(src, dst, at):
        copy = remote(src, dst, s.y_sems.at[0, at], s.y_sems.at[1, at], other_y)
        copy.start()
        sent.append(copy)
        return copy

    y_copy = swap(v.normed.at[mine, :], v.normed.at[mine, :], 8)
    for u in range(1, 8):
        gather.send(u)
    slot = t * own + lax.broadcasted_iota(jnp.int32, (own, 1), 0)
    move.wait("out_grad")
    s.top_grad[mine, :] = jnp.where(slot < count, s.out_grad[...], jnp.zeros((), BF16))
    grad_copy = swap(s.top_grad.at[mine, :], s.top_grad.at[mine, :], 9)
    pick_heads(s.head_terms, (r.decay_log, r.step_bias, r.skip_gain), t)
    v.x_padded[0:8, :] = jnp.zeros((8, inner), F32)
    v.bc_padded[0:8, :] = jnp.zeros((8, 2 * NSTATE), F32)
    s.state[...] = jnp.zeros_like(s.state)

    def save(*names):
        for name in names:
            move.start(name, getattr(v, name), getattr(out, name))

    move.wait("shared")
    v.bc_padded[pl.ds(pl.multiple_of(8 + t * own, 8), own), :] = dot(
        v.normed[mine, :], s.shared[...]
    )
    gather.relay_x(0)
    gather.relay_z(0)
    gather.relay_x(1)
    y_copy.wait_recv()
    save("normed")
    v.bc_padded[pl.ds(pl.multiple_of(8 + (1 - t) * own, 8), own), :] = dot(
        v.normed[other, :], s.shared[...]
    )
    gather.finish(0)
    move.wait("cosine", "sine")
    projected = dot(v.normed[...], v.w_in[:, :narrow_width])
    for j in range(q_tiles):
        tile = projected[:, j * LANES : (j + 1) * LANES]
        turned = tile * s.cosine[...] + half_swap(tile) * s.sine[...]
        v.qr[:, j * LANES : (j + 1) * LANES] = low(turned)
    tile = projected[:, q_width : q_width + LANES]
    is_key = first_head(length)
    turned = tile * s.cosine[...] + half_swap(tile) * s.sine[...]
    v.kv[...] = low(jnp.where(is_key, turned, tile))
    step_pre = projected[:, q_width + LANES :] + s.head_terms[1:2, :]
    v.step_in[...] = step_pre
    row = lax.broadcasted_iota(jnp.int32, (length, 1), 0)
    softplus = jnp.maximum(step_pre, 0.0) + jnp.log(1.0 + jnp.exp(-jnp.abs(step_pre)))
    s.steps[...] = jnp.where(row < count, softplus, 0.0)
    save("qr", "kv", "step_in", "bc_padded")
    for j in range(2 * NSTATE // LANES):
        cols = slice(j * LANES, (j + 1) * LANES)
        pre = causal_conv(v.bc_padded, r.conv_shared[:, cols], length, cols)
        s.conv_bc[:, cols] = pre * sigmoid(pre)
    def attend(j):
        zero = jnp.zeros((), BF16)
        keys = [jnp.where(is_key, v.kv[...], zero)]
        keys.append(low(pltpu.roll(wide(keys[0]), HEAD, 1)))
        held = [None, jnp.where(is_key, zero, v.kv[...])]
        held[0] = low(pltpu.roll(wide(held[1]), HEAD, 1))
        for i in range(length // BLOCK):
            rows, upto = slice(i * BLOCK, (i + 1) * BLOCK), (i + 1) * BLOCK
            query_slot = i * BLOCK + lax.broadcasted_iota(jnp.int32, (BLOCK, upto), 0)
            key_slot = lax.broadcasted_iota(jnp.int32, (BLOCK, upto), 1)
            allowed = (key_slot <= query_slot) & (key_slot < count)
            total = jnp.zeros((BLOCK, LANES), F32)
            for e in range(2):
                score = dot_nt(v.qr[rows, j * LANES : (j + 1) * LANES], keys[e][:upto])
                score = jnp.where(allowed, score * HEAD**-0.5, -1e30)
                expo = jnp.exp(score - jnp.max(score, axis=-1, keepdims=True))
                prob = low(expo / jnp.sum(expo, axis=-1, keepdims=True))
                v.probs[2 * j + e, rows, :upto] = prob
                total = total + dot(prob, held[e][:upto])
            v.mix[rows, j * LANES : (j + 1) * LANES] = low(total)

    attend(0)
    gather.relay_z(1)
    gather.relay_x(2)
    for j in range(1, q_tiles):
        attend(j)
    save("probs")
    gather.finish(1)
    v.x_padded[8:, :] = dot(v.normed[...], v.w_in[:, narrow_width : narrow_width + inner])
    save("x_padded")
    channel = t * inner
    for j in range(tiles):
        if j == tiles // 2:
            gather.relay_x(3)
            gather.relay_z(2)
        cols = slice(j * LANES, (j + 1) * LANES)
        taps = r.conv_main[:, pl.ds(pl.multiple_of(channel + j * LANES, LANES), LANES)]
        pre = causal_conv(v.x_padded, taps, length, cols)
        s.conv_x[:, cols] = pre * sigmoid(pre)
    gather.relay_x(4)
    rate = -jnp.exp(s.head_terms[0:1, :])
    causal = triangle()

    def scan_block(i):
        rows = slice(i * BLOCK, (i + 1) * BLOCK)
        step = s.steps[rows, :]
        total = exact_dot(causal.astype(F32), step * rate)
        total_t = total.T
        last = total[BLOCK - 1 : BLOCK, :]
        grown, rest = jnp.exp(total), jnp.exp(last - total)
        b_mat, c_mat = split(s.conv_bc[rows, :NSTATE]), split(s.conv_bc[rows, NSTATE:])
        inner_prod = jnp.where(causal, split_dot_nt(c_mat, b_mat), 0.0)
        v.states[i] = s.state[...]
        crossed = split_dot(c_mat, split(s.state[...]))
        left = first_head(BLOCK)
        for j in range(tiles):
            cols = slice(j * LANES, (j + 1) * LANES)
            stepped = spread(step, j) * s.conv_x[rows, cols]
            mixing = []
            for h in (2 * j, 2 * j + 1):
                gap = jnp.minimum(total[:, h : h + 1] - total_t[h : h + 1, :], 0.0)
                mixing.append(jnp.exp(gap) * inner_prod)
            stacked = jnp.concatenate(
                [jnp.where(left, stepped, 0.0), jnp.where(left, 0.0, stepped)], axis=0
            )
            within = split_dot(split(jnp.concatenate(mixing, axis=1)), split(stacked))
            grown_wide = spread(grown, j)
            v.scanned[rows, cols] = within + crossed[:, cols] * grown_wide
            s.state[:, cols] = s.state[:, cols] * grown_wide[BLOCK - 1 : BLOCK, :] + split_dot_tn(
                b_mat, split(stepped * spread(rest, j))
            )

    for i in range(length // BLOCK):
        scan_block(i)
        if i == 0:
            gather.relay_z(3)
            gather.finish(2)
            v.z_proj[...] = dot(v.normed[...], v.w_in[:, narrow_width + inner :])
            save("w_in", "z_proj")
        if i == 1:
            gather.relay_x(5)
            gather.relay_z(4)
    for j in range(tiles):
        cols = slice(j * LANES, (j + 1) * LANES)
        gate = v.z_proj[:, cols]
        skip = spread(s.head_terms[2:3, :], j)
        result = (v.scanned[:, cols] + skip * s.conv_x[:, cols]) * gate * sigmoid(gate)
        v.mix[:, q_width + j * LANES : q_width + (j + 1) * LANES] = low(result)
    gather.finish(3)
    gather.finish(4)

    pieces = 2
    size = own // pieces

    def mine_at(p):
        return pl.ds(pl.multiple_of(t * own + p * size, size), size)

    def other_at(p):
        return pl.ds(pl.multiple_of((1 - t) * own + p * size, size), size)

    def here(p):
        return slice(p * size, (p + 1) * size)

    mixed = []
    for p in range(pieces):
        s.leaving[0, p] = low(dot_nt(v.mix[other_at(p), :], v.w_mix[...]))
        mixed.append(swap(s.leaving.at[0, p], s.arrived.at[0, p], p))
    save("scanned", "states", "mix", "w_mix")
    for p in range(pieces):
        s.own_part[here(p), :] = dot_nt(v.mix[mine_at(p), :], v.w_mix[...])
    gather.relay_z(5)
    gather.relay_x(6)
    scale, normed_copies = [], []
    for p in range(pieces):
        mixed[p].wait_recv()
        middle = wide(r.hidden[here(p), :]) + s.own_part[here(p), :] + wide(s.arrived[0, p])
        v.resid[here(p), :] = middle
        scale.append(rms_scale(middle))
        s.normed2[mine_at(p), :] = low(middle * scale[p] * r.gain2[...])
        normed_copies.append(
            swap(s.normed2.at[mine_at(p), :], s.normed2.at[mine_at(p), :], pieces + p)
        )
    save("resid")
    gather.relay_z(6)
    gather.relay_x(7)
    gather.finish(5)
    for p in range(pieces):
        s.gate_pre[mine_at(p), :] = dot(s.normed2[mine_at(p), :], s.w_gate[...])
    gather.finish(6)
    for p in range(pieces):
        s.up_pre[mine_at(p), :] = dot(s.normed2[mine_at(p), :], s.w_up[...])

    def activate(rows):
        gate, up = s.gate_pre[rows, :], s.up_pre[rows, :]
        sig = sigmoid(gate)
        silu = gate * sig
        s.hidden_low[rows, :] = low(silu * up)
        s.gate_pre[rows, :] = up * sig * (1.0 + gate * (1.0 - sig))
        s.up_pre[rows, :] = silu

    def normed_grad(rows):
        return dot_nt(s.gate_back[rows, :], s.w_gate[...]) + dot_nt(
            s.up_back[rows, :], s.w_up[...]
        )

    span = 256

    def weight_grads(part, left, right):
        _, _, _, rows, width = part.shape
        per = span // (2 * rows)

        def one(i, carry):
            cols = pl.ds(pl.multiple_of(i * span, span), span)
            value = low(dot_tn(left[:, cols], right[...])).reshape(per, 2, rows, width)
            for k in range(per):
                at = i * per + k
                part[at // halves, lax.rem(at, halves)] = value[k]
            return carry

        lax.fori_loop(0, model // span, one, 0)

    def rows_back(rows):
        grad = dot(s.top_grad[rows, :], s.w_down[...])
        s.gate_back[rows, :] = low(grad * s.gate_pre[rows, :])
        s.up_back[rows, :] = low(grad * s.up_pre[rows, :])

    for p in range(pieces):
        activate(mine_at(p))
    gather.relay_z(7)
    grad_copy.wait_recv()
    sums = []
    for p in range(pieces):
        rows = other_at(p)
        normed_copies[p].wait_recv()
        s.gate_pre[rows, :] = dot(s.normed2[rows, :], s.w_gate[...])
        s.up_pre[rows, :] = dot(s.normed2[rows, :], s.w_up[...])
        activate(rows)
        if p == 0:
            gather.finish(7)
        if p == pieces - 1:
            weight_grads(s.p_down, s.top_grad, s.hidden_low)
            scatter.send(0)
        rows_back(rows)
        s.leaving[1, p] = low(normed_grad(rows))
        sums.append(swap(s.leaving.at[1, p], s.arrived.at[1, p], 2 * pieces + p))
    for p in range(pieces):
        rows_back(mine_at(p))
        s.own_part[here(p), :] = normed_grad(mine_at(p))
        if p == 0:
            scatter.core_stage(0)
            scatter.send_x(0)
    total = jnp.zeros((1, model), F32)
    mix_copies = []
    for p in range(pieces):
        sums[p].wait_recv()
        middle = v.resid[here(p), :]
        grad = s.own_part[here(p), :] + wide(s.arrived[1, p])
        total = total + jnp.sum(grad * middle * scale[p], axis=0, keepdims=True)
        weighted = grad * r.gain2[...]
        result = (
            wide(s.top_grad[mine_at(p), :])
            + scale[p] * weighted
            - middle
            * (scale[p] * scale[p] * scale[p])
            * jnp.mean(weighted * middle, axis=-1, keepdims=True)
        )
        v.resid_grad[here(p), :] = result
        v.mix_grad[mine_at(p), :] = low(result)
        mix_copies.append(
            swap(v.mix_grad.at[mine_at(p), :], v.mix_grad.at[mine_at(p), :], 3 * pieces + p)
        )
    out.gain2_part[...] = total
    save("resid_grad")
    weight_grads(s.p_gate, s.normed2, s.gate_back)
    scatter.send(1)
    weight_grads(s.p_up, s.normed2, s.up_back)
    scatter.send(2)

    def save_pair(name, part):
        for k in range(halves):
            move.start((name, k), part.at[:, k, c], getattr(out, name).at[k])

    scatter.core_stage(1)
    save_pair("gate_pair", s.p_gate)
    v.ffn_part[...] = low(dot_nt(s.hidden_low[...], s.w_down[...]))
    save("ffn_part")
    scatter.core_stage(2)
    save_pair("up_pair", s.p_up)
    scatter.x_stage(0)
    move.start("down_chip", s.d_chip, out.down_chip)
    for copy in mix_copies:
        copy.wait_recv()
    save("mix_grad")
    for copy in sent:
        copy.wait_send()
    gather.drain()
    scatter.drain()
    move.drain()


def forward(length_of, hidden, out_grad, gains, weights, shared, kernels, head_terms, tables):
    groups, halves = lax.axis_size("grp"), lax.axis_size("fsdp") // 2
    w_query, w_x, w_gate = weights[0], weights[4], weights[9]
    own, model = hidden.shape
    length, inner, q_width, ffn = 2 * own, w_x.shape[1], w_query.shape[1], w_gate.shape[1]
    shard = w_x.shape[0]
    narrow_width = q_width + 2 * LANES
    heads = q_width // HEAD
    rows = model // (2 * groups * halves)
    inside = pl.BlockSpec(memory_space=pltpu.VMEM)
    anywhere = pl.BlockSpec(memory_space=pl.ANY)
    shape = jax.ShapeDtypeStruct
    saved = [
        ((model, narrow_width + 2 * inner), BF16),
        ((model, q_width + inner), BF16),
        ((length, model), BF16),
        ((length, q_width + inner), BF16),
        ((length, q_width), BF16),
        ((length, LANES), BF16),
        ((heads, length, length), BF16),
        ((length + 8, inner), F32),
        ((length, inner), F32),
        ((length + 8, 2 * NSTATE), F32),
        ((length, LANES), F32),
        ((length, inner), F32),
        ((length // BLOCK, NSTATE, inner), F32),
        ((length, model), BF16),
        ((own, model), F32),
        ((own, model), F32),
        ((length, model), BF16),
    ]
    sums = [((groups, rows, ffn), BF16)] + [((halves, groups, rows, ffn), BF16)] * 2
    dma, vmem = pltpu.SemaphoreType.DMA, pltpu.VMEM
    moves = 5 + len(saved) + 2 * halves
    return pl.pallas_call(
        partial(forward_body, groups, halves),
        out_shape=[shape(*a) for a in saved + sums]
        + [shape((1, model), F32)],
        in_specs=[pl.BlockSpec(memory_space=pltpu.SMEM)]
        + [inside] * 7
        + [anywhere] * 11
        + [inside] * 5,
        out_specs=[anywhere] * (len(saved) + 3) + [inside],
        scratch_shapes=[vmem(*a) for a in saved]
        + [
            vmem((model, 2 * NSTATE), BF16),
            vmem((own, model), BF16),
            vmem((length, LANES), F32),
            vmem((length, LANES), F32),
            vmem((length, model), BF16),
            vmem((shard, narrow_width), BF16),
            vmem((length, inner), F32),
            vmem((length, 2 * NSTATE), F32),
            vmem((length, LANES), F32),
            vmem((NSTATE, inner), F32),
            vmem((8, LANES), F32),
            vmem((model, ffn), BF16),
            vmem((model, ffn), BF16),
            vmem((model, ffn), BF16),
            vmem((length, model), BF16),
            vmem((2, 2, own // 2, model), BF16),
            vmem((2, 2, own // 2, model), BF16),
            vmem((own, model), F32),
            vmem((length, ffn), F32),
            vmem((length, ffn), F32),
            vmem((length, ffn), BF16),
            vmem((length, ffn), BF16),
            vmem((length, ffn), BF16),
        ]
        + [vmem((groups, halves, 2, rows, ffn), BF16)] * 3
        + [vmem((groups, halves, rows, ffn), BF16)] * 3
        + [
            vmem((max(halves - 1, 1), groups, rows, ffn), BF16),
            vmem((groups, rows, ffn), BF16),
            dma((2, 10)),
            dma((moves,)),
        ]
        + gather_sems(8, halves)
        + scatter_sems(3, groups, halves),
        compiler_params=pltpu.CompilerParams(
            collective_id=0, has_side_effects=True, vmem_limit_bytes=VMEM_LIMIT
        ),
        name="forward",
    )(length_of, hidden, *gains, *weights, shared, out_grad, *tables, *kernels, *head_terms)


UNITS = 8


class BackwardIn(NamedTuple):
    length_ref: Any
    gain: Any
    gain2_part: Any
    conv_main: Any
    conv_shared: Any
    decay_log: Any
    step_bias: Any
    skip_gain: Any
    hidden: Any
    cosine: Any
    sine: Any
    w_shared: Any


class BackwardOut(NamedTuple):
    output: Any
    grad_in: Any
    gain: Any
    query: Any
    key: Any
    value: Any
    attn: Any
    z: Any
    x: Any
    step: Any
    shared: Any
    conv: Any
    conv_shared: Any
    decay: Any
    bias: Any
    skip: Any
    mamba: Any
    gain2: Any
    gate: Any
    up: Any
    down: Any


class BackwardScratch(NamedTuple):
    shared: Any
    hidden: Any
    cosine: Any
    sine: Any
    arrived: Any
    leaving: Any
    grad_y: Any
    grad_attn: Any
    conv_x: Any
    conv_bc: Any
    grad_x: Any
    grad_bc: Any
    steps: Any
    back: Any
    bc_back: Any
    grown_y: Any
    faded_x: Any
    state_back: Any
    key_sums: Any
    rows_sum: Any
    shared_y: Any
    shared_all: Any
    vector: Any
    vec_core: Any
    vec_x: Any
    vec_y: Any
    vec_z: Any
    head_terms: Any
    y_sems: Any
    small_sems: Any
    small_x_sems: Any
    small_z_sems: Any
    move_sems: Any


def backward_body(groups, halves, *refs):
    counts = [len(BackwardIn._fields), len(Kept._fields) - 1, len(BackwardOut._fields), 17]
    ends = np.cumsum(counts).tolist()
    r = BackwardIn(*refs[: ends[0]])
    h = Kept(*refs[ends[0] : ends[1]], None)
    out_hbm = BackwardOut(*refs[ends[1] : ends[2]])
    v = Kept(*refs[ends[2] : ends[3] - 1], *[None] * (counts[1] - 15))
    ffn_own = refs[ends[3] - 1]
    out = BackwardOut(*refs[ends[3] : ends[3] + counts[2]])
    rest = refs[ends[3] + counts[2] :]
    parts, from_core, rest = rest[:5], rest[5:10], rest[10:]
    from_x, chip_sums, rest = rest[:7], rest[7:14], rest[14:]
    from_z, relays, rest = rest[:8], rest[8:16], rest[16:]
    own_pairs, own_chip, rest = rest[:2], rest[2], rest[3:]
    s = BackwardScratch(*rest[:33])
    units = [
        dict(pair_sum=h.gate_pair, own_pair=own_pairs[0], from_x=from_x[0], chip_sum=chip_sums[0]),
        dict(pair_sum=h.up_pair, own_pair=own_pairs[1], from_x=from_x[1], chip_sum=chip_sums[1]),
        dict(chip_sum=own_chip),
    ] + [
        dict(part=parts[i], from_core=from_core[i], from_x=from_x[2 + i], chip_sum=chip_sums[2 + i])
        for i in range(5)
    ]
    for unit, ref, relay in zip(units, from_z, relays):
        unit["from_z"], unit["relay"] = ref, relay
    scatter = Scatter(units, groups, halves, rest[33:])
    move = Mover(s.move_sems)
    g, hi, c, t = place()
    own, model = r.hidden.shape
    length = 2 * own
    inner, q_width = out.x.shape[1], out.query.shape[1]
    kv_width, step_width = out.key.shape[1], out.step.shape[0]
    tiles, q_tiles = inner // LANES, q_width // LANES
    narrow_width = q_width + 2 * LANES
    other_y = (g, hi * 2 + c, 1 - t)
    devices = scatter.devices + [other_y]
    mine = pl.ds(pl.multiple_of(t * own, own), own)
    other = pl.ds(pl.multiple_of((1 - t) * own, own), own)
    greet(devices)

    def load(*names):
        for name in names:
            move.start(name, getattr(h, name), getattr(v, name))

    move.start("down_chip", h.down_chip, own_chip)
    load("mix_grad", "mix", "w_mix", "bc_padded", "step_in", "x_padded", "z_proj", "scanned")
    move.start("cosine", r.cosine, s.cosine)
    move.start("sine", r.sine, s.sine)
    load("normed", "qr", "kv", "probs", "states", "w_in")
    move.start("hidden", r.hidden, s.hidden)
    move.start("shared", r.w_shared, s.shared)
    move.start("ffn_own", h.ffn_part.at[mine, :], ffn_own)
    load("resid", "resid_grad")
    pick_heads(s.head_terms, (r.decay_log, r.step_bias, r.skip_gain), t)
    head_terms = s.head_terms
    greeted(devices)
    scatter.send_x(0)
    scatter.send_x(1)
    move.wait("down_chip")
    scatter.send_z(2)
    ffn_copy = scatter.start(
        remote(
            h.ffn_part.at[other, :], s.arrived.at[0], s.y_sems.at[0, 0], s.y_sems.at[1, 0], other_y
        )
    )
    count = r.length_ref[0]
    span = 256

    def give(*names):
        for name in names:
            move.start((name,), getattr(out, name), getattr(out_hbm, name))


    def weight_grads(part, left, right, cols, width):
        _, _, _, rows, _ = part.shape
        per = span // (2 * rows)

        def one(i, carry):
            at = pl.ds(pl.multiple_of(i * span, span), span)
            value = low(dot_tn(left[:, at], right[:, cols])).reshape(per, 2, rows, width)
            for k in range(per):
                at = i * per + k
                part[at // halves, lax.rem(at, halves)] = value[k]
            return carry

        lax.fori_loop(0, model // span, one, 0)

    move.wait("mix_grad", "mix")
    weight_grads(parts[0], v.mix_grad, v.mix, slice(None), q_width + inner)
    scatter.send(3)
    move.wait("w_mix")
    grad = dot(v.mix_grad[...], v.w_mix[...])
    s.grad_attn[...] = low(grad[:, :q_width])
    s.grad_y[...] = grad[:, q_width:]
    move.wait("bc_padded", "step_in", "x_padded")
    row = lax.broadcasted_iota(jnp.int32, (length, 1), 0)
    step_pre = v.step_in[...]
    softplus = jnp.maximum(step_pre, 0.0) + jnp.log(1.0 + jnp.exp(-jnp.abs(step_pre)))
    s.steps[...] = jnp.where(row < count, softplus, 0.0)
    channel = t * inner

    def taps_of(j):
        return r.conv_main[:, pl.ds(pl.multiple_of(channel + j * LANES, LANES), LANES)]

    for j in range(2 * NSTATE // LANES):
        cols = slice(j * LANES, (j + 1) * LANES)
        pre = causal_conv(v.bc_padded, r.conv_shared[:, cols], length, cols)
        s.conv_bc[:, cols] = pre * sigmoid(pre)
    scatter.core_stage(3)
    scatter.send_x(3)
    move.wait("z_proj", "scanned", "normed")
    skip_sum = jnp.zeros((1, LANES), F32)
    for j in range(tiles):
        cols = slice(j * LANES, (j + 1) * LANES)
        pre = causal_conv(v.x_padded, taps_of(j), length, cols)
        conv = pre * sigmoid(pre)
        s.conv_x[:, cols] = conv
        gate = v.z_proj[:, cols]
        sig = sigmoid(gate)
        grad = s.grad_y[:, cols]
        value = v.scanned[:, cols] + spread(head_terms[2:3, :], j) * conv
        at = narrow_width + inner + j * LANES
        s.back[:, at : at + LANES] = low(grad * value * sig * (1.0 + gate * (1.0 - sig)))
        grad = grad * gate * sig
        s.grad_y[:, cols] = grad
        s.rows_sum[j : j + 1, :] = column_sum(grad * conv)
    for j in range(tiles):
        skip_sum = skip_sum + head_sum(s.rows_sum[0:8, :], j)[j : j + 1, :]
    weight_grads(parts[1], v.normed, s.back, slice(narrow_width + inner, None), inner)
    scatter.send(4)
    move.wait("qr", "kv", "probs", "cosine", "sine")

    is_key = first_head(length)
    zero = jnp.zeros((), BF16)
    s.key_sums[...] = jnp.zeros_like(s.key_sums)

    def attend(j):
        tile = slice(j * LANES, (j + 1) * LANES)
        keys = [jnp.where(is_key, v.kv[...], zero)]
        keys.append(low(pltpu.roll(wide(keys[0]), HEAD, 1)))
        held = [None, jnp.where(is_key, zero, v.kv[...])]
        held[0] = low(pltpu.roll(wide(held[1]), HEAD, 1))
        for i in range(length // BLOCK):
            rows, upto = slice(i * BLOCK, (i + 1) * BLOCK), (i + 1) * BLOCK
            left = first_head(BLOCK)
            query, grad = v.qr[rows, tile], s.grad_attn[rows, tile]
            total = jnp.zeros((BLOCK, LANES), F32)
            for e in range(2):
                prob_low = v.probs[2 * j + e, rows, :upto]
                prob = wide(prob_low)
                prob_grad = dot_nt(grad, held[e][:upto])
                inside = jnp.sum(prob * prob_grad, axis=-1, keepdims=True)
                score_grad = low(prob * (prob_grad - inside))
                total = total + dot(score_grad, keys[e][:upto])
                side = left if e == 0 else jnp.logical_not(left)
                s.key_sums[0, :upto, :] += dot_tn(score_grad, jnp.where(side, query, zero))
                s.key_sums[1, :upto, :] += dot_tn(prob_low, jnp.where(side, grad, zero))
            total = total * HEAD**-0.5
            turned = total * s.cosine[rows, :] - half_swap(total) * s.sine[rows, :]
            s.back[rows, tile] = low(turned)

    scatter.relay(2)
    for j in range(q_tiles):
        attend(j)
        if j == 0:
            scatter.core_stage(4)
    key_grad = s.key_sums[0] + pltpu.roll(s.key_sums[0], HEAD, 1)
    key_grad = key_grad * HEAD**-0.5
    value_grad = s.key_sums[1] + pltpu.roll(s.key_sums[1], HEAD, 1)
    key_grad = key_grad * s.cosine[...] - half_swap(key_grad) * s.sine[...]
    s.back[:, q_width : q_width + LANES] = low(jnp.where(is_key, key_grad, value_grad))
    scatter.x_stage(0)
    scatter.send_z(0)
    move.wait("states")

    rate = -jnp.exp(head_terms[0:1, :])
    s.state_back[...] = jnp.zeros_like(s.state_back)
    upper = triangle(False)
    nblocks = length // BLOCK

    def scan_block(i, rate_sum, bias_sum):
        rows = slice(i * BLOCK, (i + 1) * BLOCK)
        step = s.steps[rows, :]
        total = exact_dot(triangle().astype(F32), step * rate)
        total_t = total.T
        last = total[BLOCK - 1 : BLOCK, :]
        grown, rest = jnp.exp(total), jnp.exp(last - total)
        b_mat, c_mat = split(s.conv_bc[rows, :NSTATE]), split(s.conv_bc[rows, NSTATE:])
        b_low, c_low = b_mat[0], c_mat[0]
        inner_t = jnp.where(upper, split_dot_nt(b_mat, c_mat), 0.0)
        state_mat = split(s.state_back[...])
        state_low = state_mat[0]
        crossed = split_dot(b_mat, state_mat)
        after = v.states[min(i + 1, nblocks - 1)] * s.state_back[...]
        left = first_head(BLOCK)
        inner_grad = jnp.zeros((BLOCK, BLOCK), F32)
        total_grad = jnp.zeros((BLOCK, LANES), F32)
        step_grad = jnp.zeros((BLOCK, LANES), F32)
        last_grad = jnp.zeros((8, LANES), F32)
        pulled = []
        for j in range(tiles):
            cols = slice(j * LANES, (j + 1) * LANES)
            conv, grad = s.conv_x[rows, cols], s.grad_y[rows, cols]
            step_wide, grown_wide, rest_wide = spread(step, j), spread(grown, j), spread(rest, j)
            stepped = step_wide * conv
            grad_low = low(grad)
            mixing = []
            for e, head in enumerate((2 * j, 2 * j + 1)):
                gap = jnp.minimum(total_t[head : head + 1, :] - total[:, head : head + 1], 0.0)
                decay = jnp.exp(gap)
                mixing.append(decay * inner_t)
                side = left if e == 0 else jnp.logical_not(left)
                inner_grad = inner_grad + decay * dot_nt(
                    low(jnp.where(side, stepped, 0.0)), grad_low
                )
            stacked = jnp.concatenate(
                [jnp.where(left, grad, 0.0), jnp.where(left, 0.0, grad)], axis=0
            )
            unstepped = split_dot(split(jnp.concatenate(mixing, axis=1)), split(stacked))
            unstepped = unstepped + rest_wide * crossed[:, cols]
            conv_grad = step_wide * unstepped
            total_grad = total_grad + head_sum(
                grad * v.scanned[rows, cols] - conv * conv_grad, j
            )
            step_grad = step_grad + head_sum(conv * unstepped, j)
            last_grad = last_grad + head_sum(
                jnp.broadcast_to(column_sum(after[:, cols]), (8, LANES)), j
            )
            s.grad_x[rows, cols] = conv_grad + spread(head_terms[2:3, :], j) * grad
            grown_grad = split(grown_wide * grad)
            s.grown_y[:, cols] = grown_grad[0]
            pulled.append(split_dot_tn(c_mat, grown_grad))
            s.faded_x[:, cols] = low(stepped * rest_wide)
        inner_low = low(jnp.where(upper, inner_grad, 0.0))
        s.grad_bc[rows, :NSTATE] = dot_nt(s.faded_x[...], state_low) + dot(inner_low, c_low)
        s.grad_bc[rows, NSTATE:] = dot_nt(s.grown_y[...], low(v.states[i])) + dot_tn(
            inner_low, b_low
        )
        for j in range(tiles):
            cols = slice(j * LANES, (j + 1) * LANES)
            fade = spread(grown[BLOCK - 1 : BLOCK, :], j)
            s.state_back[:, cols] = s.state_back[:, cols] * fade + pulled[j]
        slot = lax.broadcasted_iota(jnp.int32, (BLOCK, 1), 0)
        total_grad = total_grad + jnp.where(slot == BLOCK - 1, last_grad[0:1, :], 0.0)
        decay_grad = exact_dot(upper.astype(F32), total_grad)
        step_grad = step_grad + rate * decay_grad
        step_grad = jnp.where(i * BLOCK + slot < count, step_grad, 0.0)
        step_grad = step_grad * sigmoid(v.step_in[rows, :])
        s.back[rows, q_width + LANES : narrow_width] = low(step_grad)
        return rate_sum + column_sum(decay_grad * step), bias_sum + column_sum(step_grad)

    rate_sum = bias_sum = jnp.zeros((1, LANES), F32)
    for i in reversed(range(nblocks)):
        rate_sum, bias_sum = scan_block(i, rate_sum, bias_sum)
        if i == 0:
            scatter.relay(0)

    s.vector[...] = jnp.zeros_like(s.vector)

    def place_row(at, value):
        s.vector[at : at + 1, :] = value

    def place_halves(at, gap, value):
        place_row(at, jnp.where(t == 0, value, 0.0))
        place_row(at + gap, jnp.where(t == 0, 0.0, value))

    place_halves(72, 1, rate_sum * rate)
    place_halves(74, 1, bias_sum)
    place_halves(76, 1, skip_sum)
    for j in range(model // LANES):
        place_row(8 + j, r.gain2_part[:, j * LANES : (j + 1) * LANES])
    s.grad_bc[length:, :] = jnp.zeros((8, 2 * NSTATE), F32)
    s.grad_x[length:, :] = jnp.zeros((8, inner), F32)

    def conv_back(padded, grads, taps, cols, store):
        pre = causal_conv(padded, taps, length, cols)
        sig = sigmoid(pre)
        grads[:length, cols] = grads[:length, cols] * sig * (1.0 + pre * (1.0 - sig))
        for i in range(4):
            store(i, column_sum(grads[:length, cols] * padded[5 + i : 5 + i + length, cols]))
        total = taps[3:4, :] * grads[:length, cols]
        for i in range(3):
            total = total + taps[i : i + 1, :] * grads[3 - i : 3 - i + length, cols]
        return low(total)

    for j in range(2 * NSTATE // LANES):
        cols = slice(j * LANES, (j + 1) * LANES)
        s.bc_back[:, cols] = conv_back(
            v.bc_padded,
            s.grad_bc,
            r.conv_shared[:, cols],
            cols,
            lambda i, value, j=j: place_row(16 + 2 * i + j, value),
        )
    weight_grads(parts[2], v.normed, s.bc_back, slice(None), 2 * NSTATE)
    scatter.send(5)
    for j in range(tiles):
        cols = slice(j * LANES, (j + 1) * LANES)
        at = narrow_width + j * LANES
        s.back[:, at : at + LANES] = conv_back(
            v.x_padded,
            s.grad_x,
            taps_of(j),
            cols,
            lambda i, value, j=j: place_halves(24 + 2 * tiles * i + j, tiles, value),
        )
    scatter.core_stage(5)
    scatter.send_x(5)
    scatter.send_x(4)
    scatter.x_stage(1)
    scatter.send_z(1)
    move.wait("w_in", "shared")
    s.leaving[...] = low(
        dot_nt(s.back[other, :], v.w_in[...]) + dot_nt(s.bc_back[other, :], s.shared[...])
    )
    sum_copy = scatter.start(
        remote(s.leaving, s.arrived.at[1], s.y_sems.at[0, 1], s.y_sems.at[1, 1], other_y)
    )
    weight_grads(parts[4], v.normed, s.back, slice(narrow_width, narrow_width + inner), inner)
    scatter.send(7)
    weight_grads(parts[3], v.normed, s.back, slice(0, narrow_width), narrow_width)
    scatter.send(6)
    own_grad = dot_nt(s.back[mine, :], v.w_in[...]) + dot_nt(s.bc_back[mine, :], s.shared[...])
    scatter.x_stage(3)
    scatter.send_z(3)
    scatter.relay(1)
    sum_copy.wait_recv()
    move.wait("hidden")
    values = wide(s.hidden[...])
    scale = rms_scale(values)
    grad = own_grad + wide(s.arrived[1])
    gain_row = column_sum(grad * values * scale)
    for j in range(model // LANES):
        place_row(j, gain_row[:, j * LANES : (j + 1) * LANES])
    s.vec_core[c] = s.vector[...]
    vec_copy = scatter.start(
        remote(
            s.vector,
            s.vec_core.at[c],
            s.small_sems.at[0, 0],
            s.small_sems.at[1, 0],
            scatter.other_core,
        )
    )
    move.wait("resid", "resid_grad", "ffn_own")
    weighted = grad * r.gain[...]
    out.grad_in[...] = low(
        v.resid_grad[...]
        + scale * weighted
        - values * (scale * scale * scale) * jnp.mean(weighted * values, axis=-1, keepdims=True)
    )
    vec_copy.wait_recv()
    s.vec_x[hi] = s.vec_core[0] + s.vec_core[1]
    vec_copies = [
        scatter.start(
            remote(
                s.vec_x.at[hi],
                s.vec_x.at[hi],
                s.small_x_sems.at[0, 0, k],
                s.small_x_sems.at[1, 0, k],
                scatter.across[k - 1],
            )
        )
        for k in range(1, halves)
    ]
    scatter.core_stage(7)
    scatter.send_x(7)
    scatter.x_stage(5)
    scatter.send_z(5)
    scatter.core_stage(6)
    scatter.send_x(6)
    ffn_copy.wait_recv()
    slot = t * own + lax.broadcasted_iota(jnp.int32, (own, 1), 0)
    total = v.resid[...] + wide(ffn_own[...]) + wide(s.arrived[0])
    out.output[...] = low(jnp.where(slot < count, total, 0.0))
    give("output", "grad_in")
    scatter.relay(3)
    out.down[...] = scatter.z_stage(2)
    give("down")
    scatter.relay(5)
    out.gate[...] = scatter.z_stage(0)
    give("gate")
    scatter.x_stage(4)
    scatter.send_z(4)
    s.shared_y[t] = scatter.z_stage(5)
    shared_copy = scatter.start(
        remote(
            s.shared_y.at[t],
            s.shared_y.at[t],
            s.small_sems.at[0, 2],
            s.small_sems.at[1, 2],
            other_y,
        )
    )
    shared_copy.wait_recv()
    s.shared_all[g, hi, c] = low(s.shared_y[0] + s.shared_y[1])
    shared_copies = [
        scatter.start(
            remote(
                s.shared_all.at[g, hi, c],
                s.shared_all.at[g, hi, c],
                s.small_z_sems.at[0, 1, j],
                s.small_z_sems.at[1, 1, j],
                scatter.along[j - 1],
            )
        )
        for j in range(1, groups)
    ]
    for copy in vec_copies:
        copy.wait_recv()
    total = s.vec_x[0]
    for k in range(1, halves):
        total = total + s.vec_x[k]
    s.vec_y[t] = total
    vec_copy = scatter.start(
        remote(
            s.vec_y.at[t], s.vec_y.at[t], s.small_sems.at[0, 1], s.small_sems.at[1, 1], other_y
        )
    )
    out.up[...] = scatter.z_stage(1)
    give("up")
    vec_copy.wait_recv()
    s.vec_z[g] = s.vec_y[0] + s.vec_y[1]
    vec_copies = [
        scatter.start(
            remote(
                s.vec_z.at[g],
                s.vec_z.at[g],
                s.small_z_sems.at[0, 0, j],
                s.small_z_sems.at[1, 0, j],
                scatter.along[j - 1],
            )
        )
        for j in range(1, groups)
    ]
    total = scatter.z_stage(3)
    out.attn[...] = total[:, :q_width]
    out.mamba[...] = total[:, q_width:]
    give("attn", "mamba")
    scatter.relay(4)
    scatter.x_stage(7)
    scatter.send_z(7)
    for copy in shared_copies:
        copy.wait_recv()
    shared_copies = [
        scatter.start(
            remote(
                s.shared_all.at[:, hi, c],
                s.shared_all.at[:, hi, c],
                s.small_x_sems.at[0, 1, k],
                s.small_x_sems.at[1, 1, k],
                scatter.across[k - 1],
            )
        )
        for k in range(1, halves)
    ]
    out.z[...] = scatter.z_stage(4)
    give("z")
    for copy in vec_copies:
        copy.wait_recv()
    total = s.vec_z[0]
    for j in range(1, groups):
        total = total + s.vec_z[j]
    out.gain[...] = total[0:8, :]
    out.gain2[...] = total[8:16, :]
    for i in range(4):
        for j in range(2 * NSTATE // LANES):
            at = 16 + 2 * i + j
            out.conv_shared[i : i + 1, j * LANES : (j + 1) * LANES] = total[at : at + 1, :]
        for j in range(2 * tiles):
            at = 24 + 2 * tiles * i + j
            out.conv[i : i + 1, j * LANES : (j + 1) * LANES] = total[at : at + 1, :]
    for ref, at in ((out.decay, 72), (out.bias, 74), (out.skip, 76)):
        ref[...] = jnp.concatenate(
            [total[at : at + 1, :step_width], total[at + 1 : at + 2, :step_width]], axis=1
        )
    give("gain", "gain2", "conv", "conv_shared", "decay", "bias", "skip")
    scatter.x_stage(6)
    scatter.send_z(6)
    scatter.relay(7)
    for copy in shared_copies:
        copy.wait_recv()
    shared_copy = scatter.start(
        remote(
            s.shared_all.at[:, :, c],
            s.shared_all.at[:, :, c],
            s.small_sems.at[0, 3],
            s.small_sems.at[1, 3],
            scatter.other_core,
        )
    )
    scatter.relay(6)
    out.x[...] = scatter.z_stage(7)
    give("x")
    shared_copy.wait_recv()

    def widen(i, carry):
        block = s.shared_all[i // (2 * halves), lax.rem(i // 2, halves), lax.rem(i, 2)]
        out.shared[i] = wide(block)
        return carry

    lax.fori_loop(0, groups * halves * 2, widen, 0)
    give("shared")
    total = scatter.z_stage(6)
    out.query[...] = total[:, :q_width]
    out.key[...] = total[:, q_width : q_width + kv_width]
    out.value[...] = total[:, q_width + kv_width : q_width + 2 * kv_width]
    out.step[...] = total[:, q_width + LANES :].T[:step_width, :]
    give("query", "key", "value", "step")
    scatter.drain()
    move.drain()


def backward(
    length_of, hidden, gain, gain2_part, saved, w_shared, kernels, head_terms, tables, widths
):
    groups, halves = lax.axis_size("grp"), lax.axis_size("fsdp") // 2
    q_width, kv_width, step_width = widths
    own, model = hidden.shape
    length = 2 * own
    narrow_width = q_width + 2 * LANES
    inner = (saved[0].shape[1] - narrow_width) // 2
    rows = model // (2 * groups * halves)
    ffn = saved[-1].shape[-1]
    inside = pl.BlockSpec(memory_space=pltpu.VMEM)
    anywhere = pl.BlockSpec(memory_space=pl.ANY)
    shape, vmem, dma = jax.ShapeDtypeStruct, pltpu.VMEM, pltpu.SemaphoreType.DMA
    outs = [
        shape((own, model), BF16),
        shape((own, model), BF16),
        shape((model // LANES, LANES), F32),
        shape((rows, q_width), F32),
        shape((rows, kv_width), F32),
        shape((rows, kv_width), F32),
        shape((rows, q_width), F32),
        shape((rows, inner), F32),
        shape((rows, inner), F32),
        shape((step_width, rows), F32),
        shape((2 * groups * halves, rows, 2 * NSTATE), F32),
        shape((4, 2 * inner), F32),
        shape((4, 2 * NSTATE), F32),
        shape((1, 2 * step_width), F32),
        shape((1, 2 * step_width), F32),
        shape((1, 2 * step_width), F32),
        shape((rows, inner), F32),
        shape((model // LANES, LANES), F32),
        shape((rows, ffn), F32),
        shape((rows, ffn), F32),
        shape((rows, ffn), F32),
    ]
    part_widths = [q_width + inner, inner, 2 * NSTATE, narrow_width, inner]
    x_widths = [ffn, ffn] + part_widths
    z_widths = [ffn] * 3 + part_widths
    vector = (80, LANES)
    others = max(halves - 1, 1)
    scratch = (
        [vmem(a.shape, a.dtype) for a in saved[:16]]
        + [vmem((own, model), BF16)]
        + [vmem(a.shape, a.dtype) for a in outs]
        + [vmem((groups, halves, 2, rows, w), BF16) for w in part_widths]
        + [vmem((groups, halves, rows, w), BF16) for w in part_widths]
        + [vmem((others, groups, rows, w), BF16) for w in x_widths]
        + [vmem((groups, rows, w), BF16) for w in x_widths]
        + [vmem((groups - 1, rows, w), BF16) for w in z_widths]
        + [vmem((rows, w), BF16) for w in z_widths]
        + [vmem((groups, rows, ffn), BF16)] * 3
        + [
            vmem((model, 2 * NSTATE), BF16),
            vmem((own, model), BF16),
            vmem((length, LANES), F32),
            vmem((length, LANES), F32),
            vmem((2, own, model), BF16),
            vmem((own, model), BF16),
            vmem((length, inner), F32),
            vmem((length, q_width), BF16),
            vmem((length, inner), F32),
            vmem((length, 2 * NSTATE), F32),
            vmem((length + 8, inner), F32),
            vmem((length + 8, 2 * NSTATE), F32),
            vmem((length, LANES), F32),
            vmem((length, narrow_width + 2 * inner), BF16),
            vmem((length, 2 * NSTATE), BF16),
            vmem((BLOCK, inner), BF16),
            vmem((BLOCK, inner), BF16),
            vmem((NSTATE, inner), F32),
            vmem((2, length, LANES), F32),
            vmem((8, LANES), F32),
            vmem((2, rows, 2 * NSTATE), F32),
            vmem((groups, halves, 2, rows, 2 * NSTATE), BF16),
            vmem(vector, F32),
            vmem((2,) + vector, F32),
            vmem((halves,) + vector, F32),
            vmem((2,) + vector, F32),
            vmem((groups,) + vector, F32),
            vmem((8, LANES), F32),
            dma((2, 2)),
            dma((2, 4)),
            dma((2, 2, halves)),
            dma((2, 2, groups)),
            dma((23 + len(outs),)),
        ]
        + scatter_sems(UNITS, groups, halves)
    )
    return pl.pallas_call(
        partial(backward_body, groups, halves),
        out_shape=outs,
        in_specs=[pl.BlockSpec(memory_space=pltpu.SMEM)]
        + [inside] * 7
        + [anywhere] * (4 + len(saved)),
        out_specs=[anywhere] * len(outs),
        scratch_shapes=scratch,
        compiler_params=pltpu.CompilerParams(
            collective_id=1, has_side_effects=True, vmem_limit_bytes=VMEM_LIMIT
        ),
        name="backward",
    )(length_of, gain, gain2_part, *kernels, *head_terms, hidden, *tables, w_shared, *saved)


def emit_body(*refs):
    count = len(refs) // 3
    sources, targets, held = refs[:count], refs[count : 2 * count], refs[2 * count : 3 * count]
    sems = refs[3 * count]
    arriving = [
        pltpu.make_async_copy(source, at, sems.at[0, i])
        for i, (source, at) in enumerate(zip(sources, held))
    ]
    leaving = [
        pltpu.make_async_copy(at, target, sems.at[1, i])
        for i, (at, target) in enumerate(zip(held, targets))
    ]
    for copy in arriving:
        copy.start()
    for arrived, copy in zip(arriving, leaving):
        arrived.wait()
        copy.start()
    for copy in leaving:
        copy.wait()


def emit(arrays):
    anywhere = pl.BlockSpec(memory_space=pl.ANY)
    return pl.pallas_call(
        emit_body,
        out_shape=[jax.ShapeDtypeStruct(a.shape, a.dtype) for a in arrays],
        in_specs=[anywhere] * len(arrays),
        out_specs=[anywhere] * len(arrays),
        scratch_shapes=[pltpu.VMEM(a.shape, a.dtype) for a in arrays]
        + [pltpu.SemaphoreType.DMA((2, len(arrays)))],
        compiler_params=pltpu.CompilerParams(vmem_limit_bytes=VMEM_LIMIT),
        name="emit",
    )(*arrays)


def local(
    hidden_in,
    lengths,
    norm1_gain,
    w_query,
    key_weight,
    value_weight,
    w_attn_out,
    w_mamba_z,
    w_mamba_x,
    w_step,
    w_shared,
    conv_main,
    conv_shared,
    decay_log,
    step_bias,
    skip_gain,
    w_mamba_out,
    norm2_gain,
    w_ffn_gate,
    w_ffn_up,
    w_ffn_down,
    out_grad,
):
    own, model = hidden_in.shape
    step_width = w_step.shape[1]
    head_terms = [v.reshape(1, -1) for v in (decay_log, step_bias, skip_gain)]
    tables = rotary_tables(2 * own)
    gain1, gain2 = norm1_gain.reshape(1, model), norm2_gain.reshape(1, model)
    kernels = (conv_main, conv_shared)
    weights = (w_query, key_weight.T, value_weight.T, w_step.T, w_mamba_x, w_mamba_z)
    weights += (w_attn_out, w_mamba_out, w_ffn_down, w_ffn_gate, w_ffn_up)
    *saved, gain2_part = forward(
        lengths,
        hidden_in,
        out_grad,
        (gain1, gain2),
        weights,
        w_shared,
        kernels,
        head_terms,
        tables,
    )
    outs = backward(
        lengths,
        hidden_in,
        gain1,
        gain2_part,
        saved,
        w_shared,
        kernels,
        head_terms,
        tables,
        (w_query.shape[1], key_weight.shape[1], step_width),
    )
    outs = list(emit(outs))
    outs[9] = outs[9].T
    for i in (2, 13, 14, 15, 17):
        outs[i] = outs[i].reshape(-1)
    outs[10] = outs[10].reshape(model, -1)
    return tuple(outs)


def solution(mesh):
    rows, whole, weight = P(("grp", "fsdp", "tp"), None), P(), P("fsdp", "tp")
    grad = P(("grp", "fsdp"), "tp")
    return jax.shard_map(
        local,
        mesh=mesh,
        in_specs=(rows, P(("grp", "fsdp")), whole)
        + (weight,) * 7
        + (whole,) * 6
        + (weight, whole)
        + (weight,) * 3
        + (rows,),
        out_specs=(rows, rows, whole)
        + (grad,) * 7
        + (whole,) * 6
        + (grad, whole)
        + (grad,) * 3,
        check_vma=False,
    )
```

```python
from functools import partial
from typing import Any, NamedTuple

import jax
import jax.numpy as jnp
import numpy as np
from jax import lax
from jax.experimental import pallas as pl
from jax.experimental.pallas import tpu as pltpu
from jax.sharding import PartitionSpec as P

HEAD = 64
LANES = 128
BLOCK = 128
NSTATE = 128
EPS = 1e-05
ROPE_BASE = 100000000000.0
MESH = pl.DeviceIdType.MESH
VMEM_LIMIT = 62 << 20
F32, BF16 = jnp.float32, jnp.bfloat16
EXACT = lax.Precision.HIGHEST


def low(values):
    return values.astype(BF16)


def wide(values):
    return values.astype(F32)


def dot(a, b):
    return jnp.dot(a, b, preferred_element_type=F32)


def dot_nt(a, b):
    return lax.dot_general(a, b, (((1,), (1,)), ((), ())), preferred_element_type=F32)


def dot_tn(a, b):
    return lax.dot_general(a, b, (((0,), (0,)), ((), ())), preferred_element_type=F32)


def exact_dot(a, b):
    return jnp.dot(a, b, precision=EXACT, preferred_element_type=F32)


def split(values):
    coarse = low(values)
    return coarse, low(values - wide(coarse))


def split_dot(a, b):
    return dot(jnp.concatenate([a[0], a[0], a[1]], axis=1), jnp.concatenate([b[0], b[1], b[0]], axis=0))


def split_dot_nt(a, b):
    return dot_nt(jnp.concatenate([a[0], a[0], a[1]], axis=1), jnp.concatenate([b[0], b[1], b[0]], axis=1))


def split_dot_tn(a, b):
    return dot_tn(jnp.concatenate([a[0], a[0], a[1]], axis=0), jnp.concatenate([b[0], b[1], b[0]], axis=0))


def sigmoid(v):
    return 1.0 / (1.0 + jnp.exp(-v))


def rms_scale(values):
    return lax.rsqrt(jnp.mean(values * values, axis=-1, keepdims=True) + EPS)


def lane_ids(rows):
    return lax.broadcasted_iota(jnp.int32, (rows, LANES), 1)


def first_head(rows):
    return lane_ids(rows) < HEAD


def half_swap(tile):
    lower = lax.rem(lane_ids(tile.shape[0]), HEAD) < HEAD // 2
    return jnp.where(lower, pltpu.roll(tile, LANES - HEAD // 2, 1), pltpu.roll(tile, HEAD // 2, 1))


def spread(values, tile):
    return jnp.where(
        first_head(values.shape[0]),
        values[:, 2 * tile : 2 * tile + 1],
        values[:, 2 * tile + 1 : 2 * tile + 2],
    )


def rotary_tables(length):
    positions = np.arange(length, dtype=np.float64)[:, None]
    power = np.arange(HEAD // 2, dtype=np.float64) * (-2.0 / HEAD)
    phase = (positions * np.power(ROPE_BASE, power)[None, :]).astype(np.float32)
    cosine, sine = np.cos(phase), np.sin(phase)
    return (
        np.concatenate([cosine] * 4, axis=1).astype(np.float32),
        np.concatenate([-sine, sine] * 2, axis=1).astype(np.float32),
    )


def place():
    g, f, t = lax.axis_index("grp"), lax.axis_index("fsdp"), lax.axis_index("tp")
    return g, f // 2, lax.rem(f, 2), t


def greet(devices):
    barrier = pltpu.get_barrier_semaphore()
    for device in devices:
        pl.semaphore_signal(barrier, inc=1, device_id=device, device_id_type=MESH)


def greeted(devices):
    pl.semaphore_wait(pltpu.get_barrier_semaphore(), len(devices))


def remote(src, dst, send, recv, device):
    return pltpu.make_async_remote_copy(
        src_ref=src,
        dst_ref=dst,
        send_sem=send,
        recv_sem=recv,
        device_id=device,
        device_id_type=MESH,
    )


def pick_heads(terms, whole, t):
    terms[...] = jnp.zeros_like(terms)
    for i, ref in enumerate(whole):
        heads = ref.shape[1] // 2
        terms[i : i + 1, :heads] = jnp.where(t == 0, ref[:, :heads], ref[:, heads:])


class Gather:
    def __init__(self, units, halves, sems):
        self.units, self.halves = units, halves
        self.x, self.z, self.cx, self.cz, self.own, self.local = sems
        g, self.hi, self.c, t = place()
        f = self.hi * 2 + self.c
        self.f, self.pair = f, lax.rem(g, 2)
        self.other_core = (g, self.hi * 2 + 1 - self.c, t)
        self.other_z = (g + 1 - 2 * self.pair, f, t)
        self.across = [
            (g, lax.rem(self.hi + k, halves) * 2 + self.c, t) for k in range(1, halves)
        ]
        self.devices = [self.other_core, self.other_z] + self.across
        self.got, self.sent, self.pending = {}, [], {}

    def block(self, u, owner, part=None):
        shard, full, column, width = self.units[u]
        rows = shard.shape[0]
        size = rows if part is None else rows // 2
        start = owner * rows + (0 if part is None else part * size)
        return full.at[pl.ds(pl.multiple_of(start, size), size), pl.ds(column, width)]

    def start(self, copy):
        copy.start()
        self.sent.append(copy)
        return copy

    def send(self, u):
        shard = self.units[u][0]
        half = shard.shape[0] // 2
        mine = shard.at[pl.ds(pl.multiple_of(self.pair * half, half), half), :]
        for k in range(1, self.halves):
            self.got["x", u, k] = self.start(
                remote(
                    mine,
                    self.block(u, self.f, self.pair),
                    self.x.at[0, u, k],
                    self.x.at[1, u, k],
                    self.across[k - 1],
                )
            )
        self.got["own", u] = self.start(
            remote(
                shard,
                self.block(u, self.f),
                self.own.at[0, u],
                self.own.at[1, u],
                self.other_core,
            )
        )
        self.pending[u] = pltpu.make_async_copy(shard, self.block(u, self.f), self.local.at[u])
        self.pending[u].start()

    def owner(self, k):
        return lax.rem(self.hi - k + self.halves, self.halves) * 2 + self.c

    def relay_x(self, u):
        for k in range(1, self.halves):
            self.got.pop(("x", u, k)).wait_recv()
            block = self.block(u, self.owner(k), self.pair)
            self.got["z", u, k] = self.start(
                remote(block, block, self.z.at[0, u, k], self.z.at[1, u, k], self.other_z)
            )
            self.got["cx", u, k] = self.start(
                remote(block, block, self.cx.at[0, u, k], self.cx.at[1, u, k], self.other_core)
            )

    def relay_z(self, u):
        for k in range(1, self.halves):
            self.got.pop(("z", u, k)).wait_recv()
            block = self.block(u, self.owner(k), 1 - self.pair)
            self.got["cz", u, k] = self.start(
                remote(block, block, self.cz.at[0, u, k], self.cz.at[1, u, k], self.other_core)
            )

    def finish(self, u):
        self.got.pop(("own", u)).wait_recv()
        for k in range(1, self.halves):
            self.got.pop(("cx", u, k)).wait_recv()
            self.got.pop(("cz", u, k)).wait_recv()
        self.pending.pop(u).wait()

    def drain(self):
        assert not self.got and not self.pending
        for copy in self.sent:
            copy.wait_send()


def gather_sems(units, halves):
    dma = pltpu.SemaphoreType.DMA
    return [dma((2, units, halves))] * 4 + [dma((2, units)), dma((units,))]


def causal_conv(padded, kernel, rows, cols):
    total = kernel[3:4, :] * padded[8 : 8 + rows, cols]
    for i in range(3):
        total = total + kernel[i : i + 1, :] * padded[5 + i : 5 + i + rows, cols]
    return total


def triangle(lower=True):
    row = lax.broadcasted_iota(jnp.int32, (BLOCK, BLOCK), 0)
    col = lax.broadcasted_iota(jnp.int32, (BLOCK, BLOCK), 1)
    return row >= col if lower else row <= col


class Scatter:
    def __init__(self, units, groups, halves, sems):
        self.units = units
        self.groups, self.halves = groups, halves
        self.c_sems, self.x_sems, self.z_sems, self.l_sems = sems
        self.g, self.hi, self.c, self.t = place()
        f = self.hi * 2 + self.c
        self.other_core = (self.g, self.hi * 2 + 1 - self.c, self.t)
        self.across = [
            (self.g, lax.rem(self.hi + k, halves) * 2 + self.c, self.t) for k in range(1, halves)
        ]
        self.along = [(lax.rem(self.g + j, groups), f, self.t) for j in range(1, groups)]
        self.devices = [self.other_core] + self.across + self.along
        self.outer = (self.g == 0) | (self.g == groups - 1)
        self.got, self.sent, self.lines = {}, [], []

    def start(self, copy):
        copy.start()
        self.sent.append(copy)
        return copy

    def send(self, u):
        unit = self.units[u]
        self.got["c", u] = self.start(
            remote(
                unit["part"].at[:, :, 1 - self.c],
                unit["from_core"],
                self.c_sems.at[0, u],
                self.c_sems.at[1, u],
                self.other_core,
            )
        )

    def send_x(self, u):
        unit = self.units[u]
        for k in range(1, self.halves):
            away = lax.rem(self.hi + k, self.halves)
            self.got["x", u, k] = self.start(
                remote(
                    unit["pair_sum"].at[away]
                    if "pair_sum" in unit
                    else unit["part"].at[:, away, self.c],
                    unit["from_x"].at[k - 1],
                    self.x_sems.at[0, u, k],
                    self.x_sems.at[1, u, k],
                    self.across[k - 1],
                )
            )
        if "pair_sum" in unit:
            self.load(u, unit["pair_sum"].at[self.hi], unit["own_pair"])

    def load(self, u, source, target):
        self.got["l", u] = pltpu.make_async_copy(source, target, self.l_sems.at[u])
        self.got["l", u].start()

    def z_links(self, u):
        unit, g = self.units[u], self.g
        chip, into, last = unit["chip_sum"], unit["from_z"], self.groups - 1

        def to(where):
            return (where, self.hi * 2 + self.c, self.t)

        near = jnp.where(g == 0, 1, last - 1)
        outer = {
            0: (chip.at[near], into.at[0], to(near)),
            1: (chip.at[last - near], into.at[1], to(last - near)),
            3: (chip.at[last - g], unit["relay"], to(near)),
        }
        end = jnp.where(g == 1, 0, last)
        inner = {
            0: (chip.at[end], into.at[0], to(end)),
            1: (chip.at[last - end], into.at[1], to(last - end)),
            2: (chip.at[last - g], into.at[2], to(last - g)),
        }
        return outer, inner

    def z_copy(self, u, side, slot):
        source, target, device = self.z_links(u)[side][slot]
        return remote(
            source, target, self.z_sems.at[0, u, slot], self.z_sems.at[1, u, slot], device
        )

    def send_z(self, u):
        unit = self.units[u]
        if self.groups == 4:

            @pl.when(self.outer)
            def _():
                for slot in (3, 0, 1):
                    self.z_copy(u, 0, slot).start()

            @pl.when(jnp.logical_not(self.outer))
            def _():
                for slot in (2, 0):
                    self.z_copy(u, 1, slot).start()

            self.lines.append(u)
            return
        for j in range(1, self.groups):
            self.got["z", u, j] = self.start(
                remote(
                    unit["chip_sum"].at[lax.rem(self.g + j, self.groups)],
                    unit["from_z"].at[j - 1],
                    self.z_sems.at[0, u, j],
                    self.z_sems.at[1, u, j],
                    self.along[j - 1],
                )
            )

    def relay(self, u):
        if self.groups != 4:
            return
        unit = self.units[u]

        @pl.when(jnp.logical_not(self.outer))
        def _():
            self.z_copy(u, 0, 3).wait_recv()
            far = jnp.where(self.g == 1, self.groups - 1, 0)
            chip = unit["chip_sum"]
            chip[far] = low(wide(chip[far]) + wide(unit["relay"][...]))
            self.z_copy(u, 1, 1).start()

    def core_stage(self, u):
        part, from_core = self.units[u]["part"], self.units[u]["from_core"]
        self.got.pop(("c", u)).wait_recv()

        def add(i, carry):
            gg, h = i // self.halves, lax.rem(i, self.halves)
            part[gg, h, self.c] = low(wide(part[gg, h, self.c]) + wide(from_core[gg, h]))
            return carry

        lax.fori_loop(0, self.groups * self.halves, add, 0)

    def x_stage(self, u):
        unit = self.units[u]
        for k in range(1, self.halves):
            self.got.pop(("x", u, k)).wait_recv()
        if "pair_sum" in unit:
            self.got.pop(("l", u)).wait()

        def add(gg, carry):
            if "pair_sum" in unit:
                total = wide(unit["own_pair"][gg])
            else:
                total = wide(unit["part"][gg, self.hi, self.c])
            for k in range(1, self.halves):
                total = total + wide(unit["from_x"][k - 1, gg])
            unit["chip_sum"][gg] = low(total)
            return carry

        lax.fori_loop(0, self.groups, add, 0)

    def z_stage(self, u):
        unit = self.units[u]
        total = wide(unit["chip_sum"][self.g])
        if self.groups == 4:
            for slot in (0, 1):
                self.z_copy(u, 1, slot).wait_recv()

            @pl.when(jnp.logical_not(self.outer))
            def _():
                self.z_copy(u, 1, 2).wait_recv()

            total = total + wide(unit["from_z"][0]) + wide(unit["from_z"][1])
            return total + jnp.where(self.outer, 0.0, wide(unit["from_z"][2]))
        for j in range(1, self.groups):
            self.got.pop(("z", u, j)).wait_recv()
            total = total + wide(unit["from_z"][j - 1])
        return total

    def drain(self):
        assert not self.got
        for copy in self.sent:
            copy.wait_send()
        if not self.lines:
            return

        @pl.when(self.outer)
        def _():
            for u in self.lines:
                for slot in (0, 1, 3):
                    self.z_copy(u, 0, slot).wait_send()

        @pl.when(jnp.logical_not(self.outer))
        def _():
            for u in self.lines:
                for slot in (0, 1, 2):
                    self.z_copy(u, 1, slot).wait_send()


class Mover:
    def __init__(self, sems):
        self.sems, self.count, self.copies = sems, 0, {}

    def start(self, name, source, target):
        self.copies[name] = pltpu.make_async_copy(source, target, self.sems.at[self.count])
        self.copies[name].start()
        self.count += 1

    def wait(self, *names):
        for name in names:
            self.copies.pop(name).wait()

    def drain(self):
        self.wait(*list(self.copies))


def scatter_sems(units, groups, halves):
    dma = pltpu.SemaphoreType.DMA
    return [
        dma((2, units)),
        dma((2, units, halves)),
        dma((2, units, groups)),
        dma((units,)),
    ]


def head_sum(values, tile):
    lane = lax.broadcasted_iota(jnp.int32, (LANES, LANES), 0)
    column = lax.broadcasted_iota(jnp.int32, (LANES, LANES), 1)
    pick = low(jnp.where(column == 2 * tile + jnp.where(lane < HEAD, 0, 1), 1.0, 0.0))
    coarse = low(values)
    fine = low(values - wide(coarse))
    return dot(
        jnp.concatenate([coarse, fine], axis=1), jnp.concatenate([pick, pick], axis=0)
    )


def column_sum(values):
    return jnp.sum(values, axis=0, keepdims=True)


class ForwardIn(NamedTuple):
    length_ref: Any
    hidden: Any
    gain1: Any
    gain2: Any
    w_query: Any
    w_key: Any
    w_value: Any
    w_step: Any
    w_x: Any
    w_z: Any
    w_attn_out: Any
    w_mamba_out: Any
    w_down: Any
    w_gate: Any
    w_up: Any
    w_shared: Any
    out_grad: Any
    cosine: Any
    sine: Any
    conv_main: Any
    conv_shared: Any
    decay_log: Any
    step_bias: Any
    skip_gain: Any


class Kept(NamedTuple):
    w_in: Any
    w_mix: Any
    normed: Any
    mix: Any
    qr: Any
    kv: Any
    probs: Any
    x_padded: Any
    z_proj: Any
    bc_padded: Any
    step_in: Any
    scanned: Any
    states: Any
    mix_grad: Any
    resid_grad: Any
    resid: Any
    ffn_part: Any
    down_chip: Any
    gate_pair: Any
    up_pair: Any
    gain2_part: Any


class ForwardScratch(NamedTuple):
    shared: Any
    out_grad: Any
    cosine: Any
    sine: Any
    top_grad: Any
    narrow: Any
    conv_x: Any
    conv_bc: Any
    steps: Any
    state: Any
    head_terms: Any
    w_down: Any
    w_gate: Any
    w_up: Any
    normed2: Any
    arrived: Any
    leaving: Any
    own_part: Any
    gate_pre: Any
    up_pre: Any
    hidden_low: Any
    gate_back: Any
    up_back: Any
    p_down: Any
    p_down2: Any
    p_gate: Any
    p_up: Any
    c_down: Any
    c_down2: Any
    c_gate: Any
    c_up: Any
    x_down: Any
    x_down2: Any
    d_chip: Any
    d_chip2: Any
    y_sems: Any
    move_sems: Any


def forward_body(groups, halves, *refs):
    counts = len(ForwardIn._fields), len(Kept._fields) - 1
    r = ForwardIn(*refs[: counts[0]])
    out = Kept(*refs[counts[0] : sum(counts) + 1])
    rest = refs[sum(counts) + 1 :]
    v = Kept(*rest[:17], *[None] * (counts[1] - 16))
    s = ForwardScratch(*rest[17:54])
    sems = rest[54:]
    g, hi, c, t = place()
    own, model = r.hidden.shape
    length = 2 * own
    inner, ffn = r.w_x.shape[1], r.w_gate.shape[1]
    q_width, step_width = r.w_query.shape[1], r.w_step.shape[0]
    tiles, q_tiles = inner // LANES, q_width // LANES
    narrow_width = q_width + 2 * LANES
    gather = Gather(
        [
            (s.narrow, v.w_in, 0, narrow_width),
            (r.w_x, v.w_in, narrow_width, inner),
            (r.w_z, v.w_in, narrow_width + inner, inner),
            (r.w_attn_out, v.w_mix, 0, q_width),
            (r.w_mamba_out, v.w_mix, q_width, inner),
            (r.w_gate, s.w_gate, 0, ffn),
            (r.w_up, s.w_up, 0, ffn),
            (r.w_down, s.w_down, 0, ffn),
        ],
        halves,
        sems[:6],
    )
    scatter = Scatter(
        [
            dict(part=s.p_down, from_core=s.c_down, from_x=s.x_down, chip_sum=s.d_chip),
            dict(part=s.p_gate, from_core=s.c_gate),
            dict(part=s.p_up, from_core=s.c_up),
            dict(part=s.p_down2, from_core=s.c_down2, from_x=s.x_down2, chip_sum=s.d_chip2),
        ],
        groups,
        halves,
        sems[6:],
    )
    move = Mover(s.move_sems)
    other_y = (g, hi * 2 + c, 1 - t)
    devices = gather.devices + [other_y]
    greet(devices)
    move.start("out_grad", r.out_grad, s.out_grad)
    move.start("shared", r.w_shared, s.shared)
    move.start("cosine", r.cosine, s.cosine)
    move.start("sine", r.sine, s.sine)
    turned = jnp.concatenate([wide(r.w_key[...]), wide(r.w_value[...])], axis=0).T
    s.narrow[:, :q_width] = r.w_query[...]
    s.narrow[:, q_width : q_width + LANES] = low(turned)
    filler = jnp.zeros((LANES - step_width, s.narrow.shape[0]), F32)
    turned = jnp.concatenate([wide(r.w_step[...]), filler], axis=0).T
    s.narrow[:, q_width + LANES :] = low(turned)
    mine = pl.ds(pl.multiple_of(t * own, own), own)
    other = pl.ds(pl.multiple_of((1 - t) * own, own), own)
    values = wide(r.hidden[...])
    v.normed[mine, :] = low(values * rms_scale(values) * r.gain1[...])
    count = r.length_ref[0]
    greeted(devices)
    gather.send(0)
    sent = []

    def swap(src, dst, at):
        copy = remote(src, dst, s.y_sems.at[0, at], s.y_sems.at[1, at], other_y)
        copy.start()
        sent.append(copy)
        return copy

    y_copy = swap(v.normed.at[mine, :], v.normed.at[mine, :], 8)
    for u in range(1, 8):
        gather.send(u)
    slot = t * own + lax.broadcasted_iota(jnp.int32, (own, 1), 0)
    move.wait("out_grad")
    s.top_grad[mine, :] = jnp.where(slot < count, s.out_grad[...], jnp.zeros((), BF16))
    grad_copy = swap(s.top_grad.at[mine, :], s.top_grad.at[mine, :], 9)
    pick_heads(s.head_terms, (r.decay_log, r.step_bias, r.skip_gain), t)
    v.x_padded[0:8, :] = jnp.zeros((8, inner), F32)
    v.bc_padded[0:8, :] = jnp.zeros((8, 2 * NSTATE), F32)
    s.state[...] = jnp.zeros_like(s.state)

    def save(*names):
        for name in names:
            move.start(name, getattr(v, name), getattr(out, name))

    move.wait("shared")
    v.bc_padded[pl.ds(pl.multiple_of(8 + t * own, 8), own), :] = dot(
        v.normed[mine, :], s.shared[...]
    )
    gather.relay_x(0)
    gather.relay_z(0)
    gather.relay_x(1)
    y_copy.wait_recv()
    save("normed")
    v.bc_padded[pl.ds(pl.multiple_of(8 + (1 - t) * own, 8), own), :] = dot(
        v.normed[other, :], s.shared[...]
    )
    gather.finish(0)
    move.wait("cosine", "sine")
    projected = dot(v.normed[...], v.w_in[:, :narrow_width])
    for j in range(q_tiles):
        tile = projected[:, j * LANES : (j + 1) * LANES]
        turned = tile * s.cosine[...] + half_swap(tile) * s.sine[...]
        v.qr[:, j * LANES : (j + 1) * LANES] = low(turned)
    tile = projected[:, q_width : q_width + LANES]
    is_key = first_head(length)
    turned = tile * s.cosine[...] + half_swap(tile) * s.sine[...]
    v.kv[...] = low(jnp.where(is_key, turned, tile))
    step_pre = projected[:, q_width + LANES :] + s.head_terms[1:2, :]
    v.step_in[...] = step_pre
    row = lax.broadcasted_iota(jnp.int32, (length, 1), 0)
    softplus = jnp.maximum(step_pre, 0.0) + jnp.log(1.0 + jnp.exp(-jnp.abs(step_pre)))
    s.steps[...] = jnp.where(row < count, softplus, 0.0)
    save("qr", "kv", "step_in", "bc_padded")
    for j in range(2 * NSTATE // LANES):
        cols = slice(j * LANES, (j + 1) * LANES)
        pre = causal_conv(v.bc_padded, r.conv_shared[:, cols], length, cols)
        s.conv_bc[:, cols] = pre * sigmoid(pre)
    def attend(j):
        zero = jnp.zeros((), BF16)
        keys = [jnp.where(is_key, v.kv[...], zero)]
        keys.append(low(pltpu.roll(wide(keys[0]), HEAD, 1)))
        held = [None, jnp.where(is_key, zero, v.kv[...])]
        held[0] = low(pltpu.roll(wide(held[1]), HEAD, 1))
        for i in range(length // BLOCK):
            rows, upto = slice(i * BLOCK, (i + 1) * BLOCK), (i + 1) * BLOCK
            query_slot = i * BLOCK + lax.broadcasted_iota(jnp.int32, (BLOCK, upto), 0)
            key_slot = lax.broadcasted_iota(jnp.int32, (BLOCK, upto), 1)
            allowed = (key_slot <= query_slot) & (key_slot < count)
            total = jnp.zeros((BLOCK, LANES), F32)
            for e in range(2):
                score = dot_nt(v.qr[rows, j * LANES : (j + 1) * LANES], keys[e][:upto])
                score = jnp.where(allowed, score * HEAD**-0.5, -1e30)
                expo = jnp.exp(score - jnp.max(score, axis=-1, keepdims=True))
                prob = low(expo / jnp.sum(expo, axis=-1, keepdims=True))
                v.probs[2 * j + e, rows, :upto] = prob
                total = total + dot(prob, held[e][:upto])
            v.mix[rows, j * LANES : (j + 1) * LANES] = low(total)

    attend(0)
    gather.relay_z(1)
    gather.relay_x(2)
    for j in range(1, q_tiles):
        attend(j)
    save("probs")
    gather.finish(1)
    v.x_padded[8:, :] = dot(v.normed[...], v.w_in[:, narrow_width : narrow_width + inner])
    save("x_padded")
    channel = t * inner
    for j in range(tiles):
        if j == tiles // 2:
            gather.relay_x(3)
            gather.relay_z(2)
        cols = slice(j * LANES, (j + 1) * LANES)
        taps = r.conv_main[:, pl.ds(pl.multiple_of(channel + j * LANES, LANES), LANES)]
        pre = causal_conv(v.x_padded, taps, length, cols)
        s.conv_x[:, cols] = pre * sigmoid(pre)
    gather.relay_x(4)
    rate = -jnp.exp(s.head_terms[0:1, :])
    causal = triangle()

    def scan_block(i):
        rows = slice(i * BLOCK, (i + 1) * BLOCK)
        step = s.steps[rows, :]
        total = exact_dot(causal.astype(F32), step * rate)
        total_t = total.T
        last = total[BLOCK - 1 : BLOCK, :]
        grown, rest = jnp.exp(total), jnp.exp(last - total)
        b_mat, c_mat = split(s.conv_bc[rows, :NSTATE]), split(s.conv_bc[rows, NSTATE:])
        inner_prod = jnp.where(causal, split_dot_nt(c_mat, b_mat), 0.0)
        v.states[i] = s.state[...]
        crossed = split_dot(c_mat, split(s.state[...]))
        left = first_head(BLOCK)
        for j in range(tiles):
            cols = slice(j * LANES, (j + 1) * LANES)
            stepped = spread(step, j) * s.conv_x[rows, cols]
            mixing = []
            for h in (2 * j, 2 * j + 1):
                gap = jnp.minimum(total[:, h : h + 1] - total_t[h : h + 1, :], 0.0)
                mixing.append(jnp.exp(gap) * inner_prod)
            stacked = jnp.concatenate(
                [jnp.where(left, stepped, 0.0), jnp.where(left, 0.0, stepped)], axis=0
            )
            within = split_dot(split(jnp.concatenate(mixing, axis=1)), split(stacked))
            grown_wide = spread(grown, j)
            v.scanned[rows, cols] = within + crossed[:, cols] * grown_wide
            s.state[:, cols] = s.state[:, cols] * grown_wide[BLOCK - 1 : BLOCK, :] + split_dot_tn(
                b_mat, split(stepped * spread(rest, j))
            )

    for i in range(length // BLOCK):
        scan_block(i)
        if i == 0:
            gather.relay_z(3)
            gather.finish(2)
            v.z_proj[...] = dot(v.normed[...], v.w_in[:, narrow_width + inner :])
            save("w_in", "z_proj")
        if i == 1:
            gather.relay_x(5)
            gather.relay_z(4)
    for j in range(tiles):
        cols = slice(j * LANES, (j + 1) * LANES)
        gate = v.z_proj[:, cols]
        skip = spread(s.head_terms[2:3, :], j)
        result = (v.scanned[:, cols] + skip * s.conv_x[:, cols]) * gate * sigmoid(gate)
        v.mix[:, q_width + j * LANES : q_width + (j + 1) * LANES] = low(result)
    gather.finish(3)
    gather.finish(4)

    pieces = 2
    size = own // pieces

    def mine_at(p):
        return pl.ds(pl.multiple_of(t * own + p * size, size), size)

    def other_at(p):
        return pl.ds(pl.multiple_of((1 - t) * own + p * size, size), size)

    def here(p):
        return slice(p * size, (p + 1) * size)

    mixed = []
    for p in range(pieces):
        s.leaving[0, p] = low(dot_nt(v.mix[other_at(p), :], v.w_mix[...]))
        mixed.append(swap(s.leaving.at[0, p], s.arrived.at[0, p], p))
    save("scanned", "states", "mix", "w_mix")
    for p in range(pieces):
        s.own_part[here(p), :] = dot_nt(v.mix[mine_at(p), :], v.w_mix[...])
    gather.relay_z(5)
    gather.relay_x(6)
    scale, normed_copies = [], []
    for p in range(pieces):
        mixed[p].wait_recv()
        middle = wide(r.hidden[here(p), :]) + s.own_part[here(p), :] + wide(s.arrived[0, p])
        v.resid[here(p), :] = middle
        scale.append(rms_scale(middle))
        s.normed2[mine_at(p), :] = low(middle * scale[p] * r.gain2[...])
        normed_copies.append(
            swap(s.normed2.at[mine_at(p), :], s.normed2.at[mine_at(p), :], pieces + p)
        )
    save("resid")
    gather.relay_z(6)
    gather.relay_x(7)
    gather.finish(5)
    for p in range(pieces):
        s.gate_pre[mine_at(p), :] = dot(s.normed2[mine_at(p), :], s.w_gate[...])
    gather.finish(6)
    for p in range(pieces):
        s.up_pre[mine_at(p), :] = dot(s.normed2[mine_at(p), :], s.w_up[...])

    def activate(rows):
        gate, up = s.gate_pre[rows, :], s.up_pre[rows, :]
        sig = sigmoid(gate)
        silu = gate * sig
        s.hidden_low[rows, :] = low(silu * up)
        s.gate_pre[rows, :] = up * sig * (1.0 + gate * (1.0 - sig))
        s.up_pre[rows, :] = silu

    def normed_grad(rows):
        return dot_nt(s.gate_back[rows, :], s.w_gate[...]) + dot_nt(
            s.up_back[rows, :], s.w_up[...]
        )

    span = 256

    def weight_grads(part, left, right, first=0):
        _, _, _, rows, width = part.shape
        per = span // (2 * rows)

        def one(i, carry):
            cols = pl.ds(pl.multiple_of(i * span, span), span)
            value = low(dot_tn(left[:, cols], right[:, first : first + width]))
            value = value.reshape(per, 2, rows, width)
            for k in range(per):
                at = i * per + k
                part[at // halves, lax.rem(at, halves)] = value[k]
            return carry

        lax.fori_loop(0, model // span, one, 0)

    def rows_back(rows):
        grad = dot(s.top_grad[rows, :], s.w_down[...])
        s.gate_back[rows, :] = low(grad * s.gate_pre[rows, :])
        s.up_back[rows, :] = low(grad * s.up_pre[rows, :])

    for p in range(pieces):
        activate(mine_at(p))
    gather.relay_z(7)
    grad_copy.wait_recv()
    sums = []
    for p in range(pieces):
        rows = other_at(p)
        normed_copies[p].wait_recv()
        s.gate_pre[rows, :] = dot(s.normed2[rows, :], s.w_gate[...])
        s.up_pre[rows, :] = dot(s.normed2[rows, :], s.w_up[...])
        activate(rows)
        if p == 0:
            gather.finish(7)
        rows_back(rows)
        s.leaving[1, p] = low(normed_grad(rows))
        sums.append(swap(s.leaving.at[1, p], s.arrived.at[1, p], 2 * pieces + p))
    weight_grads(s.p_down, s.top_grad, s.hidden_low)
    scatter.send(0)
    weight_grads(s.p_down2, s.top_grad, s.hidden_low, ffn // 2)
    scatter.send(3)
    rows_back(mine_at(0))
    scatter.core_stage(0)
    scatter.send_x(0)
    for p in range(pieces):
        if p > 0:
            rows_back(mine_at(p))
        s.own_part[here(p), :] = normed_grad(mine_at(p))
        if p == 0:
            scatter.core_stage(3)
            scatter.send_x(3)
    total = jnp.zeros((1, model), F32)
    mix_copies = []
    for p in range(pieces):
        sums[p].wait_recv()
        middle = v.resid[here(p), :]
        grad = s.own_part[here(p), :] + wide(s.arrived[1, p])
        total = total + jnp.sum(grad * middle * scale[p], axis=0, keepdims=True)
        weighted = grad * r.gain2[...]
        result = (
            wide(s.top_grad[mine_at(p), :])
            + scale[p] * weighted
            - middle
            * (scale[p] * scale[p] * scale[p])
            * jnp.mean(weighted * middle, axis=-1, keepdims=True)
        )
        v.resid_grad[here(p), :] = result
        v.mix_grad[mine_at(p), :] = low(result)
        mix_copies.append(
            swap(v.mix_grad.at[mine_at(p), :], v.mix_grad.at[mine_at(p), :], 3 * pieces + p)
        )
    out.gain2_part[...] = total
    save("resid_grad")
    weight_grads(s.p_gate, s.normed2, s.gate_back)
    scatter.send(1)
    weight_grads(s.p_up, s.normed2, s.up_back)
    scatter.send(2)

    def save_pair(name, part):
        for k in range(halves):
            move.start((name, k), part.at[:, k, c], getattr(out, name).at[k])

    scatter.core_stage(1)
    save_pair("gate_pair", s.p_gate)
    v.ffn_part[...] = low(dot_nt(s.hidden_low[...], s.w_down[...]))
    save("ffn_part")
    scatter.core_stage(2)
    save_pair("up_pair", s.p_up)
    scatter.x_stage(0)
    move.start("down", s.d_chip, out.down_chip.at[:, :, pl.ds(0, ffn // 2)])
    scatter.x_stage(3)
    move.start("down2", s.d_chip2, out.down_chip.at[:, :, pl.ds(ffn // 2, ffn // 2)])
    for copy in mix_copies:
        copy.wait_recv()
    save("mix_grad")
    for copy in sent:
        copy.wait_send()
    gather.drain()
    scatter.drain()
    move.drain()


def forward(length_of, hidden, out_grad, gains, weights, shared, kernels, head_terms, tables):
    groups, halves = lax.axis_size("grp"), lax.axis_size("fsdp") // 2
    w_query, w_x, w_gate = weights[0], weights[4], weights[9]
    own, model = hidden.shape
    length, inner, q_width, ffn = 2 * own, w_x.shape[1], w_query.shape[1], w_gate.shape[1]
    shard = w_x.shape[0]
    narrow_width = q_width + 2 * LANES
    heads = q_width // HEAD
    rows = model // (2 * groups * halves)
    inside = pl.BlockSpec(memory_space=pltpu.VMEM)
    anywhere = pl.BlockSpec(memory_space=pl.ANY)
    shape = jax.ShapeDtypeStruct
    saved = [
        ((model, narrow_width + 2 * inner), BF16),
        ((model, q_width + inner), BF16),
        ((length, model), BF16),
        ((length, q_width + inner), BF16),
        ((length, q_width), BF16),
        ((length, LANES), BF16),
        ((heads, length, length), BF16),
        ((length + 8, inner), F32),
        ((length, inner), F32),
        ((length + 8, 2 * NSTATE), F32),
        ((length, LANES), F32),
        ((length, inner), F32),
        ((length // BLOCK, NSTATE, inner), F32),
        ((length, model), BF16),
        ((own, model), F32),
        ((own, model), F32),
        ((length, model), BF16),
    ]
    sums = [((groups, rows, ffn), BF16)] + [((halves, groups, rows, ffn), BF16)] * 2
    dma, vmem = pltpu.SemaphoreType.DMA, pltpu.VMEM
    grad_widths = (ffn // 2, ffn // 2, ffn, ffn)
    moves = 6 + len(saved) + 2 * halves
    return pl.pallas_call(
        partial(forward_body, groups, halves),
        out_shape=[shape(*a) for a in saved + sums]
        + [shape((1, model), F32)],
        in_specs=[pl.BlockSpec(memory_space=pltpu.SMEM)]
        + [inside] * 7
        + [anywhere] * 11
        + [inside] * 5,
        out_specs=[anywhere] * (len(saved) + 3) + [inside],
        scratch_shapes=[vmem(*a) for a in saved]
        + [
            vmem((model, 2 * NSTATE), BF16),
            vmem((own, model), BF16),
            vmem((length, LANES), F32),
            vmem((length, LANES), F32),
            vmem((length, model), BF16),
            vmem((shard, narrow_width), BF16),
            vmem((length, inner), F32),
            vmem((length, 2 * NSTATE), F32),
            vmem((length, LANES), F32),
            vmem((NSTATE, inner), F32),
            vmem((8, LANES), F32),
            vmem((model, ffn), BF16),
            vmem((model, ffn), BF16),
            vmem((model, ffn), BF16),
            vmem((length, model), BF16),
            vmem((2, 2, own // 2, model), BF16),
            vmem((2, 2, own // 2, model), BF16),
            vmem((own, model), F32),
            vmem((length, ffn), F32),
            vmem((length, ffn), F32),
            vmem((length, ffn), BF16),
            vmem((length, ffn), BF16),
            vmem((length, ffn), BF16),
        ]
        + [vmem((groups, halves, 2, rows, w), BF16) for w in grad_widths]
        + [vmem((groups, halves, rows, w), BF16) for w in grad_widths]
        + [
            vmem((max(halves - 1, 1), groups, rows, ffn // 2), BF16),
            vmem((max(halves - 1, 1), groups, rows, ffn // 2), BF16),
            vmem((groups, rows, ffn // 2), BF16),
            vmem((groups, rows, ffn // 2), BF16),
            dma((2, 10)),
            dma((moves,)),
        ]
        + gather_sems(8, halves)
        + scatter_sems(4, groups, halves),
        compiler_params=pltpu.CompilerParams(
            collective_id=0, has_side_effects=True, vmem_limit_bytes=VMEM_LIMIT
        ),
        name="forward",
    )(length_of, hidden, *gains, *weights, shared, out_grad, *tables, *kernels, *head_terms)


UNITS = 8


class BackwardIn(NamedTuple):
    length_ref: Any
    gain: Any
    gain2_part: Any
    conv_main: Any
    conv_shared: Any
    decay_log: Any
    step_bias: Any
    skip_gain: Any
    hidden: Any
    cosine: Any
    sine: Any
    w_shared: Any


class BackwardOut(NamedTuple):
    output: Any
    grad_in: Any
    gain: Any
    query: Any
    key: Any
    value: Any
    attn: Any
    z: Any
    x: Any
    step: Any
    shared: Any
    conv: Any
    conv_shared: Any
    decay: Any
    bias: Any
    skip: Any
    mamba: Any
    gain2: Any
    gate: Any
    up: Any
    down: Any


class BackwardScratch(NamedTuple):
    shared: Any
    hidden: Any
    cosine: Any
    sine: Any
    arrived: Any
    leaving: Any
    grad_y: Any
    grad_attn: Any
    conv_x: Any
    conv_bc: Any
    grad_x: Any
    grad_bc: Any
    steps: Any
    back: Any
    bc_back: Any
    grown_y: Any
    faded_x: Any
    state_back: Any
    key_sums: Any
    rows_sum: Any
    shared_y: Any
    shared_all: Any
    vector: Any
    vec_core: Any
    vec_x: Any
    vec_y: Any
    vec_z: Any
    head_terms: Any
    y_sems: Any
    small_sems: Any
    small_x_sems: Any
    small_z_sems: Any
    move_sems: Any


def backward_body(groups, halves, *refs):
    counts = [len(BackwardIn._fields), len(Kept._fields) - 1, len(BackwardOut._fields), 17]
    ends = np.cumsum(counts).tolist()
    r = BackwardIn(*refs[: ends[0]])
    h = Kept(*refs[ends[0] : ends[1]], None)
    out_hbm = BackwardOut(*refs[ends[1] : ends[2]])
    v = Kept(*refs[ends[2] : ends[3] - 1], *[None] * (counts[1] - 15))
    ffn_own = refs[ends[3] - 1]
    out = BackwardOut(*refs[ends[3] : ends[3] + counts[2]])
    rest = refs[ends[3] + counts[2] :]
    parts, from_core, rest = rest[:5], rest[5:10], rest[10:]
    from_x, chip_sums, rest = rest[:7], rest[7:14], rest[14:]
    from_z, relays, rest = rest[:8], rest[8:16], rest[16:]
    own_pairs, own_chip, rest = rest[:2], rest[2], rest[3:]
    s = BackwardScratch(*rest[:33])
    units = [
        dict(pair_sum=h.gate_pair, own_pair=own_pairs[0], from_x=from_x[0], chip_sum=chip_sums[0]),
        dict(pair_sum=h.up_pair, own_pair=own_pairs[1], from_x=from_x[1], chip_sum=chip_sums[1]),
        dict(chip_sum=own_chip),
    ] + [
        dict(part=parts[i], from_core=from_core[i], from_x=from_x[2 + i], chip_sum=chip_sums[2 + i])
        for i in range(5)
    ]
    for unit, ref, relay in zip(units, from_z, relays):
        unit["from_z"], unit["relay"] = ref, relay
    scatter = Scatter(units, groups, halves, rest[33:])
    move = Mover(s.move_sems)
    g, hi, c, t = place()
    own, model = r.hidden.shape
    length = 2 * own
    inner, q_width = out.x.shape[1], out.query.shape[1]
    kv_width, step_width = out.key.shape[1], out.step.shape[0]
    tiles, q_tiles = inner // LANES, q_width // LANES
    narrow_width = q_width + 2 * LANES
    other_y = (g, hi * 2 + c, 1 - t)
    devices = scatter.devices + [other_y]
    mine = pl.ds(pl.multiple_of(t * own, own), own)
    other = pl.ds(pl.multiple_of((1 - t) * own, own), own)
    greet(devices)

    def load(*names):
        for name in names:
            move.start(name, getattr(h, name), getattr(v, name))

    move.start("down_chip", h.down_chip, own_chip)
    load("mix_grad", "mix", "w_mix", "bc_padded", "step_in", "x_padded", "z_proj", "scanned")
    move.start("cosine", r.cosine, s.cosine)
    move.start("sine", r.sine, s.sine)
    load("normed", "qr", "kv", "probs", "states", "w_in")
    move.start("hidden", r.hidden, s.hidden)
    move.start("shared", r.w_shared, s.shared)
    move.start("ffn_own", h.ffn_part.at[mine, :], ffn_own)
    load("resid", "resid_grad")
    pick_heads(s.head_terms, (r.decay_log, r.step_bias, r.skip_gain), t)
    head_terms = s.head_terms
    greeted(devices)
    scatter.send_x(0)
    scatter.send_x(1)
    move.wait("down_chip")
    scatter.send_z(2)
    ffn_copy = scatter.start(
        remote(
            h.ffn_part.at[other, :], s.arrived.at[0], s.y_sems.at[0, 0], s.y_sems.at[1, 0], other_y
        )
    )
    count = r.length_ref[0]
    span = 256

    def give(*names):
        for name in names:
            move.start((name,), getattr(out, name), getattr(out_hbm, name))


    def weight_grads(part, left, right, cols, width):
        _, _, _, rows, _ = part.shape
        per = span // (2 * rows)

        def one(i, carry):
            at = pl.ds(pl.multiple_of(i * span, span), span)
            value = low(dot_tn(left[:, at], right[:, cols])).reshape(per, 2, rows, width)
            for k in range(per):
                at = i * per + k
                part[at // halves, lax.rem(at, halves)] = value[k]
            return carry

        lax.fori_loop(0, model // span, one, 0)

    move.wait("mix_grad", "mix")
    weight_grads(parts[0], v.mix_grad, v.mix, slice(None), q_width + inner)
    scatter.send(3)
    move.wait("w_mix")
    grad = dot(v.mix_grad[...], v.w_mix[...])
    s.grad_attn[...] = low(grad[:, :q_width])
    s.grad_y[...] = grad[:, q_width:]
    move.wait("bc_padded", "step_in", "x_padded")
    row = lax.broadcasted_iota(jnp.int32, (length, 1), 0)
    step_pre = v.step_in[...]
    softplus = jnp.maximum(step_pre, 0.0) + jnp.log(1.0 + jnp.exp(-jnp.abs(step_pre)))
    s.steps[...] = jnp.where(row < count, softplus, 0.0)
    channel = t * inner

    def taps_of(j):
        return r.conv_main[:, pl.ds(pl.multiple_of(channel + j * LANES, LANES), LANES)]

    for j in range(2 * NSTATE // LANES):
        cols = slice(j * LANES, (j + 1) * LANES)
        pre = causal_conv(v.bc_padded, r.conv_shared[:, cols], length, cols)
        s.conv_bc[:, cols] = pre * sigmoid(pre)
    scatter.core_stage(3)
    scatter.send_x(3)
    move.wait("z_proj", "scanned", "normed")
    skip_sum = jnp.zeros((1, LANES), F32)
    for j in range(tiles):
        cols = slice(j * LANES, (j + 1) * LANES)
        pre = causal_conv(v.x_padded, taps_of(j), length, cols)
        conv = pre * sigmoid(pre)
        s.conv_x[:, cols] = conv
        gate = v.z_proj[:, cols]
        sig = sigmoid(gate)
        grad = s.grad_y[:, cols]
        value = v.scanned[:, cols] + spread(head_terms[2:3, :], j) * conv
        at = narrow_width + inner + j * LANES
        s.back[:, at : at + LANES] = low(grad * value * sig * (1.0 + gate * (1.0 - sig)))
        grad = grad * gate * sig
        s.grad_y[:, cols] = grad
        s.rows_sum[j : j + 1, :] = column_sum(grad * conv)
    for j in range(tiles):
        skip_sum = skip_sum + head_sum(s.rows_sum[0:8, :], j)[j : j + 1, :]
    weight_grads(parts[1], v.normed, s.back, slice(narrow_width + inner, None), inner)
    scatter.send(4)
    move.wait("qr", "kv", "probs", "cosine", "sine")

    is_key = first_head(length)
    zero = jnp.zeros((), BF16)
    s.key_sums[...] = jnp.zeros_like(s.key_sums)

    def attend(j):
        tile = slice(j * LANES, (j + 1) * LANES)
        keys = [jnp.where(is_key, v.kv[...], zero)]
        keys.append(low(pltpu.roll(wide(keys[0]), HEAD, 1)))
        held = [None, jnp.where(is_key, zero, v.kv[...])]
        held[0] = low(pltpu.roll(wide(held[1]), HEAD, 1))
        for i in range(length // BLOCK):
            rows, upto = slice(i * BLOCK, (i + 1) * BLOCK), (i + 1) * BLOCK
            left = first_head(BLOCK)
            query, grad = v.qr[rows, tile], s.grad_attn[rows, tile]
            total = jnp.zeros((BLOCK, LANES), F32)
            for e in range(2):
                prob_low = v.probs[2 * j + e, rows, :upto]
                prob = wide(prob_low)
                prob_grad = dot_nt(grad, held[e][:upto])
                inside = jnp.sum(prob * prob_grad, axis=-1, keepdims=True)
                score_grad = low(prob * (prob_grad - inside))
                total = total + dot(score_grad, keys[e][:upto])
                side = left if e == 0 else jnp.logical_not(left)
                s.key_sums[0, :upto, :] += dot_tn(score_grad, jnp.where(side, query, zero))
                s.key_sums[1, :upto, :] += dot_tn(prob_low, jnp.where(side, grad, zero))
            total = total * HEAD**-0.5
            turned = total * s.cosine[rows, :] - half_swap(total) * s.sine[rows, :]
            s.back[rows, tile] = low(turned)

    scatter.relay(2)
    for j in range(q_tiles):
        attend(j)
        if j == 0:
            scatter.core_stage(4)
    key_grad = s.key_sums[0] + pltpu.roll(s.key_sums[0], HEAD, 1)
    key_grad = key_grad * HEAD**-0.5
    value_grad = s.key_sums[1] + pltpu.roll(s.key_sums[1], HEAD, 1)
    key_grad = key_grad * s.cosine[...] - half_swap(key_grad) * s.sine[...]
    s.back[:, q_width : q_width + LANES] = low(jnp.where(is_key, key_grad, value_grad))
    scatter.x_stage(0)
    scatter.send_z(0)
    move.wait("states")

    rate = -jnp.exp(head_terms[0:1, :])
    s.state_back[...] = jnp.zeros_like(s.state_back)
    upper = triangle(False)
    nblocks = length // BLOCK

    def scan_block(n, carry):
        rate_sum, bias_sum = carry
        i = nblocks - 1 - n
        rows = pl.ds(pl.multiple_of(i * BLOCK, BLOCK), BLOCK)
        step = s.steps[rows, :]
        total = exact_dot(triangle().astype(F32), step * rate)
        total_t = total.T
        last = total[BLOCK - 1 : BLOCK, :]
        grown, rest = jnp.exp(total), jnp.exp(last - total)
        b_mat, c_mat = split(s.conv_bc[rows, :NSTATE]), split(s.conv_bc[rows, NSTATE:])
        b_low, c_low = b_mat[0], c_mat[0]
        inner_t = jnp.where(upper, split_dot_nt(b_mat, c_mat), 0.0)
        state_mat = split(s.state_back[...])
        state_low = state_mat[0]
        crossed = split_dot(b_mat, state_mat)
        after = v.states[jnp.minimum(i + 1, nblocks - 1)] * s.state_back[...]
        left = first_head(BLOCK)
        inner_grad = jnp.zeros((BLOCK, BLOCK), F32)
        total_grad = jnp.zeros((BLOCK, LANES), F32)
        step_grad = jnp.zeros((BLOCK, LANES), F32)
        last_grad = jnp.zeros((8, LANES), F32)
        pulled = []
        for j in range(tiles):
            cols = slice(j * LANES, (j + 1) * LANES)
            conv, grad = s.conv_x[rows, cols], s.grad_y[rows, cols]
            step_wide, grown_wide, rest_wide = spread(step, j), spread(grown, j), spread(rest, j)
            stepped = step_wide * conv
            grad_low = low(grad)
            mixing = []
            for e, head in enumerate((2 * j, 2 * j + 1)):
                gap = jnp.minimum(total_t[head : head + 1, :] - total[:, head : head + 1], 0.0)
                decay = jnp.exp(gap)
                mixing.append(decay * inner_t)
                side = left if e == 0 else jnp.logical_not(left)
                inner_grad = inner_grad + decay * dot_nt(
                    low(jnp.where(side, stepped, 0.0)), grad_low
                )
            stacked = jnp.concatenate(
                [jnp.where(left, grad, 0.0), jnp.where(left, 0.0, grad)], axis=0
            )
            unstepped = split_dot(split(jnp.concatenate(mixing, axis=1)), split(stacked))
            unstepped = unstepped + rest_wide * crossed[:, cols]
            conv_grad = step_wide * unstepped
            total_grad = total_grad + head_sum(
                grad * v.scanned[rows, cols] - conv * conv_grad, j
            )
            step_grad = step_grad + head_sum(conv * unstepped, j)
            last_grad = last_grad + head_sum(
                jnp.broadcast_to(column_sum(after[:, cols]), (8, LANES)), j
            )
            s.grad_x[rows, cols] = conv_grad + spread(head_terms[2:3, :], j) * grad
            grown_grad = split(grown_wide * grad)
            s.grown_y[:, cols] = grown_grad[0]
            pulled.append(split_dot_tn(c_mat, grown_grad))
            s.faded_x[:, cols] = low(stepped * rest_wide)
        inner_low = low(jnp.where(upper, inner_grad, 0.0))
        s.grad_bc[rows, :NSTATE] = dot_nt(s.faded_x[...], state_low) + dot(inner_low, c_low)
        s.grad_bc[rows, NSTATE:] = dot_nt(s.grown_y[...], low(v.states[i])) + dot_tn(
            inner_low, b_low
        )
        for j in range(tiles):
            cols = slice(j * LANES, (j + 1) * LANES)
            fade = spread(grown[BLOCK - 1 : BLOCK, :], j)
            s.state_back[:, cols] = s.state_back[:, cols] * fade + pulled[j]
        slot = lax.broadcasted_iota(jnp.int32, (BLOCK, 1), 0)
        total_grad = total_grad + jnp.where(slot == BLOCK - 1, last_grad[0:1, :], 0.0)
        decay_grad = exact_dot(upper.astype(F32), total_grad)
        step_grad = step_grad + rate * decay_grad
        step_grad = jnp.where(i * BLOCK + slot < count, step_grad, 0.0)
        step_grad = step_grad * sigmoid(v.step_in[rows, :])
        s.back[rows, q_width + LANES : narrow_width] = low(step_grad)
        return rate_sum + column_sum(decay_grad * step), bias_sum + column_sum(step_grad)

    empty = jnp.zeros((1, LANES), F32)
    rate_sum, bias_sum = lax.fori_loop(0, nblocks, scan_block, (empty, empty))
    scatter.relay(0)

    s.vector[...] = jnp.zeros_like(s.vector)

    def place_row(at, value):
        s.vector[at : at + 1, :] = value

    def place_halves(at, gap, value):
        place_row(at, jnp.where(t == 0, value, 0.0))
        place_row(at + gap, jnp.where(t == 0, 0.0, value))

    place_halves(72, 1, rate_sum * rate)
    place_halves(74, 1, bias_sum)
    place_halves(76, 1, skip_sum)
    for j in range(model // LANES):
        place_row(8 + j, r.gain2_part[:, j * LANES : (j + 1) * LANES])
    s.grad_bc[length:, :] = jnp.zeros((8, 2 * NSTATE), F32)
    s.grad_x[length:, :] = jnp.zeros((8, inner), F32)

    def conv_back(padded, grads, taps, cols, store):
        pre = causal_conv(padded, taps, length, cols)
        sig = sigmoid(pre)
        grads[:length, cols] = grads[:length, cols] * sig * (1.0 + pre * (1.0 - sig))
        for i in range(4):
            store(i, column_sum(grads[:length, cols] * padded[5 + i : 5 + i + length, cols]))
        total = taps[3:4, :] * grads[:length, cols]
        for i in range(3):
            total = total + taps[i : i + 1, :] * grads[3 - i : 3 - i + length, cols]
        return low(total)

    for j in range(2 * NSTATE // LANES):
        cols = slice(j * LANES, (j + 1) * LANES)
        s.bc_back[:, cols] = conv_back(
            v.bc_padded,
            s.grad_bc,
            r.conv_shared[:, cols],
            cols,
            lambda i, value, j=j: place_row(16 + 2 * i + j, value),
        )
    weight_grads(parts[2], v.normed, s.bc_back, slice(None), 2 * NSTATE)
    scatter.send(5)
    for j in range(tiles):
        cols = slice(j * LANES, (j + 1) * LANES)
        at = narrow_width + j * LANES
        s.back[:, at : at + LANES] = conv_back(
            v.x_padded,
            s.grad_x,
            taps_of(j),
            cols,
            lambda i, value, j=j: place_halves(24 + 2 * tiles * i + j, tiles, value),
        )
    scatter.core_stage(5)
    scatter.send_x(5)
    scatter.send_x(4)
    scatter.x_stage(1)
    scatter.send_z(1)
    move.wait("w_in", "shared")
    s.leaving[...] = low(
        dot_nt(s.back[other, :], v.w_in[...]) + dot_nt(s.bc_back[other, :], s.shared[...])
    )
    sum_copy = scatter.start(
        remote(s.leaving, s.arrived.at[1], s.y_sems.at[0, 1], s.y_sems.at[1, 1], other_y)
    )
    weight_grads(parts[4], v.normed, s.back, slice(narrow_width, narrow_width + inner), inner)
    scatter.send(7)
    weight_grads(parts[3], v.normed, s.back, slice(0, narrow_width), narrow_width)
    scatter.send(6)
    own_grad = dot_nt(s.back[mine, :], v.w_in[...]) + dot_nt(s.bc_back[mine, :], s.shared[...])
    scatter.x_stage(3)
    scatter.send_z(3)
    scatter.relay(1)
    sum_copy.wait_recv()
    move.wait("hidden")
    values = wide(s.hidden[...])
    scale = rms_scale(values)
    grad = own_grad + wide(s.arrived[1])
    gain_row = column_sum(grad * values * scale)
    for j in range(model // LANES):
        place_row(j, gain_row[:, j * LANES : (j + 1) * LANES])
    s.vec_core[c] = s.vector[...]
    vec_copy = scatter.start(
        remote(
            s.vector,
            s.vec_core.at[c],
            s.small_sems.at[0, 0],
            s.small_sems.at[1, 0],
            scatter.other_core,
        )
    )
    move.wait("resid", "resid_grad", "ffn_own")
    weighted = grad * r.gain[...]
    out.grad_in[...] = low(
        v.resid_grad[...]
        + scale * weighted
        - values * (scale * scale * scale) * jnp.mean(weighted * values, axis=-1, keepdims=True)
    )
    vec_copy.wait_recv()
    s.vec_x[hi] = s.vec_core[0] + s.vec_core[1]
    vec_copies = [
        scatter.start(
            remote(
                s.vec_x.at[hi],
                s.vec_x.at[hi],
                s.small_x_sems.at[0, 0, k],
                s.small_x_sems.at[1, 0, k],
                scatter.across[k - 1],
            )
        )
        for k in range(1, halves)
    ]
    scatter.core_stage(7)
    scatter.send_x(7)
    scatter.x_stage(5)
    scatter.send_z(5)
    scatter.core_stage(6)
    scatter.send_x(6)
    ffn_copy.wait_recv()
    slot = t * own + lax.broadcasted_iota(jnp.int32, (own, 1), 0)
    total = v.resid[...] + wide(ffn_own[...]) + wide(s.arrived[0])
    out.output[...] = low(jnp.where(slot < count, total, 0.0))
    give("output", "grad_in")
    scatter.relay(3)
    out.down[...] = scatter.z_stage(2)
    give("down")
    scatter.relay(5)
    out.gate[...] = scatter.z_stage(0)
    give("gate")
    scatter.x_stage(4)
    scatter.send_z(4)
    s.shared_y[t] = scatter.z_stage(5)
    shared_copy = scatter.start(
        remote(
            s.shared_y.at[t],
            s.shared_y.at[t],
            s.small_sems.at[0, 2],
            s.small_sems.at[1, 2],
            other_y,
        )
    )
    shared_copy.wait_recv()
    s.shared_all[g, hi, c] = low(s.shared_y[0] + s.shared_y[1])
    shared_copies = [
        scatter.start(
            remote(
                s.shared_all.at[g, hi, c],
                s.shared_all.at[g, hi, c],
                s.small_z_sems.at[0, 1, j],
                s.small_z_sems.at[1, 1, j],
                scatter.along[j - 1],
            )
        )
        for j in range(1, groups)
    ]
    for copy in vec_copies:
        copy.wait_recv()
    total = s.vec_x[0]
    for k in range(1, halves):
        total = total + s.vec_x[k]
    s.vec_y[t] = total
    vec_copy = scatter.start(
        remote(
            s.vec_y.at[t], s.vec_y.at[t], s.small_sems.at[0, 1], s.small_sems.at[1, 1], other_y
        )
    )
    out.up[...] = scatter.z_stage(1)
    give("up")
    vec_copy.wait_recv()
    s.vec_z[g] = s.vec_y[0] + s.vec_y[1]
    vec_copies = [
        scatter.start(
            remote(
                s.vec_z.at[g],
                s.vec_z.at[g],
                s.small_z_sems.at[0, 0, j],
                s.small_z_sems.at[1, 0, j],
                scatter.along[j - 1],
            )
        )
        for j in range(1, groups)
    ]
    total = scatter.z_stage(3)
    out.attn[...] = total[:, :q_width]
    out.mamba[...] = total[:, q_width:]
    give("attn", "mamba")
    scatter.relay(4)
    scatter.x_stage(7)
    scatter.send_z(7)
    for copy in shared_copies:
        copy.wait_recv()
    shared_copies = [
        scatter.start(
            remote(
                s.shared_all.at[:, hi, c],
                s.shared_all.at[:, hi, c],
                s.small_x_sems.at[0, 1, k],
                s.small_x_sems.at[1, 1, k],
                scatter.across[k - 1],
            )
        )
        for k in range(1, halves)
    ]
    for copy in vec_copies:
        copy.wait_recv()
    total = s.vec_z[0]
    for j in range(1, groups):
        total = total + s.vec_z[j]
    out.gain[...] = total[0:8, :]
    out.gain2[...] = total[8:16, :]
    for i in range(4):
        for j in range(2 * NSTATE // LANES):
            at = 16 + 2 * i + j
            out.conv_shared[i : i + 1, j * LANES : (j + 1) * LANES] = total[at : at + 1, :]
        for j in range(2 * tiles):
            at = 24 + 2 * tiles * i + j
            out.conv[i : i + 1, j * LANES : (j + 1) * LANES] = total[at : at + 1, :]
    for ref, at in ((out.decay, 72), (out.bias, 74), (out.skip, 76)):
        ref[...] = jnp.concatenate(
            [total[at : at + 1, :step_width], total[at + 1 : at + 2, :step_width]], axis=1
        )
    give("gain", "gain2", "conv", "conv_shared", "decay", "bias", "skip")
    scatter.x_stage(6)
    scatter.send_z(6)
    scatter.relay(7)
    out.z[...] = scatter.z_stage(4)
    give("z")
    for copy in shared_copies:
        copy.wait_recv()
    shared_copy = scatter.start(
        remote(
            s.shared_all.at[:, :, c],
            s.shared_all.at[:, :, c],
            s.small_sems.at[0, 3],
            s.small_sems.at[1, 3],
            scatter.other_core,
        )
    )
    scatter.relay(6)
    out.x[...] = scatter.z_stage(7)
    give("x")
    shared_copy.wait_recv()

    def widen(i, carry):
        block = s.shared_all[i // (2 * halves), lax.rem(i // 2, halves), lax.rem(i, 2)]
        out.shared[i] = wide(block)
        return carry

    lax.fori_loop(0, groups * halves * 2, widen, 0)
    give("shared")
    total = scatter.z_stage(6)
    out.query[...] = total[:, :q_width]
    out.key[...] = total[:, q_width : q_width + kv_width]
    out.value[...] = total[:, q_width + kv_width : q_width + 2 * kv_width]
    out.step[...] = total[:, q_width + LANES :].T[:step_width, :]
    give("query", "key", "value", "step")
    scatter.drain()
    move.drain()


def backward(
    length_of, hidden, gain, gain2_part, saved, w_shared, kernels, head_terms, tables, widths
):
    groups, halves = lax.axis_size("grp"), lax.axis_size("fsdp") // 2
    q_width, kv_width, step_width = widths
    own, model = hidden.shape
    length = 2 * own
    narrow_width = q_width + 2 * LANES
    inner = (saved[0].shape[1] - narrow_width) // 2
    rows = model // (2 * groups * halves)
    ffn = saved[-1].shape[-1]
    inside = pl.BlockSpec(memory_space=pltpu.VMEM)
    anywhere = pl.BlockSpec(memory_space=pl.ANY)
    shape, vmem, dma = jax.ShapeDtypeStruct, pltpu.VMEM, pltpu.SemaphoreType.DMA
    outs = [
        shape((own, model), BF16),
        shape((own, model), BF16),
        shape((model // LANES, LANES), F32),
        shape((rows, q_width), F32),
        shape((rows, kv_width), F32),
        shape((rows, kv_width), F32),
        shape((rows, q_width), F32),
        shape((rows, inner), F32),
        shape((rows, inner), F32),
        shape((step_width, rows), F32),
        shape((2 * groups * halves, rows, 2 * NSTATE), F32),
        shape((4, 2 * inner), F32),
        shape((4, 2 * NSTATE), F32),
        shape((1, 2 * step_width), F32),
        shape((1, 2 * step_width), F32),
        shape((1, 2 * step_width), F32),
        shape((rows, inner), F32),
        shape((model // LANES, LANES), F32),
        shape((rows, ffn), F32),
        shape((rows, ffn), F32),
        shape((rows, ffn), F32),
    ]
    part_widths = [q_width + inner, inner, 2 * NSTATE, narrow_width, inner]
    x_widths = [ffn, ffn] + part_widths
    z_widths = [ffn] * 3 + part_widths
    vector = (80, LANES)
    others = max(halves - 1, 1)
    scratch = (
        [vmem(a.shape, a.dtype) for a in saved[:16]]
        + [vmem((own, model), BF16)]
        + [vmem(a.shape, a.dtype) for a in outs]
        + [vmem((groups, halves, 2, rows, w), BF16) for w in part_widths]
        + [vmem((groups, halves, rows, w), BF16) for w in part_widths]
        + [vmem((others, groups, rows, w), BF16) for w in x_widths]
        + [vmem((groups, rows, w), BF16) for w in x_widths]
        + [vmem((groups - 1, rows, w), BF16) for w in z_widths]
        + [vmem((rows, w), BF16) for w in z_widths]
        + [vmem((groups, rows, ffn), BF16)] * 3
        + [
            vmem((model, 2 * NSTATE), BF16),
            vmem((own, model), BF16),
            vmem((length, LANES), F32),
            vmem((length, LANES), F32),
            vmem((2, own, model), BF16),
            vmem((own, model), BF16),
            vmem((length, inner), F32),
            vmem((length, q_width), BF16),
            vmem((length, inner), F32),
            vmem((length, 2 * NSTATE), F32),
            vmem((length + 8, inner), F32),
            vmem((length + 8, 2 * NSTATE), F32),
            vmem((length, LANES), F32),
            vmem((length, narrow_width + 2 * inner), BF16),
            vmem((length, 2 * NSTATE), BF16),
            vmem((BLOCK, inner), BF16),
            vmem((BLOCK, inner), BF16),
            vmem((NSTATE, inner), F32),
            vmem((2, length, LANES), F32),
            vmem((8, LANES), F32),
            vmem((2, rows, 2 * NSTATE), F32),
            vmem((groups, halves, 2, rows, 2 * NSTATE), BF16),
            vmem(vector, F32),
            vmem((2,) + vector, F32),
            vmem((halves,) + vector, F32),
            vmem((2,) + vector, F32),
            vmem((groups,) + vector, F32),
            vmem((8, LANES), F32),
            dma((2, 2)),
            dma((2, 4)),
            dma((2, 2, halves)),
            dma((2, 2, groups)),
            dma((23 + len(outs),)),
        ]
        + scatter_sems(UNITS, groups, halves)
    )
    return pl.pallas_call(
        partial(backward_body, groups, halves),
        out_shape=outs,
        in_specs=[pl.BlockSpec(memory_space=pltpu.SMEM)]
        + [inside] * 7
        + [anywhere] * (4 + len(saved)),
        out_specs=[anywhere] * len(outs),
        scratch_shapes=scratch,
        compiler_params=pltpu.CompilerParams(
            collective_id=1, has_side_effects=True, vmem_limit_bytes=VMEM_LIMIT
        ),
        name="backward",
    )(length_of, gain, gain2_part, *kernels, *head_terms, hidden, *tables, w_shared, *saved)


def emit_body(*refs):
    count = len(refs) // 3
    sources, targets, held = refs[:count], refs[count : 2 * count], refs[2 * count : 3 * count]
    sems = refs[3 * count]
    arriving = [
        pltpu.make_async_copy(source, at, sems.at[0, i])
        for i, (source, at) in enumerate(zip(sources, held))
    ]
    leaving = [
        pltpu.make_async_copy(at, target, sems.at[1, i])
        for i, (at, target) in enumerate(zip(held, targets))
    ]
    for copy in arriving:
        copy.start()
    for arrived, copy in zip(arriving, leaving):
        arrived.wait()
        copy.start()
    for copy in leaving:
        copy.wait()


def emit(arrays):
    anywhere = pl.BlockSpec(memory_space=pl.ANY)
    return pl.pallas_call(
        emit_body,
        out_shape=[jax.ShapeDtypeStruct(a.shape, a.dtype) for a in arrays],
        in_specs=[anywhere] * len(arrays),
        out_specs=[anywhere] * len(arrays),
        scratch_shapes=[pltpu.VMEM(a.shape, a.dtype) for a in arrays]
        + [pltpu.SemaphoreType.DMA((2, len(arrays)))],
        compiler_params=pltpu.CompilerParams(vmem_limit_bytes=VMEM_LIMIT),
        name="emit",
    )(*arrays)


def local(
    hidden_in,
    lengths,
    norm1_gain,
    w_query,
    key_weight,
    value_weight,
    w_attn_out,
    w_mamba_z,
    w_mamba_x,
    w_step,
    w_shared,
    conv_main,
    conv_shared,
    decay_log,
    step_bias,
    skip_gain,
    w_mamba_out,
    norm2_gain,
    w_ffn_gate,
    w_ffn_up,
    w_ffn_down,
    out_grad,
):
    own, model = hidden_in.shape
    step_width = w_step.shape[1]
    head_terms = [v.reshape(1, -1) for v in (decay_log, step_bias, skip_gain)]
    tables = rotary_tables(2 * own)
    gain1, gain2 = norm1_gain.reshape(1, model), norm2_gain.reshape(1, model)
    kernels = (conv_main, conv_shared)
    weights = (w_query, key_weight.T, value_weight.T, w_step.T, w_mamba_x, w_mamba_z)
    weights += (w_attn_out, w_mamba_out, w_ffn_down, w_ffn_gate, w_ffn_up)
    *saved, gain2_part = forward(
        lengths,
        hidden_in,
        out_grad,
        (gain1, gain2),
        weights,
        w_shared,
        kernels,
        head_terms,
        tables,
    )
    outs = backward(
        lengths,
        hidden_in,
        gain1,
        gain2_part,
        saved,
        w_shared,
        kernels,
        head_terms,
        tables,
        (w_query.shape[1], key_weight.shape[1], step_width),
    )
    outs = list(emit(outs))
    outs[9] = outs[9].T
    for i in (2, 13, 14, 15, 17):
        outs[i] = outs[i].reshape(-1)
    outs[10] = outs[10].reshape(model, -1)
    return tuple(outs)


def solution(mesh):
    rows, whole, weight = P(("grp", "fsdp", "tp"), None), P(), P("fsdp", "tp")
    grad = P(("grp", "fsdp"), "tp")
    return jax.shard_map(
        local,
        mesh=mesh,
        in_specs=(rows, P(("grp", "fsdp")), whole)
        + (weight,) * 7
        + (whole,) * 6
        + (weight, whole)
        + (weight,) * 3
        + (rows,),
        out_specs=(rows, rows, whole)
        + (grad,) * 7
        + (whole,) * 6
        + (grad, whole)
        + (grad,) * 3,
        check_vma=False,
    )
```

```python
from functools import partial
from typing import Any, NamedTuple

import jax
import jax.numpy as jnp
import numpy as np
from jax import lax
from jax.experimental import pallas as pl
from jax.experimental.pallas import tpu as pltpu
from jax.sharding import PartitionSpec as P

HEAD = 64
LANES = 128
BLOCK = 128
NSTATE = 128
EPS = 1e-05
ROPE_BASE = 100000000000.0
MESH = pl.DeviceIdType.MESH
VMEM_LIMIT = 62 << 20
F32, BF16 = jnp.float32, jnp.bfloat16
EXACT = lax.Precision.HIGHEST


def low(values):
    return values.astype(BF16)


def wide(values):
    return values.astype(F32)


def dot(a, b):
    return jnp.dot(a, b, preferred_element_type=F32)


def dot_nt(a, b):
    return lax.dot_general(a, b, (((1,), (1,)), ((), ())), preferred_element_type=F32)


def dot_tn(a, b):
    return lax.dot_general(a, b, (((0,), (0,)), ((), ())), preferred_element_type=F32)


def exact_dot(a, b):
    return jnp.dot(a, b, precision=EXACT, preferred_element_type=F32)


def split(values):
    coarse = low(values)
    return coarse, low(values - wide(coarse))


def split_dot(a, b):
    return dot(jnp.concatenate([a[0], a[0], a[1]], axis=1), jnp.concatenate([b[0], b[1], b[0]], axis=0))


def split_dot_nt(a, b):
    return dot_nt(jnp.concatenate([a[0], a[0], a[1]], axis=1), jnp.concatenate([b[0], b[1], b[0]], axis=1))


def split_dot_tn(a, b):
    return dot_tn(jnp.concatenate([a[0], a[0], a[1]], axis=0), jnp.concatenate([b[0], b[1], b[0]], axis=0))


def sigmoid(v):
    return 1.0 / (1.0 + jnp.exp(-v))


def rms_scale(values):
    return lax.rsqrt(jnp.mean(values * values, axis=-1, keepdims=True) + EPS)


def lane_ids(rows):
    return lax.broadcasted_iota(jnp.int32, (rows, LANES), 1)


def first_head(rows):
    return lane_ids(rows) < HEAD


def half_swap(tile):
    lower = lax.rem(lane_ids(tile.shape[0]), HEAD) < HEAD // 2
    return jnp.where(lower, pltpu.roll(tile, LANES - HEAD // 2, 1), pltpu.roll(tile, HEAD // 2, 1))


def spread(values, tile):
    return jnp.where(
        first_head(values.shape[0]),
        values[:, 2 * tile : 2 * tile + 1],
        values[:, 2 * tile + 1 : 2 * tile + 2],
    )


def rotary_tables(length):
    positions = np.arange(length, dtype=np.float64)[:, None]
    power = np.arange(HEAD // 2, dtype=np.float64) * (-2.0 / HEAD)
    phase = (positions * np.power(ROPE_BASE, power)[None, :]).astype(np.float32)
    cosine, sine = np.cos(phase), np.sin(phase)
    return (
        np.concatenate([cosine] * 4, axis=1).astype(np.float32),
        np.concatenate([-sine, sine] * 2, axis=1).astype(np.float32),
    )


def place():
    g, f, t = lax.axis_index("grp"), lax.axis_index("fsdp"), lax.axis_index("tp")
    return g, f // 2, lax.rem(f, 2), t


def greet(devices):
    barrier = pltpu.get_barrier_semaphore()
    for device in devices:
        pl.semaphore_signal(barrier, inc=1, device_id=device, device_id_type=MESH)


def greeted(devices):
    pl.semaphore_wait(pltpu.get_barrier_semaphore(), len(devices))


def remote(src, dst, send, recv, device):
    return pltpu.make_async_remote_copy(
        src_ref=src,
        dst_ref=dst,
        send_sem=send,
        recv_sem=recv,
        device_id=device,
        device_id_type=MESH,
    )


def pick_heads(terms, whole, t):
    terms[...] = jnp.zeros_like(terms)
    for i, ref in enumerate(whole):
        heads = ref.shape[1] // 2
        terms[i : i + 1, :heads] = jnp.where(t == 0, ref[:, :heads], ref[:, heads:])


class Gather:
    def __init__(self, units, halves, sems):
        self.units, self.halves = units, halves
        self.x, self.z, self.cx, self.cz, self.own, self.local = sems
        g, self.hi, self.c, t = place()
        f = self.hi * 2 + self.c
        self.f, self.pair = f, lax.rem(g, 2)
        self.other_core = (g, self.hi * 2 + 1 - self.c, t)
        self.other_z = (g + 1 - 2 * self.pair, f, t)
        self.across = [
            (g, lax.rem(self.hi + k, halves) * 2 + self.c, t) for k in range(1, halves)
        ]
        self.devices = [self.other_core, self.other_z] + self.across
        self.got, self.sent, self.pending = {}, [], {}

    def block(self, u, owner, part=None):
        shard, full, column, width = self.units[u]
        rows = shard.shape[0]
        size = rows if part is None else rows // 2
        start = owner * rows + (0 if part is None else part * size)
        return full.at[pl.ds(pl.multiple_of(start, size), size), pl.ds(column, width)]

    def start(self, copy):
        copy.start()
        self.sent.append(copy)
        return copy

    def send(self, u):
        shard = self.units[u][0]
        half = shard.shape[0] // 2
        mine = shard.at[pl.ds(pl.multiple_of(self.pair * half, half), half), :]
        for k in range(1, self.halves):
            self.got["x", u, k] = self.start(
                remote(
                    mine,
                    self.block(u, self.f, self.pair),
                    self.x.at[0, u, k],
                    self.x.at[1, u, k],
                    self.across[k - 1],
                )
            )
        self.got["own", u] = self.start(
            remote(
                shard,
                self.block(u, self.f),
                self.own.at[0, u],
                self.own.at[1, u],
                self.other_core,
            )
        )
        self.pending[u] = pltpu.make_async_copy(shard, self.block(u, self.f), self.local.at[u])
        self.pending[u].start()

    def owner(self, k):
        return lax.rem(self.hi - k + self.halves, self.halves) * 2 + self.c

    def relay_x(self, u):
        for k in range(1, self.halves):
            self.got.pop(("x", u, k)).wait_recv()
            block = self.block(u, self.owner(k), self.pair)
            self.got["z", u, k] = self.start(
                remote(block, block, self.z.at[0, u, k], self.z.at[1, u, k], self.other_z)
            )
            self.got["cx", u, k] = self.start(
                remote(block, block, self.cx.at[0, u, k], self.cx.at[1, u, k], self.other_core)
            )

    def relay_z(self, u):
        for k in range(1, self.halves):
            self.got.pop(("z", u, k)).wait_recv()
            block = self.block(u, self.owner(k), 1 - self.pair)
            self.got["cz", u, k] = self.start(
                remote(block, block, self.cz.at[0, u, k], self.cz.at[1, u, k], self.other_core)
            )

    def finish(self, u):
        self.got.pop(("own", u)).wait_recv()
        for k in range(1, self.halves):
            self.got.pop(("cx", u, k)).wait_recv()
            self.got.pop(("cz", u, k)).wait_recv()
        self.pending.pop(u).wait()

    def drain(self):
        assert not self.got and not self.pending
        for copy in self.sent:
            copy.wait_send()


def gather_sems(units, halves):
    dma = pltpu.SemaphoreType.DMA
    return [dma((2, units, halves))] * 4 + [dma((2, units)), dma((units,))]


def causal_conv(padded, kernel, rows, cols):
    total = kernel[3:4, :] * padded[8 : 8 + rows, cols]
    for i in range(3):
        total = total + kernel[i : i + 1, :] * padded[5 + i : 5 + i + rows, cols]
    return total


def triangle(lower=True):
    row = lax.broadcasted_iota(jnp.int32, (BLOCK, BLOCK), 0)
    col = lax.broadcasted_iota(jnp.int32, (BLOCK, BLOCK), 1)
    return row >= col if lower else row <= col


class Scatter:
    def __init__(self, units, groups, halves, sems):
        self.units = units
        self.groups, self.halves = groups, halves
        self.c_sems, self.x_sems, self.z_sems, self.l_sems = sems
        self.g, self.hi, self.c, self.t = place()
        f = self.hi * 2 + self.c
        self.other_core = (self.g, self.hi * 2 + 1 - self.c, self.t)
        self.across = [
            (self.g, lax.rem(self.hi + k, halves) * 2 + self.c, self.t) for k in range(1, halves)
        ]
        self.along = [(lax.rem(self.g + j, groups), f, self.t) for j in range(1, groups)]
        self.devices = [self.other_core] + self.across + self.along
        self.outer = (self.g == 0) | (self.g == groups - 1)
        self.got, self.sent, self.lines = {}, [], []

    def start(self, copy):
        copy.start()
        self.sent.append(copy)
        return copy

    def send(self, u):
        unit = self.units[u]
        self.got["c", u] = self.start(
            remote(
                unit["part"].at[:, :, 1 - self.c],
                unit["from_core"],
                self.c_sems.at[0, u],
                self.c_sems.at[1, u],
                self.other_core,
            )
        )

    def send_x(self, u):
        unit = self.units[u]
        for k in range(1, self.halves):
            away = lax.rem(self.hi + k, self.halves)
            self.got["x", u, k] = self.start(
                remote(
                    unit["pair_sum"].at[away]
                    if "pair_sum" in unit
                    else unit["part"].at[:, away, self.c],
                    unit["from_x"].at[k - 1],
                    self.x_sems.at[0, u, k],
                    self.x_sems.at[1, u, k],
                    self.across[k - 1],
                )
            )
        if "pair_sum" in unit:
            self.load(u, unit["pair_sum"].at[self.hi], unit["own_pair"])

    def load(self, u, source, target):
        self.got["l", u] = pltpu.make_async_copy(source, target, self.l_sems.at[u])
        self.got["l", u].start()

    def z_links(self, u):
        unit, g = self.units[u], self.g
        chip, into, last = unit["chip_sum"], unit["from_z"], self.groups - 1

        def to(where):
            return (where, self.hi * 2 + self.c, self.t)

        near = jnp.where(g == 0, 1, last - 1)
        outer = {
            0: (chip.at[near], into.at[0], to(near)),
            1: (chip.at[last - near], into.at[1], to(last - near)),
            3: (chip.at[last - g], unit["relay"], to(near)),
        }
        end = jnp.where(g == 1, 0, last)
        inner = {
            0: (chip.at[end], into.at[0], to(end)),
            1: (chip.at[last - end], into.at[1], to(last - end)),
            2: (chip.at[last - g], into.at[2], to(last - g)),
        }
        return outer, inner

    def z_copy(self, u, side, slot):
        source, target, device = self.z_links(u)[side][slot]
        return remote(
            source, target, self.z_sems.at[0, u, slot], self.z_sems.at[1, u, slot], device
        )

    def send_z(self, u):
        unit = self.units[u]
        if self.groups == 4:

            @pl.when(self.outer)
            def _():
                for slot in (3, 0, 1):
                    self.z_copy(u, 0, slot).start()

            @pl.when(jnp.logical_not(self.outer))
            def _():
                for slot in (2, 0):
                    self.z_copy(u, 1, slot).start()

            self.lines.append(u)
            return
        for j in range(1, self.groups):
            self.got["z", u, j] = self.start(
                remote(
                    unit["chip_sum"].at[lax.rem(self.g + j, self.groups)],
                    unit["from_z"].at[j - 1],
                    self.z_sems.at[0, u, j],
                    self.z_sems.at[1, u, j],
                    self.along[j - 1],
                )
            )

    def relay(self, u):
        if self.groups != 4:
            return
        unit = self.units[u]

        @pl.when(jnp.logical_not(self.outer))
        def _():
            self.z_copy(u, 0, 3).wait_recv()
            far = jnp.where(self.g == 1, self.groups - 1, 0)
            chip = unit["chip_sum"]
            chip[far] = low(wide(chip[far]) + wide(unit["relay"][...]))
            self.z_copy(u, 1, 1).start()

    def core_stage(self, u):
        part, from_core = self.units[u]["part"], self.units[u]["from_core"]
        self.got.pop(("c", u)).wait_recv()

        def add(i, carry):
            gg, h = i // self.halves, lax.rem(i, self.halves)
            part[gg, h, self.c] = low(wide(part[gg, h, self.c]) + wide(from_core[gg, h]))
            return carry

        lax.fori_loop(0, self.groups * self.halves, add, 0)

    def x_stage(self, u):
        unit = self.units[u]
        for k in range(1, self.halves):
            self.got.pop(("x", u, k)).wait_recv()
        if "pair_sum" in unit:
            self.got.pop(("l", u)).wait()

        def add(gg, carry):
            if "pair_sum" in unit:
                total = wide(unit["own_pair"][gg])
            else:
                total = wide(unit["part"][gg, self.hi, self.c])
            for k in range(1, self.halves):
                total = total + wide(unit["from_x"][k - 1, gg])
            unit["chip_sum"][gg] = low(total)
            return carry

        lax.fori_loop(0, self.groups, add, 0)

    def z_stage(self, u):
        unit = self.units[u]
        total = wide(unit["chip_sum"][self.g])
        if self.groups == 4:
            for slot in (0, 1):
                self.z_copy(u, 1, slot).wait_recv()

            @pl.when(jnp.logical_not(self.outer))
            def _():
                self.z_copy(u, 1, 2).wait_recv()

            total = total + wide(unit["from_z"][0]) + wide(unit["from_z"][1])
            return total + jnp.where(self.outer, 0.0, wide(unit["from_z"][2]))
        for j in range(1, self.groups):
            self.got.pop(("z", u, j)).wait_recv()
            total = total + wide(unit["from_z"][j - 1])
        return total

    def drain(self):
        assert not self.got
        for copy in self.sent:
            copy.wait_send()
        if not self.lines:
            return

        @pl.when(self.outer)
        def _():
            for u in self.lines:
                for slot in (0, 1, 3):
                    self.z_copy(u, 0, slot).wait_send()

        @pl.when(jnp.logical_not(self.outer))
        def _():
            for u in self.lines:
                for slot in (0, 1, 2):
                    self.z_copy(u, 1, slot).wait_send()


class Mover:
    def __init__(self, sems):
        self.sems, self.count, self.copies = sems, 0, {}

    def start(self, name, source, target):
        self.copies[name] = pltpu.make_async_copy(source, target, self.sems.at[self.count])
        self.copies[name].start()
        self.count += 1

    def wait(self, *names):
        for name in names:
            self.copies.pop(name).wait()

    def drain(self):
        self.wait(*list(self.copies))


def scatter_sems(units, groups, halves):
    dma = pltpu.SemaphoreType.DMA
    return [
        dma((2, units)),
        dma((2, units, halves)),
        dma((2, units, groups)),
        dma((units,)),
    ]


def head_sum(values, tile):
    lane = lax.broadcasted_iota(jnp.int32, (LANES, LANES), 0)
    column = lax.broadcasted_iota(jnp.int32, (LANES, LANES), 1)
    pick = low(jnp.where(column == 2 * tile + jnp.where(lane < HEAD, 0, 1), 1.0, 0.0))
    coarse = low(values)
    fine = low(values - wide(coarse))
    return dot(
        jnp.concatenate([coarse, fine], axis=1), jnp.concatenate([pick, pick], axis=0)
    )


def column_sum(values):
    return jnp.sum(values, axis=0, keepdims=True)


class ForwardIn(NamedTuple):
    length_ref: Any
    hidden: Any
    gain1: Any
    gain2: Any
    w_query: Any
    w_key: Any
    w_value: Any
    w_step: Any
    w_x: Any
    w_z: Any
    w_attn_out: Any
    w_mamba_out: Any
    w_down: Any
    w_gate: Any
    w_up: Any
    w_shared: Any
    out_grad: Any
    cosine: Any
    sine: Any
    conv_main: Any
    conv_shared: Any
    decay_log: Any
    step_bias: Any
    skip_gain: Any


class Kept(NamedTuple):
    w_in: Any
    w_mix: Any
    normed: Any
    mix: Any
    qr: Any
    kv: Any
    probs: Any
    x_padded: Any
    z_proj: Any
    bc_padded: Any
    step_in: Any
    scanned: Any
    states: Any
    mix_grad: Any
    resid_grad: Any
    resid: Any
    ffn_part: Any
    down_chip: Any
    gate_pair: Any
    up_pair: Any
    gain2_part: Any


class ForwardScratch(NamedTuple):
    shared: Any
    out_grad: Any
    cosine: Any
    sine: Any
    top_grad: Any
    narrow: Any
    conv_x: Any
    conv_bc: Any
    steps: Any
    state: Any
    head_terms: Any
    w_down: Any
    w_gate: Any
    w_up: Any
    normed2: Any
    arrived: Any
    leaving: Any
    own_part: Any
    gate_pre: Any
    up_pre: Any
    hidden_low: Any
    gate_back: Any
    up_back: Any
    p_down: Any
    p_down2: Any
    p_gate: Any
    p_up: Any
    c_down: Any
    c_down2: Any
    c_gate: Any
    c_up: Any
    x_down: Any
    x_down2: Any
    d_chip: Any
    d_chip2: Any
    y_sems: Any
    move_sems: Any


def forward_body(groups, halves, *refs):
    counts = len(ForwardIn._fields), len(Kept._fields) - 1
    r = ForwardIn(*refs[: counts[0]])
    out = Kept(*refs[counts[0] : sum(counts) + 1])
    rest = refs[sum(counts) + 1 :]
    v = Kept(*rest[:17], *[None] * (counts[1] - 16))
    s = ForwardScratch(*rest[17:54])
    sems = rest[54:]
    g, hi, c, t = place()
    own, model = r.hidden.shape
    length = 2 * own
    inner, ffn = r.w_x.shape[1], r.w_gate.shape[1]
    q_width, step_width = r.w_query.shape[1], r.w_step.shape[0]
    tiles, q_tiles = inner // LANES, q_width // LANES
    narrow_width = q_width + 2 * LANES
    gather = Gather(
        [
            (s.narrow, v.w_in, 0, narrow_width),
            (r.w_x, v.w_in, narrow_width, inner),
            (r.w_z, v.w_in, narrow_width + inner, inner),
            (r.w_attn_out, v.w_mix, 0, q_width),
            (r.w_mamba_out, v.w_mix, q_width, inner),
            (r.w_gate, s.w_gate, 0, ffn),
            (r.w_up, s.w_up, 0, ffn),
            (r.w_down, s.w_down, 0, ffn),
        ],
        halves,
        sems[:6],
    )
    scatter = Scatter(
        [
            dict(part=s.p_down, from_core=s.c_down, from_x=s.x_down, chip_sum=s.d_chip),
            dict(part=s.p_gate, from_core=s.c_gate),
            dict(part=s.p_up, from_core=s.c_up),
            dict(part=s.p_down2, from_core=s.c_down2, from_x=s.x_down2, chip_sum=s.d_chip2),
        ],
        groups,
        halves,
        sems[6:],
    )
    move = Mover(s.move_sems)
    other_y = (g, hi * 2 + c, 1 - t)
    devices = gather.devices + [other_y]
    greet(devices)
    move.start("out_grad", r.out_grad, s.out_grad)
    move.start("shared", r.w_shared, s.shared)
    move.start("cosine", r.cosine, s.cosine)
    move.start("sine", r.sine, s.sine)
    turned = jnp.concatenate([wide(r.w_key[...]), wide(r.w_value[...])], axis=0).T
    s.narrow[:, :q_width] = r.w_query[...]
    s.narrow[:, q_width : q_width + LANES] = low(turned)
    filler = jnp.zeros((LANES - step_width, s.narrow.shape[0]), F32)
    turned = jnp.concatenate([wide(r.w_step[...]), filler], axis=0).T
    s.narrow[:, q_width + LANES :] = low(turned)
    mine = pl.ds(pl.multiple_of(t * own, own), own)
    other = pl.ds(pl.multiple_of((1 - t) * own, own), own)
    values = wide(r.hidden[...])
    v.normed[mine, :] = low(values * rms_scale(values) * r.gain1[...])
    count = r.length_ref[0]
    greeted(devices)
    gather.send(0)
    sent = []

    def swap(src, dst, at):
        copy = remote(src, dst, s.y_sems.at[0, at], s.y_sems.at[1, at], other_y)
        copy.start()
        sent.append(copy)
        return copy

    y_copy = swap(v.normed.at[mine, :], v.normed.at[mine, :], 12)
    for u in range(1, 8):
        gather.send(u)
    slot = t * own + lax.broadcasted_iota(jnp.int32, (own, 1), 0)
    move.wait("out_grad")
    s.top_grad[mine, :] = jnp.where(slot < count, s.out_grad[...], jnp.zeros((), BF16))
    grad_copy = swap(s.top_grad.at[mine, :], s.top_grad.at[mine, :], 13)
    pick_heads(s.head_terms, (r.decay_log, r.step_bias, r.skip_gain), t)
    v.x_padded[0:8, :] = jnp.zeros((8, inner), F32)
    v.bc_padded[0:8, :] = jnp.zeros((8, 2 * NSTATE), F32)
    s.state[...] = jnp.zeros_like(s.state)

    def save(*names):
        for name in names:
            move.start(name, getattr(v, name), getattr(out, name))

    move.wait("shared")
    v.bc_padded[pl.ds(pl.multiple_of(8 + t * own, 8), own), :] = dot(
        v.normed[mine, :], s.shared[...]
    )
    gather.relay_x(0)
    gather.relay_z(0)
    gather.relay_x(1)
    y_copy.wait_recv()
    save("normed")
    v.bc_padded[pl.ds(pl.multiple_of(8 + (1 - t) * own, 8), own), :] = dot(
        v.normed[other, :], s.shared[...]
    )
    gather.finish(0)
    move.wait("cosine", "sine")
    projected = dot(v.normed[...], v.w_in[:, :narrow_width])
    for j in range(q_tiles):
        tile = projected[:, j * LANES : (j + 1) * LANES]
        turned = tile * s.cosine[...] + half_swap(tile) * s.sine[...]
        v.qr[:, j * LANES : (j + 1) * LANES] = low(turned)
    tile = projected[:, q_width : q_width + LANES]
    is_key = first_head(length)
    turned = tile * s.cosine[...] + half_swap(tile) * s.sine[...]
    v.kv[...] = low(jnp.where(is_key, turned, tile))
    step_pre = projected[:, q_width + LANES :] + s.head_terms[1:2, :]
    v.step_in[...] = step_pre
    row = lax.broadcasted_iota(jnp.int32, (length, 1), 0)
    softplus = jnp.maximum(step_pre, 0.0) + jnp.log(1.0 + jnp.exp(-jnp.abs(step_pre)))
    s.steps[...] = jnp.where(row < count, softplus, 0.0)
    save("qr", "kv", "step_in", "bc_padded")
    for j in range(2 * NSTATE // LANES):
        cols = slice(j * LANES, (j + 1) * LANES)
        pre = causal_conv(v.bc_padded, r.conv_shared[:, cols], length, cols)
        s.conv_bc[:, cols] = pre * sigmoid(pre)
    def attend(j):
        zero = jnp.zeros((), BF16)
        keys = [jnp.where(is_key, v.kv[...], zero)]
        keys.append(low(pltpu.roll(wide(keys[0]), HEAD, 1)))
        held = [None, jnp.where(is_key, zero, v.kv[...])]
        held[0] = low(pltpu.roll(wide(held[1]), HEAD, 1))
        for i in range(length // BLOCK):
            rows, upto = slice(i * BLOCK, (i + 1) * BLOCK), (i + 1) * BLOCK
            query_slot = i * BLOCK + lax.broadcasted_iota(jnp.int32, (BLOCK, upto), 0)
            key_slot = lax.broadcasted_iota(jnp.int32, (BLOCK, upto), 1)
            allowed = (key_slot <= query_slot) & (key_slot < count)
            total = jnp.zeros((BLOCK, LANES), F32)
            for e in range(2):
                score = dot_nt(v.qr[rows, j * LANES : (j + 1) * LANES], keys[e][:upto])
                score = jnp.where(allowed, score * HEAD**-0.5, -1e30)
                expo = jnp.exp(score - jnp.max(score, axis=-1, keepdims=True))
                prob = low(expo / jnp.sum(expo, axis=-1, keepdims=True))
                v.probs[2 * j + e, rows, :upto] = prob
                total = total + dot(prob, held[e][:upto])
            v.mix[rows, j * LANES : (j + 1) * LANES] = low(total)

    attend(0)
    gather.relay_z(1)
    gather.relay_x(2)
    for j in range(1, q_tiles):
        attend(j)
    save("probs")
    gather.finish(1)
    v.x_padded[8:, :] = dot(v.normed[...], v.w_in[:, narrow_width : narrow_width + inner])
    save("x_padded")
    channel = t * inner
    for j in range(tiles):
        if j == tiles // 2:
            gather.relay_x(3)
            gather.relay_z(2)
        cols = slice(j * LANES, (j + 1) * LANES)
        taps = r.conv_main[:, pl.ds(pl.multiple_of(channel + j * LANES, LANES), LANES)]
        pre = causal_conv(v.x_padded, taps, length, cols)
        s.conv_x[:, cols] = pre * sigmoid(pre)
    gather.relay_x(4)
    rate = -jnp.exp(s.head_terms[0:1, :])
    causal = triangle()

    def scan_block(i):
        rows = slice(i * BLOCK, (i + 1) * BLOCK)
        step = s.steps[rows, :]
        total = exact_dot(causal.astype(F32), step * rate)
        total_t = total.T
        last = total[BLOCK - 1 : BLOCK, :]
        grown, rest = jnp.exp(total), jnp.exp(last - total)
        b_mat, c_mat = split(s.conv_bc[rows, :NSTATE]), split(s.conv_bc[rows, NSTATE:])
        inner_prod = jnp.where(causal, split_dot_nt(c_mat, b_mat), 0.0)
        v.states[i] = s.state[...]
        crossed = split_dot(c_mat, split(s.state[...]))
        left = first_head(BLOCK)
        for j in range(tiles):
            cols = slice(j * LANES, (j + 1) * LANES)
            stepped = spread(step, j) * s.conv_x[rows, cols]
            mixing = []
            for h in (2 * j, 2 * j + 1):
                gap = jnp.minimum(total[:, h : h + 1] - total_t[h : h + 1, :], 0.0)
                mixing.append(jnp.exp(gap) * inner_prod)
            stacked = jnp.concatenate(
                [jnp.where(left, stepped, 0.0), jnp.where(left, 0.0, stepped)], axis=0
            )
            within = split_dot(split(jnp.concatenate(mixing, axis=1)), split(stacked))
            grown_wide = spread(grown, j)
            v.scanned[rows, cols] = within + crossed[:, cols] * grown_wide
            s.state[:, cols] = s.state[:, cols] * grown_wide[BLOCK - 1 : BLOCK, :] + split_dot_tn(
                b_mat, split(stepped * spread(rest, j))
            )

    for i in range(length // BLOCK):
        scan_block(i)
        if i == 0:
            gather.relay_z(3)
            gather.finish(2)
            v.z_proj[...] = dot(v.normed[...], v.w_in[:, narrow_width + inner :])
            save("w_in", "z_proj")
        if i == 1:
            gather.relay_x(5)
            gather.relay_z(4)
    for j in range(tiles):
        cols = slice(j * LANES, (j + 1) * LANES)
        gate = v.z_proj[:, cols]
        skip = spread(s.head_terms[2:3, :], j)
        result = (v.scanned[:, cols] + skip * s.conv_x[:, cols]) * gate * sigmoid(gate)
        v.mix[:, q_width + j * LANES : q_width + (j + 1) * LANES] = low(result)
    gather.finish(3)
    gather.finish(4)

    pieces = 3
    size = own // pieces

    def mine_at(p):
        return pl.ds(pl.multiple_of(t * own + p * size, size), size)

    def other_at(p):
        return pl.ds(pl.multiple_of((1 - t) * own + p * size, size), size)

    def here(p):
        return slice(p * size, (p + 1) * size)

    mixed = []
    for p in range(pieces):
        s.leaving[0, p] = low(dot_nt(v.mix[other_at(p), :], v.w_mix[...]))
        mixed.append(swap(s.leaving.at[0, p], s.arrived.at[0, p], p))
    save("scanned", "states", "mix", "w_mix")
    for p in range(pieces):
        s.own_part[here(p), :] = dot_nt(v.mix[mine_at(p), :], v.w_mix[...])
    gather.relay_z(5)
    gather.relay_x(6)
    scale, normed_copies = [], []
    for p in range(pieces):
        mixed[p].wait_recv()
        middle = wide(r.hidden[here(p), :]) + s.own_part[here(p), :] + wide(s.arrived[0, p])
        v.resid[here(p), :] = middle
        scale.append(rms_scale(middle))
        s.normed2[mine_at(p), :] = low(middle * scale[p] * r.gain2[...])
        normed_copies.append(
            swap(s.normed2.at[mine_at(p), :], s.normed2.at[mine_at(p), :], pieces + p)
        )
    save("resid")
    gather.relay_z(6)
    gather.relay_x(7)
    gather.finish(5)
    for p in range(pieces):
        s.gate_pre[mine_at(p), :] = dot(s.normed2[mine_at(p), :], s.w_gate[...])
    gather.finish(6)
    for p in range(pieces):
        s.up_pre[mine_at(p), :] = dot(s.normed2[mine_at(p), :], s.w_up[...])

    def activate(rows):
        gate, up = s.gate_pre[rows, :], s.up_pre[rows, :]
        sig = sigmoid(gate)
        silu = gate * sig
        s.hidden_low[rows, :] = low(silu * up)
        s.gate_pre[rows, :] = up * sig * (1.0 + gate * (1.0 - sig))
        s.up_pre[rows, :] = silu

    def normed_grad(rows):
        return dot_nt(s.gate_back[rows, :], s.w_gate[...]) + dot_nt(
            s.up_back[rows, :], s.w_up[...]
        )

    span = 256

    def weight_grads(part, left, right, first=0):
        _, _, _, rows, width = part.shape
        per = span // (2 * rows)

        def one(i, carry):
            cols = pl.ds(pl.multiple_of(i * span, span), span)
            value = low(dot_tn(left[:, cols], right[:, first : first + width]))
            value = value.reshape(per, 2, rows, width)
            for k in range(per):
                at = i * per + k
                part[at // halves, lax.rem(at, halves)] = value[k]
            return carry

        lax.fori_loop(0, model // span, one, 0)

    def rows_back(rows):
        grad = dot(s.top_grad[rows, :], s.w_down[...])
        s.gate_back[rows, :] = low(grad * s.gate_pre[rows, :])
        s.up_back[rows, :] = low(grad * s.up_pre[rows, :])

    for p in range(pieces):
        activate(mine_at(p))
    gather.relay_z(7)
    grad_copy.wait_recv()
    sums = []
    for p in range(pieces):
        rows = other_at(p)
        normed_copies[p].wait_recv()
        s.gate_pre[rows, :] = dot(s.normed2[rows, :], s.w_gate[...])
        s.up_pre[rows, :] = dot(s.normed2[rows, :], s.w_up[...])
        activate(rows)
        if p == 0:
            gather.finish(7)
        rows_back(rows)
        s.leaving[1, p] = low(normed_grad(rows))
        sums.append(swap(s.leaving.at[1, p], s.arrived.at[1, p], 2 * pieces + p))
    weight_grads(s.p_down, s.top_grad, s.hidden_low)
    scatter.send(0)
    weight_grads(s.p_down2, s.top_grad, s.hidden_low, ffn // 2)
    scatter.send(3)
    rows_back(mine_at(0))
    scatter.core_stage(0)
    scatter.send_x(0)
    for p in range(pieces):
        if p > 0:
            rows_back(mine_at(p))
        s.own_part[here(p), :] = normed_grad(mine_at(p))
        if p == 0:
            scatter.core_stage(3)
            scatter.send_x(3)
    total = jnp.zeros((1, model), F32)
    mix_copies = []
    for p in range(pieces):
        sums[p].wait_recv()
        middle = v.resid[here(p), :]
        grad = s.own_part[here(p), :] + wide(s.arrived[1, p])
        total = total + jnp.sum(grad * middle * scale[p], axis=0, keepdims=True)
        weighted = grad * r.gain2[...]
        result = (
            wide(s.top_grad[mine_at(p), :])
            + scale[p] * weighted
            - middle
            * (scale[p] * scale[p] * scale[p])
            * jnp.mean(weighted * middle, axis=-1, keepdims=True)
        )
        v.resid_grad[here(p), :] = result
        v.mix_grad[mine_at(p), :] = low(result)
        mix_copies.append(
            swap(v.mix_grad.at[mine_at(p), :], v.mix_grad.at[mine_at(p), :], 3 * pieces + p)
        )
    out.gain2_part[...] = total
    save("resid_grad")
    weight_grads(s.p_gate, s.normed2, s.gate_back)
    scatter.send(1)
    weight_grads(s.p_up, s.normed2, s.up_back)
    scatter.send(2)

    def save_pair(name, part):
        for k in range(halves):
            move.start((name, k), part.at[:, k, c], getattr(out, name).at[k])

    scatter.core_stage(1)
    save_pair("gate_pair", s.p_gate)
    v.ffn_part[...] = low(dot_nt(s.hidden_low[...], s.w_down[...]))
    save("ffn_part")
    scatter.core_stage(2)
    save_pair("up_pair", s.p_up)
    scatter.x_stage(0)
    move.start("down", s.d_chip, out.down_chip.at[:, :, pl.ds(0, ffn // 2)])
    scatter.x_stage(3)
    move.start("down2", s.d_chip2, out.down_chip.at[:, :, pl.ds(ffn // 2, ffn // 2)])
    for copy in mix_copies:
        copy.wait_recv()
    save("mix_grad")
    for copy in sent:
        copy.wait_send()
    gather.drain()
    scatter.drain()
    move.drain()


def forward(length_of, hidden, out_grad, gains, weights, shared, kernels, head_terms, tables):
    groups, halves = lax.axis_size("grp"), lax.axis_size("fsdp") // 2
    w_query, w_x, w_gate = weights[0], weights[4], weights[9]
    own, model = hidden.shape
    length, inner, q_width, ffn = 2 * own, w_x.shape[1], w_query.shape[1], w_gate.shape[1]
    shard = w_x.shape[0]
    narrow_width = q_width + 2 * LANES
    heads = q_width // HEAD
    rows = model // (2 * groups * halves)
    inside = pl.BlockSpec(memory_space=pltpu.VMEM)
    anywhere = pl.BlockSpec(memory_space=pl.ANY)
    shape = jax.ShapeDtypeStruct
    saved = [
        ((model, narrow_width + 2 * inner), BF16),
        ((model, q_width + inner), BF16),
        ((length, model), BF16),
        ((length, q_width + inner), BF16),
        ((length, q_width), BF16),
        ((length, LANES), BF16),
        ((heads, length, length), BF16),
        ((length + 8, inner), F32),
        ((length, inner), F32),
        ((length + 8, 2 * NSTATE), F32),
        ((length, LANES), F32),
        ((length, inner), F32),
        ((length // BLOCK, NSTATE, inner), F32),
        ((length, model), BF16),
        ((own, model), F32),
        ((own, model), F32),
        ((length, model), BF16),
    ]
    sums = [((groups, rows, ffn), BF16)] + [((halves, groups, rows, ffn), BF16)] * 2
    dma, vmem = pltpu.SemaphoreType.DMA, pltpu.VMEM
    grad_widths = (ffn // 2, ffn // 2, ffn, ffn)
    moves = 6 + len(saved) + 2 * halves
    return pl.pallas_call(
        partial(forward_body, groups, halves),
        out_shape=[shape(*a) for a in saved + sums]
        + [shape((1, model), F32)],
        in_specs=[pl.BlockSpec(memory_space=pltpu.SMEM)]
        + [inside] * 7
        + [anywhere] * 11
        + [inside] * 5,
        out_specs=[anywhere] * (len(saved) + 3) + [inside],
        scratch_shapes=[vmem(*a) for a in saved]
        + [
            vmem((model, 2 * NSTATE), BF16),
            vmem((own, model), BF16),
            vmem((length, LANES), F32),
            vmem((length, LANES), F32),
            vmem((length, model), BF16),
            vmem((shard, narrow_width), BF16),
            vmem((length, inner), F32),
            vmem((length, 2 * NSTATE), F32),
            vmem((length, LANES), F32),
            vmem((NSTATE, inner), F32),
            vmem((8, LANES), F32),
            vmem((model, ffn), BF16),
            vmem((model, ffn), BF16),
            vmem((model, ffn), BF16),
            vmem((length, model), BF16),
            vmem((2, 3, own // 3, model), BF16),
            vmem((2, 3, own // 3, model), BF16),
            vmem((own, model), F32),
            vmem((length, ffn), F32),
            vmem((length, ffn), F32),
            vmem((length, ffn), BF16),
            vmem((length, ffn), BF16),
            vmem((length, ffn), BF16),
        ]
        + [vmem((groups, halves, 2, rows, w), BF16) for w in grad_widths]
        + [vmem((groups, halves, rows, w), BF16) for w in grad_widths]
        + [
            vmem((max(halves - 1, 1), groups, rows, ffn // 2), BF16),
            vmem((max(halves - 1, 1), groups, rows, ffn // 2), BF16),
            vmem((groups, rows, ffn // 2), BF16),
            vmem((groups, rows, ffn // 2), BF16),
            dma((2, 14)),
            dma((moves,)),
        ]
        + gather_sems(8, halves)
        + scatter_sems(4, groups, halves),
        compiler_params=pltpu.CompilerParams(
            collective_id=0, has_side_effects=True, vmem_limit_bytes=VMEM_LIMIT
        ),
        name="forward",
    )(length_of, hidden, *gains, *weights, shared, out_grad, *tables, *kernels, *head_terms)


UNITS = 8


class BackwardIn(NamedTuple):
    length_ref: Any
    gain: Any
    gain2_part: Any
    conv_main: Any
    conv_shared: Any
    decay_log: Any
    step_bias: Any
    skip_gain: Any
    hidden: Any
    cosine: Any
    sine: Any
    w_shared: Any


class BackwardOut(NamedTuple):
    output: Any
    grad_in: Any
    gain: Any
    query: Any
    key: Any
    value: Any
    attn: Any
    z: Any
    x: Any
    step: Any
    shared: Any
    conv: Any
    conv_shared: Any
    decay: Any
    bias: Any
    skip: Any
    mamba: Any
    gain2: Any
    gate: Any
    up: Any
    down: Any


class BackwardScratch(NamedTuple):
    shared: Any
    hidden: Any
    cosine: Any
    sine: Any
    arrived: Any
    leaving: Any
    grad_y: Any
    grad_attn: Any
    conv_x: Any
    conv_bc: Any
    grad_x: Any
    grad_bc: Any
    steps: Any
    back: Any
    bc_back: Any
    grown_y: Any
    faded_x: Any
    state_back: Any
    key_sums: Any
    rows_sum: Any
    shared_y: Any
    shared_all: Any
    vector: Any
    vec_core: Any
    vec_x: Any
    vec_y: Any
    vec_z: Any
    head_terms: Any
    y_sems: Any
    small_sems: Any
    small_x_sems: Any
    small_z_sems: Any
    move_sems: Any


def backward_body(groups, halves, *refs):
    counts = [len(BackwardIn._fields), len(Kept._fields) - 1, len(BackwardOut._fields), 17]
    ends = np.cumsum(counts).tolist()
    r = BackwardIn(*refs[: ends[0]])
    h = Kept(*refs[ends[0] : ends[1]], None)
    out_hbm = BackwardOut(*refs[ends[1] : ends[2]])
    v = Kept(*refs[ends[2] : ends[3] - 1], *[None] * (counts[1] - 15))
    ffn_own = refs[ends[3] - 1]
    out = BackwardOut(*refs[ends[3] : ends[3] + counts[2]])
    rest = refs[ends[3] + counts[2] :]
    parts, from_core, rest = rest[:5], rest[5:10], rest[10:]
    from_x, chip_sums, rest = rest[:7], rest[7:14], rest[14:]
    from_z, relays, rest = rest[:8], rest[8:16], rest[16:]
    own_pairs, own_chip, rest = rest[:2], rest[2], rest[3:]
    s = BackwardScratch(*rest[:33])
    units = [
        dict(pair_sum=h.gate_pair, own_pair=own_pairs[0], from_x=from_x[0], chip_sum=chip_sums[0]),
        dict(pair_sum=h.up_pair, own_pair=own_pairs[1], from_x=from_x[1], chip_sum=chip_sums[1]),
        dict(chip_sum=own_chip),
    ] + [
        dict(part=parts[i], from_core=from_core[i], from_x=from_x[2 + i], chip_sum=chip_sums[2 + i])
        for i in range(5)
    ]
    for unit, ref, relay in zip(units, from_z, relays):
        unit["from_z"], unit["relay"] = ref, relay
    scatter = Scatter(units, groups, halves, rest[33:])
    move = Mover(s.move_sems)
    g, hi, c, t = place()
    own, model = r.hidden.shape
    length = 2 * own
    inner, q_width = out.x.shape[1], out.query.shape[1]
    kv_width, step_width = out.key.shape[1], out.step.shape[0]
    tiles, q_tiles = inner // LANES, q_width // LANES
    narrow_width = q_width + 2 * LANES
    other_y = (g, hi * 2 + c, 1 - t)
    devices = scatter.devices + [other_y]
    mine = pl.ds(pl.multiple_of(t * own, own), own)
    other = pl.ds(pl.multiple_of((1 - t) * own, own), own)
    greet(devices)

    def load(*names):
        for name in names:
            move.start(name, getattr(h, name), getattr(v, name))

    move.start("down_chip", h.down_chip, own_chip)
    load("mix_grad", "mix", "w_mix", "bc_padded", "step_in", "x_padded", "z_proj", "scanned")
    move.start("cosine", r.cosine, s.cosine)
    move.start("sine", r.sine, s.sine)
    load("normed", "qr", "kv", "probs", "states", "w_in")
    move.start("hidden", r.hidden, s.hidden)
    move.start("shared", r.w_shared, s.shared)
    move.start("ffn_own", h.ffn_part.at[mine, :], ffn_own)
    load("resid", "resid_grad")
    pick_heads(s.head_terms, (r.decay_log, r.step_bias, r.skip_gain), t)
    head_terms = s.head_terms
    greeted(devices)
    scatter.send_x(0)
    scatter.send_x(1)
    move.wait("down_chip")
    scatter.send_z(2)
    ffn_copy = scatter.start(
        remote(
            h.ffn_part.at[other, :], s.arrived.at[0], s.y_sems.at[0, 0], s.y_sems.at[1, 0], other_y
        )
    )
    count = r.length_ref[0]
    span = 256

    def give(*names):
        for name in names:
            move.start((name,), getattr(out, name), getattr(out_hbm, name))


    def weight_grads(part, left, right, cols, width):
        _, _, _, rows, _ = part.shape
        per = span // (2 * rows)

        def one(i, carry):
            at = pl.ds(pl.multiple_of(i * span, span), span)
            value = low(dot_tn(left[:, at], right[:, cols])).reshape(per, 2, rows, width)
            for k in range(per):
                at = i * per + k
                part[at // halves, lax.rem(at, halves)] = value[k]
            return carry

        lax.fori_loop(0, model // span, one, 0)

    move.wait("mix_grad", "mix")
    weight_grads(parts[0], v.mix_grad, v.mix, slice(None), q_width + inner)
    scatter.send(3)
    move.wait("w_mix")
    grad = dot(v.mix_grad[...], v.w_mix[...])
    s.grad_attn[...] = low(grad[:, :q_width])
    s.grad_y[...] = grad[:, q_width:]
    move.wait("bc_padded", "step_in", "x_padded")
    row = lax.broadcasted_iota(jnp.int32, (length, 1), 0)
    step_pre = v.step_in[...]
    softplus = jnp.maximum(step_pre, 0.0) + jnp.log(1.0 + jnp.exp(-jnp.abs(step_pre)))
    s.steps[...] = jnp.where(row < count, softplus, 0.0)
    channel = t * inner

    def taps_of(j):
        return r.conv_main[:, pl.ds(pl.multiple_of(channel + j * LANES, LANES), LANES)]

    for j in range(2 * NSTATE // LANES):
        cols = slice(j * LANES, (j + 1) * LANES)
        pre = causal_conv(v.bc_padded, r.conv_shared[:, cols], length, cols)
        s.conv_bc[:, cols] = pre * sigmoid(pre)
    scatter.core_stage(3)
    scatter.send_x(3)
    move.wait("z_proj", "scanned", "normed")
    skip_sum = jnp.zeros((1, LANES), F32)
    for j in range(tiles):
        cols = slice(j * LANES, (j + 1) * LANES)
        pre = causal_conv(v.x_padded, taps_of(j), length, cols)
        conv = pre * sigmoid(pre)
        s.conv_x[:, cols] = conv
        gate = v.z_proj[:, cols]
        sig = sigmoid(gate)
        grad = s.grad_y[:, cols]
        value = v.scanned[:, cols] + spread(head_terms[2:3, :], j) * conv
        at = narrow_width + inner + j * LANES
        s.back[:, at : at + LANES] = low(grad * value * sig * (1.0 + gate * (1.0 - sig)))
        grad = grad * gate * sig
        s.grad_y[:, cols] = grad
        s.rows_sum[j : j + 1, :] = column_sum(grad * conv)
    for j in range(tiles):
        skip_sum = skip_sum + head_sum(s.rows_sum[0:8, :], j)[j : j + 1, :]
    weight_grads(parts[1], v.normed, s.back, slice(narrow_width + inner, None), inner)
    scatter.send(4)
    move.wait("qr", "kv", "probs", "cosine", "sine")

    is_key = first_head(length)
    zero = jnp.zeros((), BF16)
    s.key_sums[...] = jnp.zeros_like(s.key_sums)

    def attend(j):
        tile = slice(j * LANES, (j + 1) * LANES)
        keys = [jnp.where(is_key, v.kv[...], zero)]
        keys.append(low(pltpu.roll(wide(keys[0]), HEAD, 1)))
        held = [None, jnp.where(is_key, zero, v.kv[...])]
        held[0] = low(pltpu.roll(wide(held[1]), HEAD, 1))
        for i in range(length // BLOCK):
            rows, upto = slice(i * BLOCK, (i + 1) * BLOCK), (i + 1) * BLOCK
            left = first_head(BLOCK)
            query, grad = v.qr[rows, tile], s.grad_attn[rows, tile]
            total = jnp.zeros((BLOCK, LANES), F32)
            for e in range(2):
                prob_low = v.probs[2 * j + e, rows, :upto]
                prob = wide(prob_low)
                prob_grad = dot_nt(grad, held[e][:upto])
                inside = jnp.sum(prob * prob_grad, axis=-1, keepdims=True)
                score_grad = low(prob * (prob_grad - inside))
                total = total + dot(score_grad, keys[e][:upto])
                side = left if e == 0 else jnp.logical_not(left)
                s.key_sums[0, :upto, :] += dot_tn(score_grad, jnp.where(side, query, zero))
                s.key_sums[1, :upto, :] += dot_tn(prob_low, jnp.where(side, grad, zero))
            total = total * HEAD**-0.5
            turned = total * s.cosine[rows, :] - half_swap(total) * s.sine[rows, :]
            s.back[rows, tile] = low(turned)

    scatter.relay(2)
    for j in range(q_tiles):
        attend(j)
        if j == 0:
            scatter.core_stage(4)
    key_grad = s.key_sums[0] + pltpu.roll(s.key_sums[0], HEAD, 1)
    key_grad = key_grad * HEAD**-0.5
    value_grad = s.key_sums[1] + pltpu.roll(s.key_sums[1], HEAD, 1)
    key_grad = key_grad * s.cosine[...] - half_swap(key_grad) * s.sine[...]
    s.back[:, q_width : q_width + LANES] = low(jnp.where(is_key, key_grad, value_grad))
    scatter.x_stage(0)
    scatter.send_z(0)
    move.wait("states")

    rate = -jnp.exp(head_terms[0:1, :])
    s.state_back[...] = jnp.zeros_like(s.state_back)
    upper = triangle(False)
    nblocks = length // BLOCK

    def scan_block(n, carry):
        rate_sum, bias_sum = carry
        i = nblocks - 1 - n
        rows = pl.ds(pl.multiple_of(i * BLOCK, BLOCK), BLOCK)
        step = s.steps[rows, :]
        total = exact_dot(triangle().astype(F32), step * rate)
        total_t = total.T
        last = total[BLOCK - 1 : BLOCK, :]
        grown, rest = jnp.exp(total), jnp.exp(last - total)
        b_mat, c_mat = split(s.conv_bc[rows, :NSTATE]), split(s.conv_bc[rows, NSTATE:])
        b_low, c_low = b_mat[0], c_mat[0]
        inner_t = jnp.where(upper, split_dot_nt(b_mat, c_mat), 0.0)
        state_mat = split(s.state_back[...])
        state_low = state_mat[0]
        crossed = split_dot(b_mat, state_mat)
        after = v.states[jnp.minimum(i + 1, nblocks - 1)] * s.state_back[...]
        left = first_head(BLOCK)
        inner_grad = jnp.zeros((BLOCK, BLOCK), F32)
        total_grad = jnp.zeros((BLOCK, LANES), F32)
        step_grad = jnp.zeros((BLOCK, LANES), F32)
        last_grad = jnp.zeros((8, LANES), F32)
        pulled = []
        for j in range(tiles):
            cols = slice(j * LANES, (j + 1) * LANES)
            conv, grad = s.conv_x[rows, cols], s.grad_y[rows, cols]
            step_wide, grown_wide, rest_wide = spread(step, j), spread(grown, j), spread(rest, j)
            stepped = step_wide * conv
            grad_low = low(grad)
            mixing = []
            for e, head in enumerate((2 * j, 2 * j + 1)):
                gap = jnp.minimum(total_t[head : head + 1, :] - total[:, head : head + 1], 0.0)
                decay = jnp.exp(gap)
                mixing.append(decay * inner_t)
                side = left if e == 0 else jnp.logical_not(left)
                inner_grad = inner_grad + decay * dot_nt(
                    low(jnp.where(side, stepped, 0.0)), grad_low
                )
            stacked = jnp.concatenate(
                [jnp.where(left, grad, 0.0), jnp.where(left, 0.0, grad)], axis=0
            )
            unstepped = split_dot(split(jnp.concatenate(mixing, axis=1)), split(stacked))
            unstepped = unstepped + rest_wide * crossed[:, cols]
            conv_grad = step_wide * unstepped
            total_grad = total_grad + head_sum(
                grad * v.scanned[rows, cols] - conv * conv_grad, j
            )
            step_grad = step_grad + head_sum(conv * unstepped, j)
            last_grad = last_grad + head_sum(
                jnp.broadcast_to(column_sum(after[:, cols]), (8, LANES)), j
            )
            s.grad_x[rows, cols] = conv_grad + spread(head_terms[2:3, :], j) * grad
            grown_grad = split(grown_wide * grad)
            s.grown_y[:, cols] = grown_grad[0]
            pulled.append(split_dot_tn(c_mat, grown_grad))
            s.faded_x[:, cols] = low(stepped * rest_wide)
        inner_low = low(jnp.where(upper, inner_grad, 0.0))
        s.grad_bc[rows, :NSTATE] = dot_nt(s.faded_x[...], state_low) + dot(inner_low, c_low)
        s.grad_bc[rows, NSTATE:] = dot_nt(s.grown_y[...], low(v.states[i])) + dot_tn(
            inner_low, b_low
        )
        for j in range(tiles):
            cols = slice(j * LANES, (j + 1) * LANES)
            fade = spread(grown[BLOCK - 1 : BLOCK, :], j)
            s.state_back[:, cols] = s.state_back[:, cols] * fade + pulled[j]
        slot = lax.broadcasted_iota(jnp.int32, (BLOCK, 1), 0)
        total_grad = total_grad + jnp.where(slot == BLOCK - 1, last_grad[0:1, :], 0.0)
        decay_grad = exact_dot(upper.astype(F32), total_grad)
        step_grad = step_grad + rate * decay_grad
        step_grad = jnp.where(i * BLOCK + slot < count, step_grad, 0.0)
        step_grad = step_grad * sigmoid(v.step_in[rows, :])
        s.back[rows, q_width + LANES : narrow_width] = low(step_grad)
        return rate_sum + column_sum(decay_grad * step), bias_sum + column_sum(step_grad)

    empty = jnp.zeros((1, LANES), F32)
    rate_sum, bias_sum = lax.fori_loop(0, nblocks, scan_block, (empty, empty))
    scatter.relay(0)

    s.vector[...] = jnp.zeros_like(s.vector)

    def place_row(at, value):
        s.vector[at : at + 1, :] = value

    def place_halves(at, gap, value):
        place_row(at, jnp.where(t == 0, value, 0.0))
        place_row(at + gap, jnp.where(t == 0, 0.0, value))

    place_halves(72, 1, rate_sum * rate)
    place_halves(74, 1, bias_sum)
    place_halves(76, 1, skip_sum)
    for j in range(model // LANES):
        place_row(8 + j, r.gain2_part[:, j * LANES : (j + 1) * LANES])
    s.grad_bc[length:, :] = jnp.zeros((8, 2 * NSTATE), F32)
    s.grad_x[length:, :] = jnp.zeros((8, inner), F32)

    def conv_back(padded, grads, taps, cols, store):
        pre = causal_conv(padded, taps, length, cols)
        sig = sigmoid(pre)
        grads[:length, cols] = grads[:length, cols] * sig * (1.0 + pre * (1.0 - sig))
        for i in range(4):
            store(i, column_sum(grads[:length, cols] * padded[5 + i : 5 + i + length, cols]))
        total = taps[3:4, :] * grads[:length, cols]
        for i in range(3):
            total = total + taps[i : i + 1, :] * grads[3 - i : 3 - i + length, cols]
        return low(total)

    for j in range(2 * NSTATE // LANES):
        cols = slice(j * LANES, (j + 1) * LANES)
        s.bc_back[:, cols] = conv_back(
            v.bc_padded,
            s.grad_bc,
            r.conv_shared[:, cols],
            cols,
            lambda i, value, j=j: place_row(16 + 2 * i + j, value),
        )
    weight_grads(parts[2], v.normed, s.bc_back, slice(None), 2 * NSTATE)
    scatter.send(5)
    for j in range(tiles):
        cols = slice(j * LANES, (j + 1) * LANES)
        at = narrow_width + j * LANES
        s.back[:, at : at + LANES] = conv_back(
            v.x_padded,
            s.grad_x,
            taps_of(j),
            cols,
            lambda i, value, j=j: place_halves(24 + 2 * tiles * i + j, tiles, value),
        )
    scatter.core_stage(5)
    scatter.send_x(5)
    scatter.send_x(4)
    scatter.x_stage(1)
    scatter.send_z(1)
    move.wait("w_in", "shared")
    s.leaving[...] = low(
        dot_nt(s.back[other, :], v.w_in[...]) + dot_nt(s.bc_back[other, :], s.shared[...])
    )
    sum_copy = scatter.start(
        remote(s.leaving, s.arrived.at[1], s.y_sems.at[0, 1], s.y_sems.at[1, 1], other_y)
    )
    weight_grads(parts[4], v.normed, s.back, slice(narrow_width, narrow_width + inner), inner)
    scatter.send(7)
    weight_grads(parts[3], v.normed, s.back, slice(0, narrow_width), narrow_width)
    scatter.send(6)
    own_grad = dot_nt(s.back[mine, :], v.w_in[...]) + dot_nt(s.bc_back[mine, :], s.shared[...])
    scatter.x_stage(3)
    scatter.send_z(3)
    scatter.relay(1)
    sum_copy.wait_recv()
    move.wait("hidden")
    values = wide(s.hidden[...])
    scale = rms_scale(values)
    grad = own_grad + wide(s.arrived[1])
    gain_row = column_sum(grad * values * scale)
    for j in range(model // LANES):
        place_row(j, gain_row[:, j * LANES : (j + 1) * LANES])
    s.vec_core[c] = s.vector[...]
    vec_copy = scatter.start(
        remote(
            s.vector,
            s.vec_core.at[c],
            s.small_sems.at[0, 0],
            s.small_sems.at[1, 0],
            scatter.other_core,
        )
    )
    move.wait("resid", "resid_grad", "ffn_own")
    weighted = grad * r.gain[...]
    out.grad_in[...] = low(
        v.resid_grad[...]
        + scale * weighted
        - values * (scale * scale * scale) * jnp.mean(weighted * values, axis=-1, keepdims=True)
    )
    vec_copy.wait_recv()
    s.vec_x[hi] = s.vec_core[0] + s.vec_core[1]
    vec_copies = [
        scatter.start(
            remote(
                s.vec_x.at[hi],
                s.vec_x.at[hi],
                s.small_x_sems.at[0, 0, k],
                s.small_x_sems.at[1, 0, k],
                scatter.across[k - 1],
            )
        )
        for k in range(1, halves)
    ]
    scatter.core_stage(7)
    scatter.send_x(7)
    scatter.x_stage(5)
    scatter.send_z(5)
    scatter.core_stage(6)
    scatter.send_x(6)
    ffn_copy.wait_recv()
    slot = t * own + lax.broadcasted_iota(jnp.int32, (own, 1), 0)
    total = v.resid[...] + wide(ffn_own[...]) + wide(s.arrived[0])
    out.output[...] = low(jnp.where(slot < count, total, 0.0))
    give("output", "grad_in")
    scatter.relay(3)
    out.down[...] = scatter.z_stage(2)
    give("down")
    scatter.relay(5)
    out.gate[...] = scatter.z_stage(0)
    give("gate")
    scatter.x_stage(4)
    scatter.send_z(4)
    s.shared_y[t] = scatter.z_stage(5)
    shared_copy = scatter.start(
        remote(
            s.shared_y.at[t],
            s.shared_y.at[t],
            s.small_sems.at[0, 2],
            s.small_sems.at[1, 2],
            other_y,
        )
    )
    shared_copy.wait_recv()
    s.shared_all[g, hi, c] = low(s.shared_y[0] + s.shared_y[1])
    shared_copies = [
        scatter.start(
            remote(
                s.shared_all.at[g, hi, c],
                s.shared_all.at[g, hi, c],
                s.small_z_sems.at[0, 1, j],
                s.small_z_sems.at[1, 1, j],
                scatter.along[j - 1],
            )
        )
        for j in range(1, groups)
    ]
    for copy in vec_copies:
        copy.wait_recv()
    total = s.vec_x[0]
    for k in range(1, halves):
        total = total + s.vec_x[k]
    s.vec_y[t] = total
    vec_copy = scatter.start(
        remote(
            s.vec_y.at[t], s.vec_y.at[t], s.small_sems.at[0, 1], s.small_sems.at[1, 1], other_y
        )
    )
    out.up[...] = scatter.z_stage(1)
    give("up")
    vec_copy.wait_recv()
    s.vec_z[g] = s.vec_y[0] + s.vec_y[1]
    vec_copies = [
        scatter.start(
            remote(
                s.vec_z.at[g],
                s.vec_z.at[g],
                s.small_z_sems.at[0, 0, j],
                s.small_z_sems.at[1, 0, j],
                scatter.along[j - 1],
            )
        )
        for j in range(1, groups)
    ]
    total = scatter.z_stage(3)
    out.attn[...] = total[:, :q_width]
    out.mamba[...] = total[:, q_width:]
    give("attn", "mamba")
    scatter.relay(4)
    scatter.x_stage(7)
    scatter.send_z(7)
    for copy in shared_copies:
        copy.wait_recv()
    shared_copies = [
        scatter.start(
            remote(
                s.shared_all.at[:, hi, c],
                s.shared_all.at[:, hi, c],
                s.small_x_sems.at[0, 1, k],
                s.small_x_sems.at[1, 1, k],
                scatter.across[k - 1],
            )
        )
        for k in range(1, halves)
    ]
    for copy in vec_copies:
        copy.wait_recv()
    total = s.vec_z[0]
    for j in range(1, groups):
        total = total + s.vec_z[j]
    out.gain[...] = total[0:8, :]
    out.gain2[...] = total[8:16, :]
    for i in range(4):
        for j in range(2 * NSTATE // LANES):
            at = 16 + 2 * i + j
            out.conv_shared[i : i + 1, j * LANES : (j + 1) * LANES] = total[at : at + 1, :]
        for j in range(2 * tiles):
            at = 24 + 2 * tiles * i + j
            out.conv[i : i + 1, j * LANES : (j + 1) * LANES] = total[at : at + 1, :]
    for ref, at in ((out.decay, 72), (out.bias, 74), (out.skip, 76)):
        ref[...] = jnp.concatenate(
            [total[at : at + 1, :step_width], total[at + 1 : at + 2, :step_width]], axis=1
        )
    give("gain", "gain2", "conv", "conv_shared", "decay", "bias", "skip")
    scatter.x_stage(6)
    scatter.send_z(6)
    scatter.relay(7)
    out.z[...] = scatter.z_stage(4)
    give("z")
    for copy in shared_copies:
        copy.wait_recv()
    shared_copy = scatter.start(
        remote(
            s.shared_all.at[:, :, c],
            s.shared_all.at[:, :, c],
            s.small_sems.at[0, 3],
            s.small_sems.at[1, 3],
            scatter.other_core,
        )
    )
    scatter.relay(6)
    out.x[...] = scatter.z_stage(7)
    give("x")
    shared_copy.wait_recv()

    def widen(i, carry):
        block = s.shared_all[i // (2 * halves), lax.rem(i // 2, halves), lax.rem(i, 2)]
        out.shared[i] = wide(block)
        return carry

    lax.fori_loop(0, groups * halves * 2, widen, 0)
    give("shared")
    total = scatter.z_stage(6)
    out.query[...] = total[:, :q_width]
    out.key[...] = total[:, q_width : q_width + kv_width]
    out.value[...] = total[:, q_width + kv_width : q_width + 2 * kv_width]
    out.step[...] = total[:, q_width + LANES :].T[:step_width, :]
    give("query", "key", "value", "step")
    scatter.drain()
    move.drain()


def backward(
    length_of, hidden, gain, gain2_part, saved, w_shared, kernels, head_terms, tables, widths
):
    groups, halves = lax.axis_size("grp"), lax.axis_size("fsdp") // 2
    q_width, kv_width, step_width = widths
    own, model = hidden.shape
    length = 2 * own
    narrow_width = q_width + 2 * LANES
    inner = (saved[0].shape[1] - narrow_width) // 2
    rows = model // (2 * groups * halves)
    ffn = saved[-1].shape[-1]
    inside = pl.BlockSpec(memory_space=pltpu.VMEM)
    anywhere = pl.BlockSpec(memory_space=pl.ANY)
    shape, vmem, dma = jax.ShapeDtypeStruct, pltpu.VMEM, pltpu.SemaphoreType.DMA
    outs = [
        shape((own, model), BF16),
        shape((own, model), BF16),
        shape((model // LANES, LANES), F32),
        shape((rows, q_width), F32),
        shape((rows, kv_width), F32),
        shape((rows, kv_width), F32),
        shape((rows, q_width), F32),
        shape((rows, inner), F32),
        shape((rows, inner), F32),
        shape((step_width, rows), F32),
        shape((2 * groups * halves, rows, 2 * NSTATE), F32),
        shape((4, 2 * inner), F32),
        shape((4, 2 * NSTATE), F32),
        shape((1, 2 * step_width), F32),
        shape((1, 2 * step_width), F32),
        shape((1, 2 * step_width), F32),
        shape((rows, inner), F32),
        shape((model // LANES, LANES), F32),
        shape((rows, ffn), F32),
        shape((rows, ffn), F32),
        shape((rows, ffn), F32),
    ]
    part_widths = [q_width + inner, inner, 2 * NSTATE, narrow_width, inner]
    x_widths = [ffn, ffn] + part_widths
    z_widths = [ffn] * 3 + part_widths
    vector = (80, LANES)
    others = max(halves - 1, 1)
    scratch = (
        [vmem(a.shape, a.dtype) for a in saved[:16]]
        + [vmem((own, model), BF16)]
        + [vmem(a.shape, a.dtype) for a in outs]
        + [vmem((groups, halves, 2, rows, w), BF16) for w in part_widths]
        + [vmem((groups, halves, rows, w), BF16) for w in part_widths]
        + [vmem((others, groups, rows, w), BF16) for w in x_widths]
        + [vmem((groups, rows, w), BF16) for w in x_widths]
        + [vmem((groups - 1, rows, w), BF16) for w in z_widths]
        + [vmem((rows, w), BF16) for w in z_widths]
        + [vmem((groups, rows, ffn), BF16)] * 3
        + [
            vmem((model, 2 * NSTATE), BF16),
            vmem((own, model), BF16),
            vmem((length, LANES), F32),
            vmem((length, LANES), F32),
            vmem((2, own, model), BF16),
            vmem((own, model), BF16),
            vmem((length, inner), F32),
            vmem((length, q_width), BF16),
            vmem((length, inner), F32),
            vmem((length, 2 * NSTATE), F32),
            vmem((length + 8, inner), F32),
            vmem((length + 8, 2 * NSTATE), F32),
            vmem((length, LANES), F32),
            vmem((length, narrow_width + 2 * inner), BF16),
            vmem((length, 2 * NSTATE), BF16),
            vmem((BLOCK, inner), BF16),
            vmem((BLOCK, inner), BF16),
            vmem((NSTATE, inner), F32),
            vmem((2, length, LANES), F32),
            vmem((8, LANES), F32),
            vmem((2, rows, 2 * NSTATE), F32),
            vmem((groups, halves, 2, rows, 2 * NSTATE), BF16),
            vmem(vector, F32),
            vmem((2,) + vector, F32),
            vmem((halves,) + vector, F32),
            vmem((2,) + vector, F32),
            vmem((groups,) + vector, F32),
            vmem((8, LANES), F32),
            dma((2, 2)),
            dma((2, 4)),
            dma((2, 2, halves)),
            dma((2, 2, groups)),
            dma((23 + len(outs),)),
        ]
        + scatter_sems(UNITS, groups, halves)
    )
    return pl.pallas_call(
        partial(backward_body, groups, halves),
        out_shape=outs,
        in_specs=[pl.BlockSpec(memory_space=pltpu.SMEM)]
        + [inside] * 7
        + [anywhere] * (4 + len(saved)),
        out_specs=[anywhere] * len(outs),
        scratch_shapes=scratch,
        compiler_params=pltpu.CompilerParams(
            collective_id=1, has_side_effects=True, vmem_limit_bytes=VMEM_LIMIT
        ),
        name="backward",
    )(length_of, gain, gain2_part, *kernels, *head_terms, hidden, *tables, w_shared, *saved)


def emit_body(*refs):
    count = len(refs) // 3
    sources, targets, held = refs[:count], refs[count : 2 * count], refs[2 * count : 3 * count]
    sems = refs[3 * count]
    arriving = [
        pltpu.make_async_copy(source, at, sems.at[0, i])
        for i, (source, at) in enumerate(zip(sources, held))
    ]
    leaving = [
        pltpu.make_async_copy(at, target, sems.at[1, i])
        for i, (at, target) in enumerate(zip(held, targets))
    ]
    for copy in arriving:
        copy.start()
    for arrived, copy in zip(arriving, leaving):
        arrived.wait()
        copy.start()
    for copy in leaving:
        copy.wait()


def emit(arrays):
    anywhere = pl.BlockSpec(memory_space=pl.ANY)
    return pl.pallas_call(
        emit_body,
        out_shape=[jax.ShapeDtypeStruct(a.shape, a.dtype) for a in arrays],
        in_specs=[anywhere] * len(arrays),
        out_specs=[anywhere] * len(arrays),
        scratch_shapes=[pltpu.VMEM(a.shape, a.dtype) for a in arrays]
        + [pltpu.SemaphoreType.DMA((2, len(arrays)))],
        compiler_params=pltpu.CompilerParams(vmem_limit_bytes=VMEM_LIMIT),
        name="emit",
    )(*arrays)


def local(
    hidden_in,
    lengths,
    norm1_gain,
    w_query,
    key_weight,
    value_weight,
    w_attn_out,
    w_mamba_z,
    w_mamba_x,
    w_step,
    w_shared,
    conv_main,
    conv_shared,
    decay_log,
    step_bias,
    skip_gain,
    w_mamba_out,
    norm2_gain,
    w_ffn_gate,
    w_ffn_up,
    w_ffn_down,
    out_grad,
):
    own, model = hidden_in.shape
    step_width = w_step.shape[1]
    head_terms = [v.reshape(1, -1) for v in (decay_log, step_bias, skip_gain)]
    tables = rotary_tables(2 * own)
    gain1, gain2 = norm1_gain.reshape(1, model), norm2_gain.reshape(1, model)
    kernels = (conv_main, conv_shared)
    weights = (w_query, key_weight.T, value_weight.T, w_step.T, w_mamba_x, w_mamba_z)
    weights += (w_attn_out, w_mamba_out, w_ffn_down, w_ffn_gate, w_ffn_up)
    *saved, gain2_part = forward(
        lengths,
        hidden_in,
        out_grad,
        (gain1, gain2),
        weights,
        w_shared,
        kernels,
        head_terms,
        tables,
    )
    outs = backward(
        lengths,
        hidden_in,
        gain1,
        gain2_part,
        saved,
        w_shared,
        kernels,
        head_terms,
        tables,
        (w_query.shape[1], key_weight.shape[1], step_width),
    )
    outs = list(emit(outs))
    outs[9] = outs[9].T
    for i in (2, 13, 14, 15, 17):
        outs[i] = outs[i].reshape(-1)
    outs[10] = outs[10].reshape(model, -1)
    return tuple(outs)


def solution(mesh):
    rows, whole, weight = P(("grp", "fsdp", "tp"), None), P(), P("fsdp", "tp")
    grad = P(("grp", "fsdp"), "tp")
    return jax.shard_map(
        local,
        mesh=mesh,
        in_specs=(rows, P(("grp", "fsdp")), whole)
        + (weight,) * 7
        + (whole,) * 6
        + (weight, whole)
        + (weight,) * 3
        + (rows,),
        out_specs=(rows, rows, whole)
        + (grad,) * 7
        + (whole,) * 6
        + (grad, whole)
        + (grad,) * 3,
        check_vma=False,
    )
```
